32 devices in a mesh: lat: 8 (over y, x, core), lon: 4 (over z).
Axes of the slice: x: 2, y: 2, z: 4, core: 2. Of those that a mesh axis runs over, the one named last changes fastest.
Arguments:
- state: float32 [3, 384, 49152], P(None, 'lat', 'lon'), may hold values from -6 to 6
- sigma: float32 [3, 384, 768], P(None, 'lat', 'lon'), may hold values from 0.3 to 3
- vert: float32 [3, 64, 64], replicated, may hold values from -0.75 to 0.75
- bal_temp: float32 [64, 64], replicated, may hold values from -0.75 to 0.75
- chi_coef: float32 [64], replicated, may hold values from -1 to 1
- scales: float32 [8], replicated, may hold values from 6 to 40
- classes: int32 [192], replicated, may hold values from 0 to 7
- owner: int32 [192], replicated, may hold values from 0 to 31, as said below
Outputs:
- applied: float32 [3, 384, 49152], P(None, 'lat', 'lon')
- slab_energy: float32 [32, 7], P(('lat', 'lon'))
The draws below stay inside these ranges and needn't reach their ends.
Inputs may be any that keep to these rules, and one draw needn't show every extreme that they name: `owner`: every device owns at most 7 slabs, and some device owns exactly 7.
All inputs are finite; a program needn't handle non-finite values.
Results may differ from the reference program's by a relative error of at most 0.0003.
Values sent between devices are 32-bit elements; how exact they have to be, the bound alone decides.
No kernel may reach another device: no remote copies, remote signals or barrier semaphores. Data moves between devices by JAX's collectives and lax.ppermute only.
A program may use at most 128 MiB of HBM per device.

```python
import math
import jax
import jax.numpy as jnp
from jax import lax

NLAT = 384
NLON = 768
L = 64
NVAR = 3
NCLASS = 8
CAP = 7
N_LAT = 8
N_LON = 4


def draw_owner(key, part):
    slots = N_LAT * N_LON * CAP
    count = NVAR * L
    perm = jax.random.permutation(jax.random.fold_in(key, 11), slots)
    rank = jnp.argsort(perm)
    chosen = perm[0] // CAP
    score = rank + jnp.where(jnp.arange(slots) // CAP == chosen, -slots, 0)
    picked = jnp.argsort(score)[:count]
    order = jax.random.permutation(jax.random.fold_in(key, 12), count)
    return (picked[order] // CAP).astype(jnp.int32)


def place_ends(values, key, smallest, high):
    extent = values.shape
    index_at = [jax.random.randint(jax.random.fold_in(key, axis), (), 0, extent[axis]) for axis in range(len(extent))]
    values = values.at[tuple(index_at)].set(smallest)
    longest = extent.index(max(extent))
    index_at[longest] = (index_at[longest] + 1) % extent[longest]
    return values.at[tuple(index_at)].set(high)


def block_levels(rng, extent, shards, smallest, top_value):
    level = 1.0
    for axis_at, parts in shards:
        steps = jax.random.uniform(jax.random.fold_in(jax.random.fold_in(rng, 6), axis_at), (parts,), jnp.float32, smallest / len(shards), top_value / len(shards))
        level = level * jnp.repeat(jnp.exp(steps), extent[axis_at] // parts).reshape((-1,) + (1,) * (len(extent) - 1 - axis_at))
    return level


def noise(own_key, shape, width, bound, shards=(), kind=jnp.bfloat16):
    drawn = width * jax.random.normal(own_key, shape, jnp.float32)
    if shards:
        drawn = drawn * block_levels(own_key, shape, shards, -0.22, 0.18)
    return jnp.clip(drawn, -bound, bound).astype(kind)


def setup_inputs(seed: int = 0) -> dict:
    arg_keys = jax.random.split(jax.random.key(seed), 9)
    state = noise(arg_keys[0], (NVAR, NLAT, NLON * L), 1.0, 6.0, ((1, 8), (2, 4)), jnp.float32)
    sigma = jnp.clip(jnp.exp(math.log(3.0) - 2.3025851 * jax.random.uniform(arg_keys[1], (NVAR, NLAT, NLON), jnp.float32) ** block_levels(arg_keys[1], (NVAR, NLAT, NLON), ((1, 8), (2, 4)), -0.2, 0.2)), 0.3, 3.0)
    vert = noise(arg_keys[2], (NVAR, L, L), L ** -0.5, 0.75, (), jnp.float32)
    bal_temp = noise(arg_keys[3], (L, L), L ** -0.5, 0.75, (), jnp.float32)
    chi_coef = jnp.clip(jax.random.uniform(arg_keys[4], (L,), jnp.float32, -1.0, 1.0), -1.0, 1.0)
    scales = jnp.clip(jnp.exp(jax.random.uniform(arg_keys[5], (NCLASS,), jnp.float32, math.log(6.0), math.log(40.0))), 6.0, 40.0)
    classes = place_ends(jax.random.randint(arg_keys[6], (NVAR * L,), 0, NCLASS), jax.random.fold_in(arg_keys[6], 1), 0, NCLASS - 1).astype(jnp.int32)
    owner = draw_owner(jax.random.fold_in(arg_keys[8], 71), 0)
    return {"state": state, "sigma": sigma, "vert": vert, "bal_temp": bal_temp, "chi_coef": chi_coef, "scales": scales, "classes": classes, "owner": owner}


def laplace(field):
    pad_spec = [(0, 0)] * (field.ndim - 2) + [(1, 1), (1, 1)]
    padded = jnp.pad(field, pad_spec)
    return (4.0 * field - padded[..., 2:, 1:-1] - padded[..., :-2, 1:-1]
            - padded[..., 1:-1, 2:] - padded[..., 1:-1, :-2])


def recur(field, coef, axis, backward):
    moved = jnp.moveaxis(field, axis, 0)
    if backward:
        moved = moved[::-1]
    decay = coef[:, None]

    def step(state, item):
        nxt = decay * state + (1.0 - decay) * item
        return nxt, nxt

    start = jnp.zeros(moved.shape[1:], jnp.float32)
    _, out = lax.scan(step, start, moved)
    if backward:
        out = out[::-1]
    return jnp.moveaxis(out, 0, axis)


def smooth(field, coef, amp):
    field = recur(field, coef, 2, False)
    field = recur(field, coef, 2, True)
    field = recur(field, coef, 1, False)
    field = recur(field, coef, 1, True)
    return field * amp[:, None, None]


def reference(state, sigma, vert, bal_temp, chi_coef, scales, classes, owner):
    highest = lax.Precision.HIGHEST
    field = state.reshape(NVAR, NLAT, NLON, L).transpose(0, 3, 1, 2)
    psi = field[0]
    chi = field[1]
    temp = field[2]
    folded = jnp.einsum('lk,lij->kij', bal_temp, temp, precision=highest)
    adj_psi = psi + chi_coef[:, None, None] * chi + laplace(folded)
    scaled = jnp.stack([adj_psi, chi, temp]) * sigma[:, None]
    w = jnp.einsum('vkl,vkij->vlij', vert, scaled, precision=highest)
    length = jnp.take(scales, classes)
    coef = jnp.exp(-1.0 / length).reshape(NVAR, L)
    amp = (length ** 0.75).reshape(NVAR, L)

    def per_var(items):
        slabs, decay, gain = items
        ctrl = smooth(slabs, decay, gain)
        energy = jnp.mean(ctrl * ctrl, axis=(1, 2))
        return smooth(ctrl, decay, gain), energy

    back, energy = lax.map(per_var, (w, coef, amp))
    count = NVAR * L
    index = jnp.arange(count, dtype=jnp.int32)
    same = (owner[:, None] == owner[None, :]) & (index[None, :] < index[:, None])
    slot = jnp.sum(same.astype(jnp.int32), axis=1).astype(jnp.int32)
    devices = N_LAT * N_LON
    flat = jnp.zeros((devices * CAP,), jnp.float32).at[owner * CAP + slot].set(energy.reshape(-1))
    slab_energy = flat.reshape(devices, CAP)
    z = jnp.einsum('vlk,vkij->vlij', vert, back, precision=highest) * sigma[:, None]
    out_chi = z[1] + chi_coef[:, None, None] * z[0]
    out_temp = z[2] + jnp.einsum('lk,kij->lij', bal_temp, laplace(z[0]), precision=highest)
    mixed = jnp.stack([z[0], out_chi, out_temp])
    applied = mixed.transpose(0, 2, 3, 1).reshape(NVAR, NLAT, NLON * L)
    return applied, slab_energy
```

```python
import functools

import jax
import jax.numpy as jnp
from jax import lax
from jax.experimental import pallas as pl
from jax.experimental.pallas import tpu as pltpu
from jax.sharding import PartitionSpec as P

highest = lax.Precision.HIGHEST
f32 = jnp.float32
bf16 = jnp.bfloat16
LANES = 128
PAIRS = 8
LIMIT = 60 * 1024 * 1024


def params():
    return pltpu.CompilerParams(vmem_limit_bytes=LIMIT)


def full(shape):
    return pl.BlockSpec(shape, lambda g: (0,) * len(shape))


def swap(x):
    return pltpu.roll(x, 64, x.ndim - 1)


def low_lanes(shape):
    return lax.broadcasted_iota(jnp.int32, shape, len(shape) - 1) < 64


def halves(x):
    hi = x.astype(bf16)
    return hi, (x - hi.astype(f32)).astype(bf16)


def dot(x, y):
    return jnp.dot(x, y, preferred_element_type=f32)


def product(x, wh, wl):
    hi, lo = halves(x)
    return dot(hi, wh) + dot(lo, wh) + dot(hi, wl)


def expand(mat, mixed):
    wide = jnp.concatenate([mat, mat], axis=1)
    wide = jnp.concatenate([wide, wide], axis=0)
    src = lax.broadcasted_iota(jnp.int32, (256, 256), 0) // 64
    dst = lax.broadcasted_iota(jnp.int32, (256, 256), 1) // 64
    if mixed:
        src = jnp.where(src == 1, 2, jnp.where(src == 2, 1, src))
    return halves(jnp.where(src == dst, wide, 0.0))


def constants(length, decay, m):
    span = jnp.exp(-float(m) / length)
    d = 1.0 - decay * decay
    k1 = decay * (1.0 - span * span) / d
    k2 = (m * span - decay * decay * (span - span * span * span) / d) / d
    tail = decay * decay * (1.0 + span * span) * (1.0 - span * span) / d
    k3 = decay / (d * d) * (1.0 - (2.0 * m + 1.0) * span * span + tail)
    return span, k1, k2, k3


def responses(length, decay, m):
    j = lax.broadcasted_iota(jnp.int32, (m, LANES), 0).astype(f32)
    up = jnp.exp(-j / length)
    down = jnp.exp(-(m - j) / length)
    span = jnp.exp(-float(m) / length)
    d = 1.0 - decay * decay
    diff = up - span * down
    g3 = decay * diff / d
    g2 = ((m - j) * down - decay * decay * (span * up - span * span * down) / d) / d
    part = decay * decay * (1.0 + span * span) * diff / d
    g1 = decay / (d * d) * ((j + 1.0) * up - (2.0 * m + 1.0 - j) * span * down + part)
    return g1, g2, g3, down


def solve_carries(n, edge, const, me):
    span, k1, k2, k3 = const
    first = edge(0, 0)
    zero = jnp.zeros_like(first)
    e1 = [first] + [edge(t, 0) for t in range(1, n)]
    c1, c2, c3, c4 = ([None] * n for _ in range(4))
    c = zero
    for t in range(n):
        c1[t] = c
        c = e1[t] + span * c
    c = zero
    for t in reversed(range(n)):
        c2[t] = c
        c = edge(t, 1) + k1 * c1[t] + span * c
    c = zero
    for t in range(n):
        c3[t] = c
        c = edge(t, 2) + k2 * c1[t] + k1 * c2[t] + span * c
    c = zero
    for t in reversed(range(n)):
        c4[t] = c
        c = edge(t, 3) + k3 * c1[t] + k2 * c2[t] + k1 * c3[t] + span * c
    out = []
    for cs in (c1, c2, c3, c4):
        mine = cs[0]
        for t in range(1, n):
            mine = jnp.where(me == t, cs[t], mine)
        out.append(mine)
    return out


def cascade(count, load, store, decay, start):
    step = 8
    edges = []
    for stage in range(4):
        back = stage % 2 == 1

        def body(b, states, back=back):
            base = (count // step - 1 - b) * step if back else b * step
            order = range(step - 1, -1, -1) if back else range(step)
            for o in order:
                new = [decay_k * s + x for decay_k, s, x in zip(decay, states, load(base + o))]
                store(base + o, new)
                states = new
            return tuple(states)

        states = lax.fori_loop(0, count // step, body, tuple(start))
        edges.append(list(states))
    return edges


def filter_tile(u_ref, k0, nv, rows, decay):
    count = u_ref.shape[2]
    zero = jnp.zeros((count, LANES), f32)

    def load(i):
        return [u_ref[k, i] for k in range(nv)]

    def store(i, values):
        for k in range(nv):
            u_ref[k, i] = values[k]

    return cascade(rows, load, store, decay, [zero] * nv)


def prepare_mats(mats, wh, wl, mixed):
    for k in range(mats.shape[0]):
        hi, lo = expand(mats[k], mixed[k])
        wh[k] = hi
        wl[k] = lo


def sigma_tile(sig, idx):
    return jnp.take_along_axis(sig, idx, axis=1)


def lat_finish(vs, rows, prm, results, w_ref, u_ref, e_ref):
    for k, res in enumerate(results):
        for p in range(PAIRS):
            part = res[p * rows : (p + 1) * rows]
            w_ref[k, 2 * p] = part[:, :LANES]
            w_ref[k, 2 * p + 1] = part[:, LANES:]
        u_ref[k] = jnp.swapaxes(w_ref[k], 0, 1)
    decay = [prm[v, 1:2, :] for v in vs]
    edges = filter_tile(u_ref, 0, len(vs), rows, decay)
    for e in range(4):
        for k in range(len(vs)):
            e_ref[k, e] = edges[e][k]


def lat_plain(vs, rows, prm, sig, mats, b1lo, b1hi, b2lo, b2hi, w_ref, u_ref, e_ref, xs, wh, wl):
    g = pl.program_id(0)

    @pl.when(g == 0)
    def _():
        prepare_mats(mats, wh, wl, (True, True))

    lane = lax.broadcasted_iota(jnp.int32, (rows, LANES), 1)
    high = (lane >= 64).astype(jnp.int32)
    for p in range(PAIRS):
        at = slice(p * rows, (p + 1) * rows)
        cols = slice(p * LANES, (p + 1) * LANES)
        idx = 2 * (g * PAIRS + p) + high
        for k, sides in enumerate(((b1lo, b1hi), (b2lo, b2hi))):
            for side in range(2):
                s = sigma_tile(sig[vs[k], side], idx)
                xs[k, at, side * LANES : (side + 1) * LANES] = sides[side][0, :, cols] * s
    results = [product(xs[k], wh[k], wl[k]) for k in range(2)]
    lat_finish(vs, rows, prm, results, w_ref, u_ref, e_ref)


def lat_balance(
    rows, pairs, prm, sig, mats, plo, phi, clo, chi, temp, north, south, west, east,
    w_ref, u_ref, e_ref, xs, wh, wl,
):
    g = pl.program_id(0)

    @pl.when(g == 0)
    def _():
        prepare_mats(mats, wh, wl, (True, True))

    lane = lax.broadcasted_iota(jnp.int32, (rows, LANES), 1)
    row_id = lax.broadcasted_iota(jnp.int32, (rows, LANES), 0)
    high = (lane >= 64).astype(jnp.int32)
    chi_row = prm[0, 2:3, :]
    last = 2 * pairs - 1

    def at_tile(m):
        return pl.ds(pl.multiple_of(m * LANES, LANES), LANES)

    def laplace(m):
        x = temp[0, :, at_tile(m)]
        left = jnp.where(m == 0, swap(west[...]), temp[0, :, at_tile(jnp.maximum(m - 1, 0))])
        right = jnp.where(m == last, east[...], temp[0, :, at_tile(jnp.minimum(m + 1, last))])
        beside = swap(x + jnp.where(lane >= 64, left, right))
        above = jnp.where(row_id == 0, north[:, at_tile(m)], pltpu.roll(x, 1, 0))
        below = jnp.where(row_id == rows - 1, south[:, at_tile(m)], pltpu.roll(x, rows - 1, 0))
        return 4.0 * x - beside - above - below

    for p in range(PAIRS):
        at = slice(p * rows, (p + 1) * rows)
        cols = slice(p * LANES, (p + 1) * LANES)
        m = g * PAIRS + p
        for side, (pr, cr) in enumerate(((plo, clo), (phi, chi))):
            s = sigma_tile(sig[0, side], 2 * m + high)
            to = slice(side * LANES, (side + 1) * LANES)
            xs[0, at, to] = (pr[0, :, cols] + chi_row * cr[0, :, cols]) * s
            xs[1, at, to] = laplace(m + side * pairs) * s
    result = product(xs[0], wh[0], wl[0]) + product(xs[1], wh[1], wl[1])
    lat_finish((0,), rows, prm, [result], w_ref, u_ref, e_ref)


def lon_kernel(vs, n_lat, rows, rb, ext, place, prm, u_ref, gathered, *rest):
    if ext:
        o_ref, ox_ref, el_ref, es_ref, carry, resp = rest
    else:
        o_ref, el_ref, es_ref, carry, resp = rest
    nv = len(vs)
    g = pl.program_id(0)
    half = u_ref.shape[2]
    me = place[0]

    @pl.when(g == 0)
    def _():
        for k, v in enumerate(vs):
            length = prm[v, 0:1, :]
            decay = prm[v, 1:2, :]
            const = constants(length, decay, rows)

            def body(b, _, k=k, const=const):
                at = pl.ds(pl.multiple_of(b * 8, 8), 8)
                c = solve_carries(n_lat, lambda t, e: gathered[t, k, e, at, :], const, me)
                for e in range(4):
                    carry[k, e, at, :] = c[e]
                return 0

            lax.fori_loop(0, half // 8, body, 0)
            for e, r in enumerate(responses(length, decay, rows)):
                for s in range(rows // rb):
                    resp[s, k, e] = r[s * rb : (s + 1) * rb]

    def fix(b, _):
        at = pl.ds(pl.multiple_of(b * 8, 8), 8)
        for k in range(nv):
            c = [carry[k, e, at, :] for e in range(4)]
            lines = []
            for i in range(rb):
                y = u_ref[k, i, at, :]
                for e in range(4):
                    y = y + resp[g, k, e, i : i + 1, :] * c[e]
                lines.append(y)
            for q in range(rb // 8):
                block = jnp.stack(lines[q * 8 : (q + 1) * 8], axis=0)
                o_ref[k, at, q * 8 : (q + 1) * 8, :] = jnp.swapaxes(block, 0, 1)
            if ext:
                above = jnp.where(me > 0, c[2] + prm[vs[k], 1:2, :] * lines[0], 0.0)
                zero = jnp.zeros_like(above)
                block = jnp.stack([above, c[3]] + [zero] * 6, axis=0)
                ox_ref[at] = jnp.swapaxes(block, 0, 1)
        return 0

    lax.fori_loop(0, half // 8, fix, 0)

    decay = [prm[v, 1:2, :] for v in vs]

    def load(j):
        out = [o_ref[k, j] for k in range(nv)]
        return out + [ox_ref[j]] if ext else out

    def store(j, values):
        for k in range(nv):
            o_ref[k, j] = values[k]
        if ext:
            ox_ref[j] = values[nv]

    start = [jnp.zeros((rb, LANES), f32)] * nv
    if ext:
        start = start + [jnp.zeros((8, LANES), f32)]
        decay = decay + [decay[0]]
    edges = cascade(half, load, store, decay, start)
    for k in range(nv + ext):
        v = vs[min(k, nv - 1)]
        count = 8 if k == nv else rb
        at = pl.ds(rows, 8) if k == nv else pl.ds(pl.multiple_of(g * rb, 8), rb)
        kk = min(k, nv - 1)
        span, k1, k2, k3 = constants(prm[v, 0:1, :], prm[v, 1:2, :], half)
        low = low_lanes((count, LANES))
        e1, e2, e3, e4 = (edges[e][k] for e in range(4))
        c1 = jnp.where(low, 0.0, swap(e1))
        t1 = e1 + span * c1
        t2 = e2 + k1 * c1
        c2 = jnp.where(low, swap(t2), 0.0)
        t2 = t2 + span * c2
        t3 = e3 + k2 * c1 + k1 * c2
        c3 = jnp.where(low, 0.0, swap(t3))
        t3 = t3 + span * c3
        t4 = e4 + k3 * c1 + k2 * c2 + k1 * c3
        c4 = jnp.where(low, swap(t4), 0.0)
        t4 = t4 + span * c4
        es_ref[kk, 0, at, :] = jnp.where(low, t2, t1)
        es_ref[kk, 1, at, :] = jnp.where(low, t4, t3)
        for e, x in enumerate((e1, e2, e3, e4)):
            el_ref[kk, e, at, :] = x


def end_kernel(
    n_lon, rows, pairs, place, prm, sig, sigx, west, east, mats, balm,
    u0, ux, ua, w0, wa, el0, ela, es0, esa,
    out, energy, carry, resp, cols, zx, xs, wh, wl,
):
    g = pl.program_id(0)
    me = place[1]
    half = 2 * pairs
    wide = 2 * half * 64
    ext = rows + 8
    low8 = low_lanes((8, LANES))

    @pl.when(g == 0)
    def _():
        prepare_mats(mats, wh, wl, (True, True, True))
        hi, lo = expand(balm[0], False)
        wh[3] = hi
        wl[3] = lo
        energy[...] = jnp.zeros_like(energy)
        for v in range(3):
            length = prm[v, 0:1, :]
            decay = prm[v, 1:2, :]
            whole = constants(length, decay, 2 * half)
            span, k1, k2, k3 = constants(length, decay, half)
            sent, own, k = (es0, el0, 0) if v == 0 else (esa, ela, v - 1)
            count = ext if v == 0 else rows

            def body(b, _, v=v, whole=whole, half_c=(span, k1, k2, k3), sent=sent, own=own, k=k):
                span, k1, k2, k3 = half_c
                at = pl.ds(pl.multiple_of(b * 8, 8), 8)
                cache = {}

                def edge(t, e):
                    if (t, e // 2) not in cache:
                        x = sent[t, k, e // 2, at, :]
                        y = swap(x)
                        cache[t, e // 2] = (jnp.where(low8, y, x), jnp.where(low8, x, y))
                    return cache[t, e // 2][e % 2]

                d1, d2, d3, d4 = solve_carries(n_lon, edge, whole, me)
                e1, e2, e3, e4 = (own[k, e, at, :] for e in range(4))
                c1 = jnp.where(low8, d1, swap(e1 + span * d1))
                c2 = jnp.where(low8, swap(e2 + k1 * c1 + span * d2), d2)
                c3 = jnp.where(low8, d3, swap(e3 + k2 * c1 + k1 * c2 + span * d3))
                c4 = jnp.where(low8, swap(e4 + k3 * c1 + k2 * c2 + k1 * c3 + span * d4), d4)
                for e, c in enumerate((c1, c2, c3, c4)):
                    carry[v, e, at, :] = c
                if v == 0:
                    cols[0, at, :] = d3
                    cols[1, at, :] = d4
                return 0

            lax.fori_loop(0, count // 8, body, 0)
            for e, r in enumerate(responses(length, decay, half)):
                resp[v, e] = r
        first = u0[0, 0]
        for e in range(4):
            first = first + resp[0, e, 0:1, :] * carry[0, e, 0:rows, :]
        beside = jnp.where(me > 0, cols[0, 0:rows, :] + prm[0, 1:2, :] * first, 0.0)
        low = low_lanes((rows, LANES))
        lhs = jnp.where(low, beside, cols[1, 0:rows, :])
        lhs = jnp.concatenate([lhs, jnp.zeros_like(lhs)], axis=1)
        res = product(lhs, wh[0], wl[0])
        cols[0, 0:rows, :] = swap(res[:, :LANES] * swap(west[...]))
        cols[1, 0:rows, :] = res[:, LANES:] * swap(east[...])

    lane = lax.broadcasted_iota(jnp.int32, (rows, LANES), 1)
    high = (lane >= 64).astype(jnp.int32)
    chi_row = prm[0, 2:3, :]

    def at_tile(m):
        return pl.ds(pl.multiple_of(m * LANES, LANES), LANES)

    for v in range(3):
        u_ref, w_ref, k = (u0, w0, 0) if v == 0 else (ua, wa, v - 1)
        c = [carry[v, e, 0:rows, :] for e in range(4)]
        total = jnp.zeros((rows, LANES), f32)
        for p in range(2 * PAIRS):
            y = u_ref[k, p]
            jh = g * 2 * PAIRS + p
            for e in range(4):
                y = y + resp[v, e, pl.ds(jh, 1), :] * c[e]
            total = total + y * w_ref[k, p]
            at = slice((p // 2) * rows, (p // 2 + 1) * rows)
            to = slice((p % 2) * LANES, (p % 2 + 1) * LANES)
            xs[v, at, to] = y
        energy[v] += jnp.sum(total.reshape(rows // 8, 8, LANES), axis=0)
    c = [carry[0, e, rows:ext, :] for e in range(4)]
    pieces = []
    for p in range(2 * PAIRS):
        y = ux[p]
        jh = g * 2 * PAIRS + p
        for e in range(4):
            y = y + resp[0, e, pl.ds(jh, 1), :] * c[e]
        pieces.append(y)
    lhs = jnp.concatenate(
        [jnp.concatenate([pieces[2 * p], pieces[2 * p + 1]], axis=1) for p in range(PAIRS)], axis=0
    )
    res = product(lhs, wh[0], wl[0])
    high8 = 1 - low8.astype(jnp.int32)
    for p in range(PAIRS):
        m = g * PAIRS + p
        for side in range(2):
            s = sigma_tile(sigx[side], 2 * m + high8)
            part = res[p * 8 : (p + 1) * 8, side * LANES : (side + 1) * LANES]
            zx[:, at_tile(m + side * pairs)] = part * s
    results = [product(xs[v], wh[v], wl[v]) for v in range(3)]
    for p in range(PAIRS):
        m = g * PAIRS + p
        idx = 2 * m + high
        for side in range(2):
            at = at_tile(m + side * pairs)
            z = [
                results[v][p * rows : (p + 1) * rows, side * LANES : (side + 1) * LANES]
                * sigma_tile(sig[v, side], idx)
                for v in range(3)
            ]
            out[0, :, at] = z[0]
            out[1, :, at] = z[1] + chi_row * z[0]
            out[2, :, at] = z[2]

    @pl.when(g == pl.num_programs(0) - 1)
    def _():
        row_id = lax.broadcasted_iota(jnp.int32, (rows, LANES), 0)
        last = half - 1

        def body(b, _):
            for p in range(PAIRS):
                for side in range(2):
                    m = b * PAIRS + p + side * pairs
                    x = out[0, :, at_tile(m)]
                    left = jnp.where(m == 0, cols[0, 0:rows, :], out[0, :, at_tile(jnp.maximum(m - 1, 0))])
                    right = jnp.where(
                        m == last, cols[1, 0:rows, :], out[0, :, at_tile(jnp.minimum(m + 1, last))]
                    )
                    beside = swap(x + jnp.where(lane >= 64, left, right))
                    above = jnp.where(row_id == 0, zx[0:1, at_tile(m)], pltpu.roll(x, 1, 0))
                    below = jnp.where(row_id == rows - 1, zx[1:2, at_tile(m)], pltpu.roll(x, rows - 1, 0))
                    lap = 4.0 * x - beside - above - below
                    xs[0, p * rows : (p + 1) * rows, side * LANES : (side + 1) * LANES] = lap
            res = product(xs[0], wh[3], wl[3])
            for p in range(PAIRS):
                for side in range(2):
                    at = at_tile(b * PAIRS + p + side * pairs)
                    part = res[p * rows : (p + 1) * rows, side * LANES : (side + 1) * LANES]
                    out[2, :, at] = out[2, :, at] + part
            return 0

        lax.fori_loop(0, pairs // PAIRS, body, 0)


def shards(state, sigma, vert, bal_temp, chi_coef, scales, classes, owner):
    n_lat = lax.axis_size("lat")
    n_lon = lax.axis_size("lon")
    devices = n_lat * n_lon
    nvars, rows, merged = state.shape
    levels = vert.shape[1]
    lon = merged // levels
    half = lon // 2
    pairs = half // 2
    steps = pairs // PAIRS
    count = nvars * levels
    capacity = (count + devices - 1) // devices + 1
    i_lat = lax.axis_index("lat")
    i_lon = lax.axis_index("lon")

    ups, downs = ([(i, i + 1) for i in range(n - 1)] for n in (n_lat, n_lon))
    back_lat = [(j, i) for i, j in ups]
    back_lon = [(j, i) for i, j in downs]

    def row(i):
        return jnp.concatenate([state[2, i : i + 1, :], sigma[0, i : i + 1, :]], axis=1)

    def column(j):
        temp = state[2, :, j * levels : (j + 1) * levels]
        sig = jnp.broadcast_to(sigma[0, :, j : j + 1], (rows, levels))
        return jnp.concatenate([temp, sig], axis=1)

    north = lax.ppermute(row(rows - 1), "lat", ups)
    south = lax.ppermute(row(0), "lat", back_lat)
    west = lax.ppermute(column(lon - 1), "lon", downs)
    east = lax.ppermute(column(0), "lon", back_lon)

    class_ids = jnp.arange(scales.shape[0], dtype=jnp.int32)
    length = jnp.sum(jnp.where(classes[:, None] == class_ids[None, :], scales[None, :], 0.0), axis=1)
    length = length.reshape(nvars, levels)
    decay = jnp.exp(-1.0 / length)
    norm = 1.0 - decay
    norm = norm * norm
    norm = norm * norm
    gain = length**1.5 * norm * norm
    table = jnp.stack([length, decay, jnp.broadcast_to(chi_coef, (nvars, levels))], axis=1)
    prm = jnp.pad(jnp.concatenate([table, table], axis=2), ((0, 0), (0, 5), (0, 0)))

    def spread(m):
        return jnp.tile(m, (1, 2, 2))

    fold = jnp.dot(bal_temp, vert[0], precision=highest)
    mats_a = spread(vert[1:])
    mats_0 = spread(jnp.stack([vert[0], fold]))
    mats_z = spread(jnp.swapaxes(vert, 1, 2) * gain[:, :, None])
    mats_b = spread(bal_temp.T[None])

    def by_half(s):
        s = s.reshape(s.shape[0], s.shape[1], 2, half).transpose(0, 2, 1, 3)
        return jnp.pad(s, ((0, 0), (0, 0), (0, 0), (0, LANES - half)))

    sig = by_half(sigma)
    place = jnp.stack([i_lat, i_lon]).astype(jnp.int32)

    block = PAIRS * LANES
    packed = 2 * PAIRS

    def part(v, side):
        return pl.BlockSpec((1, rows, block), lambda g: (v, 0, g + side * steps))

    def lat_call(vs, body, mats, arrays, specs):
        nv = len(vs)
        return pl.pallas_call(
            body,
            grid=(steps,),
            in_specs=[full(prm.shape), full(sig.shape), full(mats.shape)] + specs,
            out_specs=[
                pl.BlockSpec((nv, packed, rows, LANES), lambda g: (0, g, 0, 0)),
                pl.BlockSpec((nv, rows, packed, LANES), lambda g: (0, 0, g, 0)),
                pl.BlockSpec((nv, 4, packed, LANES), lambda g: (0, 0, g, 0)),
            ],
            out_shape=[
                jax.ShapeDtypeStruct((nv, half, rows, LANES), f32),
                jax.ShapeDtypeStruct((nv, rows, half, LANES), f32),
                jax.ShapeDtypeStruct((nv, 4, half, LANES), f32),
            ],
            scratch_shapes=[
                pltpu.VMEM((2, PAIRS * rows, 256), f32),
                pltpu.VMEM((2, 256, 256), bf16),
                pltpu.VMEM((2, 256, 256), bf16),
            ],
            compiler_params=params(),
            cost_estimate=pl.CostEstimate(
                flops=nv * 60000000, bytes_accessed=nv * 3 * rows * merged * 4, transcendentals=0
            ),
            name="lat_" + "".join(map(str, vs)),
        )(prm, sig, mats, *arrays)

    wa, ua, ea = lat_call(
        (1, 2),
        functools.partial(lat_plain, (1, 2), rows),
        mats_a,
        [state] * 4,
        [part(1, 0), part(1, 1), part(2, 0), part(2, 1)],
    )
    ga = lax.all_gather(ea, "lat")
    w0, u0, e0 = lat_call(
        (0,),
        functools.partial(lat_balance, rows, pairs),
        mats_0,
        [state] * 5 + [north, south, west, east],
        [part(0, 0), part(0, 1), part(1, 0), part(1, 1)]
        + [pl.BlockSpec((1, rows, merged), lambda g: (2, 0, 0))]
        + [full(north.shape), full(south.shape), full(west.shape), full(east.shape)],
    )
    g0 = lax.all_gather(e0, "lat")

    def lon_call(vs, u, gathered, ext):
        nv = len(vs)
        rb = rows if ext else (16 if rows % 16 == 0 else 8)
        total = rows + 8 * ext
        shapes = [(nv, half, rows, LANES)]
        specs = [pl.BlockSpec((nv, half, rb, LANES), lambda g: (0, 0, g, 0))]
        if ext:
            shapes.append((half, 8, LANES))
            specs.append(full((half, 8, LANES)))
        for s in ((nv, 4, total, LANES), (nv, 2, total, LANES)):
            shapes.append(s)
            specs.append(full(s))
        return pl.pallas_call(
            functools.partial(lon_kernel, vs, n_lat, rows, rb, ext),
            grid=(rows // rb,),
            in_specs=[
                pl.BlockSpec(memory_space=pltpu.SMEM),
                full(prm.shape),
                pl.BlockSpec((nv, rb, half, LANES), lambda g: (0, g, 0, 0)),
                full(gathered.shape),
            ],
            out_specs=specs,
            out_shape=[jax.ShapeDtypeStruct(s, f32) for s in shapes],
            scratch_shapes=[
                pltpu.VMEM((nv, 4, half, LANES), f32),
                pltpu.VMEM((rows // rb, nv, 4, rb, LANES), f32),
            ],
            compiler_params=params(),
            cost_estimate=pl.CostEstimate(
                flops=nv * 60000000, bytes_accessed=nv * 3 * rows * merged * 4, transcendentals=0
            ),
            name="lon_" + "".join(map(str, vs)),
        )(place, prm, u, gathered)

    xa, ela, esa = lon_call((1, 2), ua, ga, False)
    ha = lax.all_gather(esa, "lon")
    x0, xx, el0, es0 = lon_call((0,), u0, g0, True)
    h0 = lax.all_gather(es0, "lon")

    sigx = jnp.concatenate([north[:, merged:], south[:, merged:]], axis=0)
    sigx = by_half(jnp.pad(sigx, ((0, 6), (0, 0)))[None])[0]

    def columns(nv):
        return pl.BlockSpec((nv, packed, rows, LANES), lambda g: (0, g, 0, 0))

    ins = [place, prm, sig, sigx, west, east, mats_z, mats_b, x0, xx, xa, w0, wa, el0, ela, h0, ha]
    specs = [full(x.shape) for x in ins]
    specs[0] = pl.BlockSpec(memory_space=pltpu.SMEM)
    specs[8] = columns(1)
    specs[9] = pl.BlockSpec((packed, 8, LANES), lambda g: (g, 0, 0))
    specs[10] = columns(2)
    specs[11] = columns(1)
    specs[12] = columns(2)
    applied, energy = pl.pallas_call(
        functools.partial(end_kernel, n_lon, rows, pairs),
        grid=(steps,),
        in_specs=specs,
        out_specs=[full(state.shape), full((nvars, 8, LANES))],
        out_shape=[
            jax.ShapeDtypeStruct(state.shape, f32),
            jax.ShapeDtypeStruct((nvars, 8, LANES), f32),
        ],
        scratch_shapes=[
            pltpu.VMEM((nvars, 4, rows + 8, LANES), f32),
            pltpu.VMEM((nvars, 4, half, LANES), f32),
            pltpu.VMEM((2, rows + 8, LANES), f32),
            pltpu.VMEM((8, merged), f32),
            pltpu.VMEM((nvars, PAIRS * rows, 256), f32),
            pltpu.VMEM((4, 256, 256), bf16),
            pltpu.VMEM((4, 256, 256), bf16),
        ],
        compiler_params=params(),
        cost_estimate=pl.CostEstimate(
            flops=300000000, bytes_accessed=9 * rows * merged * 4, transcendentals=0
        ),
        name="finish",
    )(*ins)

    energy = jnp.sum(energy.reshape(nvars, 8, 2, levels), axis=(1, 2)) * gain
    energy = lax.psum(energy.reshape(count), ("lat", "lon")) / (devices * rows * lon)
    index = jnp.arange(count, dtype=jnp.int32)
    same = (owner[:, None] == owner[None, :]) & (index[None, :] < index[:, None])
    slot = jnp.sum(same.astype(jnp.int32), axis=1)
    rank = i_lat * n_lon + i_lon
    hit = (owner[:, None] == rank) & (slot[:, None] == jnp.arange(capacity)[None, :])
    slab_energy = jnp.sum(jnp.where(hit, energy[:, None], 0.0), axis=0)[None, :]
    return (applied, slab_energy)


def solution(mesh):
    return jax.shard_map(
        shards,
        mesh=mesh,
        in_specs=(P(None, "lat", "lon"), P(None, "lat", "lon"), P(), P(), P(), P(), P(), P()),
        out_specs=(P(None, "lat", "lon"), P(("lat", "lon"), None)),
        check_vma=False,
    )
```

```python
import functools

import jax
import jax.numpy as jnp
from jax import lax
from jax.experimental import pallas as pl
from jax.experimental.pallas import tpu as pltpu
from jax.sharding import PartitionSpec as P

highest = lax.Precision.HIGHEST
f32 = jnp.float32
bf16 = jnp.bfloat16
LANES = 128
PAIRS = 8
BLOCK = 24
ORDER = (1, 2, 0)
LIMIT = 60 * 1024 * 1024


def params():
    return pltpu.CompilerParams(vmem_limit_bytes=LIMIT)


def full(shape):
    return pl.BlockSpec(shape, lambda g: (0,) * len(shape))


def swap(x):
    return pltpu.roll(x, 64, x.ndim - 1)


def low_lanes(shape):
    return lax.broadcasted_iota(jnp.int32, shape, len(shape) - 1) < 64


def halves(x):
    hi = x.astype(bf16)
    return hi, (x - hi.astype(f32)).astype(bf16)


def dot(x, y):
    return jnp.dot(x, y, preferred_element_type=f32)


def product(x, wh, wl):
    hi, lo = halves(x)
    return dot(hi, wh) + dot(lo, wh) + dot(hi, wl)


def expand(mat, mixed):
    wide = quad(mat)
    wide = jnp.concatenate([wide, wide], axis=1)
    wide = jnp.concatenate([wide, wide], axis=0)
    src = lax.broadcasted_iota(jnp.int32, (256, 256), 0) // 64
    dst = lax.broadcasted_iota(jnp.int32, (256, 256), 1) // 64
    if mixed:
        src = jnp.where(src == 1, 2, jnp.where(src == 2, 1, src))
    return halves(jnp.where(src == dst, wide, 0.0))


def quad(mat):
    if mat.shape[0] == LANES:
        return mat
    wide = jnp.concatenate([mat, mat], axis=1)
    return jnp.concatenate([wide, wide], axis=0)


def constants(length, decay, m):
    span = jnp.exp(-float(m) / length)
    d = 1.0 - decay * decay
    k1 = decay * (1.0 - span * span) / d
    k2 = (m * span - decay * decay * (span - span * span * span) / d) / d
    tail = decay * decay * (1.0 + span * span) * (1.0 - span * span) / d
    k3 = decay / (d * d) * (1.0 - (2.0 * m + 1.0) * span * span + tail)
    return span, k1, k2, k3


def responses(length, decay, m):
    j = lax.broadcasted_iota(jnp.int32, (m, LANES), 0).astype(f32)
    up = jnp.exp(-j / length)
    down = jnp.exp(-(m - j) / length)
    span = jnp.exp(-float(m) / length)
    d = 1.0 - decay * decay
    diff = up - span * down
    g3 = decay * diff / d
    g2 = ((m - j) * down - decay * decay * (span * up - span * span * down) / d) / d
    part = decay * decay * (1.0 + span * span) * diff / d
    g1 = decay / (d * d) * ((j + 1.0) * up - (2.0 * m + 1.0 - j) * span * down + part)
    return g1, g2, g3, down


def solve_carries(n, edge, const, me):
    span, k1, k2, k3 = const
    first = edge(0, 0)
    zero = jnp.zeros_like(first)
    e1 = [first] + [edge(t, 0) for t in range(1, n)]
    c1, c2, c3, c4 = ([None] * n for _ in range(4))
    c = zero
    for t in range(n):
        c1[t] = c
        c = e1[t] + span * c
    c = zero
    for t in reversed(range(n)):
        c2[t] = c
        c = edge(t, 1) + k1 * c1[t] + span * c
    c = zero
    for t in range(n):
        c3[t] = c
        c = edge(t, 2) + k2 * c1[t] + k1 * c2[t] + span * c
    c = zero
    for t in reversed(range(n)):
        c4[t] = c
        c = edge(t, 3) + k3 * c1[t] + k2 * c2[t] + k1 * c3[t] + span * c
    out = []
    for cs in (c1, c2, c3, c4):
        mine = cs[0]
        for t in range(1, n):
            mine = jnp.where(me == t, cs[t], mine)
        out.append(mine)
    return out


def cascade(count, load, store, decay, start):
    step = 8
    edges = []
    for stage in range(4):
        back = stage % 2 == 1

        def body(b, states, back=back):
            base = (count // step - 1 - b) * step if back else b * step
            order = range(step - 1, -1, -1) if back else range(step)
            for o in order:
                new = [decay_k * s + x for decay_k, s, x in zip(decay, states, load(base + o))]
                store(base + o, new)
                states = new
            return tuple(states)

        states = lax.fori_loop(0, count // step, body, tuple(start))
        edges.append(list(states))
    return edges


def stage_sigma(sigma, sg, variables):
    lon = sigma.shape[2]
    for v in variables:
        for at in range(0, lon, LANES):
            width = min(LANES, lon - at)
            sg[v, at // LANES, :, 0:width] = sigma[v, :, at : at + width]


def sigma_tile(sg, v, m, high):
    idx = 2 * (m & 63) + high
    return jnp.take_along_axis(sg[v, m >> 6], idx, axis=1, mode="promise_in_bounds")


def set_weights(wh, wl, k, mat, mixed):
    hi, lo = expand(mat, mixed)
    wh[k] = hi
    wl[k] = lo


def lat_filter(vs, rows, prm, u_ref, e_ref):
    nv = len(vs)
    decay = [prm[v, 1:2, :] for v in vs]

    def load(i):
        return [u_ref[k, i] for k in range(nv)]

    def store(i, values):
        for k in range(nv):
            u_ref[k, i] = values[k]

    zero = jnp.zeros((u_ref.shape[2], LANES), f32)
    edges = cascade(rows, load, store, decay, [zero] * nv)
    for e in range(4):
        for k in range(nv):
            e_ref[k, e] = edges[e][k]


def put_mixed(k, b, rows, res, w_ref, u_ref):
    base = b * 2 * PAIRS
    for p in range(PAIRS):
        part = res[p * rows : (p + 1) * rows]
        w_ref[k, base + 2 * p] = part[:, :LANES]
        w_ref[k, base + 2 * p + 1] = part[:, LANES:]
    at = pl.ds(pl.multiple_of(base, 2 * PAIRS), 2 * PAIRS)
    u_ref[k, :, at, :] = jnp.swapaxes(w_ref[k, at], 0, 1)


def lat_plain(rows, pairs, prm, sigma, vert, b1lo, b1hi, b2lo, b2hi, w_ref, u_ref, e_ref, xs, wh, wl, sg):
    g = pl.program_id(0)

    @pl.when(g == 0)
    def _():
        set_weights(wh, wl, 0, vert[1], True)
        set_weights(wh, wl, 1, vert[2], True)
        stage_sigma(sigma, sg, (1, 2))

    lane = lax.broadcasted_iota(jnp.int32, (rows, LANES), 1)
    high = (lane >= 64).astype(jnp.int32)

    def body(b, _):
        for p in range(PAIRS):
            at = slice(p * rows, (p + 1) * rows)
            cols = pl.ds(pl.multiple_of((b * PAIRS + p) * LANES, LANES), LANES)
            m = g * BLOCK + b * PAIRS + p
            for k, sides in enumerate(((b1lo, b1hi), (b2lo, b2hi))):
                for side in range(2):
                    s = sigma_tile(sg, k + 1, m + side * pairs, high)
                    xs[k, at, side * LANES : (side + 1) * LANES] = sides[side][0, :, cols] * s
        for k in range(2):
            put_mixed(k, b, rows, product(xs[k], wh[k], wl[k]), w_ref, u_ref)
        return 0

    lax.fori_loop(0, BLOCK // PAIRS, body, 0)
    lat_filter((1, 2), rows, prm, u_ref, e_ref)


def lat_balance(
    rows, pairs, prm, sigma, vert, bal, plo, phi, clo, chi, temp, north, south, west, east, w_in, u_in, e_in,
    w_ref, u_ref, e_ref, xs, wh, wl, sg,
):
    del w_in, u_in, e_in
    g = pl.program_id(0)

    @pl.when(g == 0)
    def _():
        set_weights(wh, wl, 0, vert[0], True)
        vh, vl = halves(vert[0])
        set_weights(wh, wl, 1, product(bal[...], vh, vl), True)
        stage_sigma(sigma, sg, (0,))

    lane = lax.broadcasted_iota(jnp.int32, (rows, LANES), 1)
    row_id = lax.broadcasted_iota(jnp.int32, (rows, LANES), 0)
    high = (lane >= 64).astype(jnp.int32)
    chi_row = prm[0, 2:3, :]
    last = 2 * pairs - 1

    def at_tile(m):
        return pl.ds(pl.multiple_of(m * LANES, LANES), LANES)

    def laplace(m):
        x = temp[0, :, at_tile(m)]
        left = jnp.where(m == 0, swap(west[...]), temp[0, :, at_tile(jnp.maximum(m - 1, 0))])
        right = jnp.where(m == last, east[...], temp[0, :, at_tile(jnp.minimum(m + 1, last))])
        beside = swap(x + jnp.where(lane >= 64, left, right))
        above = jnp.where(row_id == 0, north[:, at_tile(m)], pltpu.roll(x, 1, 0))
        below = jnp.where(row_id == rows - 1, south[:, at_tile(m)], pltpu.roll(x, rows - 1, 0))
        return 4.0 * x - beside - above - below

    def body(b, _):
        for p in range(PAIRS):
            at = slice(p * rows, (p + 1) * rows)
            cols = at_tile(b * PAIRS + p)
            m = g * BLOCK + b * PAIRS + p
            for side, (pr, cr) in enumerate(((plo, clo), (phi, chi))):
                s = sigma_tile(sg, 0, m + side * pairs, high)
                to = slice(side * LANES, (side + 1) * LANES)
                xs[0, at, to] = (pr[0, :, cols] + chi_row * cr[0, :, cols]) * s
                xs[1, at, to] = laplace(m + side * pairs) * s
        res = product(xs[0], wh[0], wl[0]) + product(xs[1], wh[1], wl[1])
        put_mixed(0, b, rows, res, w_ref, u_ref)
        return 0

    lax.fori_loop(0, BLOCK // PAIRS, body, 0)
    lat_filter((0,), rows, prm, u_ref, e_ref)


def lon_filter(prm, rb, o_ref, el_ref, es_ref, at):
    half = o_ref.shape[1]
    nv = len(ORDER)
    decay = [prm[v, 1:2, :] for v in ORDER]

    def load(j):
        return [o_ref[k, j] for k in range(nv)]

    def store(j, values):
        for k in range(nv):
            o_ref[k, j] = values[k]

    edges = cascade(half, load, store, decay, [jnp.zeros((rb, LANES), f32)] * nv)
    low = low_lanes((rb, LANES))
    for k, v in enumerate(ORDER):
        span, k1, k2, k3 = constants(prm[v, 0:1, :], prm[v, 1:2, :], half)
        e1, e2, e3, e4 = (edges[e][k] for e in range(4))
        c1 = jnp.where(low, 0.0, swap(e1))
        t1 = e1 + span * c1
        t2 = e2 + k1 * c1
        c2 = jnp.where(low, swap(t2), 0.0)
        t2 = t2 + span * c2
        t3 = e3 + k2 * c1 + k1 * c2
        c3 = jnp.where(low, 0.0, swap(t3))
        t3 = t3 + span * c3
        t4 = e4 + k3 * c1 + k2 * c2 + k1 * c3
        c4 = jnp.where(low, swap(t4), 0.0)
        t4 = t4 + span * c4
        es_ref[k, 0, at, :] = jnp.where(low, t2, t1)
        es_ref[k, 1, at, :] = jnp.where(low, t4, t3)
        for e, x in enumerate((e1, e2, e3, e4)):
            el_ref[k, e, at, :] = x


def lon_kernel(rb, prm, u_ref, o_ref, el_ref, es_ref):
    g = pl.program_id(0)
    half = u_ref.shape[2]

    def turn(b, _):
        at = pl.ds(pl.multiple_of(b * 8, 8), 8)
        for k in range(len(ORDER)):
            for q in range(0, rb, 8):
                o_ref[k, at, q : q + 8, :] = jnp.swapaxes(u_ref[k, q : q + 8, at, :], 0, 1)
        return 0

    lax.fori_loop(0, half // 8, turn, 0)
    lon_filter(prm, rb, o_ref, el_ref, es_ref, pl.ds(pl.multiple_of(g * rb, 8), rb))


def carry_kernel(n_lat, rows, place, prm, gathered, o_ref, el_ref, es_ref):
    half = o_ref.shape[1]
    me = place[0]
    for k, v in enumerate(ORDER):
        const = constants(prm[v, 0:1, :], prm[v, 1:2, :], rows)

        def body(b, _, k=k, const=const):
            at = pl.ds(pl.multiple_of(b * 8, 8), 8)
            c = solve_carries(n_lat, lambda t, e: gathered[t, k, e, at, :], const, me)
            block = jnp.stack(c + [jnp.zeros_like(c[0])] * 4, axis=0)
            o_ref[k, at] = jnp.swapaxes(block, 0, 1)
            return 0

        lax.fori_loop(0, half // 8, body, 0)
    lon_filter(prm, 8, o_ref, el_ref, es_ref, pl.ds(0, 8))


def join_kernel(n_lon, rows, packed, rq, place, prm, u_ref, w_ref, x_ref, el, es, elc, *rest):
    sent = rest[:n_lon]
    y_ref, yx_ref, col_ref, energy, carry, extra, resp_x, resp_y, esx = rest[n_lon:]
    g = pl.program_id(0)
    half = resp_x.shape[2]
    lat, me = place[0], place[1]
    low8 = low_lanes((8, LANES))

    @pl.when(g == 0)
    def _():
        energy[...] = jnp.zeros_like(energy)
        for s in range(n_lon):
            esx[lax.rem(me - s + n_lon, n_lon)] = sent[s][...]
        for k, v in enumerate(ORDER):
            length = prm[v, 0:1, :]
            decay = prm[v, 1:2, :]
            whole = constants(length, decay, 2 * half)
            span, k1, k2, k3 = constants(length, decay, half)

            def solve(gathered, own, at, k=k, whole=whole, half_c=(span, k1, k2, k3)):
                span, k1, k2, k3 = half_c
                cache = {}

                def edge(t, e):
                    if (t, e // 2) not in cache:
                        x = gathered[t, k, e // 2, at, :]
                        y = swap(x)
                        cache[t, e // 2] = (jnp.where(low8, y, x), jnp.where(low8, x, y))
                    return cache[t, e // 2][e % 2]

                d1, d2, d3, d4 = solve_carries(n_lon, edge, whole, me)
                e1, e2, e3, e4 = (own[k, e, at, :] for e in range(4))
                c1 = jnp.where(low8, d1, swap(e1 + span * d1))
                c2 = jnp.where(low8, swap(e2 + k1 * c1 + span * d2), d2)
                c3 = jnp.where(low8, d3, swap(e3 + k2 * c1 + k1 * c2 + span * d3))
                c4 = jnp.where(low8, swap(e4 + k3 * c1 + k2 * c2 + k1 * c3 + span * d4), d4)
                return (c1, c2, c3, c4), d3, d4

            for e, r in enumerate(responses(length, decay, half)):
                resp_x[k, e] = r
            for e, r in enumerate(responses(length, decay, rows)):
                resp_y[k, e] = r
            cc, f3, f4 = solve(esx, elc, slice(0, 8))
            for e in range(4):
                extra[k, e] = cc[e]

            def body(b, _, k=k, v=v, cc=cc, f3=f3, f4=f4, solve=solve):
                at = pl.ds(pl.multiple_of(b * 8, 8), 8)
                c, d3, d4 = solve(es, el, at)
                ry = [resp_y[k, e, at, :] for e in range(4)]

                def total(x, rows_of):
                    for e in range(4):
                        x = x + ry[e] * rows_of[e : e + 1, :]
                    return x

                for e in range(4):
                    carry[k, e, at, :] = total(c[e], cc[e])
                if v == 0:
                    col_ref[0, at, :] = total(d3, f3)
                    col_ref[1, at, :] = total(d4, f4)
                return 0

            lax.fori_loop(0, rows // 8, body, 0)

    row8 = lax.broadcasted_iota(jnp.int32, (8, LANES), 0)
    for k, v in enumerate(ORDER):
        total = jnp.zeros((8, LANES), f32)
        for q in range(0, rows, rq):
            at = slice(q, q + rq)
            c = [carry[k, e, at, :] for e in range(4)]
            ry = [resp_y[k, e, at, :] for e in range(4)]

            def body(b, total, k=k, v=v, q=q, at=at, c=c, ry=ry):
                base = g * packed + b * 8
                rx = [resp_x[k, e, pl.ds(pl.multiple_of(base, 8), 8), :] for e in range(4)]
                for o in range(8):
                    p = b * 8 + o
                    x = x_ref[k, p]
                    y = u_ref[k, p, at, :]
                    for e in range(4):
                        y = y + rx[e][o : o + 1, :] * c[e] + ry[e] * x[e : e + 1, :]
                    y_ref[k, p, at, :] = y
                    t = y * w_ref[k, p, at, :]
                    for i in range(0, rq, 8):
                        total = total + t[i : i + 8]
                    if v == 0 and q == 0:
                        for e in range(4):
                            x = x + rx[e][o : o + 1, :] * extra[k, e]
                        x = pltpu.roll(x, 6, 0)
                        above = jnp.where(lat > 0, x + prm[0, 1:2, :] * y[0:1, :], 0.0)
                        yx_ref[p] = jnp.where(row8 == 0, above, jnp.where(row8 == 1, x, 0.0))
                return total

            total = lax.fori_loop(0, packed // 8, body, total)
        energy[k] += total

    @pl.when(g == 0)
    def _():
        beside = col_ref[0] + prm[0, 1:2, :] * y_ref[ORDER.index(0), 0]
        col_ref[0] = jnp.where(me > 0, beside, 0.0)


def end_kernel(
    rows, pairs, prm, sigma, north, south, west, east, vert, bal, col, y_ref, yx_ref,
    out, xs, zx, zc, wh, wl, sg, sx,
):
    g = pl.program_id(0)
    half = 2 * pairs
    merged = out.shape[2]
    lon = sigma.shape[2]

    @pl.when(g == 0)
    def _():
        for v in range(3):
            scaled = quad(vert[v]) * prm[v, 3:4, :]
            set_weights(wh, wl, v, scaled.T, True)
        set_weights(wh, wl, 3, quad(bal[...]).T, False)
        stage_sigma(sigma, sg, (0, 1, 2))
        for at in range(0, lon, LANES):
            width = min(LANES, lon - at)
            sx[at // LANES, 0:1, 0:width] = north[:, merged + at : merged + at + width]
            sx[at // LANES, 1:2, 0:width] = south[:, merged + at : merged + at + width]
        lhs = jnp.where(low_lanes((rows, LANES)), col[0], col[1])
        lhs = jnp.concatenate([lhs, jnp.zeros_like(lhs)], axis=1)
        res = product(lhs, wh[0], wl[0])
        zc[0] = swap(res[:, :LANES] * swap(west[...]))
        zc[1] = res[:, LANES:] * swap(east[...])

    lane = lax.broadcasted_iota(jnp.int32, (rows, LANES), 1)
    high = (lane >= 64).astype(jnp.int32)
    high8 = high[0:8]
    chi_row = prm[0, 2:3, :]

    def at_tile(m):
        return pl.ds(pl.multiple_of(m * LANES, LANES), LANES)

    lhs = jnp.concatenate(
        [jnp.concatenate([yx_ref[2 * p], yx_ref[2 * p + 1]], axis=1) for p in range(PAIRS)], axis=0
    )
    res = product(lhs, wh[0], wl[0])
    for p in range(PAIRS):
        m = g * PAIRS + p
        for side in range(2):
            tile = m + side * pairs
            s = jnp.take_along_axis(sx[tile >> 6], 2 * (tile & 63) + high8, axis=1, mode="promise_in_bounds")
            part = res[p * 8 : (p + 1) * 8, side * LANES : (side + 1) * LANES]
            zx[:, at_tile(tile)] = jnp.where(lax.broadcasted_iota(jnp.int32, (8, LANES), 0) < 2, part * s, 0.0)
    for k in range(3):
        for p in range(2 * PAIRS):
            at = slice((p // 2) * rows, (p // 2 + 1) * rows)
            xs[k, at, (p % 2) * LANES : (p % 2 + 1) * LANES] = y_ref[k, p]
    results = {v: product(xs[k], wh[v], wl[v]) for k, v in enumerate(ORDER)}
    for p in range(PAIRS):
        m = g * PAIRS + p
        for side in range(2):
            at = at_tile(m + side * pairs)
            z = [
                results[v][p * rows : (p + 1) * rows, side * LANES : (side + 1) * LANES]
                * sigma_tile(sg, v, m + side * pairs, high)
                for v in range(3)
            ]
            out[0, :, at] = z[0]
            out[1, :, at] = z[1] + chi_row * z[0]
            out[2, :, at] = z[2]

    @pl.when(g == pl.num_programs(0) - 1)
    def _():
        row_id = lax.broadcasted_iota(jnp.int32, (rows, LANES), 0)
        last = half - 1

        def body(b, _):
            for p in range(PAIRS):
                for side in range(2):
                    m = b * PAIRS + p + side * pairs
                    x = out[0, :, at_tile(m)]
                    left = jnp.where(m == 0, zc[0], out[0, :, at_tile(jnp.maximum(m - 1, 0))])
                    right = jnp.where(m == last, zc[1], out[0, :, at_tile(jnp.minimum(m + 1, last))])
                    beside = swap(x + jnp.where(lane >= 64, left, right))
                    above = jnp.where(row_id == 0, zx[0:1, at_tile(m)], pltpu.roll(x, 1, 0))
                    below = jnp.where(row_id == rows - 1, zx[1:2, at_tile(m)], pltpu.roll(x, rows - 1, 0))
                    lap = 4.0 * x - beside - above - below
                    xs[0, p * rows : (p + 1) * rows, side * LANES : (side + 1) * LANES] = lap
            res = product(xs[0], wh[3], wl[3])
            for p in range(PAIRS):
                for side in range(2):
                    at = at_tile(b * PAIRS + p + side * pairs)
                    part = res[p * rows : (p + 1) * rows, side * LANES : (side + 1) * LANES]
                    out[2, :, at] = out[2, :, at] + part
            return 0

        lax.fori_loop(0, pairs // PAIRS, body, 0)


def shards(state, sigma, vert, bal_temp, chi_coef, scales, classes, owner):
    n_lat = lax.axis_size("lat")
    n_lon = lax.axis_size("lon")
    devices = n_lat * n_lon
    nvars, rows, merged = state.shape
    levels = vert.shape[1]
    lon = merged // levels
    half = lon // 2
    pairs = half // 2
    pieces = (lon + LANES - 1) // LANES
    count = nvars * levels
    capacity = (count + devices - 1) // devices + 1
    i_lat = lax.axis_index("lat")
    i_lon = lax.axis_index("lon")

    up_lat, up_lon = ([(i, i + 1) for i in range(n - 1)] for n in (n_lat, n_lon))
    down_lat, down_lon = ([(j, i) for i, j in up] for up in (up_lat, up_lon))

    def row(i):
        return jnp.concatenate([state[2, i : i + 1, :], sigma[0, i : i + 1, :]], axis=1)

    def column(j):
        temp = state[2, :, j * levels : (j + 1) * levels]
        sig = jnp.broadcast_to(sigma[0, :, j : j + 1], (rows, levels))
        return jnp.concatenate([temp, sig], axis=1)

    north = lax.ppermute(row(rows - 1), "lat", up_lat)
    south = lax.ppermute(row(0), "lat", down_lat)
    west = lax.ppermute(column(lon - 1), "lon", up_lon)
    east = lax.ppermute(column(0), "lon", down_lon)

    class_ids = jnp.arange(scales.shape[0], dtype=jnp.int32)
    kind = classes.reshape(nvars, levels)
    kind = jnp.concatenate([kind, kind], axis=1)
    length = jnp.sum(jnp.where(kind[:, None, :] == class_ids[None, :, None], scales[None, :, None], 0.0), axis=1)
    decay = jnp.exp(-1.0 / length)
    norm = 1.0 - decay
    norm = norm * norm
    norm = norm * norm
    gain = length * jnp.sqrt(length) * norm * norm
    coef = jnp.broadcast_to(jnp.concatenate([chi_coef, chi_coef]), (nvars, 2 * levels))
    prm = jnp.stack([length, decay, coef, gain], axis=1)
    place = jnp.stack([i_lat, i_lon]).astype(jnp.int32)

    anywhere = pl.BlockSpec(memory_space=pl.ANY)
    steps = pairs // BLOCK

    def part(v, side):
        return pl.BlockSpec((1, rows, BLOCK * LANES), lambda g: (v, 0, g + side * steps))

    packed_shapes = [(nvars, half, rows, LANES), (nvars, rows, half, LANES), (nvars, 4, half, LANES)]

    def lat_call(nv, first, body, arrays, specs, name, aliases):
        return pl.pallas_call(
            body,
            grid=(steps,),
            in_specs=specs,
            out_specs=[
                pl.BlockSpec((nv, 2 * BLOCK, rows, LANES), lambda g: (first, g, 0, 0)),
                pl.BlockSpec((nv, rows, 2 * BLOCK, LANES), lambda g: (first, 0, g, 0)),
                pl.BlockSpec((nv, 4, 2 * BLOCK, LANES), lambda g: (first, 0, g, 0)),
            ],
            out_shape=[jax.ShapeDtypeStruct(s, f32) for s in packed_shapes],
            scratch_shapes=[
                pltpu.VMEM((2, PAIRS * rows, 256), f32),
                pltpu.VMEM((2, 256, 256), bf16),
                pltpu.VMEM((2, 256, 256), bf16),
                pltpu.VMEM((nvars, pieces, rows, LANES), f32),
            ],
            compiler_params=params(),
            cost_estimate=pl.CostEstimate(
                flops=nv * 60000000, bytes_accessed=nv * 3 * rows * merged * 4, transcendentals=0
            ),
            input_output_aliases=aliases,
            name=name,
        )(*arrays)

    ins = [prm, sigma, vert] + [state] * 4
    specs = [full(x.shape) for x in ins[:3]] + [part(1, 0), part(1, 1), part(2, 0), part(2, 1)]
    wue = lat_call(2, 0, functools.partial(lat_plain, rows, pairs), ins, specs, "lat_chi_temp", {})
    ins = [prm, sigma, vert, bal_temp] + [state] * 5 + [north, south, west, east] + list(wue)
    specs = [full(x.shape) for x in ins[:4]] + [part(0, 0), part(0, 1), part(1, 0), part(1, 1)]
    specs += [pl.BlockSpec((1, rows, merged), lambda g: (2, 0, 0))]
    specs += [full(x.shape) for x in (north, south, west, east)] + [anywhere] * 3
    aliases = {13: 0, 14: 1, 15: 2}
    w, u, edges = lat_call(1, 2, functools.partial(lat_balance, rows, pairs), ins, specs, "lat_psi", aliases)
    gathered = lax.all_gather(edges, "lat")

    rb = BLOCK
    local, el, es = pl.pallas_call(
        functools.partial(lon_kernel, rb),
        grid=(rows // rb,),
        in_specs=[full(prm.shape), pl.BlockSpec((nvars, rb, half, LANES), lambda g: (0, g, 0, 0))],
        out_specs=[
            pl.BlockSpec((nvars, half, rb, LANES), lambda g: (0, 0, g, 0)),
            full((nvars, 4, rows, LANES)),
            full((nvars, 2, rows, LANES)),
        ],
        out_shape=[
            jax.ShapeDtypeStruct((nvars, half, rows, LANES), f32),
            jax.ShapeDtypeStruct((nvars, 4, rows, LANES), f32),
            jax.ShapeDtypeStruct((nvars, 2, rows, LANES), f32),
        ],
        compiler_params=params(),
        cost_estimate=pl.CostEstimate(
            flops=180000000, bytes_accessed=6 * rows * merged * 4, transcendentals=0
        ),
        name="lon_tile",
    )(prm, u)
    es_all = lax.all_gather(es, "lon")

    crossed, elc, esc = pl.pallas_call(
        functools.partial(carry_kernel, n_lat, rows),
        grid=(1,),
        in_specs=[pl.BlockSpec(memory_space=pltpu.SMEM), full(prm.shape), full(gathered.shape)],
        out_specs=[full((nvars, half, 8, LANES)), full((nvars, 4, 8, LANES)), full((nvars, 2, 8, LANES))],
        out_shape=[
            jax.ShapeDtypeStruct((nvars, half, 8, LANES), f32),
            jax.ShapeDtypeStruct((nvars, 4, 8, LANES), f32),
            jax.ShapeDtypeStruct((nvars, 2, 8, LANES), f32),
        ],
        compiler_params=params(),
        cost_estimate=pl.CostEstimate(
            flops=30000000, bytes_accessed=4 * nvars * 5 * n_lat * half * LANES, transcendentals=0
        ),
        name="lon_carry",
    )(place, prm, gathered)
    sent = [esc] + [
        lax.ppermute(esc, "lon", [(i, (i + s) % n_lon) for i in range(n_lon)]) for s in range(1, n_lon)
    ]

    packed = 2 * PAIRS

    def columns(r):
        return pl.BlockSpec((nvars, packed, r, LANES), lambda g: (0, g, 0, 0))

    ins = [place, prm, local, w, crossed, el, es_all, elc] + sent
    specs = [full(x.shape) for x in ins]
    specs[0] = pl.BlockSpec(memory_space=pltpu.SMEM)
    specs[2:5] = [columns(rows), columns(rows), columns(8)]
    y, yx, col, energy = pl.pallas_call(
        functools.partial(join_kernel, n_lon, rows, packed, 24),
        grid=(half // packed,),
        in_specs=specs,
        out_specs=[
            columns(rows),
            pl.BlockSpec((packed, 8, LANES), lambda g: (g, 0, 0)),
            full((2, rows, LANES)),
            full((nvars, 8, LANES)),
        ],
        out_shape=[
            jax.ShapeDtypeStruct((nvars, half, rows, LANES), f32),
            jax.ShapeDtypeStruct((half, 8, LANES), f32),
            jax.ShapeDtypeStruct((2, rows, LANES), f32),
            jax.ShapeDtypeStruct((nvars, 8, LANES), f32),
        ],
        scratch_shapes=[
            pltpu.VMEM((nvars, 4, rows, LANES), f32),
            pltpu.VMEM((nvars, 4, 8, LANES), f32),
            pltpu.VMEM((nvars, 4, half, LANES), f32),
            pltpu.VMEM((nvars, 4, rows, LANES), f32),
            pltpu.VMEM((n_lon, nvars, 2, 8, LANES), f32),
        ],
        compiler_params=params(),
        cost_estimate=pl.CostEstimate(
            flops=60000000, bytes_accessed=9 * rows * merged * 4, transcendentals=0
        ),
        name="join",
    )(*ins)

    index = jnp.arange(count, dtype=jnp.int32)
    same = (owner[:, None] == owner[None, :]) & (index[None, :] < index[:, None])
    slot = jnp.sum(same.astype(jnp.int32), axis=1)
    target = owner * capacity + slot
    hit = target[:, None] == jnp.arange(devices * capacity)[None, :]
    energy = jnp.stack([energy[ORDER.index(v)] for v in range(nvars)])
    energy = jnp.sum(energy, axis=1) * gain
    energy = (energy[:, :levels] + energy[:, levels:]).reshape(count)
    table = jnp.sum(jnp.where(hit, energy[:, None], 0.0), axis=0).reshape(devices, capacity)
    table = lax.all_to_all(table, ("lat", "lon"), split_axis=0, concat_axis=0, tiled=True)
    slab_energy = (jnp.sum(table, axis=0) / (devices * rows * lon))[None, :]

    ins = [prm, sigma, north, south, west, east, vert, bal_temp, col, y, yx]
    specs = [full(x.shape) for x in ins]
    specs[9] = columns(rows)
    specs[10] = pl.BlockSpec((packed, 8, LANES), lambda g: (g, 0, 0))
    applied = pl.pallas_call(
        functools.partial(end_kernel, rows, pairs),
        grid=(half // packed,),
        in_specs=specs,
        out_specs=full(state.shape),
        out_shape=jax.ShapeDtypeStruct(state.shape, f32),
        scratch_shapes=[
            pltpu.VMEM((nvars, PAIRS * rows, 256), f32),
            pltpu.VMEM((8, merged), f32),
            pltpu.VMEM((2, rows, LANES), f32),
            pltpu.VMEM((4, 256, 256), bf16),
            pltpu.VMEM((4, 256, 256), bf16),
            pltpu.VMEM((nvars, pieces, rows, LANES), f32),
            pltpu.VMEM((pieces, 8, LANES), f32),
        ],
        compiler_params=params(),
        cost_estimate=pl.CostEstimate(
            flops=300000000, bytes_accessed=6 * rows * merged * 4, transcendentals=0
        ),
        name="finish",
    )(*ins)
    return (applied, slab_energy)


def solution(mesh):
    return jax.shard_map(
        shards,
        mesh=mesh,
        in_specs=(P(None, "lat", "lon"), P(None, "lat", "lon"), P(), P(), P(), P(), P(), P()),
        out_specs=(P(None, "lat", "lon"), P(("lat", "lon"), None)),
        check_vma=False,
    )
```

```python
import functools

import jax
import jax.numpy as jnp
from jax import lax
from jax.experimental import pallas as pl
from jax.experimental.pallas import tpu as pltpu
from jax.sharding import PartitionSpec as P

highest = lax.Precision.HIGHEST
f32 = jnp.float32
bf16 = jnp.bfloat16
LANES = 128
PAIRS = 8
BLOCK = 24
ORDER = (1, 2, 0)
LIMIT = 60 * 1024 * 1024


def params():
    return pltpu.CompilerParams(vmem_limit_bytes=LIMIT)


def full(shape):
    return pl.BlockSpec(shape, lambda g: (0,) * len(shape))


def swap(x):
    return pltpu.roll(x, 64, x.ndim - 1)


def low_lanes(shape):
    return lax.broadcasted_iota(jnp.int32, shape, len(shape) - 1) < 64


def halves(x):
    hi = x.astype(bf16)
    return hi, (x - hi.astype(f32)).astype(bf16)


def dot(x, y):
    return jnp.dot(x, y, preferred_element_type=f32)


def product(x, wh, wl):
    hi, lo = halves(x)
    return dot(hi, wh) + dot(lo, wh) + dot(hi, wl)


def expand(mat, mixed):
    wide = quad(mat)
    wide = jnp.concatenate([wide, wide], axis=1)
    wide = jnp.concatenate([wide, wide], axis=0)
    src = lax.broadcasted_iota(jnp.int32, (256, 256), 0) // 64
    dst = lax.broadcasted_iota(jnp.int32, (256, 256), 1) // 64
    if mixed:
        src = jnp.where(src == 1, 2, jnp.where(src == 2, 1, src))
    return halves(jnp.where(src == dst, wide, 0.0))


def quad(mat):
    if mat.shape[0] == LANES:
        return mat
    wide = jnp.concatenate([mat, mat], axis=1)
    return jnp.concatenate([wide, wide], axis=0)


def constants(length, decay, m):
    span = jnp.exp(-float(m) / length)
    d = 1.0 - decay * decay
    k1 = decay * (1.0 - span * span) / d
    k2 = (m * span - decay * decay * (span - span * span * span) / d) / d
    tail = decay * decay * (1.0 + span * span) * (1.0 - span * span) / d
    k3 = decay / (d * d) * (1.0 - (2.0 * m + 1.0) * span * span + tail)
    return span, k1, k2, k3


def responses(length, decay, m):
    j = lax.broadcasted_iota(jnp.int32, (m, LANES), 0).astype(f32)
    up = jnp.exp(-j / length)
    down = jnp.exp(-(m - j) / length)
    span = jnp.exp(-float(m) / length)
    d = 1.0 - decay * decay
    diff = up - span * down
    g3 = decay * diff / d
    g2 = ((m - j) * down - decay * decay * (span * up - span * span * down) / d) / d
    part = decay * decay * (1.0 + span * span) * diff / d
    g1 = decay / (d * d) * ((j + 1.0) * up - (2.0 * m + 1.0 - j) * span * down + part)
    return g1, g2, g3, down


def pick(all_carries, me):
    out = []
    for cs in all_carries:
        mine = cs[0]
        for t in range(1, len(cs)):
            mine = jnp.where(me == t, cs[t], mine)
        out.append(mine)
    return out


def solve_carries(n, edge, const):
    span, k1, k2, k3 = const
    first = edge(0, 0)
    zero = jnp.zeros_like(first)
    e1 = [first] + [edge(t, 0) for t in range(1, n)]
    c1, c2, c3, c4 = ([None] * n for _ in range(4))
    c = zero
    for t in range(n):
        c1[t] = c
        c = e1[t] + span * c
    c = zero
    for t in reversed(range(n)):
        c2[t] = c
        c = edge(t, 1) + k1 * c1[t] + span * c
    c = zero
    for t in range(n):
        c3[t] = c
        c = edge(t, 2) + k2 * c1[t] + k1 * c2[t] + span * c
    c = zero
    for t in reversed(range(n)):
        c4[t] = c
        c = edge(t, 3) + k3 * c1[t] + k2 * c2[t] + k1 * c3[t] + span * c
    return c1, c2, c3, c4


def cascade(count, load, store, decay, start):
    step = 8
    edges = []
    for stage in range(4):
        back = stage % 2 == 1

        def body(b, states, back=back):
            base = (count // step - 1 - b) * step if back else b * step
            order = range(step - 1, -1, -1) if back else range(step)
            for o in order:
                new = [decay_k * s + x for decay_k, s, x in zip(decay, states, load(base + o))]
                store(base + o, new)
                states = new
            return tuple(states)

        states = lax.fori_loop(0, count // step, body, tuple(start))
        edges.append(list(states))
    return edges


def stage_sigma(sigma, sg, variables):
    lon = sigma.shape[2]
    for v in variables:
        for at in range(0, lon, LANES):
            width = min(LANES, lon - at)
            sg[v, at // LANES, :, 0:width] = sigma[v, :, at : at + width]


def sigma_tile(sg, v, m, high):
    idx = 2 * (m & 63) + high
    return jnp.take_along_axis(sg[v, m >> 6], idx, axis=1, mode="promise_in_bounds")


def set_weights(wh, wl, k, mat, mixed):
    hi, lo = expand(mat, mixed)
    wh[k] = hi
    wl[k] = lo


def lat_filter(vs, rows, prm, u_ref, e_ref):
    nv = len(vs)
    decay = [prm[v, 1:2, :] for v in vs]

    def load(i):
        return [u_ref[k, i] for k in range(nv)]

    def store(i, values):
        for k in range(nv):
            u_ref[k, i] = values[k]

    zero = jnp.zeros((u_ref.shape[2], LANES), f32)
    edges = cascade(rows, load, store, decay, [zero] * nv)
    width = e_ref.shape[2] // 4
    for e in range(4):
        for k in range(nv):
            for c in range(e_ref.shape[0]):
                e_ref[c, k, e * width : (e + 1) * width] = edges[e][k][c * width : (c + 1) * width]


def put_mixed(k, b, rows, res, w_ref, u_ref):
    base = b * 2 * PAIRS
    for p in range(PAIRS):
        part = res[p * rows : (p + 1) * rows]
        w_ref[k, base + 2 * p] = part[:, :LANES]
        w_ref[k, base + 2 * p + 1] = part[:, LANES:]
    at = pl.ds(pl.multiple_of(base, 2 * PAIRS), 2 * PAIRS)
    u_ref[k, :, at, :] = jnp.swapaxes(w_ref[k, at], 0, 1)


def set_params(scales, classes, chi_coef, prm):
    coef = jnp.concatenate([chi_coef[...], chi_coef[...]], axis=1)
    for v in range(3):
        kind = classes[:, 64 * v : 64 * (v + 1)]
        kind = jnp.concatenate([kind, kind], axis=1)
        length = jnp.zeros((1, LANES), f32)
        for n in range(scales.shape[0]):
            length = jnp.where(kind == n, scales[n], length)
        decay = jnp.exp(-1.0 / length)
        norm = 1.0 - decay
        norm = norm * norm
        norm = norm * norm
        prm[v, 0:1, :] = length
        prm[v, 1:2, :] = decay
        prm[v, 2:3, :] = coef
        prm[v, 3:4, :] = length * jnp.sqrt(length) * norm * norm


def lat_plain(
    rows, pairs, scales, classes, chi_coef, sigma, vert, b1lo, b1hi, b2lo, b2hi,
    w_ref, u_ref, e_ref, prm, xs, wh, wl, sg,
):
    g = pl.program_id(0)

    @pl.when(g == 0)
    def _():
        set_params(scales, classes, chi_coef, prm)
        set_weights(wh, wl, 0, vert[1], True)
        set_weights(wh, wl, 1, vert[2], True)
        stage_sigma(sigma, sg, (1, 2))

    lane = lax.broadcasted_iota(jnp.int32, (rows, LANES), 1)
    high = (lane >= 64).astype(jnp.int32)

    def body(b, _):
        for p in range(PAIRS):
            at = slice(p * rows, (p + 1) * rows)
            cols = pl.ds(pl.multiple_of((b * PAIRS + p) * LANES, LANES), LANES)
            m = g * BLOCK + b * PAIRS + p
            for k, sides in enumerate(((b1lo, b1hi), (b2lo, b2hi))):
                for side in range(2):
                    s = sigma_tile(sg, k + 1, m + side * pairs, high)
                    xs[k, at, side * LANES : (side + 1) * LANES] = sides[side][0, :, cols] * s
        for k in range(2):
            put_mixed(k, b, rows, product(xs[k], wh[k], wl[k]), w_ref, u_ref)
        return 0

    lax.fori_loop(0, BLOCK // PAIRS, body, 0)
    lat_filter((1, 2), rows, prm, u_ref, e_ref)


def lat_balance(
    rows, pairs, prm, sigma, vert, bal, plo, phi, clo, chi, temp, north, south, west, east, w_in, u_in, e_in,
    w_ref, u_ref, e_ref, xs, wh, wl, sg,
):
    del w_in, u_in, e_in
    g = pl.program_id(0)

    @pl.when(g == 0)
    def _():
        set_weights(wh, wl, 0, vert[0], True)
        vh, vl = halves(vert[0])
        set_weights(wh, wl, 1, product(bal[...], vh, vl), True)
        stage_sigma(sigma, sg, (0,))

    lane = lax.broadcasted_iota(jnp.int32, (rows, LANES), 1)
    row_id = lax.broadcasted_iota(jnp.int32, (rows, LANES), 0)
    high = (lane >= 64).astype(jnp.int32)
    chi_row = prm[0, 2:3, :]
    last = 2 * pairs - 1
    beyond = [jnp.concatenate([x[...], x[...]], axis=1) for x in (west, east)]

    def at_tile(m):
        return pl.ds(pl.multiple_of(m * LANES, LANES), LANES)

    def laplace(m):
        x = temp[0, :, at_tile(m)]
        left = jnp.where(m == 0, beyond[0], temp[0, :, at_tile(jnp.maximum(m - 1, 0))])
        right = jnp.where(m == last, beyond[1], temp[0, :, at_tile(jnp.minimum(m + 1, last))])
        beside = swap(x + jnp.where(lane >= 64, left, right))
        above = jnp.where(row_id == 0, north[:, at_tile(m)], pltpu.roll(x, 1, 0))
        below = jnp.where(row_id == rows - 1, south[:, at_tile(m)], pltpu.roll(x, rows - 1, 0))
        return 4.0 * x - beside - above - below

    def body(b, _):
        for p in range(PAIRS):
            at = slice(p * rows, (p + 1) * rows)
            cols = at_tile(b * PAIRS + p)
            m = g * BLOCK + b * PAIRS + p
            for side, (pr, cr) in enumerate(((plo, clo), (phi, chi))):
                s = sigma_tile(sg, 0, m + side * pairs, high)
                to = slice(side * LANES, (side + 1) * LANES)
                xs[0, at, to] = (pr[0, :, cols] + chi_row * cr[0, :, cols]) * s
                xs[1, at, to] = laplace(m + side * pairs) * s
        res = product(xs[0], wh[0], wl[0]) + product(xs[1], wh[1], wl[1])
        put_mixed(0, b, rows, res, w_ref, u_ref)
        return 0

    lax.fori_loop(0, BLOCK // PAIRS, body, 0)
    lat_filter((0,), rows, prm, u_ref, e_ref)


def lon_filter(prm, rb, o_ref, el_ref, es_ref, at):
    half = o_ref.shape[1]
    nv = len(ORDER)
    decay = [prm[v, 1:2, :] for v in ORDER]

    def load(j):
        return [o_ref[k, j] for k in range(nv)]

    def store(j, values):
        for k in range(nv):
            o_ref[k, j] = values[k]

    edges = cascade(half, load, store, decay, [jnp.zeros((rb, LANES), f32)] * nv)
    low = low_lanes((rb, LANES))
    for k, v in enumerate(ORDER):
        span, k1, k2, k3 = constants(prm[v, 0:1, :], prm[v, 1:2, :], half)
        e1, e2, e3, e4 = (edges[e][k] for e in range(4))
        c1 = jnp.where(low, 0.0, swap(e1))
        t1 = e1 + span * c1
        t2 = e2 + k1 * c1
        c2 = jnp.where(low, swap(t2), 0.0)
        t2 = t2 + span * c2
        t3 = e3 + k2 * c1 + k1 * c2
        c3 = jnp.where(low, 0.0, swap(t3))
        t3 = t3 + span * c3
        t4 = e4 + k3 * c1 + k2 * c2 + k1 * c3
        c4 = jnp.where(low, swap(t4), 0.0)
        t4 = t4 + span * c4
        es_ref[2 * k, at, :] = jnp.where(low, t2, t1)
        es_ref[2 * k + 1, at, :] = jnp.where(low, t4, t3)
        for e, x in enumerate((e1, e2, e3, e4)):
            el_ref[k, e, at, :] = x


def lon_kernel(rb, prm, sigma, u_ref, o_ref, el_ref, es_ref):
    g = pl.program_id(0)
    half = u_ref.shape[2]

    @pl.when(g == 0)
    def _():
        x = sigma[0]
        lon = x.shape[1]
        es_ref[6] = jnp.where(low_lanes((x.shape[0], LANES)), x[:, 0:1], x[:, lon - 1 : lon])

    def turn(b, _):
        at = pl.ds(pl.multiple_of(b * 8, 8), 8)
        for k in range(len(ORDER)):
            for q in range(0, rb, 8):
                o_ref[k, at, q : q + 8, :] = jnp.swapaxes(u_ref[k, q : q + 8, at, :], 0, 1)
        return 0

    lax.fori_loop(0, half // 8, turn, 0)
    lon_filter(prm, rb, o_ref, el_ref, es_ref, pl.ds(pl.multiple_of(g * rb, 8), rb))


def solve_kernel(n_lat, rows, prm, edges, carries):
    width = edges.shape[2] // 4
    for k, v in enumerate(ORDER):
        const = constants(prm[v, 0:1, :], prm[v, 1:2, :], rows)
        c = solve_carries(n_lat, lambda t, e: edges[t, k, e * width : (e + 1) * width, :], const)
        for e in range(4):
            for t in range(n_lat):
                carries[t, k, e * width : (e + 1) * width, :] = c[e][t]


def carry_kernel(prm, carries, o_ref, el_ref, es_ref):
    width = carries.shape[2] // 4
    zero = jnp.zeros((8, LANES), f32)

    def body(d, _):
        for k in range(len(ORDER)):
            for j in range(width):
                at = d * width + j
                o_ref[k, at] = zero
                for e in range(4):
                    o_ref[k, at, e : e + 1, :] = carries[d, k, e * width + j : e * width + j + 1, :]
        return 0

    lax.fori_loop(0, carries.shape[0], body, 0)
    lon_filter(prm, 8, o_ref, el_ref, es_ref, slice(0, 8))


def join_kernel(n_lon, rows, packed, rq, place, prm, u_ref, w_ref, x_ref, el, elc, *rest):
    sent, sent_x = rest[:n_lon], rest[n_lon : 2 * n_lon]
    y_ref, yx_ref, col_ref, side_ref, energy, carry, extra, resp_x, resp_y, esm, esx = rest[2 * n_lon :]
    g = pl.program_id(0)
    half = resp_x.shape[2]
    lat, me = place[0], place[1]

    @pl.when(g == 0)
    def _():
        energy[...] = jnp.zeros_like(energy)
        for s in range(n_lon):
            t = lax.rem(me - s + n_lon, n_lon)
            esm[t] = sent[s][...]
            esx[t] = sent_x[s][...]
        side_ref[0] = esm[jnp.maximum(me - 1, 0), 6]
        side_ref[1] = esm[jnp.minimum(me + 1, n_lon - 1), 6]
        for k, v in enumerate(ORDER):
            length = prm[v, 0:1, :]
            decay = prm[v, 1:2, :]
            whole = constants(length, decay, 2 * half)
            span, k1, k2, k3 = constants(length, decay, half)

            def solve(gathered, own, k=k, whole=whole, half_c=(span, k1, k2, k3)):
                span, k1, k2, k3 = half_c
                low = low_lanes(own.shape[2:])
                cache = {}

                def edge(t, e):
                    if (t, e // 2) not in cache:
                        x = gathered[t, 2 * k + e // 2]
                        y = swap(x)
                        cache[t, e // 2] = (jnp.where(low, y, x), jnp.where(low, x, y))
                    return cache[t, e // 2][e % 2]

                d1, d2, d3, d4 = pick(solve_carries(n_lon, edge, whole), me)
                e1, e2, e3, e4 = (own[k, e] for e in range(4))
                c1 = jnp.where(low, d1, swap(e1 + span * d1))
                c2 = jnp.where(low, swap(e2 + k1 * c1 + span * d2), d2)
                c3 = jnp.where(low, d3, swap(e3 + k2 * c1 + k1 * c2 + span * d3))
                c4 = jnp.where(low, swap(e4 + k3 * c1 + k2 * c2 + k1 * c3 + span * d4), d4)
                return (c1, c2, c3, c4), d3, d4

            for e, r in enumerate(responses(length, decay, half)):
                resp_x[k, e] = r
            ry = responses(length, decay, rows)
            for e in range(4):
                resp_y[k, e] = ry[e]
            cc, f3, f4 = solve(esx, elc)
            c, d3, d4 = solve(esm, el)

            def total(x, rows_of, ry=ry):
                for e in range(4):
                    x = x + ry[e] * rows_of[e : e + 1, :]
                return x

            for e in range(4):
                extra[k, e] = cc[e]
                carry[k, e] = total(c[e], cc[e])
            if v == 0:
                col_ref[0] = total(d3, f3)
                col_ref[1] = total(d4, f4)

    row8 = lax.broadcasted_iota(jnp.int32, (8, LANES), 0)
    for k, v in enumerate(ORDER):
        total = jnp.zeros((rq, LANES), f32)
        for q in range(0, rows, rq):
            at = slice(q, q + rq)
            c = [carry[k, e, at, :] for e in range(4)]
            ry = [resp_y[k, e, at, :] for e in range(4)]

            def body(b, total, k=k, v=v, q=q, at=at, c=c, ry=ry):
                base = g * packed + b * 8
                rx = [resp_x[k, e, pl.ds(pl.multiple_of(base, 8), 8), :] for e in range(4)]
                for o in range(8):
                    p = b * 8 + o
                    x = x_ref[k, p]
                    y = u_ref[k, p, at, :]
                    for e in range(4):
                        y = y + rx[e][o : o + 1, :] * c[e] + ry[e] * x[e : e + 1, :]
                    y_ref[k, p, at, :] = y
                    total = total + y * w_ref[k, p, at, :]
                    if v == 0 and q == 0:
                        for e in range(4):
                            x = x + rx[e][o : o + 1, :] * extra[k, e]
                        x = pltpu.roll(x, 6, 0)
                        above = jnp.where(lat > 0, x + prm[0, 1:2, :] * y[0:1, :], 0.0)
                        yx_ref[p] = jnp.where(row8 == 0, above, jnp.where(row8 == 1, x, 0.0))
                return total

            total = lax.fori_loop(0, packed // 8, body, total)
        energy[k] += jnp.sum(total.reshape(rq // 8, 8, LANES), axis=0)

    @pl.when(g == 0)
    def _():
        beside = col_ref[0] + prm[0, 1:2, :] * y_ref[ORDER.index(0), 0]
        col_ref[0] = jnp.where(me > 0, beside, 0.0)


def end_kernel(
    rows, pairs, prm, sigma, north, south, vert, bal, col, side, y_ref, yx_ref,
    out, xs, zx, zc, wh, wl, sg, sx,
):
    g = pl.program_id(0)
    half = 2 * pairs
    lon = sigma.shape[2]

    @pl.when(g == 0)
    def _():
        for v in range(3):
            scaled = quad(vert[v]) * prm[v, 3:4, :]
            set_weights(wh, wl, v, scaled.T, True)
        set_weights(wh, wl, 3, quad(bal[...]).T, False)
        stage_sigma(sigma, sg, (0, 1, 2))
        for at in range(0, lon, LANES):
            width = min(LANES, lon - at)
            sx[at // LANES, 0:1, 0:width] = north[:, at : at + width]
            sx[at // LANES, 1:2, 0:width] = south[:, at : at + width]
        lhs = jnp.where(low_lanes((rows, LANES)), col[0], col[1])
        lhs = jnp.concatenate([lhs, jnp.zeros_like(lhs)], axis=1)
        res = product(lhs, wh[0], wl[0])
        zc[0] = swap(res[:, :LANES] * swap(side[0]))
        zc[1] = res[:, LANES:] * side[1]

    lane = lax.broadcasted_iota(jnp.int32, (rows, LANES), 1)
    high = (lane >= 64).astype(jnp.int32)
    high8 = high[0:8]
    chi_row = prm[0, 2:3, :]

    def at_tile(m):
        return pl.ds(pl.multiple_of(m * LANES, LANES), LANES)

    lhs = jnp.concatenate(
        [jnp.concatenate([yx_ref[2 * p], yx_ref[2 * p + 1]], axis=1) for p in range(PAIRS)], axis=0
    )
    res = product(lhs, wh[0], wl[0])
    for p in range(PAIRS):
        m = g * PAIRS + p
        for side in range(2):
            tile = m + side * pairs
            s = jnp.take_along_axis(sx[tile >> 6], 2 * (tile & 63) + high8, axis=1, mode="promise_in_bounds")
            part = res[p * 8 : (p + 1) * 8, side * LANES : (side + 1) * LANES]
            zx[:, at_tile(tile)] = jnp.where(lax.broadcasted_iota(jnp.int32, (8, LANES), 0) < 2, part * s, 0.0)
    for k in range(3):
        for p in range(2 * PAIRS):
            at = slice((p // 2) * rows, (p // 2 + 1) * rows)
            xs[k, at, (p % 2) * LANES : (p % 2 + 1) * LANES] = y_ref[k, p]
    results = {v: product(xs[k], wh[v], wl[v]) for k, v in enumerate(ORDER)}
    for p in range(PAIRS):
        m = g * PAIRS + p
        for side in range(2):
            at = at_tile(m + side * pairs)
            z = [
                results[v][p * rows : (p + 1) * rows, side * LANES : (side + 1) * LANES]
                * sigma_tile(sg, v, m + side * pairs, high)
                for v in range(3)
            ]
            out[0, :, at] = z[0]
            out[1, :, at] = z[1] + chi_row * z[0]
            out[2, :, at] = z[2]

    @pl.when(g == pl.num_programs(0) - 1)
    def _():
        row_id = lax.broadcasted_iota(jnp.int32, (rows, LANES), 0)
        last = half - 1

        def body(b, _):
            for p in range(PAIRS):
                for side in range(2):
                    m = b * PAIRS + p + side * pairs
                    x = out[0, :, at_tile(m)]
                    left = jnp.where(m == 0, zc[0], out[0, :, at_tile(jnp.maximum(m - 1, 0))])
                    right = jnp.where(m == last, zc[1], out[0, :, at_tile(jnp.minimum(m + 1, last))])
                    beside = swap(x + jnp.where(lane >= 64, left, right))
                    above = jnp.where(row_id == 0, zx[0:1, at_tile(m)], pltpu.roll(x, 1, 0))
                    below = jnp.where(row_id == rows - 1, zx[1:2, at_tile(m)], pltpu.roll(x, rows - 1, 0))
                    lap = 4.0 * x - beside - above - below
                    xs[0, p * rows : (p + 1) * rows, side * LANES : (side + 1) * LANES] = lap
            res = product(xs[0], wh[3], wl[3])
            for p in range(PAIRS):
                for side in range(2):
                    at = at_tile(b * PAIRS + p + side * pairs)
                    part = res[p * rows : (p + 1) * rows, side * LANES : (side + 1) * LANES]
                    out[2, :, at] = out[2, :, at] + part
            return 0

        lax.fori_loop(0, pairs // PAIRS, body, 0)


def shards(state, sigma, vert, bal_temp, chi_coef, scales, classes, owner):
    n_lat = lax.axis_size("lat")
    n_lon = lax.axis_size("lon")
    devices = n_lat * n_lon
    nvars, rows, merged = state.shape
    levels = vert.shape[1]
    lon = merged // levels
    half = lon // 2
    pairs = half // 2
    pieces = (lon + LANES - 1) // LANES
    count = nvars * levels
    capacity = (count + devices - 1) // devices + 1
    i_lat = lax.axis_index("lat")
    i_lon = lax.axis_index("lon")

    up_lat, up_lon = ([(i, i + 1) for i in range(n - 1)] for n in (n_lat, n_lon))
    down_lat, down_lon = ([(j, i) for i, j in up] for up in (up_lat, up_lon))
    north = lax.ppermute(state[2, rows - 1 : rows, :], "lat", up_lat)
    south = lax.ppermute(state[2, 0:1, :], "lat", down_lat)
    west = lax.ppermute(state[2, :, merged - levels :], "lon", up_lon)
    east = lax.ppermute(state[2, :, :levels], "lon", down_lon)
    place = jnp.stack([i_lat, i_lon]).astype(jnp.int32)

    anywhere = pl.BlockSpec(memory_space=pl.ANY)
    steps = pairs // BLOCK

    def part(v, side):
        return pl.BlockSpec((1, rows, BLOCK * LANES), lambda g: (v, 0, g + side * steps))

    width = half // n_lat
    shapes = [(nvars, half, rows, LANES), (nvars, rows, half, LANES), (n_lat, nvars, 4 * width, LANES)]

    def lat_call(nv, first, body, arrays, specs, name, aliases, more=()):
        return pl.pallas_call(
            body,
            grid=(steps,),
            in_specs=specs,
            out_specs=[
                pl.BlockSpec((nv, 2 * BLOCK, rows, LANES), lambda g: (first, g, 0, 0)),
                pl.BlockSpec((nv, rows, 2 * BLOCK, LANES), lambda g: (first, 0, g, 0)),
                pl.BlockSpec((2 * BLOCK // width, nv, 4 * width, LANES), lambda g: (g, first, 0, 0)),
            ]
            + [full(s) for s in more],
            out_shape=[jax.ShapeDtypeStruct(s, f32) for s in shapes + list(more)],
            scratch_shapes=[
                pltpu.VMEM((2, PAIRS * rows, 256), f32),
                pltpu.VMEM((2, 256, 256), bf16),
                pltpu.VMEM((2, 256, 256), bf16),
                pltpu.VMEM((nvars, pieces, rows, LANES), f32),
            ],
            compiler_params=params(),
            cost_estimate=pl.CostEstimate(
                flops=nv * 60000000, bytes_accessed=nv * 3 * rows * merged * 4, transcendentals=0
            ),
            input_output_aliases=aliases,
            name=name,
        )(*arrays)

    ins = [scales, classes.reshape(1, count), chi_coef.reshape(1, levels), sigma, vert] + [state] * 4
    specs = [full(x.shape) for x in ins[:5]] + [part(1, 0), part(1, 1), part(2, 0), part(2, 1)]
    specs[0] = pl.BlockSpec(memory_space=pltpu.SMEM)
    body = functools.partial(lat_plain, rows, pairs)
    *wue, prm = lat_call(2, 0, body, ins, specs, "lat_chi_temp", {}, [(nvars, 4, LANES)])
    ins = [prm, sigma, vert, bal_temp] + [state] * 5 + [north, south, west, east] + list(wue)
    specs = [full(x.shape) for x in ins[:4]] + [part(0, 0), part(0, 1), part(1, 0), part(1, 1)]
    specs += [pl.BlockSpec((1, rows, merged), lambda g: (2, 0, 0))]
    specs += [full(x.shape) for x in (north, south, west, east)] + [anywhere] * 3
    aliases = {13: 0, 14: 1, 15: 2}
    w, u, edges = lat_call(1, 2, functools.partial(lat_balance, rows, pairs), ins, specs, "lat_psi", aliases)
    def trade(x):
        return lax.all_to_all(x, "lat", split_axis=0, concat_axis=0, tiled=True)

    shares = trade(edges)

    rb = BLOCK
    local, el, es = pl.pallas_call(
        functools.partial(lon_kernel, rb),
        grid=(rows // rb,),
        in_specs=[
            full(prm.shape),
            pl.BlockSpec((1, rows, lon), lambda g: (0, 0, 0)),
            pl.BlockSpec((nvars, rb, half, LANES), lambda g: (0, g, 0, 0)),
        ],
        out_specs=[
            pl.BlockSpec((nvars, half, rb, LANES), lambda g: (0, 0, g, 0)),
            full((nvars, 4, rows, LANES)),
            full((7, rows, LANES)),
        ],
        out_shape=[
            jax.ShapeDtypeStruct((nvars, half, rows, LANES), f32),
            jax.ShapeDtypeStruct((nvars, 4, rows, LANES), f32),
            jax.ShapeDtypeStruct((7, rows, LANES), f32),
        ],
        compiler_params=params(),
        cost_estimate=pl.CostEstimate(
            flops=180000000, bytes_accessed=6 * rows * merged * 4, transcendentals=0
        ),
        name="lon_tile",
    )(prm, sigma, u)

    def round_lon(x):
        return [x] + [
            lax.ppermute(x, "lon", [(i, (i + s) % n_lon) for i in range(n_lon)]) for s in range(1, n_lon)
        ]

    sent = round_lon(es)
    carries = pl.pallas_call(
        functools.partial(solve_kernel, n_lat, rows),
        grid=(1,),
        in_specs=[full(prm.shape), full(shares.shape)],
        out_specs=full(shares.shape),
        out_shape=jax.ShapeDtypeStruct(shares.shape, f32),
        compiler_params=params(),
        cost_estimate=pl.CostEstimate(flops=1000000, bytes_accessed=2 * shares.size * 4, transcendentals=0),
        name="solve",
    )(prm, shares)
    carries = trade(carries)

    row, _ = lax.optimization_barrier((sigma[0], es))
    sig_n = lax.ppermute(row[rows - 1 : rows], "lat", up_lat)
    sig_s = lax.ppermute(row[0:1], "lat", down_lat)

    crossed, elc, esc = pl.pallas_call(
        carry_kernel,
        grid=(1,),
        in_specs=[full(prm.shape), full(carries.shape)],
        out_specs=[full((nvars, half, 8, LANES)), full((nvars, 4, 8, LANES)), full((6, 8, LANES))],
        out_shape=[
            jax.ShapeDtypeStruct((nvars, half, 8, LANES), f32),
            jax.ShapeDtypeStruct((nvars, 4, 8, LANES), f32),
            jax.ShapeDtypeStruct((6, 8, LANES), f32),
        ],
        compiler_params=params(),
        cost_estimate=pl.CostEstimate(
            flops=30000000, bytes_accessed=4 * nvars * 12 * half * LANES, transcendentals=0
        ),
        name="lon_carry",
    )(prm, carries)
    sent_x = round_lon(esc)

    packed = 2 * PAIRS

    def columns(r):
        return pl.BlockSpec((nvars, packed, r, LANES), lambda g: (0, g, 0, 0))

    ins = [place, prm, local, w, crossed, el, elc] + sent + sent_x
    specs = [full(x.shape) for x in ins]
    specs[0] = pl.BlockSpec(memory_space=pltpu.SMEM)
    specs[2:5] = [columns(rows), columns(rows), columns(8)]
    y, yx, col, side, energy = pl.pallas_call(
        functools.partial(join_kernel, n_lon, rows, packed, 24),
        grid=(half // packed,),
        in_specs=specs,
        out_specs=[
            columns(rows),
            pl.BlockSpec((packed, 8, LANES), lambda g: (g, 0, 0)),
            full((2, rows, LANES)),
            full((2, rows, LANES)),
            full((nvars, 8, LANES)),
        ],
        out_shape=[
            jax.ShapeDtypeStruct((nvars, half, rows, LANES), f32),
            jax.ShapeDtypeStruct((half, 8, LANES), f32),
            jax.ShapeDtypeStruct((2, rows, LANES), f32),
            jax.ShapeDtypeStruct((2, rows, LANES), f32),
            jax.ShapeDtypeStruct((nvars, 8, LANES), f32),
        ],
        scratch_shapes=[
            pltpu.VMEM((nvars, 4, rows, LANES), f32),
            pltpu.VMEM((nvars, 4, 8, LANES), f32),
            pltpu.VMEM((nvars, 4, half, LANES), f32),
            pltpu.VMEM((nvars, 4, rows, LANES), f32),
            pltpu.VMEM((n_lon, 7, rows, LANES), f32),
            pltpu.VMEM((n_lon, 6, 8, LANES), f32),
        ],
        compiler_params=params(),
        cost_estimate=pl.CostEstimate(
            flops=60000000, bytes_accessed=9 * rows * merged * 4, transcendentals=0
        ),
        name="join",
    )(*ins)

    index = jnp.arange(count, dtype=jnp.int32)
    same = (owner[:, None] == owner[None, :]) & (index[None, :] < index[:, None])
    slot = jnp.sum(same.astype(jnp.int32), axis=1)
    target = owner * capacity + slot
    hit = target[:, None] == jnp.arange(devices * capacity)[None, :]
    energy = jnp.stack([energy[ORDER.index(v)] for v in range(nvars)])
    energy = jnp.sum(energy, axis=1) * prm[:, 3]
    energy = (energy[:, :levels] + energy[:, levels:]).reshape(count)
    table = jnp.sum(jnp.where(hit, energy[:, None], 0.0), axis=0).reshape(devices, capacity)
    table = lax.all_to_all(table, ("lat", "lon"), split_axis=0, concat_axis=0, tiled=True)
    slab_energy = (jnp.sum(table, axis=0) / (devices * rows * lon))[None, :]

    ins = [prm, sigma, sig_n, sig_s, vert, bal_temp, col, side, y, yx]
    specs = [full(x.shape) for x in ins]
    specs[8] = columns(rows)
    specs[9] = pl.BlockSpec((packed, 8, LANES), lambda g: (g, 0, 0))
    applied = pl.pallas_call(
        functools.partial(end_kernel, rows, pairs),
        grid=(half // packed,),
        in_specs=specs,
        out_specs=full(state.shape),
        out_shape=jax.ShapeDtypeStruct(state.shape, f32),
        scratch_shapes=[
            pltpu.VMEM((nvars, PAIRS * rows, 256), f32),
            pltpu.VMEM((8, merged), f32),
            pltpu.VMEM((2, rows, LANES), f32),
            pltpu.VMEM((4, 256, 256), bf16),
            pltpu.VMEM((4, 256, 256), bf16),
            pltpu.VMEM((nvars, pieces, rows, LANES), f32),
            pltpu.VMEM((pieces, 8, LANES), f32),
        ],
        compiler_params=params(),
        cost_estimate=pl.CostEstimate(
            flops=300000000, bytes_accessed=6 * rows * merged * 4, transcendentals=0
        ),
        name="finish",
    )(*ins)
    return (applied, slab_energy)


def solution(mesh):
    return jax.shard_map(
        shards,
        mesh=mesh,
        in_specs=(P(None, "lat", "lon"), P(None, "lat", "lon"), P(), P(), P(), P(), P(), P()),
        out_specs=(P(None, "lat", "lon"), P(("lat", "lon"), None)),
        check_vma=False,
    )
```

```python
import functools

import jax
import jax.numpy as jnp
from jax import lax
from jax.experimental import pallas as pl
from jax.experimental.pallas import tpu as pltpu
from jax.sharding import PartitionSpec as P

highest = lax.Precision.HIGHEST
f32 = jnp.float32
bf16 = jnp.bfloat16
LANES = 128
PAIRS = 8
BLOCK = 24
ORDER = (1, 2, 0)
LIMIT = 60 * 1024 * 1024


def params():
    return pltpu.CompilerParams(vmem_limit_bytes=LIMIT)


def full(shape):
    return pl.BlockSpec(shape, lambda g: (0,) * len(shape))


def swap(x):
    return pltpu.roll(x, 64, x.ndim - 1)


def low_lanes(shape):
    return lax.broadcasted_iota(jnp.int32, shape, len(shape) - 1) < 64


def halves(x):
    hi = x.astype(bf16)
    return hi, (x - hi.astype(f32)).astype(bf16)


def dot(x, y):
    return jnp.dot(x, y, preferred_element_type=f32)


def split(x):
    hi, lo = halves(x)
    return jnp.concatenate([hi, lo, hi], axis=1)


def product(x, weights):
    return dot(split(x), weights)


def expand(mat, mixed):
    wide = quad(mat)
    wide = jnp.concatenate([wide, wide], axis=1)
    wide = jnp.concatenate([wide, wide], axis=0)
    src = lax.broadcasted_iota(jnp.int32, (256, 256), 0) // 64
    dst = lax.broadcasted_iota(jnp.int32, (256, 256), 1) // 64
    if mixed:
        src = jnp.where(src == 1, 2, jnp.where(src == 2, 1, src))
    return halves(jnp.where(src == dst, wide, 0.0))


def quad(mat):
    if mat.shape[0] == LANES:
        return mat
    wide = jnp.concatenate([mat, mat], axis=1)
    return jnp.concatenate([wide, wide], axis=0)


def constants(length, decay, m):
    span = jnp.exp(-float(m) / length)
    d = 1.0 - decay * decay
    k1 = decay * (1.0 - span * span) / d
    k2 = (m * span - decay * decay * (span - span * span * span) / d) / d
    tail = decay * decay * (1.0 + span * span) * (1.0 - span * span) / d
    k3 = decay / (d * d) * (1.0 - (2.0 * m + 1.0) * span * span + tail)
    return span, k1, k2, k3


def responses(length, decay, m):
    j = lax.broadcasted_iota(jnp.int32, (m, LANES), 0).astype(f32)
    up = jnp.exp(-j / length)
    down = jnp.exp(-(m - j) / length)
    span = jnp.exp(-float(m) / length)
    d = 1.0 - decay * decay
    diff = up - span * down
    g3 = decay * diff / d
    g2 = ((m - j) * down - decay * decay * (span * up - span * span * down) / d) / d
    part = decay * decay * (1.0 + span * span) * diff / d
    g1 = decay / (d * d) * ((j + 1.0) * up - (2.0 * m + 1.0 - j) * span * down + part)
    return g1, g2, g3, down


def pick(all_carries, me):
    out = []
    for cs in all_carries:
        mine = cs[0]
        for t in range(1, len(cs)):
            mine = jnp.where(me == t, cs[t], mine)
        out.append(mine)
    return out


def solve_carries(n, edge, const):
    span, k1, k2, k3 = const
    first = edge(0, 0)
    zero = jnp.zeros_like(first)
    e1 = [first] + [edge(t, 0) for t in range(1, n)]
    c1, c2, c3, c4 = ([None] * n for _ in range(4))
    c = zero
    for t in range(n):
        c1[t] = c
        c = e1[t] + span * c
    c = zero
    for t in reversed(range(n)):
        c2[t] = c
        c = edge(t, 1) + k1 * c1[t] + span * c
    c = zero
    for t in range(n):
        c3[t] = c
        c = edge(t, 2) + k2 * c1[t] + k1 * c2[t] + span * c
    c = zero
    for t in reversed(range(n)):
        c4[t] = c
        c = edge(t, 3) + k3 * c1[t] + k2 * c2[t] + k1 * c3[t] + span * c
    return c1, c2, c3, c4


def cascade(count, load, store, decay, start):
    step = 8
    edges = []
    for stage in range(4):
        back = stage % 2 == 1

        def body(b, states, back=back):
            base = (count // step - 1 - b) * step if back else b * step
            order = range(step - 1, -1, -1) if back else range(step)
            for o in order:
                new = [decay_k * s + x for decay_k, s, x in zip(decay, states, load(base + o))]
                store(base + o, new)
                states = new
            return tuple(states)

        states = lax.fori_loop(0, count // step, body, tuple(start))
        edges.append(list(states))
    return edges


def stage_sigma(sigma, sg, variables):
    lon = sigma.shape[2]
    for v in variables:
        for at in range(0, lon, LANES):
            width = min(LANES, lon - at)
            sg[v, at // LANES, :, 0:width] = sigma[v, :, at : at + width]


def sigma_tile(sg, v, m, high):
    idx = 2 * (m & 63) + high
    return jnp.take_along_axis(sg[v, m >> 6], idx, axis=1, mode="promise_in_bounds")


def set_weights(weights, k, mat, mixed):
    hi, lo = expand(mat, mixed)
    weights[768 * k : 768 * k + 256] = hi
    weights[768 * k + 256 : 768 * k + 512] = hi
    weights[768 * k + 512 : 768 * k + 768] = lo


def weight(weights, k):
    return weights[768 * k : 768 * (k + 1)]


def lat_filter(vs, rows, prm, u_ref, e_ref):
    nv = len(vs)
    decay = [prm[v, 1:2, :] for v in vs]

    def load(i):
        return [u_ref[k, i] for k in range(nv)]

    def store(i, values):
        for k in range(nv):
            u_ref[k, i] = values[k]

    zero = jnp.zeros((u_ref.shape[2], LANES), f32)
    edges = cascade(rows, load, store, decay, [zero] * nv)
    width = e_ref.shape[2] // 4
    for e in range(4):
        for k in range(nv):
            for c in range(e_ref.shape[0]):
                e_ref[c, k, e * width : (e + 1) * width] = edges[e][k][c * width : (c + 1) * width]


def put_mixed(k, b, rows, res, w_ref, u_ref):
    base = b * 2 * PAIRS
    for p in range(PAIRS):
        part = res[p * rows : (p + 1) * rows]
        w_ref[k, base + 2 * p] = part[:, :LANES]
        w_ref[k, base + 2 * p + 1] = part[:, LANES:]
    at = pl.ds(pl.multiple_of(base, 2 * PAIRS), 2 * PAIRS)
    u_ref[k, :, at, :] = jnp.swapaxes(w_ref[k, at], 0, 1)


def set_params(scales, classes, chi_coef, prm):
    coef = jnp.concatenate([chi_coef[...], chi_coef[...]], axis=1)
    for v in range(3):
        kind = classes[:, 64 * v : 64 * (v + 1)]
        kind = jnp.concatenate([kind, kind], axis=1)
        length = jnp.zeros((1, LANES), f32)
        for n in range(scales.shape[0]):
            length = jnp.where(kind == n, scales[n], length)
        decay = jnp.exp(-1.0 / length)
        norm = 1.0 - decay
        norm = norm * norm
        norm = norm * norm
        prm[v, 0:1, :] = length
        prm[v, 1:2, :] = decay
        prm[v, 2:3, :] = coef
        prm[v, 3:4, :] = length * jnp.sqrt(length) * norm * norm


def lat_plain(
    rows, pairs, scales, classes, chi_coef, sigma, vert, b1lo, b1hi, b2lo, b2hi,
    w_ref, u_ref, e_ref, prm, xs, wt, sg,
):
    g = pl.program_id(0)

    @pl.when(g == 0)
    def _():
        set_params(scales, classes, chi_coef, prm)
        set_weights(wt, 0, vert[1], True)
        set_weights(wt, 1, vert[2], True)
        stage_sigma(sigma, sg, (1, 2))

    lane = lax.broadcasted_iota(jnp.int32, (rows, LANES), 1)
    high = (lane >= 64).astype(jnp.int32)

    def body(b, _):
        for p in range(PAIRS):
            at = slice(p * rows, (p + 1) * rows)
            cols = pl.ds(pl.multiple_of((b * PAIRS + p) * LANES, LANES), LANES)
            m = g * BLOCK + b * PAIRS + p
            for k, sides in enumerate(((b1lo, b1hi), (b2lo, b2hi))):
                for side in range(2):
                    s = sigma_tile(sg, k + 1, m + side * pairs, high)
                    xs[k, at, side * LANES : (side + 1) * LANES] = sides[side][0, :, cols] * s
        for k in range(2):
            put_mixed(k, b, rows, product(xs[k], weight(wt, k)), w_ref, u_ref)
        return 0

    lax.fori_loop(0, BLOCK // PAIRS, body, 0)
    lat_filter((1, 2), rows, prm, u_ref, e_ref)


def lat_balance(
    rows, pairs, prm, sigma, vert, bal, plo, phi, clo, chi, temp, north, south, west, east, w_in, u_in, e_in,
    w_ref, u_ref, e_ref, xs, wt, sg,
):
    del w_in, u_in, e_in
    g = pl.program_id(0)

    @pl.when(g == 0)
    def _():
        set_weights(wt, 0, vert[0], True)
        (bh, bl), (vh, vl) = halves(bal[...]), halves(vert[0])
        set_weights(wt, 1, dot(bh, vh) + dot(bl, vh) + dot(bh, vl), True)
        stage_sigma(sigma, sg, (0,))

    lane = lax.broadcasted_iota(jnp.int32, (rows, LANES), 1)
    row_id = lax.broadcasted_iota(jnp.int32, (rows, LANES), 0)
    high = (lane >= 64).astype(jnp.int32)
    chi_row = prm[0, 2:3, :]
    last = 2 * pairs - 1
    beyond = [jnp.concatenate([x[...], x[...]], axis=1) for x in (west, east)]

    def at_tile(m):
        return pl.ds(pl.multiple_of(m * LANES, LANES), LANES)

    def laplace(m):
        x = temp[0, :, at_tile(m)]
        left = jnp.where(m == 0, beyond[0], temp[0, :, at_tile(jnp.maximum(m - 1, 0))])
        right = jnp.where(m == last, beyond[1], temp[0, :, at_tile(jnp.minimum(m + 1, last))])
        beside = swap(x + jnp.where(lane >= 64, left, right))
        above = jnp.where(row_id == 0, north[:, at_tile(m)], pltpu.roll(x, 1, 0))
        below = jnp.where(row_id == rows - 1, south[:, at_tile(m)], pltpu.roll(x, rows - 1, 0))
        return 4.0 * x - beside - above - below

    def body(b, _):
        for p in range(PAIRS):
            at = slice(p * rows, (p + 1) * rows)
            cols = at_tile(b * PAIRS + p)
            m = g * BLOCK + b * PAIRS + p
            for side, (pr, cr) in enumerate(((plo, clo), (phi, chi))):
                s = sigma_tile(sg, 0, m + side * pairs, high)
                to = slice(side * LANES, (side + 1) * LANES)
                xs[0, at, to] = (pr[0, :, cols] + chi_row * cr[0, :, cols]) * s
                xs[1, at, to] = laplace(m + side * pairs) * s
        res = dot(jnp.concatenate([split(xs[0]), split(xs[1])], axis=1), wt[...])
        put_mixed(0, b, rows, res, w_ref, u_ref)
        return 0

    lax.fori_loop(0, BLOCK // PAIRS, body, 0)
    lat_filter((0,), rows, prm, u_ref, e_ref)


def lon_filter(prm, rb, o_ref, el_ref, es_ref, at):
    half = o_ref.shape[1]
    nv = len(ORDER)
    decay = [prm[v, 1:2, :] for v in ORDER]

    def load(j):
        return [o_ref[k, j] for k in range(nv)]

    def store(j, values):
        for k in range(nv):
            o_ref[k, j] = values[k]

    edges = cascade(half, load, store, decay, [jnp.zeros((rb, LANES), f32)] * nv)
    low = low_lanes((rb, LANES))
    for k, v in enumerate(ORDER):
        span, k1, k2, k3 = constants(prm[v, 0:1, :], prm[v, 1:2, :], half)
        e1, e2, e3, e4 = (edges[e][k] for e in range(4))
        c1 = jnp.where(low, 0.0, swap(e1))
        t1 = e1 + span * c1
        t2 = e2 + k1 * c1
        c2 = jnp.where(low, swap(t2), 0.0)
        t2 = t2 + span * c2
        t3 = e3 + k2 * c1 + k1 * c2
        c3 = jnp.where(low, 0.0, swap(t3))
        t3 = t3 + span * c3
        t4 = e4 + k3 * c1 + k2 * c2 + k1 * c3
        c4 = jnp.where(low, swap(t4), 0.0)
        t4 = t4 + span * c4
        es_ref[2 * k, at, :] = jnp.where(low, t2, t1)
        es_ref[2 * k + 1, at, :] = jnp.where(low, t4, t3)
        for e, x in enumerate((e1, e2, e3, e4)):
            el_ref[k, e, at, :] = x


def lon_kernel(rb, prm, sigma, u_ref, o_ref, el_ref, es_ref):
    g = pl.program_id(0)
    half = u_ref.shape[2]

    @pl.when(g == 0)
    def _():
        x = sigma[0]
        lon = x.shape[1]
        es_ref[6] = jnp.where(low_lanes((x.shape[0], LANES)), x[:, 0:1], x[:, lon - 1 : lon])

    def turn(b, _):
        at = pl.ds(pl.multiple_of(b * 8, 8), 8)
        for k in range(len(ORDER)):
            for q in range(0, rb, 8):
                o_ref[k, at, q : q + 8, :] = jnp.swapaxes(u_ref[k, q : q + 8, at, :], 0, 1)
        return 0

    lax.fori_loop(0, half // 8, turn, 0)
    lon_filter(prm, rb, o_ref, el_ref, es_ref, pl.ds(pl.multiple_of(g * rb, 8), rb))


def solve_kernel(n_lat, rows, prm, edges, carries):
    width = edges.shape[2] // 4
    for k, v in enumerate(ORDER):
        const = constants(prm[v, 0:1, :], prm[v, 1:2, :], rows)
        c = solve_carries(n_lat, lambda t, e: edges[t, k, e * width : (e + 1) * width, :], const)
        for e in range(4):
            for t in range(n_lat):
                carries[t, k, e * width : (e + 1) * width, :] = c[e][t]


def carry_kernel(prm, carries, o_ref, el_ref, es_ref):
    width = carries.shape[2] // 4
    zero = jnp.zeros((8, LANES), f32)

    def body(d, _):
        for k in range(len(ORDER)):
            for j in range(width):
                at = d * width + j
                o_ref[k, at] = zero
                for e in range(4):
                    o_ref[k, at, e : e + 1, :] = carries[d, k, e * width + j : e * width + j + 1, :]
        return 0

    lax.fori_loop(0, carries.shape[0], body, 0)
    lon_filter(prm, 8, o_ref, el_ref, es_ref, slice(0, 8))


def join_kernel(n_lon, rows, packed, rq, place, prm, u_ref, w_ref, x_ref, el, elc, *rest):
    sent, sent_x = rest[:n_lon], rest[n_lon : 2 * n_lon]
    y_ref, yx_ref, col_ref, side_ref, energy, carry, extra, resp_x, resp_y, esm, esx = rest[2 * n_lon :]
    g = pl.program_id(0)
    half = resp_x.shape[2]
    lat, me = place[0], place[1]

    @pl.when(g == 0)
    def _():
        energy[...] = jnp.zeros_like(energy)
        for s in range(n_lon):
            t = lax.rem(me - s + n_lon, n_lon)
            esm[t] = sent[s][...]
            esx[t] = sent_x[s][...]
        side_ref[0] = esm[jnp.maximum(me - 1, 0), 6]
        side_ref[1] = esm[jnp.minimum(me + 1, n_lon - 1), 6]
        for k, v in enumerate(ORDER):
            length = prm[v, 0:1, :]
            decay = prm[v, 1:2, :]
            whole = constants(length, decay, 2 * half)
            span, k1, k2, k3 = constants(length, decay, half)

            def solve(gathered, own, k=k, whole=whole, half_c=(span, k1, k2, k3)):
                span, k1, k2, k3 = half_c
                low = low_lanes(own.shape[2:])
                cache = {}

                def edge(t, e):
                    if (t, e // 2) not in cache:
                        x = gathered[t, 2 * k + e // 2]
                        y = swap(x)
                        cache[t, e // 2] = (jnp.where(low, y, x), jnp.where(low, x, y))
                    return cache[t, e // 2][e % 2]

                d1, d2, d3, d4 = pick(solve_carries(n_lon, edge, whole), me)
                e1, e2, e3, e4 = (own[k, e] for e in range(4))
                c1 = jnp.where(low, d1, swap(e1 + span * d1))
                c2 = jnp.where(low, swap(e2 + k1 * c1 + span * d2), d2)
                c3 = jnp.where(low, d3, swap(e3 + k2 * c1 + k1 * c2 + span * d3))
                c4 = jnp.where(low, swap(e4 + k3 * c1 + k2 * c2 + k1 * c3 + span * d4), d4)
                return (c1, c2, c3, c4), d3, d4

            for e, r in enumerate(responses(length, decay, half)):
                resp_x[k, e] = r
            ry = responses(length, decay, rows)
            for e in range(4):
                resp_y[k, e] = ry[e]
            cc, f3, f4 = solve(esx, elc)
            c, d3, d4 = solve(esm, el)

            def total(x, rows_of, ry=ry):
                for e in range(4):
                    x = x + ry[e] * rows_of[e : e + 1, :]
                return x

            for e in range(4):
                extra[k, e] = cc[e]
                carry[k, e] = total(c[e], cc[e])
            if v == 0:
                col_ref[0] = total(d3, f3)
                col_ref[1] = total(d4, f4)

    row8 = lax.broadcasted_iota(jnp.int32, (8, LANES), 0)
    for k, v in enumerate(ORDER):
        total = jnp.zeros((rq, LANES), f32)
        for q in range(0, rows, rq):
            at = slice(q, q + rq)
            c = [carry[k, e, at, :] for e in range(4)]
            ry = [resp_y[k, e, at, :] for e in range(4)]

            def body(b, total, k=k, v=v, q=q, at=at, c=c, ry=ry):
                base = g * packed + b * 8
                rx = [resp_x[k, e, pl.ds(pl.multiple_of(base, 8), 8), :] for e in range(4)]
                for o in range(8):
                    p = b * 8 + o
                    x = x_ref[k, p]
                    y = u_ref[k, p, at, :]
                    for e in range(4):
                        y = y + rx[e][o : o + 1, :] * c[e] + ry[e] * x[e : e + 1, :]
                    y_ref[k, p, at, :] = y
                    total = total + y * w_ref[k, p, at, :]
                    if v == 0 and q == 0:
                        for e in range(4):
                            x = x + rx[e][o : o + 1, :] * extra[k, e]
                        x = pltpu.roll(x, 6, 0)
                        above = jnp.where(lat > 0, x + prm[0, 1:2, :] * y[0:1, :], 0.0)
                        yx_ref[p] = jnp.where(row8 == 0, above, jnp.where(row8 == 1, x, 0.0))
                return total

            total = lax.fori_loop(0, packed // 8, body, total)
        energy[v] += jnp.sum(total.reshape(rq // 8, 8, LANES), axis=0)

    @pl.when(g == 0)
    def _():
        beside = col_ref[0] + prm[0, 1:2, :] * y_ref[ORDER.index(0), 0]
        col_ref[0] = jnp.where(me > 0, beside, 0.0)


def end_kernel(
    rows, pairs, prm, sigma, north, south, vert, bal, col, side, y_ref, yx_ref,
    out, xs, zx, zc, wt, sg, sx,
):
    g = pl.program_id(0)
    half = 2 * pairs
    lon = sigma.shape[2]
    merged = out.shape[2]

    @pl.when(g == 0)
    def _():
        for v in range(3):
            scaled = quad(vert[v]) * prm[v, 3:4, :]
            set_weights(wt, v, scaled.T, True)
        set_weights(wt, 3, quad(bal[...]).T, False)
        stage_sigma(sigma, sg, (0, 1, 2))
        for at in range(0, lon, LANES):
            width = min(LANES, lon - at)
            sx[at // LANES, 0:1, 0:width] = north[:, merged + at : merged + at + width]
            sx[at // LANES, 1:2, 0:width] = south[:, merged + at : merged + at + width]
        lhs = jnp.where(low_lanes((rows, LANES)), col[0], col[1])
        lhs = jnp.concatenate([lhs, jnp.zeros_like(lhs)], axis=1)
        res = product(lhs, weight(wt, 0))
        zc[0] = swap(res[:, :LANES] * swap(side[0]))
        zc[1] = res[:, LANES:] * side[1]

    lane = lax.broadcasted_iota(jnp.int32, (rows, LANES), 1)
    high = (lane >= 64).astype(jnp.int32)
    high8 = high[0:8]
    chi_row = prm[0, 2:3, :]

    def at_tile(m):
        return pl.ds(pl.multiple_of(m * LANES, LANES), LANES)

    lhs = jnp.concatenate(
        [jnp.concatenate([yx_ref[2 * p], yx_ref[2 * p + 1]], axis=1) for p in range(PAIRS)], axis=0
    )
    res = product(lhs, weight(wt, 0))
    for p in range(PAIRS):
        m = g * PAIRS + p
        for side in range(2):
            tile = m + side * pairs
            s = jnp.take_along_axis(sx[tile >> 6], 2 * (tile & 63) + high8, axis=1, mode="promise_in_bounds")
            part = res[p * 8 : (p + 1) * 8, side * LANES : (side + 1) * LANES]
            zx[:, at_tile(tile)] = jnp.where(lax.broadcasted_iota(jnp.int32, (8, LANES), 0) < 2, part * s, 0.0)
    for k in range(3):
        for p in range(2 * PAIRS):
            at = slice((p // 2) * rows, (p // 2 + 1) * rows)
            xs[k, at, (p % 2) * LANES : (p % 2 + 1) * LANES] = y_ref[k, p]
    results = {v: product(xs[k], weight(wt, v)) for k, v in enumerate(ORDER)}
    for p in range(PAIRS):
        m = g * PAIRS + p
        for side in range(2):
            at = at_tile(m + side * pairs)
            z = [
                results[v][p * rows : (p + 1) * rows, side * LANES : (side + 1) * LANES]
                * sigma_tile(sg, v, m + side * pairs, high)
                for v in range(3)
            ]
            out[0, :, at] = z[0]
            out[1, :, at] = z[1] + chi_row * z[0]
            out[2, :, at] = z[2]

    @pl.when(g == pl.num_programs(0) - 1)
    def _():
        row_id = lax.broadcasted_iota(jnp.int32, (rows, LANES), 0)
        last = half - 1

        def body(b, _):
            for p in range(PAIRS):
                for side in range(2):
                    m = b * PAIRS + p + side * pairs
                    x = out[0, :, at_tile(m)]
                    left = jnp.where(m == 0, zc[0], out[0, :, at_tile(jnp.maximum(m - 1, 0))])
                    right = jnp.where(m == last, zc[1], out[0, :, at_tile(jnp.minimum(m + 1, last))])
                    beside = swap(x + jnp.where(lane >= 64, left, right))
                    above = jnp.where(row_id == 0, zx[0:1, at_tile(m)], pltpu.roll(x, 1, 0))
                    below = jnp.where(row_id == rows - 1, zx[1:2, at_tile(m)], pltpu.roll(x, rows - 1, 0))
                    lap = 4.0 * x - beside - above - below
                    xs[0, p * rows : (p + 1) * rows, side * LANES : (side + 1) * LANES] = lap
            res = product(xs[0], weight(wt, 3))
            for p in range(PAIRS):
                for side in range(2):
                    at = at_tile(b * PAIRS + p + side * pairs)
                    part = res[p * rows : (p + 1) * rows, side * LANES : (side + 1) * LANES]
                    out[2, :, at] = out[2, :, at] + part
            return 0

        lax.fori_loop(0, pairs // PAIRS, body, 0)


def shards(state, sigma, vert, bal_temp, chi_coef, scales, classes, owner):
    n_lat = lax.axis_size("lat")
    n_lon = lax.axis_size("lon")
    devices = n_lat * n_lon
    nvars, rows, merged = state.shape
    levels = vert.shape[1]
    lon = merged // levels
    half = lon // 2
    pairs = half // 2
    pieces = (lon + LANES - 1) // LANES
    count = nvars * levels
    capacity = (count + devices - 1) // devices + 1
    i_lat = lax.axis_index("lat")
    i_lon = lax.axis_index("lon")

    up_lat, up_lon = ([(i, i + 1) for i in range(n - 1)] for n in (n_lat, n_lon))
    down_lat, down_lon = ([(j, i) for i, j in up] for up in (up_lat, up_lon))

    def row(i):
        return jnp.concatenate([state[2, i : i + 1, :], sigma[0, i : i + 1, :]], axis=1)

    north = lax.ppermute(row(rows - 1), "lat", up_lat)
    south = lax.ppermute(row(0), "lat", down_lat)
    west = lax.ppermute(state[2, :, merged - levels :], "lon", up_lon)
    east = lax.ppermute(state[2, :, :levels], "lon", down_lon)
    place = jnp.stack([i_lat, i_lon]).astype(jnp.int32)

    anywhere = pl.BlockSpec(memory_space=pl.ANY)
    steps = pairs // BLOCK

    def part(v, side):
        return pl.BlockSpec((1, rows, BLOCK * LANES), lambda g: (v, 0, g + side * steps))

    width = half // n_lat
    shapes = [(nvars, half, rows, LANES), (nvars, rows, half, LANES), (n_lat, nvars, 4 * width, LANES)]

    def lat_call(nv, first, body, arrays, specs, name, aliases, more=()):
        return pl.pallas_call(
            body,
            grid=(steps,),
            in_specs=specs,
            out_specs=[
                pl.BlockSpec((nv, 2 * BLOCK, rows, LANES), lambda g: (first, g, 0, 0)),
                pl.BlockSpec((nv, rows, 2 * BLOCK, LANES), lambda g: (first, 0, g, 0)),
                pl.BlockSpec((2 * BLOCK // width, nv, 4 * width, LANES), lambda g: (g, first, 0, 0)),
            ]
            + [full(s) for s in more],
            out_shape=[jax.ShapeDtypeStruct(s, f32) for s in shapes + list(more)],
            scratch_shapes=[
                pltpu.VMEM((2, PAIRS * rows, 256), f32),
                pltpu.VMEM((2 * 768, 256), bf16),
                pltpu.VMEM((nvars, pieces, rows, LANES), f32),
            ],
            compiler_params=params(),
            cost_estimate=pl.CostEstimate(
                flops=nv * 60000000, bytes_accessed=nv * 3 * rows * merged * 4, transcendentals=0
            ),
            input_output_aliases=aliases,
            name=name,
        )(*arrays)

    ins = [scales, classes.reshape(1, count), chi_coef.reshape(1, levels), sigma, vert] + [state] * 4
    specs = [full(x.shape) for x in ins[:5]] + [part(1, 0), part(1, 1), part(2, 0), part(2, 1)]
    specs[0] = pl.BlockSpec(memory_space=pltpu.SMEM)
    body = functools.partial(lat_plain, rows, pairs)
    *wue, prm = lat_call(2, 0, body, ins, specs, "lat_chi_temp", {}, [(nvars, 4, LANES)])
    ins = [prm, sigma, vert, bal_temp] + [state] * 5 + [north, south, west, east] + list(wue)
    specs = [full(x.shape) for x in ins[:4]] + [part(0, 0), part(0, 1), part(1, 0), part(1, 1)]
    specs += [pl.BlockSpec((1, rows, merged), lambda g: (2, 0, 0))]
    specs += [full(x.shape) for x in (north, south, west, east)] + [anywhere] * 3
    aliases = {13: 0, 14: 1, 15: 2}
    w, u, edges = lat_call(1, 2, functools.partial(lat_balance, rows, pairs), ins, specs, "lat_psi", aliases)
    def trade(x):
        return lax.all_to_all(x, "lat", split_axis=0, concat_axis=0, tiled=True)

    shares = trade(edges)

    rb = BLOCK
    local, el, es = pl.pallas_call(
        functools.partial(lon_kernel, rb),
        grid=(rows // rb,),
        in_specs=[
            full(prm.shape),
            pl.BlockSpec((1, rows, lon), lambda g: (0, 0, 0)),
            pl.BlockSpec((nvars, rb, half, LANES), lambda g: (0, g, 0, 0)),
        ],
        out_specs=[
            pl.BlockSpec((nvars, half, rb, LANES), lambda g: (0, 0, g, 0)),
            full((nvars, 4, rows, LANES)),
            full((7, rows, LANES)),
        ],
        out_shape=[
            jax.ShapeDtypeStruct((nvars, half, rows, LANES), f32),
            jax.ShapeDtypeStruct((nvars, 4, rows, LANES), f32),
            jax.ShapeDtypeStruct((7, rows, LANES), f32),
        ],
        compiler_params=params(),
        cost_estimate=pl.CostEstimate(
            flops=180000000, bytes_accessed=6 * rows * merged * 4, transcendentals=0
        ),
        name="lon_tile",
    )(prm, sigma, u)

    def round_lon(x):
        return [x] + [
            lax.ppermute(x, "lon", [(i, (i + s) % n_lon) for i in range(n_lon)]) for s in range(1, n_lon)
        ]

    shares, _ = lax.optimization_barrier((shares, es))
    sent = round_lon(es)
    carries = pl.pallas_call(
        functools.partial(solve_kernel, n_lat, rows),
        grid=(1,),
        in_specs=[full(prm.shape), full(shares.shape)],
        out_specs=full(shares.shape),
        out_shape=jax.ShapeDtypeStruct(shares.shape, f32),
        compiler_params=params(),
        cost_estimate=pl.CostEstimate(flops=1000000, bytes_accessed=2 * shares.size * 4, transcendentals=0),
        name="solve",
    )(prm, shares)
    carries = trade(carries)

    crossed, elc, esc = pl.pallas_call(
        carry_kernel,
        grid=(1,),
        in_specs=[full(prm.shape), full(carries.shape)],
        out_specs=[full((nvars, half, 8, LANES)), full((nvars, 4, 8, LANES)), full((6, 8, LANES))],
        out_shape=[
            jax.ShapeDtypeStruct((nvars, half, 8, LANES), f32),
            jax.ShapeDtypeStruct((nvars, 4, 8, LANES), f32),
            jax.ShapeDtypeStruct((6, 8, LANES), f32),
        ],
        compiler_params=params(),
        cost_estimate=pl.CostEstimate(
            flops=30000000, bytes_accessed=4 * nvars * 12 * half * LANES, transcendentals=0
        ),
        name="lon_carry",
    )(prm, carries)
    sent_x = round_lon(esc)

    packed = 2 * PAIRS

    def columns(r):
        return pl.BlockSpec((nvars, packed, r, LANES), lambda g: (0, g, 0, 0))

    ins = [place, prm, local, w, crossed, el, elc] + sent + sent_x
    specs = [full(x.shape) for x in ins]
    specs[0] = pl.BlockSpec(memory_space=pltpu.SMEM)
    specs[2:5] = [columns(rows), columns(rows), columns(8)]
    y, yx, col, side, energy = pl.pallas_call(
        functools.partial(join_kernel, n_lon, rows, packed, 24),
        grid=(half // packed,),
        in_specs=specs,
        out_specs=[
            columns(rows),
            pl.BlockSpec((packed, 8, LANES), lambda g: (g, 0, 0)),
            full((2, rows, LANES)),
            full((2, rows, LANES)),
            full((nvars, 8, LANES)),
        ],
        out_shape=[
            jax.ShapeDtypeStruct((nvars, half, rows, LANES), f32),
            jax.ShapeDtypeStruct((half, 8, LANES), f32),
            jax.ShapeDtypeStruct((2, rows, LANES), f32),
            jax.ShapeDtypeStruct((2, rows, LANES), f32),
            jax.ShapeDtypeStruct((nvars, 8, LANES), f32),
        ],
        scratch_shapes=[
            pltpu.VMEM((nvars, 4, rows, LANES), f32),
            pltpu.VMEM((nvars, 4, 8, LANES), f32),
            pltpu.VMEM((nvars, 4, half, LANES), f32),
            pltpu.VMEM((nvars, 4, rows, LANES), f32),
            pltpu.VMEM((n_lon, 7, rows, LANES), f32),
            pltpu.VMEM((n_lon, 6, 8, LANES), f32),
        ],
        compiler_params=params(),
        cost_estimate=pl.CostEstimate(
            flops=60000000, bytes_accessed=9 * rows * merged * 4, transcendentals=0
        ),
        name="join",
    )(*ins)

    index = jnp.arange(count, dtype=jnp.int32)
    same = (owner[:, None] == owner[None, :]) & (index[None, :] < index[:, None])
    slot = jnp.sum(same.astype(jnp.int32), axis=1)
    target = owner * capacity + slot
    hit = target[:, None] == jnp.arange(devices * capacity)[None, :]
    energy = jnp.sum(energy, axis=1) * prm[:, 3]
    energy = (energy[:, :levels] + energy[:, levels:]).reshape(count)
    table = jnp.sum(jnp.where(hit, energy[:, None], 0.0), axis=0).reshape(devices, capacity)
    table = lax.all_to_all(table, ("lat", "lon"), split_axis=0, concat_axis=0, tiled=True)
    slab_energy = (jnp.sum(table, axis=0) / (devices * rows * lon))[None, :]

    ins = [prm, sigma, north, south, vert, bal_temp, col, side, y, yx]
    specs = [full(x.shape) for x in ins]
    specs[8] = columns(rows)
    specs[9] = pl.BlockSpec((packed, 8, LANES), lambda g: (g, 0, 0))
    applied = pl.pallas_call(
        functools.partial(end_kernel, rows, pairs),
        grid=(half // packed,),
        in_specs=specs,
        out_specs=full(state.shape),
        out_shape=jax.ShapeDtypeStruct(state.shape, f32),
        scratch_shapes=[
            pltpu.VMEM((nvars, PAIRS * rows, 256), f32),
            pltpu.VMEM((8, merged), f32),
            pltpu.VMEM((2, rows, LANES), f32),
            pltpu.VMEM((4 * 768, 256), bf16),
            pltpu.VMEM((nvars, pieces, rows, LANES), f32),
            pltpu.VMEM((pieces, 8, LANES), f32),
        ],
        compiler_params=params(),
        cost_estimate=pl.CostEstimate(
            flops=300000000, bytes_accessed=6 * rows * merged * 4, transcendentals=0
        ),
        name="finish",
    )(*ins)
    return (applied, slab_energy)


def solution(mesh):
    return jax.shard_map(
        shards,
        mesh=mesh,
        in_specs=(P(None, "lat", "lon"), P(None, "lat", "lon"), P(), P(), P(), P(), P(), P()),
        out_specs=(P(None, "lat", "lon"), P(("lat", "lon"), None)),
        check_vma=False,
    )
```

```python
import functools

import jax
import jax.numpy as jnp
from jax import lax
from jax.experimental import pallas as pl
from jax.experimental.pallas import tpu as pltpu
from jax.sharding import PartitionSpec as P

highest = lax.Precision.HIGHEST
f32 = jnp.float32
bf16 = jnp.bfloat16
LANES = 128
PAIRS = 8
BLOCK = 24
ORDER = (1, 2, 0)
LIMIT = 60 * 1024 * 1024


def params():
    return pltpu.CompilerParams(vmem_limit_bytes=LIMIT)


def full(shape):
    return pl.BlockSpec(shape, lambda g: (0,) * len(shape))


def swap(x):
    return pltpu.roll(x, 64, x.ndim - 1)


def low_lanes(shape):
    return lax.broadcasted_iota(jnp.int32, shape, len(shape) - 1) < 64


def halves(x):
    hi = x.astype(bf16)
    return hi, (x - hi.astype(f32)).astype(bf16)


def products(sources, wh, wl, store, pieces=3):
    count = sources[0][0].shape[0] // (2 * pieces)

    def run(*acc):
        for x, k in sources:
            for unit in range(2):
                pltpu.matmul_push_rhs(wh[k], 0, unit)
                pltpu.matmul_push_rhs(wl[k], 1, unit)
            parts = {}
            for c in range(pieces):
                for unit in range(2):
                    at = (unit * pieces + c) * count
                    parts[unit, c] = hi, lo = halves(x[at : at + count])
                    ref = acc[unit * pieces + c]
                    pltpu.matmul_acc_lhs(ref, hi, load_staged_rhs=0 if c == 0 else None)
                    pltpu.matmul_acc_lhs(ref, lo)
            for c in range(pieces):
                for unit in range(2):
                    ref = acc[unit * pieces + c]
                    pltpu.matmul_acc_lhs(ref, parts[unit, c][0], load_staged_rhs=1 if c == 0 else None)
        for c in range(pieces):
            for unit in range(2):
                store((unit * pieces + c) * count, pltpu.matmul_pop(acc[unit * pieces + c]))

    pl.run_scoped(run, *[pltpu.ACC(unit)((count, 256), f32) for unit in (0, 1) for _ in range(pieces)])


def expand(mat, mixed):
    wide = quad(mat)
    wide = jnp.concatenate([wide, wide], axis=1)
    wide = jnp.concatenate([wide, wide], axis=0)
    src = lax.broadcasted_iota(jnp.int32, (256, 256), 0) // 64
    dst = lax.broadcasted_iota(jnp.int32, (256, 256), 1) // 64
    if mixed:
        src = jnp.where(src == 1, 2, jnp.where(src == 2, 1, src))
    return jnp.where(src == dst, wide, 0.0)


def quad(mat):
    if mat.shape[0] == LANES:
        return mat
    wide = jnp.concatenate([mat, mat], axis=1)
    return jnp.concatenate([wide, wide], axis=0)


def constants(length, decay, m):
    span = jnp.exp(-float(m) / length)
    d = 1.0 - decay * decay
    k1 = decay * (1.0 - span * span) / d
    k2 = (m * span - decay * decay * (span - span * span * span) / d) / d
    tail = decay * decay * (1.0 + span * span) * (1.0 - span * span) / d
    k3 = decay / (d * d) * (1.0 - (2.0 * m + 1.0) * span * span + tail)
    return span, k1, k2, k3


def responses(length, decay, m):
    j = lax.broadcasted_iota(jnp.int32, (m, LANES), 0).astype(f32)
    up = jnp.exp(-j / length)
    down = jnp.exp(-(m - j) / length)
    span = jnp.exp(-float(m) / length)
    d = 1.0 - decay * decay
    diff = up - span * down
    g3 = decay * diff / d
    g2 = ((m - j) * down - decay * decay * (span * up - span * span * down) / d) / d
    part = decay * decay * (1.0 + span * span) * diff / d
    g1 = decay / (d * d) * ((j + 1.0) * up - (2.0 * m + 1.0 - j) * span * down + part)
    return g1, g2, g3, down


def pick(all_carries, me):
    out = []
    for cs in all_carries:
        mine = cs[0]
        for t in range(1, len(cs)):
            mine = jnp.where(me == t, cs[t], mine)
        out.append(mine)
    return out


def solve_carries(n, edge, const):
    span, k1, k2, k3 = const
    first = edge(0, 0)
    zero = jnp.zeros_like(first)
    e1 = [first] + [edge(t, 0) for t in range(1, n)]
    c1, c2, c3, c4 = ([None] * n for _ in range(4))
    c = zero
    for t in range(n):
        c1[t] = c
        c = e1[t] + span * c
    c = zero
    for t in reversed(range(n)):
        c2[t] = c
        c = edge(t, 1) + k1 * c1[t] + span * c
    c = zero
    for t in range(n):
        c3[t] = c
        c = edge(t, 2) + k2 * c1[t] + k1 * c2[t] + span * c
    c = zero
    for t in reversed(range(n)):
        c4[t] = c
        c = edge(t, 3) + k3 * c1[t] + k2 * c2[t] + k1 * c3[t] + span * c
    return c1, c2, c3, c4


def cascade(count, load, store, decay, start):
    step = 8
    edges = []
    for stage in range(4):
        back = stage % 2 == 1

        def body(b, states, back=back):
            base = (count // step - 1 - b) * step if back else b * step
            order = range(step - 1, -1, -1) if back else range(step)
            for o in order:
                new = [decay_k * s + x for decay_k, s, x in zip(decay, states, load(base + o))]
                store(base + o, new)
                states = new
            return tuple(states)

        states = lax.fori_loop(0, count // step, body, tuple(start))
        edges.append(list(states))
    return edges


def stage_sigma(sigma, sg, variables):
    lon = sigma.shape[2]
    for v in variables:
        for at in range(0, lon, LANES):
            width = min(LANES, lon - at)
            sg[v, at // LANES, :, 0:width] = sigma[v, :, at : at + width]


def sigma_tile(sg, v, m, high):
    idx = 2 * (m & 63) + high
    return jnp.take_along_axis(sg[v, m >> 6], idx, axis=1, mode="promise_in_bounds")


def set_weights(wh, wl, k, wide):
    hi, lo = halves(wide)
    wh[k] = hi
    wl[k] = lo


def lat_filter(vs, rows, prm, u_ref, e_ref):
    nv = len(vs)
    decay = [prm[v, 1:2, :] for v in vs]

    def load(i):
        return [u_ref[k, i] for k in range(nv)]

    def store(i, values):
        for k in range(nv):
            u_ref[k, i] = values[k]

    zero = jnp.zeros((u_ref.shape[2], LANES), f32)
    edges = cascade(rows, load, store, decay, [zero] * nv)
    width = e_ref.shape[2] // 4
    for e in range(4):
        for k in range(nv):
            for c in range(e_ref.shape[0]):
                e_ref[c, k, e * width : (e + 1) * width] = edges[e][k][c * width : (c + 1) * width]


def put_mixed(k, rows, res, w_ref, u_ref):
    def body(b, _):
        base = pl.multiple_of(b * 8, 8)
        for o in range(4):
            at = pl.ds(pl.multiple_of((b * 4 + o) * rows, 8), rows)
            w_ref[k, base + 2 * o] = res[at, 0:LANES]
            w_ref[k, base + 2 * o + 1] = res[at, LANES:]
        at = pl.ds(base, 8)
        u_ref[k, :, at, :] = jnp.swapaxes(w_ref[k, at], 0, 1)
        return 0

    lax.fori_loop(0, BLOCK // 4, body, 0)


def set_params(scales, classes, chi_coef, prm):
    coef = jnp.concatenate([chi_coef[...], chi_coef[...]], axis=1)
    for v in range(3):
        kind = classes[:, 64 * v : 64 * (v + 1)]
        kind = jnp.concatenate([kind, kind], axis=1)
        length = jnp.zeros((1, LANES), f32)
        for n in range(scales.shape[0]):
            length = jnp.where(kind == n, scales[n], length)
        decay = jnp.exp(-1.0 / length)
        norm = 1.0 - decay
        norm = norm * norm
        norm = norm * norm
        prm[v, 0:1, :] = length
        prm[v, 1:2, :] = decay
        prm[v, 2:3, :] = coef
        prm[v, 3:4, :] = length * jnp.sqrt(length) * norm * norm


def lat_plain(
    rows, pairs, scales, classes, chi_coef, sigma, vert, b1lo, b1hi, b2lo, b2hi,
    w_ref, u_ref, e_ref, prm, xs, wh, wl, sg,
):
    g = pl.program_id(0)

    @pl.when(g == 0)
    def _():
        set_params(scales, classes, chi_coef, prm)
        set_weights(wh, wl, 0, expand(vert[1], True))
        set_weights(wh, wl, 1, expand(vert[2], True))
        stage_sigma(sigma, sg, (1, 2))

    lane = lax.broadcasted_iota(jnp.int32, (rows, LANES), 1)
    high = (lane >= 64).astype(jnp.int32)

    def body(b, _):
        for o in range(4):
            p = b * 4 + o
            at = pl.ds(pl.multiple_of(p * rows, 8), rows)
            cols = pl.ds(pl.multiple_of(p * LANES, LANES), LANES)
            for k, sides in enumerate(((b1lo, b1hi), (b2lo, b2hi))):
                for side in range(2):
                    s = sigma_tile(sg, k + 1, g * BLOCK + p + side * pairs, high)
                    xs[k, at, side * LANES : (side + 1) * LANES] = sides[side][0, :, cols] * s
        return 0

    lax.fori_loop(0, BLOCK // 4, body, 0)
    for k in range(2):

        def store(first, res, k=k):
            xs[k, first : first + res.shape[0], :] = res

        products([(xs.at[k], k)], wh, wl, store)
        put_mixed(k, rows, xs.at[k], w_ref, u_ref)
    lat_filter((1, 2), rows, prm, u_ref, e_ref)


def lat_balance(
    rows, pairs, prm, sigma, vert, bal, plo, phi, clo, chi, temp, north, south, west, east, w_in, u_in, e_in,
    w_ref, u_ref, e_ref, xs, wh, wl, sg,
):
    del w_in, u_in, e_in
    g = pl.program_id(0)

    @pl.when(g == 0)
    def _():
        set_weights(wh, wl, 0, expand(vert[0], True))
        xs[0, 0:256, :] = expand(bal[...], False)

        def fold(first, res):
            set_rows = slice(first, first + res.shape[0])
            wh[1, set_rows], wl[1, set_rows] = halves(res)

        products([(xs.at[0, 0:256], 0)], wh, wl, fold, 1)
        stage_sigma(sigma, sg, (0,))

    lane = lax.broadcasted_iota(jnp.int32, (rows, LANES), 1)
    row_id = lax.broadcasted_iota(jnp.int32, (rows, LANES), 0)
    high = (lane >= 64).astype(jnp.int32)
    chi_row = prm[0, 2:3, :]
    last = 2 * pairs - 1
    beyond = [jnp.concatenate([x[...], x[...]], axis=1) for x in (west, east)]

    def at_tile(m):
        return pl.ds(pl.multiple_of(m * LANES, LANES), LANES)

    def laplace(m):
        x = temp[0, :, at_tile(m)]
        left = jnp.where(m == 0, beyond[0], temp[0, :, at_tile(jnp.maximum(m - 1, 0))])
        right = jnp.where(m == last, beyond[1], temp[0, :, at_tile(jnp.minimum(m + 1, last))])
        beside = swap(x + jnp.where(lane >= 64, left, right))
        above = jnp.where(row_id == 0, north[:, at_tile(m)], pltpu.roll(x, 1, 0))
        below = jnp.where(row_id == rows - 1, south[:, at_tile(m)], pltpu.roll(x, rows - 1, 0))
        return 4.0 * x - beside - above - below

    def body(b, _):
        for o in range(4):
            p = b * 4 + o
            at = pl.ds(pl.multiple_of(p * rows, 8), rows)
            m = g * BLOCK + p
            for side, (pr, cr) in enumerate(((plo, clo), (phi, chi))):
                s = sigma_tile(sg, 0, m + side * pairs, high)
                to = slice(side * LANES, (side + 1) * LANES)
                xs[0, at, to] = (pr[0, :, at_tile(p)] + chi_row * cr[0, :, at_tile(p)]) * s
                xs[1, at, to] = laplace(m + side * pairs) * s
        return 0

    lax.fori_loop(0, BLOCK // 4, body, 0)

    def store(first, res):
        xs[0, first : first + res.shape[0], :] = res

    products([(xs.at[0], 0), (xs.at[1], 1)], wh, wl, store)
    put_mixed(0, rows, xs.at[0], w_ref, u_ref)
    lat_filter((0,), rows, prm, u_ref, e_ref)


def lon_filter(prm, rb, o_ref, el_ref, es_ref, at):
    half = o_ref.shape[1]
    nv = len(ORDER)
    decay = [prm[v, 1:2, :] for v in ORDER]

    def load(j):
        return [o_ref[k, j] for k in range(nv)]

    def store(j, values):
        for k in range(nv):
            o_ref[k, j] = values[k]

    edges = cascade(half, load, store, decay, [jnp.zeros((rb, LANES), f32)] * nv)
    low = low_lanes((rb, LANES))
    for k, v in enumerate(ORDER):
        span, k1, k2, k3 = constants(prm[v, 0:1, :], prm[v, 1:2, :], half)
        e1, e2, e3, e4 = (edges[e][k] for e in range(4))
        c1 = jnp.where(low, 0.0, swap(e1))
        t1 = e1 + span * c1
        t2 = e2 + k1 * c1
        c2 = jnp.where(low, swap(t2), 0.0)
        t2 = t2 + span * c2
        t3 = e3 + k2 * c1 + k1 * c2
        c3 = jnp.where(low, 0.0, swap(t3))
        t3 = t3 + span * c3
        t4 = e4 + k3 * c1 + k2 * c2 + k1 * c3
        c4 = jnp.where(low, swap(t4), 0.0)
        t4 = t4 + span * c4
        for t in range(es_ref.shape[0]):
            es_ref[t, 2 * k, at, :] = jnp.where(low, t2, t1)
            es_ref[t, 2 * k + 1, at, :] = jnp.where(low, t4, t3)
        for e, x in enumerate((e1, e2, e3, e4)):
            el_ref[k, e, at, :] = x


def lon_kernel(rb, prm, sigma, u_ref, o_ref, el_ref, es_ref):
    g = pl.program_id(0)
    half = u_ref.shape[2]

    @pl.when(g == 0)
    def _():
        x = sigma[0]
        lon = x.shape[1]
        outer = jnp.where(low_lanes((x.shape[0], LANES)), x[:, 0:1], x[:, lon - 1 : lon])
        for t in range(es_ref.shape[0]):
            es_ref[t, 6] = outer

    def turn(b, _):
        at = pl.ds(pl.multiple_of(b * 8, 8), 8)
        for k in range(len(ORDER)):
            for q in range(0, rb, 8):
                o_ref[k, at, q : q + 8, :] = jnp.swapaxes(u_ref[k, q : q + 8, at, :], 0, 1)
        return 0

    lax.fori_loop(0, half // 8, turn, 0)
    lon_filter(prm, rb, o_ref, el_ref, es_ref, pl.ds(pl.multiple_of(g * rb, 8), rb))


def solve_kernel(n_lat, rows, prm, edges, carries):
    width = edges.shape[2] // 4
    for k, v in enumerate(ORDER):
        const = constants(prm[v, 0:1, :], prm[v, 1:2, :], rows)
        c = solve_carries(n_lat, lambda t, e: edges[t, k, e * width : (e + 1) * width, :], const)
        for e in range(4):
            for t in range(n_lat):
                carries[t, k, e * width : (e + 1) * width, :] = c[e][t]


def carry_kernel(prm, carries, o_ref, el_ref, es_ref):
    width = carries.shape[2] // 4
    zero = jnp.zeros((8, LANES), f32)

    def body(d, _):
        for k in range(len(ORDER)):
            for j in range(width):
                at = d * width + j
                o_ref[k, at] = zero
                for e in range(4):
                    o_ref[k, at, e : e + 1, :] = carries[d, k, e * width + j : e * width + j + 1, :]
        return 0

    lax.fori_loop(0, carries.shape[0], body, 0)
    lon_filter(prm, 8, o_ref, el_ref, es_ref, slice(0, 8))


def join_kernel(
    n_lon, rows, packed, rq, place, prm, u_ref, w_ref, x_ref, el, elc, esm, esx,
    y_ref, yx_ref, col_ref, side_ref, energy, carry, extra, resp_x, resp_y,
):
    g = pl.program_id(0)
    half = resp_x.shape[2]
    lat, me = place[0], place[1]

    @pl.when(g == 0)
    def _():
        energy[...] = jnp.zeros_like(energy)
        side_ref[0] = esm[jnp.maximum(me - 1, 0), 6]
        side_ref[1] = esm[jnp.minimum(me + 1, n_lon - 1), 6]
        for k, v in enumerate(ORDER):
            length = prm[v, 0:1, :]
            decay = prm[v, 1:2, :]
            whole = constants(length, decay, 2 * half)
            span, k1, k2, k3 = constants(length, decay, half)

            def solve(gathered, own, k=k, whole=whole, half_c=(span, k1, k2, k3)):
                span, k1, k2, k3 = half_c
                low = low_lanes(own.shape[2:])
                cache = {}

                def edge(t, e):
                    if (t, e // 2) not in cache:
                        x = gathered[t, 2 * k + e // 2]
                        y = swap(x)
                        cache[t, e // 2] = (jnp.where(low, y, x), jnp.where(low, x, y))
                    return cache[t, e // 2][e % 2]

                d1, d2, d3, d4 = pick(solve_carries(n_lon, edge, whole), me)
                e1, e2, e3, e4 = (own[k, e] for e in range(4))
                c1 = jnp.where(low, d1, swap(e1 + span * d1))
                c2 = jnp.where(low, swap(e2 + k1 * c1 + span * d2), d2)
                c3 = jnp.where(low, d3, swap(e3 + k2 * c1 + k1 * c2 + span * d3))
                c4 = jnp.where(low, swap(e4 + k3 * c1 + k2 * c2 + k1 * c3 + span * d4), d4)
                return (c1, c2, c3, c4), d3, d4

            for e, r in enumerate(responses(length, decay, half)):
                resp_x[k, e] = r
            ry = responses(length, decay, rows)
            for e in range(4):
                resp_y[k, e] = ry[e]
            cc, f3, f4 = solve(esx, elc)
            c, d3, d4 = solve(esm, el)

            def total(x, rows_of, ry=ry):
                for e in range(4):
                    x = x + ry[e] * rows_of[e : e + 1, :]
                return x

            for e in range(4):
                extra[k, e] = cc[e]
                carry[k, e] = total(c[e], cc[e])
            if v == 0:
                col_ref[0] = total(d3, f3)
                col_ref[1] = total(d4, f4)

    row8 = lax.broadcasted_iota(jnp.int32, (8, LANES), 0)
    for k, v in enumerate(ORDER):
        total = jnp.zeros((rq, LANES), f32)
        for q in range(0, rows, rq):
            at = slice(q, q + rq)
            c = [carry[k, e, at, :] for e in range(4)]
            ry = [resp_y[k, e, at, :] for e in range(4)]

            def body(b, total, k=k, v=v, q=q, at=at, c=c, ry=ry):
                base = g * packed + b * 8
                rx = [resp_x[k, e, pl.ds(pl.multiple_of(base, 8), 8), :] for e in range(4)]
                for o in range(8):
                    p = b * 8 + o
                    x = x_ref[k, p]
                    y = u_ref[k, p, at, :]
                    for e in range(4):
                        y = y + rx[e][o : o + 1, :] * c[e] + ry[e] * x[e : e + 1, :]
                    y_ref[k, p, at, :] = y
                    total = total + y * w_ref[k, p, at, :]
                    if v == 0 and q == 0:
                        for e in range(4):
                            x = x + rx[e][o : o + 1, :] * extra[k, e]
                        x = pltpu.roll(x, 6, 0)
                        above = jnp.where(lat > 0, x + prm[0, 1:2, :] * y[0:1, :], 0.0)
                        yx_ref[p] = jnp.where(row8 == 0, above, jnp.where(row8 == 1, x, 0.0))
                return total

            total = lax.fori_loop(0, packed // 8, body, total)
        energy[v] += jnp.sum(total.reshape(rq // 8, 8, LANES), axis=0)

    @pl.when(g == 0)
    def _():
        beside = col_ref[0] + prm[0, 1:2, :] * y_ref[ORDER.index(0), 0]
        col_ref[0] = jnp.where(me > 0, beside, 0.0)


def end_kernel(
    rows, pairs, prm, sigma, north, south, vert, bal, col, side, y_ref, yx_ref,
    out, xs, xe, zx, zc, wh, wl, sg, sx,
):
    g = pl.program_id(0)
    half = 2 * pairs
    lon = sigma.shape[2]
    merged = out.shape[2]

    @pl.when(g == 0)
    def _():
        for v in range(3):
            scaled = quad(vert[v]) * prm[v, 3:4, :]
            set_weights(wh, wl, v, expand(scaled.T, True))
        set_weights(wh, wl, 3, expand(quad(bal[...]).T, False))
        stage_sigma(sigma, sg, (0, 1, 2))
        for at in range(0, lon, LANES):
            width = min(LANES, lon - at)
            sx[at // LANES, 0:1, 0:width] = north[:, merged + at : merged + at + width]
            sx[at // LANES, 1:2, 0:width] = south[:, merged + at : merged + at + width]

    lane = lax.broadcasted_iota(jnp.int32, (rows, LANES), 1)
    high = (lane >= 64).astype(jnp.int32)
    high8 = high[0:8]
    chi_row = prm[0, 2:3, :]

    def at_tile(m):
        return pl.ds(pl.multiple_of(m * LANES, LANES), LANES)

    row8 = lax.broadcasted_iota(jnp.int32, (8, LANES), 0)
    for p in range(BLOCK):
        xe[p * 8 : (p + 1) * 8, 0:LANES] = yx_ref[2 * p]
        xe[p * 8 : (p + 1) * 8, LANES:] = yx_ref[2 * p + 1]
    at_cols = slice(BLOCK * 8, BLOCK * 8 + rows)
    xe[at_cols, 0:LANES] = jnp.where(lane < 64, col[0], col[1])
    xe[at_cols, LANES:] = jnp.zeros((rows, LANES), f32)

    def keep(first, res):
        xe[first : first + res.shape[0], :] = res

    products([(xe, 0)], wh, wl, keep, 1)
    zc[0] = swap(xe[at_cols, 0:LANES] * swap(side[0]))
    zc[1] = xe[at_cols, LANES:] * side[1]
    for p in range(BLOCK):
        for half_at in range(2):
            tile = g * BLOCK + p + half_at * pairs
            s = jnp.take_along_axis(sx[tile >> 6], 2 * (tile & 63) + high8, axis=1, mode="promise_in_bounds")
            part = xe[p * 8 : (p + 1) * 8, half_at * LANES : (half_at + 1) * LANES]
            zx[:, at_tile(tile)] = jnp.where(row8 < 2, part * s, 0.0)

    def gather_rows(b, _):
        for o in range(4):
            p = b * 4 + o
            at = pl.ds(pl.multiple_of(p * rows, 8), rows)
            for k in range(3):
                xs[k, at, 0:LANES] = y_ref[k, 2 * p]
                xs[k, at, LANES:] = y_ref[k, 2 * p + 1]
        return 0

    lax.fori_loop(0, BLOCK // 4, gather_rows, 0)
    for k, v in enumerate(ORDER):

        def store(first, res, k=k):
            xs[k, first : first + res.shape[0], :] = res

        products([(xs.at[k], v)], wh, wl, store)

    def scale(b, _):
        for o in range(4):
            p = b * 4 + o
            for half_at in range(2):
                m = g * BLOCK + p + half_at * pairs
                z = [
                    xs[
                        ORDER.index(v),
                        pl.ds(pl.multiple_of(p * rows, 8), rows),
                        half_at * LANES : (half_at + 1) * LANES,
                    ]
                    * sigma_tile(sg, v, m, high)
                    for v in range(3)
                ]
                out[0, :, at_tile(m)] = z[0]
                out[1, :, at_tile(m)] = z[1] + chi_row * z[0]
                out[2, :, at_tile(m)] = z[2]
        return 0

    lax.fori_loop(0, BLOCK // 4, scale, 0)

    @pl.when(g == pl.num_programs(0) - 1)
    def _():
        row_id = lax.broadcasted_iota(jnp.int32, (rows, LANES), 0)
        last = half - 1

        def laplace(b, base):
            for o in range(4):
                p = b * 4 + o
                for side in range(2):
                    m = base + p + side * pairs
                    x = out[0, :, at_tile(m)]
                    left = jnp.where(m == 0, zc[0], out[0, :, at_tile(jnp.maximum(m - 1, 0))])
                    right = jnp.where(m == last, zc[1], out[0, :, at_tile(jnp.minimum(m + 1, last))])
                    beside = swap(x + jnp.where(lane >= 64, left, right))
                    above = jnp.where(row_id == 0, zx[0:1, at_tile(m)], pltpu.roll(x, 1, 0))
                    below = jnp.where(row_id == rows - 1, zx[1:2, at_tile(m)], pltpu.roll(x, rows - 1, 0))
                    at = pl.ds(pl.multiple_of(p * rows, 8), rows)
                    xs[0, at, side * LANES : (side + 1) * LANES] = 4.0 * x - beside - above - below
            return base

        def add(b, base):
            for o in range(4):
                p = b * 4 + o
                at = pl.ds(pl.multiple_of(p * rows, 8), rows)
                for side in range(2):
                    to = at_tile(base + p + side * pairs)
                    out[2, :, to] = out[2, :, to] + xs[0, at, side * LANES : (side + 1) * LANES]
            return base

        def store(first, res):
            xs[0, first : first + res.shape[0], :] = res

        def block(n, _):
            lax.fori_loop(0, BLOCK // 4, laplace, n * BLOCK)
            products([(xs.at[0], 3)], wh, wl, store)
            lax.fori_loop(0, BLOCK // 4, add, n * BLOCK)
            return 0

        lax.fori_loop(0, pairs // BLOCK, block, 0)


def shards(state, sigma, vert, bal_temp, chi_coef, scales, classes, owner):
    n_lat = lax.axis_size("lat")
    n_lon = lax.axis_size("lon")
    devices = n_lat * n_lon
    nvars, rows, merged = state.shape
    levels = vert.shape[1]
    lon = merged // levels
    half = lon // 2
    pairs = half // 2
    pieces = (lon + LANES - 1) // LANES
    count = nvars * levels
    capacity = (count + devices - 1) // devices + 1
    i_lat = lax.axis_index("lat")
    i_lon = lax.axis_index("lon")

    up_lat, up_lon = ([(i, i + 1) for i in range(n - 1)] for n in (n_lat, n_lon))
    down_lat, down_lon = ([(j, i) for i, j in up] for up in (up_lat, up_lon))

    def row(i):
        return jnp.concatenate([state[2, i : i + 1, :], sigma[0, i : i + 1, :]], axis=1)

    north = lax.ppermute(row(rows - 1), "lat", up_lat)
    south = lax.ppermute(row(0), "lat", down_lat)
    west = lax.ppermute(state[2, :, merged - levels :], "lon", up_lon)
    east = lax.ppermute(state[2, :, :levels], "lon", down_lon)
    place = jnp.stack([i_lat, i_lon]).astype(jnp.int32)

    anywhere = pl.BlockSpec(memory_space=pl.ANY)
    steps = pairs // BLOCK

    def part(v, side):
        return pl.BlockSpec((1, rows, BLOCK * LANES), lambda g: (v, 0, g + side * steps))

    width = half // n_lat
    shapes = [(nvars, half, rows, LANES), (nvars, rows, half, LANES), (n_lat, nvars, 4 * width, LANES)]

    def lat_call(nv, first, body, arrays, specs, name, aliases, more=()):
        return pl.pallas_call(
            body,
            grid=(steps,),
            in_specs=specs,
            out_specs=[
                pl.BlockSpec((nv, 2 * BLOCK, rows, LANES), lambda g: (first, g, 0, 0)),
                pl.BlockSpec((nv, rows, 2 * BLOCK, LANES), lambda g: (first, 0, g, 0)),
                pl.BlockSpec((2 * BLOCK // width, nv, 4 * width, LANES), lambda g: (g, first, 0, 0)),
            ]
            + [full(s) for s in more],
            out_shape=[jax.ShapeDtypeStruct(s, f32) for s in shapes + list(more)],
            scratch_shapes=[
                pltpu.VMEM((2, BLOCK * rows, 256), f32),
                pltpu.VMEM((2, 256, 256), bf16),
                pltpu.VMEM((2, 256, 256), bf16),
                pltpu.VMEM((nvars, pieces, rows, LANES), f32),
            ],
            compiler_params=params(),
            cost_estimate=pl.CostEstimate(
                flops=nv * 60000000, bytes_accessed=nv * 3 * rows * merged * 4, transcendentals=0
            ),
            input_output_aliases=aliases,
            name=name,
        )(*arrays)

    ins = [scales, classes.reshape(1, count), chi_coef.reshape(1, levels), sigma, vert] + [state] * 4
    specs = [full(x.shape) for x in ins[:5]] + [part(1, 0), part(1, 1), part(2, 0), part(2, 1)]
    specs[0] = pl.BlockSpec(memory_space=pltpu.SMEM)
    body = functools.partial(lat_plain, rows, pairs)
    *wue, prm = lat_call(2, 0, body, ins, specs, "lat_chi_temp", {}, [(nvars, 4, LANES)])
    ins = [prm, sigma, vert, bal_temp] + [state] * 5 + [north, south, west, east] + list(wue)
    specs = [full(x.shape) for x in ins[:4]] + [part(0, 0), part(0, 1), part(1, 0), part(1, 1)]
    specs += [pl.BlockSpec((1, rows, merged), lambda g: (2, 0, 0))]
    specs += [full(x.shape) for x in (north, south, west, east)] + [anywhere] * 3
    aliases = {13: 0, 14: 1, 15: 2}
    w, u, edges = lat_call(1, 2, functools.partial(lat_balance, rows, pairs), ins, specs, "lat_psi", aliases)
    def trade(x, axis):
        return lax.all_to_all(x, axis, split_axis=0, concat_axis=0, tiled=True)

    shares = trade(edges, "lat")

    rb = BLOCK
    local, el, es = pl.pallas_call(
        functools.partial(lon_kernel, rb),
        grid=(rows // rb,),
        in_specs=[
            full(prm.shape),
            pl.BlockSpec((1, rows, lon), lambda g: (0, 0, 0)),
            pl.BlockSpec((nvars, rb, half, LANES), lambda g: (0, g, 0, 0)),
        ],
        out_specs=[
            pl.BlockSpec((nvars, half, rb, LANES), lambda g: (0, 0, g, 0)),
            full((nvars, 4, rows, LANES)),
            full((n_lon, 7, rows, LANES)),
        ],
        out_shape=[
            jax.ShapeDtypeStruct((nvars, half, rows, LANES), f32),
            jax.ShapeDtypeStruct((nvars, 4, rows, LANES), f32),
            jax.ShapeDtypeStruct((n_lon, 7, rows, LANES), f32),
        ],
        compiler_params=params(),
        cost_estimate=pl.CostEstimate(
            flops=180000000, bytes_accessed=6 * rows * merged * 4, transcendentals=0
        ),
        name="lon_tile",
    )(prm, sigma, u)

    shares, _ = lax.optimization_barrier((shares, es))
    sent = trade(es, "lon")
    carries = pl.pallas_call(
        functools.partial(solve_kernel, n_lat, rows),
        grid=(1,),
        in_specs=[full(prm.shape), full(shares.shape)],
        out_specs=full(shares.shape),
        out_shape=jax.ShapeDtypeStruct(shares.shape, f32),
        compiler_params=params(),
        cost_estimate=pl.CostEstimate(flops=1000000, bytes_accessed=2 * shares.size * 4, transcendentals=0),
        name="solve",
    )(prm, shares)
    carries = trade(carries, "lat")

    crossed, elc, esc = pl.pallas_call(
        carry_kernel,
        grid=(1,),
        in_specs=[full(prm.shape), full(carries.shape)],
        out_specs=[full((nvars, half, 8, LANES)), full((nvars, 4, 8, LANES)), full((n_lon, 6, 8, LANES))],
        out_shape=[
            jax.ShapeDtypeStruct((nvars, half, 8, LANES), f32),
            jax.ShapeDtypeStruct((nvars, 4, 8, LANES), f32),
            jax.ShapeDtypeStruct((n_lon, 6, 8, LANES), f32),
        ],
        compiler_params=params(),
        cost_estimate=pl.CostEstimate(
            flops=30000000, bytes_accessed=4 * nvars * 12 * half * LANES, transcendentals=0
        ),
        name="lon_carry",
    )(prm, carries)
    sent_x = trade(esc, "lon")

    packed = 2 * PAIRS

    def columns(r):
        return pl.BlockSpec((nvars, packed, r, LANES), lambda g: (0, g, 0, 0))

    ins = [place, prm, local, w, crossed, el, elc, sent, sent_x]
    specs = [full(x.shape) for x in ins]
    specs[0] = pl.BlockSpec(memory_space=pltpu.SMEM)
    specs[2:5] = [columns(rows), columns(rows), columns(8)]
    y, yx, col, side, energy = pl.pallas_call(
        functools.partial(join_kernel, n_lon, rows, packed, 24),
        grid=(half // packed,),
        in_specs=specs,
        out_specs=[
            columns(rows),
            pl.BlockSpec((packed, 8, LANES), lambda g: (g, 0, 0)),
            full((2, rows, LANES)),
            full((2, rows, LANES)),
            full((nvars, 8, LANES)),
        ],
        out_shape=[
            jax.ShapeDtypeStruct((nvars, half, rows, LANES), f32),
            jax.ShapeDtypeStruct((half, 8, LANES), f32),
            jax.ShapeDtypeStruct((2, rows, LANES), f32),
            jax.ShapeDtypeStruct((2, rows, LANES), f32),
            jax.ShapeDtypeStruct((nvars, 8, LANES), f32),
        ],
        scratch_shapes=[
            pltpu.VMEM((nvars, 4, rows, LANES), f32),
            pltpu.VMEM((nvars, 4, 8, LANES), f32),
            pltpu.VMEM((nvars, 4, half, LANES), f32),
            pltpu.VMEM((nvars, 4, rows, LANES), f32),
        ],
        compiler_params=params(),
        cost_estimate=pl.CostEstimate(
            flops=60000000, bytes_accessed=9 * rows * merged * 4, transcendentals=0
        ),
        name="join",
    )(*ins)

    index = jnp.arange(count, dtype=jnp.int32)
    same = (owner[:, None] == owner[None, :]) & (index[None, :] < index[:, None])
    slot = jnp.sum(same.astype(jnp.int32), axis=1)
    target = owner * capacity + slot
    hit = target[:, None] == jnp.arange(devices * capacity)[None, :]
    energy = jnp.sum(energy, axis=1) * prm[:, 3]
    energy = (energy[:, :levels] + energy[:, levels:]).reshape(count)
    table = jnp.sum(jnp.where(hit, energy[:, None], 0.0), axis=0).reshape(devices, capacity)
    table = lax.all_to_all(table, ("lat", "lon"), split_axis=0, concat_axis=0, tiled=True)
    slab_energy = (jnp.sum(table, axis=0) / (devices * rows * lon))[None, :]

    ins = [prm, sigma, north, south, vert, bal_temp, col, side, y, yx]
    specs = [full(x.shape) for x in ins]
    specs[8] = pl.BlockSpec((nvars, 2 * BLOCK, rows, LANES), lambda g: (0, g, 0, 0))
    specs[9] = pl.BlockSpec((2 * BLOCK, 8, LANES), lambda g: (g, 0, 0))
    applied = pl.pallas_call(
        functools.partial(end_kernel, rows, pairs),
        grid=(steps,),
        in_specs=specs,
        out_specs=full(state.shape),
        out_shape=jax.ShapeDtypeStruct(state.shape, f32),
        scratch_shapes=[
            pltpu.VMEM((nvars, BLOCK * rows, 256), f32),
            pltpu.VMEM((256, 256), f32),
            pltpu.VMEM((8, merged), f32),
            pltpu.VMEM((2, rows, LANES), f32),
            pltpu.VMEM((4, 256, 256), bf16),
            pltpu.VMEM((4, 256, 256), bf16),
            pltpu.VMEM((nvars, pieces, rows, LANES), f32),
            pltpu.VMEM((pieces, 8, LANES), f32),
        ],
        compiler_params=params(),
        cost_estimate=pl.CostEstimate(
            flops=300000000, bytes_accessed=6 * rows * merged * 4, transcendentals=0
        ),
        name="finish",
    )(*ins)
    return (applied, slab_energy)


def solution(mesh):
    return jax.shard_map(
        shards,
        mesh=mesh,
        in_specs=(P(None, "lat", "lon"), P(None, "lat", "lon"), P(), P(), P(), P(), P(), P()),
        out_specs=(P(None, "lat", "lon"), P(("lat", "lon"), None)),
        check_vma=False,
    )
```

```python
import functools

import jax
import jax.numpy as jnp
from jax import lax
from jax.experimental import pallas as pl
from jax.experimental.pallas import tpu as pltpu
from jax.sharding import PartitionSpec as P

highest = lax.Precision.HIGHEST
f32 = jnp.float32
bf16 = jnp.bfloat16
LANES = 128
PAIRS = 8
BLOCK = 24
ORDER = (1, 2, 0)
LIMIT = 22 * 1024 * 1024


def params():
    return pltpu.CompilerParams(vmem_limit_bytes=LIMIT)


def full(shape):
    return pl.BlockSpec(shape, lambda g: (0,) * len(shape))


def swap(x):
    return pltpu.roll(x, 64, x.ndim - 1)


def low_lanes(shape):
    return lax.broadcasted_iota(jnp.int32, shape, len(shape) - 1) < 64


def halves(x):
    hi = x.astype(bf16)
    return hi, (x - hi.astype(f32)).astype(bf16)


def dot(x, y):
    return jnp.dot(x, y, preferred_element_type=f32)


def split(x):
    hi, lo = halves(x)
    return jnp.concatenate([hi, lo, hi], axis=1)


def product(x, weights):
    return dot(split(x), weights)


def expand(mat, mixed):
    wide = quad(mat)
    wide = jnp.concatenate([wide, wide], axis=1)
    wide = jnp.concatenate([wide, wide], axis=0)
    src = lax.broadcasted_iota(jnp.int32, (256, 256), 0) // 64
    dst = lax.broadcasted_iota(jnp.int32, (256, 256), 1) // 64
    if mixed:
        src = jnp.where(src == 1, 2, jnp.where(src == 2, 1, src))
    return halves(jnp.where(src == dst, wide, 0.0))


def quad(mat):
    if mat.shape[0] == LANES:
        return mat
    wide = jnp.concatenate([mat, mat], axis=1)
    return jnp.concatenate([wide, wide], axis=0)


def constants(length, decay, m):
    span = jnp.exp(-float(m) / length)
    d = 1.0 - decay * decay
    k1 = decay * (1.0 - span * span) / d
    k2 = (m * span - decay * decay * (span - span * span * span) / d) / d
    tail = decay * decay * (1.0 + span * span) * (1.0 - span * span) / d
    k3 = decay / (d * d) * (1.0 - (2.0 * m + 1.0) * span * span + tail)
    return span, k1, k2, k3


def responses(length, decay, m):
    j = lax.broadcasted_iota(jnp.int32, (m, LANES), 0).astype(f32)
    up = jnp.exp(-j / length)
    down = jnp.exp(-(m - j) / length)
    span = jnp.exp(-float(m) / length)
    d = 1.0 - decay * decay
    diff = up - span * down
    g3 = decay * diff / d
    g2 = ((m - j) * down - decay * decay * (span * up - span * span * down) / d) / d
    part = decay * decay * (1.0 + span * span) * diff / d
    g1 = decay / (d * d) * ((j + 1.0) * up - (2.0 * m + 1.0 - j) * span * down + part)
    return g1, g2, g3, down


def pick(all_carries, me):
    out = []
    for cs in all_carries:
        mine = cs[0]
        for t in range(1, len(cs)):
            mine = jnp.where(me == t, cs[t], mine)
        out.append(mine)
    return out


def solve_carries(n, edge, const):
    span, k1, k2, k3 = const
    first = edge(0, 0)
    zero = jnp.zeros_like(first)
    e1 = [first] + [edge(t, 0) for t in range(1, n)]
    c1, c2, c3, c4 = ([None] * n for _ in range(4))
    c = zero
    for t in range(n):
        c1[t] = c
        c = e1[t] + span * c
    c = zero
    for t in reversed(range(n)):
        c2[t] = c
        c = edge(t, 1) + k1 * c1[t] + span * c
    c = zero
    for t in range(n):
        c3[t] = c
        c = edge(t, 2) + k2 * c1[t] + k1 * c2[t] + span * c
    c = zero
    for t in reversed(range(n)):
        c4[t] = c
        c = edge(t, 3) + k3 * c1[t] + k2 * c2[t] + k1 * c3[t] + span * c
    return c1, c2, c3, c4


def cascade(count, load, store, decay, start):
    step = 24
    edges = []
    for stage in range(4):
        back = stage % 2 == 1

        def body(b, states, back=back):
            base = (count // step - 1 - b) * step if back else b * step
            order = range(step - 1, -1, -1) if back else range(step)
            for o in order:
                new = [decay_k * s + x for decay_k, s, x in zip(decay, states, load(base + o))]
                store(base + o, new)
                states = new
            return tuple(states)

        states = lax.fori_loop(0, count // step, body, tuple(start))
        edges.append(list(states))
    return edges


def stage_sigma(sigma, sg, variables):
    lon = sigma.shape[2]
    for v in variables:
        for at in range(0, lon, LANES):
            width = min(LANES, lon - at)
            sg[v, at // LANES, :, 0:width] = sigma[v, :, at : at + width]


def sigma_tile(sg, v, m, high):
    idx = 2 * (m & 63) + high
    return jnp.take_along_axis(sg[v, m >> 6], idx, axis=1, mode="promise_in_bounds")


def set_weights(weights, k, mat, mixed):
    hi, lo = expand(mat, mixed)
    weights[768 * k : 768 * k + 256] = hi
    weights[768 * k + 256 : 768 * k + 512] = hi
    weights[768 * k + 512 : 768 * k + 768] = lo


def weight(weights, k):
    return weights[768 * k : 768 * (k + 1)]


def lat_filter(vs, rows, prm, u_ref, e_ref):
    nv = len(vs)
    decay = [prm[v, 1:2, :] for v in vs]

    def load(i):
        return [u_ref[k, i] for k in range(nv)]

    def store(i, values):
        for k in range(nv):
            u_ref[k, i] = values[k]

    zero = jnp.zeros((u_ref.shape[2], LANES), f32)
    edges = cascade(rows, load, store, decay, [zero] * nv)
    width = e_ref.shape[2] // 4
    for e in range(4):
        for k in range(nv):
            for c in range(e_ref.shape[0]):
                e_ref[c, k, e * width : (e + 1) * width] = edges[e][k][c * width : (c + 1) * width]


def put_mixed(k, b, rows, res, w_ref, u_ref):
    base = b * 2 * PAIRS
    for p in range(PAIRS):
        part = res[p * rows : (p + 1) * rows]
        w_ref[k, base + 2 * p] = part[:, :LANES]
        w_ref[k, base + 2 * p + 1] = part[:, LANES:]
    at = pl.ds(pl.multiple_of(base, 2 * PAIRS), 2 * PAIRS)
    u_ref[k, :, at, :] = jnp.swapaxes(w_ref[k, at], 0, 1)


def set_params(scales, classes, chi_coef, prm):
    coef = jnp.concatenate([chi_coef[...], chi_coef[...]], axis=1)
    for v in range(3):
        kind = classes[:, 64 * v : 64 * (v + 1)]
        kind = jnp.concatenate([kind, kind], axis=1)
        length = jnp.zeros((1, LANES), f32)
        for n in range(scales.shape[0]):
            length = jnp.where(kind == n, scales[n], length)
        decay = jnp.exp(-1.0 / length)
        norm = 1.0 - decay
        norm = norm * norm
        norm = norm * norm
        prm[v, 0:1, :] = length
        prm[v, 1:2, :] = decay
        prm[v, 2:3, :] = coef
        prm[v, 3:4, :] = length * jnp.sqrt(length) * norm * norm


def lat_plain(
    rows, pairs, scales, classes, chi_coef, sigma, vert, b1lo, b1hi, b2lo, b2hi,
    w_ref, u_ref, e_ref, prm, xs, wt, sg,
):
    g = pl.program_id(0)

    @pl.when(g == 0)
    def _():
        set_params(scales, classes, chi_coef, prm)
        set_weights(wt, 0, vert[1], True)
        set_weights(wt, 1, vert[2], True)
        stage_sigma(sigma, sg, (1, 2))

    lane = lax.broadcasted_iota(jnp.int32, (rows, LANES), 1)
    high = (lane >= 64).astype(jnp.int32)

    def body(b, _):
        for p in range(PAIRS):
            at = slice(p * rows, (p + 1) * rows)
            cols = pl.ds(pl.multiple_of((b * PAIRS + p) * LANES, LANES), LANES)
            m = g * BLOCK + b * PAIRS + p
            for k, sides in enumerate(((b1lo, b1hi), (b2lo, b2hi))):
                for side in range(2):
                    s = sigma_tile(sg, k + 1, m + side * pairs, high)
                    xs[k, at, side * LANES : (side + 1) * LANES] = sides[side][0, :, cols] * s
        for k in range(2):
            put_mixed(k, b, rows, product(xs[k], weight(wt, k)), w_ref, u_ref)
        return 0

    lax.fori_loop(0, BLOCK // PAIRS, body, 0)
    lat_filter((1, 2), rows, prm, u_ref, e_ref)


def lat_balance(
    rows, pairs, prm, sigma, vert, bal, plo, phi, clo, chi, temp, north, south, west, east, w_in, u_in, e_in,
    w_ref, u_ref, e_ref, xs, wt, sg,
):
    del w_in, u_in, e_in
    g = pl.program_id(0)

    @pl.when(g == 0)
    def _():
        set_weights(wt, 0, vert[0], True)
        (bh, bl), (vh, vl) = halves(bal[...]), halves(vert[0])
        set_weights(wt, 1, dot(bh, vh) + dot(bl, vh) + dot(bh, vl), True)
        stage_sigma(sigma, sg, (0,))

    lane = lax.broadcasted_iota(jnp.int32, (rows, LANES), 1)
    row_id = lax.broadcasted_iota(jnp.int32, (rows, LANES), 0)
    high = (lane >= 64).astype(jnp.int32)
    chi_row = prm[0, 2:3, :]
    last = 2 * pairs - 1
    beyond = [jnp.concatenate([x[...], x[...]], axis=1) for x in (west, east)]

    def at_tile(m):
        return pl.ds(pl.multiple_of(m * LANES, LANES), LANES)

    def laplace(m):
        x = temp[0, :, at_tile(m)]
        left = jnp.where(m == 0, beyond[0], temp[0, :, at_tile(jnp.maximum(m - 1, 0))])
        right = jnp.where(m == last, beyond[1], temp[0, :, at_tile(jnp.minimum(m + 1, last))])
        beside = swap(x + jnp.where(lane >= 64, left, right))
        above = jnp.where(row_id == 0, north[:, at_tile(m)], pltpu.roll(x, 1, 0))
        below = jnp.where(row_id == rows - 1, south[:, at_tile(m)], pltpu.roll(x, rows - 1, 0))
        return 4.0 * x - beside - above - below

    def body(b, _):
        for p in range(PAIRS):
            at = slice(p * rows, (p + 1) * rows)
            cols = at_tile(b * PAIRS + p)
            m = g * BLOCK + b * PAIRS + p
            for side, (pr, cr) in enumerate(((plo, clo), (phi, chi))):
                s = sigma_tile(sg, 0, m + side * pairs, high)
                to = slice(side * LANES, (side + 1) * LANES)
                xs[0, at, to] = (pr[0, :, cols] + chi_row * cr[0, :, cols]) * s
                xs[1, at, to] = laplace(m + side * pairs) * s
        res = dot(jnp.concatenate([split(xs[0]), split(xs[1])], axis=1), wt[...])
        put_mixed(0, b, rows, res, w_ref, u_ref)
        return 0

    lax.fori_loop(0, BLOCK // PAIRS, body, 0)
    lat_filter((0,), rows, prm, u_ref, e_ref)


def lon_filter(prm, rb, o_ref, el_ref, es_ref, at):
    half = o_ref.shape[1]
    nv = len(ORDER)
    decay = [prm[v, 1:2, :] for v in ORDER]

    def load(j):
        return [o_ref[k, j] for k in range(nv)]

    def store(j, values):
        for k in range(nv):
            o_ref[k, j] = values[k]

    edges = cascade(half, load, store, decay, [jnp.zeros((rb, LANES), f32)] * nv)
    low = low_lanes((rb, LANES))
    for k, v in enumerate(ORDER):
        span, k1, k2, k3 = constants(prm[v, 0:1, :], prm[v, 1:2, :], half)
        e1, e2, e3, e4 = (edges[e][k] for e in range(4))
        c1 = jnp.where(low, 0.0, swap(e1))
        t1 = e1 + span * c1
        t2 = e2 + k1 * c1
        c2 = jnp.where(low, swap(t2), 0.0)
        t2 = t2 + span * c2
        t3 = e3 + k2 * c1 + k1 * c2
        c3 = jnp.where(low, 0.0, swap(t3))
        t3 = t3 + span * c3
        t4 = e4 + k3 * c1 + k2 * c2 + k1 * c3
        c4 = jnp.where(low, swap(t4), 0.0)
        t4 = t4 + span * c4
        es_ref[2 * k, at, :] = jnp.where(low, t2, t1)
        es_ref[2 * k + 1, at, :] = jnp.where(low, t4, t3)
        for e, x in enumerate((e1, e2, e3, e4)):
            el_ref[k, e, at, :] = x


def lon_kernel(rb, prm, sigma, u_ref, o_ref, el_ref, es_ref):
    g = pl.program_id(0)
    half = u_ref.shape[2]

    @pl.when(g == 0)
    def _():
        x = sigma[0]
        lon = x.shape[1]
        es_ref[6] = jnp.where(low_lanes((x.shape[0], LANES)), x[:, 0:1], x[:, lon - 1 : lon])

    def turn(b, _):
        at = pl.ds(pl.multiple_of(b * 8, 8), 8)
        for k in range(len(ORDER)):
            for q in range(0, rb, 8):
                o_ref[k, at, q : q + 8, :] = jnp.swapaxes(u_ref[k, q : q + 8, at, :], 0, 1)
        return 0

    lax.fori_loop(0, half // 8, turn, 0)
    lon_filter(prm, rb, o_ref, el_ref, es_ref, pl.ds(pl.multiple_of(g * rb, 8), rb))


def solve_kernel(n_lat, rows, prm, edges, carries):
    width = edges.shape[2] // 4
    for k, v in enumerate(ORDER):
        const = constants(prm[v, 0:1, :], prm[v, 1:2, :], rows)
        c = solve_carries(n_lat, lambda t, e: edges[t, k, e * width : (e + 1) * width, :], const)
        for e in range(4):
            for t in range(n_lat):
                carries[t, k, e * width : (e + 1) * width, :] = c[e][t]


def carry_kernel(prm, carries, o_ref, el_ref, es_ref):
    width = carries.shape[2] // 4
    zero = jnp.zeros((8, LANES), f32)

    def body(d, _):
        for k in range(len(ORDER)):
            for j in range(width):
                at = d * width + j
                o_ref[k, at] = zero
                for e in range(4):
                    o_ref[k, at, e : e + 1, :] = carries[d, k, e * width + j : e * width + j + 1, :]
        return 0

    lax.fori_loop(0, carries.shape[0], body, 0)
    lon_filter(prm, 8, o_ref, el_ref, es_ref, slice(0, 8))


def join_kernel(n_lon, rows, packed, rq, place, prm, u_ref, w_ref, x_ref, el, elc, *rest):
    sent, sent_x = rest[:n_lon], rest[n_lon : 2 * n_lon]
    y_ref, yx_ref, col_ref, side_ref, energy, carry, extra, resp_x, resp_y, esm, esx = rest[2 * n_lon :]
    g = pl.program_id(0)
    half = resp_x.shape[2]
    lat, me = place[0], place[1]

    @pl.when(g == 0)
    def _():
        energy[...] = jnp.zeros_like(energy)
        for s in range(n_lon):
            t = lax.rem(me - s + n_lon, n_lon)
            esm[t] = sent[s][...]
            esx[t] = sent_x[s][...]
        side_ref[0] = esm[jnp.maximum(me - 1, 0), 6]
        side_ref[1] = esm[jnp.minimum(me + 1, n_lon - 1), 6]
        length = jnp.stack([prm[v, 0:1, :] for v in ORDER])
        decay = jnp.stack([prm[v, 1:2, :] for v in ORDER])
        whole = constants(length, decay, 2 * half)
        span, k1, k2, k3 = constants(length, decay, half)
        low = low_lanes((len(ORDER), rows + 8, LANES))
        cache = {}

        def both(main, more):
            parts = [jnp.concatenate([main(k), more(k)], axis=0) for k in range(len(ORDER))]
            return jnp.stack(parts)

        def edge(t, e):
            i = e // 2
            if (t, i) not in cache:
                x = both(lambda k: esm[t, 2 * k + i], lambda k: esx[t, 2 * k + i])
                y = swap(x)
                cache[t, i] = (jnp.where(low, y, x), jnp.where(low, x, y))
            return cache[t, i][e % 2]

        d1, d2, d3, d4 = pick(solve_carries(n_lon, edge, whole), me)
        e1, e2, e3, e4 = (both(lambda k, e=e: el[k, e], lambda k, e=e: elc[k, e]) for e in range(4))
        c1 = jnp.where(low, d1, swap(e1 + span * d1))
        c2 = jnp.where(low, swap(e2 + k1 * c1 + span * d2), d2)
        c3 = jnp.where(low, d3, swap(e3 + k2 * c1 + k1 * c2 + span * d3))
        c4 = jnp.where(low, swap(e4 + k3 * c1 + k2 * c2 + k1 * c3 + span * d4), d4)
        for k, v in enumerate(ORDER):
            for e, r in enumerate(responses(prm[v, 0:1, :], prm[v, 1:2, :], half)):
                resp_x[k, e] = r
            ry = responses(prm[v, 0:1, :], prm[v, 1:2, :], rows)
            for e in range(4):
                resp_y[k, e] = ry[e]

            def total(x, ry=ry):
                y = x[:rows]
                for e in range(4):
                    y = y + ry[e] * x[rows + e : rows + e + 1]
                return y

            for e, c in enumerate((c1, c2, c3, c4)):
                extra[k, e] = c[k, rows:]
                carry[k, e] = total(c[k])
            if v == 0:
                col_ref[0] = total(d3[k])
                col_ref[1] = total(d4[k])

    row8 = lax.broadcasted_iota(jnp.int32, (8, LANES), 0)
    for k, v in enumerate(ORDER):
        total = jnp.zeros((rq, LANES), f32)
        for q in range(0, rows, rq):
            at = slice(q, q + rq)
            c = [carry[k, e, at, :] for e in range(4)]
            ry = [resp_y[k, e, at, :] for e in range(4)]

            def body(b, total, k=k, v=v, q=q, at=at, c=c, ry=ry):
                base = g * packed + b * 8
                rx = [resp_x[k, e, pl.ds(pl.multiple_of(base, 8), 8), :] for e in range(4)]
                for o in range(8):
                    p = b * 8 + o
                    x = x_ref[k, p]
                    y = u_ref[k, p, at, :]
                    for e in range(4):
                        y = y + rx[e][o : o + 1, :] * c[e] + ry[e] * x[e : e + 1, :]
                    y_ref[k, p, at, :] = y
                    total = total + y * w_ref[k, p, at, :]
                    if v == 0 and q == 0:
                        for e in range(4):
                            x = x + rx[e][o : o + 1, :] * extra[k, e]
                        x = pltpu.roll(x, 6, 0)
                        above = jnp.where(lat > 0, x + prm[0, 1:2, :] * y[0:1, :], 0.0)
                        yx_ref[p] = jnp.where(row8 == 0, above, jnp.where(row8 == 1, x, 0.0))
                return total

            total = lax.fori_loop(0, packed // 8, body, total)
        energy[v] += jnp.sum(total.reshape(rq // 8, 8, LANES), axis=0)

    @pl.when(g == 0)
    def _():
        beside = col_ref[0] + prm[0, 1:2, :] * y_ref[ORDER.index(0), 0]
        col_ref[0] = jnp.where(me > 0, beside, 0.0)


def end_kernel(
    rows, pairs, prm, sigma, north, south, vert, bal, col, side, y_ref, yx_ref,
    out, xs, zx, zc, wt, sg, sx,
):
    g = pl.program_id(0)
    half = 2 * pairs
    lon = sigma.shape[2]
    merged = out.shape[2]

    @pl.when(g == 0)
    def _():
        for v in range(3):
            scaled = quad(vert[v]) * prm[v, 3:4, :]
            set_weights(wt, v, scaled.T, True)
        set_weights(wt, 3, quad(bal[...]).T, False)
        stage_sigma(sigma, sg, (0, 1, 2))
        for at in range(0, lon, LANES):
            width = min(LANES, lon - at)
            sx[at // LANES, 0:1, 0:width] = north[:, merged + at : merged + at + width]
            sx[at // LANES, 1:2, 0:width] = south[:, merged + at : merged + at + width]
        lhs = jnp.where(low_lanes((rows, LANES)), col[0], col[1])
        lhs = jnp.concatenate([lhs, jnp.zeros_like(lhs)], axis=1)
        res = product(lhs, weight(wt, 0))
        zc[0] = swap(res[:, :LANES] * swap(side[0]))
        zc[1] = res[:, LANES:] * side[1]

    lane = lax.broadcasted_iota(jnp.int32, (rows, LANES), 1)
    high = (lane >= 64).astype(jnp.int32)
    high8 = high[0:8]
    chi_row = prm[0, 2:3, :]

    def at_tile(m):
        return pl.ds(pl.multiple_of(m * LANES, LANES), LANES)

    lhs = jnp.concatenate(
        [jnp.concatenate([yx_ref[2 * p], yx_ref[2 * p + 1]], axis=1) for p in range(PAIRS)], axis=0
    )
    res = product(lhs, weight(wt, 0))
    for p in range(PAIRS):
        m = g * PAIRS + p
        for side in range(2):
            tile = m + side * pairs
            s = jnp.take_along_axis(sx[tile >> 6], 2 * (tile & 63) + high8, axis=1, mode="promise_in_bounds")
            part = res[p * 8 : (p + 1) * 8, side * LANES : (side + 1) * LANES]
            zx[:, at_tile(tile)] = jnp.where(lax.broadcasted_iota(jnp.int32, (8, LANES), 0) < 2, part * s, 0.0)
    for k in range(3):
        for p in range(2 * PAIRS):
            at = slice((p // 2) * rows, (p // 2 + 1) * rows)
            xs[k, at, (p % 2) * LANES : (p % 2 + 1) * LANES] = y_ref[k, p]
    results = {v: product(xs[k], weight(wt, v)) for k, v in enumerate(ORDER)}
    for p in range(PAIRS):
        m = g * PAIRS + p
        for side in range(2):
            at = at_tile(m + side * pairs)
            z = [
                results[v][p * rows : (p + 1) * rows, side * LANES : (side + 1) * LANES]
                * sigma_tile(sg, v, m + side * pairs, high)
                for v in range(3)
            ]
            out[0, :, at] = z[0]
            out[1, :, at] = z[1] + chi_row * z[0]
            out[2, :, at] = z[2]

    @pl.when(g == pl.num_programs(0) - 1)
    def _():
        row_id = lax.broadcasted_iota(jnp.int32, (rows, LANES), 0)
        last = half - 1

        def body(b, _):
            for p in range(PAIRS):
                for side in range(2):
                    m = b * PAIRS + p + side * pairs
                    x = out[0, :, at_tile(m)]
                    left = jnp.where(m == 0, zc[0], out[0, :, at_tile(jnp.maximum(m - 1, 0))])
                    right = jnp.where(m == last, zc[1], out[0, :, at_tile(jnp.minimum(m + 1, last))])
                    beside = swap(x + jnp.where(lane >= 64, left, right))
                    above = jnp.where(row_id == 0, zx[0:1, at_tile(m)], pltpu.roll(x, 1, 0))
                    below = jnp.where(row_id == rows - 1, zx[1:2, at_tile(m)], pltpu.roll(x, rows - 1, 0))
                    lap = 4.0 * x - beside - above - below
                    xs[0, p * rows : (p + 1) * rows, side * LANES : (side + 1) * LANES] = lap
            res = product(xs[0], weight(wt, 3))
            for p in range(PAIRS):
                for side in range(2):
                    at = at_tile(b * PAIRS + p + side * pairs)
                    part = res[p * rows : (p + 1) * rows, side * LANES : (side + 1) * LANES]
                    out[2, :, at] = out[2, :, at] + part
            return 0

        lax.fori_loop(0, pairs // PAIRS, body, 0)


def shards(state, sigma, vert, bal_temp, chi_coef, scales, classes, owner):
    n_lat = lax.axis_size("lat")
    n_lon = lax.axis_size("lon")
    devices = n_lat * n_lon
    nvars, rows, merged = state.shape
    levels = vert.shape[1]
    lon = merged // levels
    half = lon // 2
    pairs = half // 2
    pieces = (lon + LANES - 1) // LANES
    count = nvars * levels
    capacity = (count + devices - 1) // devices + 1
    i_lat = lax.axis_index("lat")
    i_lon = lax.axis_index("lon")

    up_lat, up_lon = ([(i, i + 1) for i in range(n - 1)] for n in (n_lat, n_lon))
    down_lat, down_lon = ([(j, i) for i, j in up] for up in (up_lat, up_lon))

    def row(i):
        return jnp.concatenate([state[2, i : i + 1, :], sigma[0, i : i + 1, :]], axis=1)

    north = lax.ppermute(row(rows - 1), "lat", up_lat)
    south = lax.ppermute(row(0), "lat", down_lat)
    west = lax.ppermute(state[2, :, merged - levels :], "lon", up_lon)
    east = lax.ppermute(state[2, :, :levels], "lon", down_lon)
    place = jnp.stack([i_lat, i_lon]).astype(jnp.int32)

    anywhere = pl.BlockSpec(memory_space=pl.ANY)
    steps = pairs // BLOCK

    def part(v, side):
        return pl.BlockSpec((1, rows, BLOCK * LANES), lambda g: (v, 0, g + side * steps))

    width = half // n_lat
    shapes = [(nvars, half, rows, LANES), (nvars, rows, half, LANES), (n_lat, nvars, 4 * width, LANES)]

    def lat_call(nv, first, body, arrays, specs, name, aliases, more=()):
        return pl.pallas_call(
            body,
            grid=(steps,),
            in_specs=specs,
            out_specs=[
                pl.BlockSpec((nv, 2 * BLOCK, rows, LANES), lambda g: (first, g, 0, 0)),
                pl.BlockSpec((nv, rows, 2 * BLOCK, LANES), lambda g: (first, 0, g, 0)),
                pl.BlockSpec((2 * BLOCK // width, nv, 4 * width, LANES), lambda g: (g, first, 0, 0)),
            ]
            + [full(s) for s in more],
            out_shape=[jax.ShapeDtypeStruct(s, f32) for s in shapes + list(more)],
            scratch_shapes=[
                pltpu.VMEM((2, PAIRS * rows, 256), f32),
                pltpu.VMEM((2 * 768, 256), bf16),
                pltpu.VMEM((nvars, pieces, rows, LANES), f32),
            ],
            compiler_params=params(),
            cost_estimate=pl.CostEstimate(
                flops=nv * 60000000, bytes_accessed=nv * 3 * rows * merged * 4, transcendentals=0
            ),
            input_output_aliases=aliases,
            name=name,
        )(*arrays)

    ins = [scales, classes.reshape(1, count), chi_coef.reshape(1, levels), sigma, vert] + [state] * 4
    specs = [full(x.shape) for x in ins[:5]] + [part(1, 0), part(1, 1), part(2, 0), part(2, 1)]
    specs[0] = pl.BlockSpec(memory_space=pltpu.SMEM)
    body = functools.partial(lat_plain, rows, pairs)
    *wue, prm = lat_call(2, 0, body, ins, specs, "lat_chi_temp", {}, [(nvars, 4, LANES)])
    ins = [prm, sigma, vert, bal_temp] + [state] * 5 + [north, south, west, east] + list(wue)
    specs = [full(x.shape) for x in ins[:4]] + [part(0, 0), part(0, 1), part(1, 0), part(1, 1)]
    specs += [pl.BlockSpec((1, rows, merged), lambda g: (2, 0, 0))]
    specs += [full(x.shape) for x in (north, south, west, east)] + [anywhere] * 3
    aliases = {13: 0, 14: 1, 15: 2}
    w, u, edges = lat_call(1, 2, functools.partial(lat_balance, rows, pairs), ins, specs, "lat_psi", aliases)
    def trade(x):
        return lax.all_to_all(x, "lat", split_axis=0, concat_axis=0, tiled=True)

    shares = trade(edges)

    rb = BLOCK
    local, el, es = pl.pallas_call(
        functools.partial(lon_kernel, rb),
        grid=(rows // rb,),
        in_specs=[
            full(prm.shape),
            pl.BlockSpec((1, rows, lon), lambda g: (0, 0, 0)),
            pl.BlockSpec((nvars, rb, half, LANES), lambda g: (0, g, 0, 0)),
        ],
        out_specs=[
            pl.BlockSpec((nvars, half, rb, LANES), lambda g: (0, 0, g, 0)),
            full((nvars, 4, rows, LANES)),
            full((7, rows, LANES)),
        ],
        out_shape=[
            jax.ShapeDtypeStruct((nvars, half, rows, LANES), f32),
            jax.ShapeDtypeStruct((nvars, 4, rows, LANES), f32),
            jax.ShapeDtypeStruct((7, rows, LANES), f32),
        ],
        compiler_params=params(),
        cost_estimate=pl.CostEstimate(
            flops=180000000, bytes_accessed=6 * rows * merged * 4, transcendentals=0
        ),
        name="lon_tile",
    )(prm, sigma, u)

    def round_lon(x):
        return [x] + [
            lax.ppermute(x, "lon", [(i, (i + s) % n_lon) for i in range(n_lon)]) for s in range(1, n_lon)
        ]

    shares, _ = lax.optimization_barrier((shares, es))
    sent = round_lon(es)
    carries = pl.pallas_call(
        functools.partial(solve_kernel, n_lat, rows),
        grid=(1,),
        in_specs=[full(prm.shape), full(shares.shape)],
        out_specs=full(shares.shape),
        out_shape=jax.ShapeDtypeStruct(shares.shape, f32),
        compiler_params=params(),
        cost_estimate=pl.CostEstimate(flops=1000000, bytes_accessed=2 * shares.size * 4, transcendentals=0),
        name="solve",
    )(prm, shares)
    carries = trade(carries)

    crossed, elc, esc = pl.pallas_call(
        carry_kernel,
        grid=(1,),
        in_specs=[full(prm.shape), full(carries.shape)],
        out_specs=[full((nvars, half, 8, LANES)), full((nvars, 4, 8, LANES)), full((6, 8, LANES))],
        out_shape=[
            jax.ShapeDtypeStruct((nvars, half, 8, LANES), f32),
            jax.ShapeDtypeStruct((nvars, 4, 8, LANES), f32),
            jax.ShapeDtypeStruct((6, 8, LANES), f32),
        ],
        compiler_params=params(),
        cost_estimate=pl.CostEstimate(
            flops=30000000, bytes_accessed=4 * nvars * 12 * half * LANES, transcendentals=0
        ),
        name="lon_carry",
    )(prm, carries)
    sent_x = round_lon(esc)

    packed = 2 * PAIRS

    def columns(r):
        return pl.BlockSpec((nvars, packed, r, LANES), lambda g: (0, g, 0, 0))

    ins = [place, prm, local, w, crossed, el, elc] + sent + sent_x
    specs = [full(x.shape) for x in ins]
    specs[0] = pl.BlockSpec(memory_space=pltpu.SMEM)
    specs[2:5] = [columns(rows), columns(rows), columns(8)]
    y, yx, col, side, energy = pl.pallas_call(
        functools.partial(join_kernel, n_lon, rows, packed, 24),
        grid=(half // packed,),
        in_specs=specs,
        out_specs=[
            columns(rows),
            pl.BlockSpec((packed, 8, LANES), lambda g: (g, 0, 0)),
            full((2, rows, LANES)),
            full((2, rows, LANES)),
            full((nvars, 8, LANES)),
        ],
        out_shape=[
            jax.ShapeDtypeStruct((nvars, half, rows, LANES), f32),
            jax.ShapeDtypeStruct((half, 8, LANES), f32),
            jax.ShapeDtypeStruct((2, rows, LANES), f32),
            jax.ShapeDtypeStruct((2, rows, LANES), f32),
            jax.ShapeDtypeStruct((nvars, 8, LANES), f32),
        ],
        scratch_shapes=[
            pltpu.VMEM((nvars, 4, rows, LANES), f32),
            pltpu.VMEM((nvars, 4, 8, LANES), f32),
            pltpu.VMEM((nvars, 4, half, LANES), f32),
            pltpu.VMEM((nvars, 4, rows, LANES), f32),
            pltpu.VMEM((n_lon, 7, rows, LANES), f32),
            pltpu.VMEM((n_lon, 6, 8, LANES), f32),
        ],
        compiler_params=params(),
        cost_estimate=pl.CostEstimate(
            flops=60000000, bytes_accessed=9 * rows * merged * 4, transcendentals=0
        ),
        name="join",
    )(*ins)

    index = jnp.arange(count, dtype=jnp.int32)
    same = (owner[:, None] == owner[None, :]) & (index[None, :] < index[:, None])
    slot = jnp.sum(same.astype(jnp.int32), axis=1)
    target = owner * capacity + slot
    hit = target[:, None] == jnp.arange(devices * capacity)[None, :]
    energy = jnp.sum(energy, axis=1) * prm[:, 3]
    energy = (energy[:, :levels] + energy[:, levels:]).reshape(count)
    table = jnp.sum(jnp.where(hit, energy[:, None], 0.0), axis=0).reshape(devices, capacity)
    table = lax.all_to_all(table, ("lat", "lon"), split_axis=0, concat_axis=0, tiled=True)
    slab_energy = (jnp.sum(table, axis=0) / (devices * rows * lon))[None, :]

    ins = [prm, sigma, north, south, vert, bal_temp, col, side, y, yx]
    specs = [full(x.shape) for x in ins]
    specs[8] = columns(rows)
    specs[9] = pl.BlockSpec((packed, 8, LANES), lambda g: (g, 0, 0))
    applied = pl.pallas_call(
        functools.partial(end_kernel, rows, pairs),
        grid=(half // packed,),
        in_specs=specs,
        out_specs=full(state.shape),
        out_shape=jax.ShapeDtypeStruct(state.shape, f32),
        scratch_shapes=[
            pltpu.VMEM((nvars, PAIRS * rows, 256), f32),
            pltpu.VMEM((8, merged), f32),
            pltpu.VMEM((2, rows, LANES), f32),
            pltpu.VMEM((4 * 768, 256), bf16),
            pltpu.VMEM((nvars, pieces, rows, LANES), f32),
            pltpu.VMEM((pieces, 8, LANES), f32),
        ],
        compiler_params=params(),
        cost_estimate=pl.CostEstimate(
            flops=300000000, bytes_accessed=6 * rows * merged * 4, transcendentals=0
        ),
        name="finish",
    )(*ins)
    return (applied, slab_energy)


def solution(mesh):
    return jax.shard_map(
        shards,
        mesh=mesh,
        in_specs=(P(None, "lat", "lon"), P(None, "lat", "lon"), P(), P(), P(), P(), P(), P()),
        out_specs=(P(None, "lat", "lon"), P(("lat", "lon"), None)),
        check_vma=False,
    )
```

```python
import functools

import jax
import jax.numpy as jnp
from jax import lax
from jax.experimental import pallas as pl
from jax.experimental.pallas import tpu as pltpu
from jax.sharding import PartitionSpec as P

highest = lax.Precision.HIGHEST
f32 = jnp.float32
bf16 = jnp.bfloat16
LANES = 128
PAIRS = 8
BLOCK = 24
ORDER = (1, 2, 0)
LIMIT = 30 * 1024 * 1024


def params():
    return pltpu.CompilerParams(vmem_limit_bytes=LIMIT)


def in_hbm(x):
    return pltpu.with_memory_space_constraint(x, pltpu.HBM)


def full(shape):
    return pl.BlockSpec(shape, lambda g: (0,) * len(shape))


def swap(x):
    return pltpu.roll(x, 64, x.ndim - 1)


def low_lanes(shape):
    return lax.broadcasted_iota(jnp.int32, shape, len(shape) - 1) < 64


def halves(x):
    hi = x.astype(bf16)
    return hi, (x - hi.astype(f32)).astype(bf16)


def dot(x, y):
    return jnp.dot(x, y, preferred_element_type=f32)


def split(x):
    hi, lo = halves(x)
    return jnp.concatenate([hi, lo, hi], axis=1)


def product(x, weights):
    return dot(split(x), weights)


def expand(mat, mixed):
    wide = quad(mat)
    wide = jnp.concatenate([wide, wide], axis=1)
    wide = jnp.concatenate([wide, wide], axis=0)
    src = lax.broadcasted_iota(jnp.int32, (256, 256), 0) // 64
    dst = lax.broadcasted_iota(jnp.int32, (256, 256), 1) // 64
    if mixed:
        src = jnp.where(src == 1, 2, jnp.where(src == 2, 1, src))
    return halves(jnp.where(src == dst, wide, 0.0))


def quad(mat):
    if mat.shape[0] == LANES:
        return mat
    wide = jnp.concatenate([mat, mat], axis=1)
    return jnp.concatenate([wide, wide], axis=0)


def constants(length, decay, m):
    span = jnp.exp(-float(m) / length)
    d = 1.0 - decay * decay
    k1 = decay * (1.0 - span * span) / d
    k2 = (m * span - decay * decay * (span - span * span * span) / d) / d
    tail = decay * decay * (1.0 + span * span) * (1.0 - span * span) / d
    k3 = decay / (d * d) * (1.0 - (2.0 * m + 1.0) * span * span + tail)
    return span, k1, k2, k3


def responses(length, decay, m):
    j = lax.broadcasted_iota(jnp.int32, (m, LANES), 0).astype(f32)
    up = jnp.exp(-j / length)
    down = jnp.exp(-(m - j) / length)
    span = jnp.exp(-float(m) / length)
    d = 1.0 - decay * decay
    diff = up - span * down
    g3 = decay * diff / d
    g2 = ((m - j) * down - decay * decay * (span * up - span * span * down) / d) / d
    part = decay * decay * (1.0 + span * span) * diff / d
    g1 = decay / (d * d) * ((j + 1.0) * up - (2.0 * m + 1.0 - j) * span * down + part)
    return g1, g2, g3, down


def pick(all_carries, me):
    out = []
    for cs in all_carries:
        mine = cs[0]
        for t in range(1, len(cs)):
            mine = jnp.where(me == t, cs[t], mine)
        out.append(mine)
    return out


def solve_carries(n, edge, const):
    span, k1, k2, k3 = const
    first = edge(0, 0)
    zero = jnp.zeros_like(first)
    e1 = [first] + [edge(t, 0) for t in range(1, n)]
    c1, c2, c3, c4 = ([None] * n for _ in range(4))
    c = zero
    for t in range(n):
        c1[t] = c
        c = e1[t] + span * c
    c = zero
    for t in reversed(range(n)):
        c2[t] = c
        c = edge(t, 1) + k1 * c1[t] + span * c
    c = zero
    for t in range(n):
        c3[t] = c
        c = edge(t, 2) + k2 * c1[t] + k1 * c2[t] + span * c
    c = zero
    for t in reversed(range(n)):
        c4[t] = c
        c = edge(t, 3) + k3 * c1[t] + k2 * c2[t] + k1 * c3[t] + span * c
    return c1, c2, c3, c4


def cascade(count, load, store, decay, start):
    step = 24
    edges = []
    for stage in range(4):
        back = stage % 2 == 1

        def body(b, states, back=back):
            base = (count // step - 1 - b) * step if back else b * step
            order = range(step - 1, -1, -1) if back else range(step)
            for o in order:
                new = [decay_k * s + x for decay_k, s, x in zip(decay, states, load(base + o))]
                store(base + o, new)
                states = new
            return tuple(states)

        states = lax.fori_loop(0, count // step, body, tuple(start))
        edges.append(list(states))
    return edges


def stage_sigma(sigma, sg, variables):
    lon = sigma.shape[2]
    for v in variables:
        for at in range(0, lon, LANES):
            width = min(LANES, lon - at)
            sg[v, at // LANES, :, 0:width] = sigma[v, :, at : at + width]


def sigma_tile(sg, v, m, high):
    idx = 2 * (m & 63) + high
    return jnp.take_along_axis(sg[v, m >> 6], idx, axis=1, mode="promise_in_bounds")


def set_weights(weights, k, mat, mixed):
    hi, lo = expand(mat, mixed)
    weights[768 * k : 768 * k + 256] = hi
    weights[768 * k + 256 : 768 * k + 512] = hi
    weights[768 * k + 512 : 768 * k + 768] = lo


def weight(weights, k):
    return weights[768 * k : 768 * (k + 1)]


def lat_filter(vs, rows, prm, u_ref, e_ref):
    nv = len(vs)
    decay = [prm[v, 1:2, :] for v in vs]

    def load(i):
        return [u_ref[k, i] for k in range(nv)]

    def store(i, values):
        for k in range(nv):
            u_ref[k, i] = values[k]

    zero = jnp.zeros((u_ref.shape[2], LANES), f32)
    edges = cascade(rows, load, store, decay, [zero] * nv)
    width = e_ref.shape[2] // 4
    for e in range(4):
        for k in range(nv):
            for c in range(e_ref.shape[0]):
                e_ref[c, k, e * width : (e + 1) * width] = edges[e][k][c * width : (c + 1) * width]


def put_mixed(k, b, rows, res, w_ref, u_ref):
    base = b * 2 * PAIRS
    for p in range(PAIRS):
        part = res[p * rows : (p + 1) * rows]
        w_ref[k, base + 2 * p] = part[:, :LANES]
        w_ref[k, base + 2 * p + 1] = part[:, LANES:]
    at = pl.ds(pl.multiple_of(base, 2 * PAIRS), 2 * PAIRS)
    u_ref[k, :, at, :] = jnp.swapaxes(w_ref[k, at], 0, 1)


def set_params(scales, classes, chi_coef, prm):
    coef = jnp.concatenate([chi_coef[...], chi_coef[...]], axis=1)
    for v in range(3):
        kind = classes[:, 64 * v : 64 * (v + 1)]
        kind = jnp.concatenate([kind, kind], axis=1)
        length = jnp.zeros((1, LANES), f32)
        for n in range(scales.shape[1]):
            length = jnp.where(kind == n, scales[:, n : n + 1], length)
        decay = jnp.exp(-1.0 / length)
        norm = 1.0 - decay
        norm = norm * norm
        norm = norm * norm
        prm[v, 0:1, :] = length
        prm[v, 1:2, :] = decay
        prm[v, 2:3, :] = coef
        prm[v, 3:4, :] = length * jnp.sqrt(length) * norm * norm


def lat_plain(
    rows, pairs, scales, classes, chi_coef, sigma, vert, b1lo, b1hi, b2lo, b2hi,
    w_ref, u_ref, e_ref, prm, xs, wt, sg,
):
    g = pl.program_id(0)

    @pl.when(g == 0)
    def _():
        set_params(scales, classes, chi_coef, prm)
        set_weights(wt, 0, vert[1], True)
        set_weights(wt, 1, vert[2], True)
        stage_sigma(sigma, sg, (1, 2))

    lane = lax.broadcasted_iota(jnp.int32, (rows, LANES), 1)
    high = (lane >= 64).astype(jnp.int32)

    def body(b, _):
        for p in range(PAIRS):
            at = slice(p * rows, (p + 1) * rows)
            cols = pl.ds(pl.multiple_of((b * PAIRS + p) * LANES, LANES), LANES)
            m = g * BLOCK + b * PAIRS + p
            for k, sides in enumerate(((b1lo, b1hi), (b2lo, b2hi))):
                for side in range(2):
                    s = sigma_tile(sg, k + 1, m + side * pairs, high)
                    xs[k, at, side * LANES : (side + 1) * LANES] = sides[side][0, :, cols] * s
        for k in range(2):
            put_mixed(k, b, rows, product(xs[k], weight(wt, k)), w_ref, u_ref)
        return 0

    lax.fori_loop(0, BLOCK // PAIRS, body, 0)
    lat_filter((1, 2), rows, prm, u_ref, e_ref)


def lat_balance(
    rows, pairs, prm, sigma, vert, bal, plo, phi, clo, chi, temp, north, south, west, east, w_in, u_in, e_in,
    w_ref, u_ref, e_ref, xs, wt, sg,
):
    del w_in, u_in, e_in
    g = pl.program_id(0)

    @pl.when(g == 0)
    def _():
        set_weights(wt, 0, vert[0], True)
        (bh, bl), (vh, vl) = halves(bal[...]), halves(vert[0])
        set_weights(wt, 1, dot(bh, vh) + dot(bl, vh) + dot(bh, vl), True)
        stage_sigma(sigma, sg, (0,))

    lane = lax.broadcasted_iota(jnp.int32, (rows, LANES), 1)
    row_id = lax.broadcasted_iota(jnp.int32, (rows, LANES), 0)
    high = (lane >= 64).astype(jnp.int32)
    chi_row = prm[0, 2:3, :]
    last = 2 * pairs - 1
    beyond = [jnp.concatenate([x[...], x[...]], axis=1) for x in (west, east)]

    def at_tile(m):
        return pl.ds(pl.multiple_of(m * LANES, LANES), LANES)

    def laplace(m):
        x = temp[0, :, at_tile(m)]
        left = jnp.where(m == 0, beyond[0], temp[0, :, at_tile(jnp.maximum(m - 1, 0))])
        right = jnp.where(m == last, beyond[1], temp[0, :, at_tile(jnp.minimum(m + 1, last))])
        beside = swap(x + jnp.where(lane >= 64, left, right))
        above = jnp.where(row_id == 0, north[:, at_tile(m)], pltpu.roll(x, 1, 0))
        below = jnp.where(row_id == rows - 1, south[:, at_tile(m)], pltpu.roll(x, rows - 1, 0))
        return 4.0 * x - beside - above - below

    def body(b, _):
        for p in range(PAIRS):
            at = slice(p * rows, (p + 1) * rows)
            cols = at_tile(b * PAIRS + p)
            m = g * BLOCK + b * PAIRS + p
            for side, (pr, cr) in enumerate(((plo, clo), (phi, chi))):
                s = sigma_tile(sg, 0, m + side * pairs, high)
                to = slice(side * LANES, (side + 1) * LANES)
                xs[0, at, to] = (pr[0, :, cols] + chi_row * cr[0, :, cols]) * s
                xs[1, at, to] = laplace(m + side * pairs) * s
        res = dot(jnp.concatenate([split(xs[0]), split(xs[1])], axis=1), wt[...])
        put_mixed(0, b, rows, res, w_ref, u_ref)
        return 0

    lax.fori_loop(0, BLOCK // PAIRS, body, 0)
    lat_filter((0,), rows, prm, u_ref, e_ref)


def lon_filter(prm, rb, o_ref, el_ref, es_ref, at):
    half = o_ref.shape[1]
    nv = len(ORDER)
    decay = [prm[v, 1:2, :] for v in ORDER]

    def load(j):
        return [o_ref[k, j] for k in range(nv)]

    def store(j, values):
        for k in range(nv):
            o_ref[k, j] = values[k]

    edges = cascade(half, load, store, decay, [jnp.zeros((rb, LANES), f32)] * nv)
    low = low_lanes((rb, LANES))
    for k, v in enumerate(ORDER):
        span, k1, k2, k3 = constants(prm[v, 0:1, :], prm[v, 1:2, :], half)
        e1, e2, e3, e4 = (edges[e][k] for e in range(4))
        c1 = jnp.where(low, 0.0, swap(e1))
        t1 = e1 + span * c1
        t2 = e2 + k1 * c1
        c2 = jnp.where(low, swap(t2), 0.0)
        t2 = t2 + span * c2
        t3 = e3 + k2 * c1 + k1 * c2
        c3 = jnp.where(low, 0.0, swap(t3))
        t3 = t3 + span * c3
        t4 = e4 + k3 * c1 + k2 * c2 + k1 * c3
        c4 = jnp.where(low, swap(t4), 0.0)
        t4 = t4 + span * c4
        es_ref[2 * k, at, :] = jnp.where(low, t2, t1)
        es_ref[2 * k + 1, at, :] = jnp.where(low, t4, t3)
        for e, x in enumerate((e1, e2, e3, e4)):
            el_ref[k, e, at, :] = x


def lon_kernel(rb, prm, sigma, u_ref, o_ref, el_ref, es_ref):
    g = pl.program_id(0)
    half = u_ref.shape[2]

    @pl.when(g == 0)
    def _():
        x = sigma[0]
        lon = x.shape[1]
        es_ref[6] = jnp.where(low_lanes((x.shape[0], LANES)), x[:, 0:1], x[:, lon - 1 : lon])

    def turn(b, _):
        at = pl.ds(pl.multiple_of(b * 8, 8), 8)
        for k in range(len(ORDER)):
            for q in range(0, rb, 8):
                o_ref[k, at, q : q + 8, :] = jnp.swapaxes(u_ref[k, q : q + 8, at, :], 0, 1)
        return 0

    lax.fori_loop(0, half // 8, turn, 0)
    lon_filter(prm, rb, o_ref, el_ref, es_ref, pl.ds(pl.multiple_of(g * rb, 8), rb))


def solve_kernel(n_lat, rows, prm, edges, carries):
    width = edges.shape[2] // 4
    for k, v in enumerate(ORDER):
        const = constants(prm[v, 0:1, :], prm[v, 1:2, :], rows)
        c = solve_carries(n_lat, lambda t, e: edges[t, k, e * width : (e + 1) * width, :], const)
        for e in range(4):
            for t in range(n_lat):
                carries[t, k, e * width : (e + 1) * width, :] = c[e][t]


def carry_kernel(prm, carries, o_ref, el_ref, es_ref):
    width = carries.shape[2] // 4
    zero = jnp.zeros((8, LANES), f32)

    def body(d, _):
        for k in range(len(ORDER)):
            for j in range(width):
                at = d * width + j
                o_ref[k, at] = zero
                for e in range(4):
                    o_ref[k, at, e : e + 1, :] = carries[d, k, e * width + j : e * width + j + 1, :]
        return 0

    lax.fori_loop(0, carries.shape[0], body, 0)
    lon_filter(prm, 8, o_ref, el_ref, es_ref, slice(0, 8))


def join_kernel(n_lon, rows, packed, rq, place, prm, u_ref, w_ref, x_ref, el, elc, *rest):
    sent, sent_x = rest[:n_lon], rest[n_lon : 2 * n_lon]
    y_ref, yx_ref, col_ref, side_ref, energy, carry, extra, resp_x, resp_y, esm, esx = rest[2 * n_lon :]
    g = pl.program_id(0)
    half = resp_x.shape[2]
    lat, me = place[0], place[1]

    @pl.when(g == 0)
    def _():
        energy[...] = jnp.zeros_like(energy)
        for s in range(n_lon):
            t = lax.rem(me - s + n_lon, n_lon)
            esm[t] = sent[s][...]
            esx[t] = sent_x[s][...]
        side_ref[0] = esm[jnp.maximum(me - 1, 0), 6]
        side_ref[1] = esm[jnp.minimum(me + 1, n_lon - 1), 6]
        length = jnp.stack([prm[v, 0:1, :] for v in ORDER])
        decay = jnp.stack([prm[v, 1:2, :] for v in ORDER])
        whole = constants(length, decay, 2 * half)
        span, k1, k2, k3 = constants(length, decay, half)
        low = low_lanes((len(ORDER), rows + 8, LANES))
        cache = {}

        def both(main, more):
            parts = [jnp.concatenate([main(k), more(k)], axis=0) for k in range(len(ORDER))]
            return jnp.stack(parts)

        def edge(t, e):
            i = e // 2
            if (t, i) not in cache:
                x = both(lambda k: esm[t, 2 * k + i], lambda k: esx[t, 2 * k + i])
                y = swap(x)
                cache[t, i] = (jnp.where(low, y, x), jnp.where(low, x, y))
            return cache[t, i][e % 2]

        d1, d2, d3, d4 = pick(solve_carries(n_lon, edge, whole), me)
        e1, e2, e3, e4 = (both(lambda k, e=e: el[k, e], lambda k, e=e: elc[k, e]) for e in range(4))
        c1 = jnp.where(low, d1, swap(e1 + span * d1))
        c2 = jnp.where(low, swap(e2 + k1 * c1 + span * d2), d2)
        c3 = jnp.where(low, d3, swap(e3 + k2 * c1 + k1 * c2 + span * d3))
        c4 = jnp.where(low, swap(e4 + k3 * c1 + k2 * c2 + k1 * c3 + span * d4), d4)
        for k, v in enumerate(ORDER):
            for e, r in enumerate(responses(prm[v, 0:1, :], prm[v, 1:2, :], half)):
                resp_x[k, e] = r
            ry = responses(prm[v, 0:1, :], prm[v, 1:2, :], rows)
            for e in range(4):
                resp_y[k, e] = ry[e]

            def total(x, ry=ry):
                y = x[:rows]
                for e in range(4):
                    y = y + ry[e] * x[rows + e : rows + e + 1]
                return y

            for e, c in enumerate((c1, c2, c3, c4)):
                extra[k, e] = c[k, rows:]
                carry[k, e] = total(c[k])
            if v == 0:
                col_ref[0] = total(d3[k])
                col_ref[1] = total(d4[k])

    row8 = lax.broadcasted_iota(jnp.int32, (8, LANES), 0)
    for k, v in enumerate(ORDER):
        total = jnp.zeros((rq, LANES), f32)
        for q in range(0, rows, rq):
            at = slice(q, q + rq)
            c = [carry[k, e, at, :] for e in range(4)]
            ry = [resp_y[k, e, at, :] for e in range(4)]

            def body(b, total, k=k, v=v, q=q, at=at, c=c, ry=ry):
                base = g * packed + b * 8
                rx = [resp_x[k, e, pl.ds(pl.multiple_of(base, 8), 8), :] for e in range(4)]
                for o in range(8):
                    p = b * 8 + o
                    x = x_ref[k, p]
                    y = u_ref[k, p, at, :]
                    for e in range(4):
                        y = y + rx[e][o : o + 1, :] * c[e] + ry[e] * x[e : e + 1, :]
                    y_ref[k, p, at, :] = y
                    total = total + y * w_ref[k, p, at, :]
                    if v == 0 and q == 0:
                        for e in range(4):
                            x = x + rx[e][o : o + 1, :] * extra[k, e]
                        x = pltpu.roll(x, 6, 0)
                        above = jnp.where(lat > 0, x + prm[0, 1:2, :] * y[0:1, :], 0.0)
                        yx_ref[p] = jnp.where(row8 == 0, above, jnp.where(row8 == 1, x, 0.0))
                return total

            total = lax.fori_loop(0, packed // 8, body, total)
        energy[v] += jnp.sum(total.reshape(rq // 8, 8, LANES), axis=0)

    @pl.when(g == 0)
    def _():
        beside = col_ref[0] + prm[0, 1:2, :] * y_ref[ORDER.index(0), 0]
        col_ref[0] = jnp.where(me > 0, beside, 0.0)


def end_kernel(
    rows, pairs, prm, sigma, north, south, vert, bal, col, side, y_ref, yx_ref,
    out, xs, zx, zc, wt, sg, sx,
):
    g = pl.program_id(0)
    half = 2 * pairs
    lon = sigma.shape[2]
    merged = out.shape[2]

    @pl.when(g == 0)
    def _():
        for v in range(3):
            scaled = quad(vert[v]) * prm[v, 3:4, :]
            set_weights(wt, v, scaled.T, True)
        set_weights(wt, 3, quad(bal[...]).T, False)
        stage_sigma(sigma, sg, (0, 1, 2))
        for at in range(0, lon, LANES):
            width = min(LANES, lon - at)
            sx[at // LANES, 0:1, 0:width] = north[:, merged + at : merged + at + width]
            sx[at // LANES, 1:2, 0:width] = south[:, merged + at : merged + at + width]
        lhs = jnp.where(low_lanes((rows, LANES)), col[0], col[1])
        lhs = jnp.concatenate([lhs, jnp.zeros_like(lhs)], axis=1)
        res = product(lhs, weight(wt, 0))
        zc[0] = swap(res[:, :LANES] * swap(side[0]))
        zc[1] = res[:, LANES:] * side[1]

    lane = lax.broadcasted_iota(jnp.int32, (rows, LANES), 1)
    high = (lane >= 64).astype(jnp.int32)
    high8 = high[0:8]
    chi_row = prm[0, 2:3, :]

    def at_tile(m):
        return pl.ds(pl.multiple_of(m * LANES, LANES), LANES)

    lhs = jnp.concatenate(
        [jnp.concatenate([yx_ref[2 * p], yx_ref[2 * p + 1]], axis=1) for p in range(PAIRS)], axis=0
    )
    res = product(lhs, weight(wt, 0))
    for p in range(PAIRS):
        m = g * PAIRS + p
        for side in range(2):
            tile = m + side * pairs
            s = jnp.take_along_axis(sx[tile >> 6], 2 * (tile & 63) + high8, axis=1, mode="promise_in_bounds")
            part = res[p * 8 : (p + 1) * 8, side * LANES : (side + 1) * LANES]
            zx[:, at_tile(tile)] = jnp.where(lax.broadcasted_iota(jnp.int32, (8, LANES), 0) < 2, part * s, 0.0)
    for k in range(3):
        for p in range(2 * PAIRS):
            at = slice((p // 2) * rows, (p // 2 + 1) * rows)
            xs[k, at, (p % 2) * LANES : (p % 2 + 1) * LANES] = y_ref[k, p]
    results = {v: product(xs[k], weight(wt, v)) for k, v in enumerate(ORDER)}
    for p in range(PAIRS):
        m = g * PAIRS + p
        for side in range(2):
            at = at_tile(m + side * pairs)
            z = [
                results[v][p * rows : (p + 1) * rows, side * LANES : (side + 1) * LANES]
                * sigma_tile(sg, v, m + side * pairs, high)
                for v in range(3)
            ]
            out[0, :, at] = z[0]
            out[1, :, at] = z[1] + chi_row * z[0]
            out[2, :, at] = z[2]

    @pl.when(g == pl.num_programs(0) - 1)
    def _():
        row_id = lax.broadcasted_iota(jnp.int32, (rows, LANES), 0)
        last = half - 1

        def body(b, _):
            for p in range(PAIRS):
                for side in range(2):
                    m = b * PAIRS + p + side * pairs
                    x = out[0, :, at_tile(m)]
                    left = jnp.where(m == 0, zc[0], out[0, :, at_tile(jnp.maximum(m - 1, 0))])
                    right = jnp.where(m == last, zc[1], out[0, :, at_tile(jnp.minimum(m + 1, last))])
                    beside = swap(x + jnp.where(lane >= 64, left, right))
                    above = jnp.where(row_id == 0, zx[0:1, at_tile(m)], pltpu.roll(x, 1, 0))
                    below = jnp.where(row_id == rows - 1, zx[1:2, at_tile(m)], pltpu.roll(x, rows - 1, 0))
                    lap = 4.0 * x - beside - above - below
                    xs[0, p * rows : (p + 1) * rows, side * LANES : (side + 1) * LANES] = lap
            res = product(xs[0], weight(wt, 3))
            for p in range(PAIRS):
                for side in range(2):
                    at = at_tile(b * PAIRS + p + side * pairs)
                    part = res[p * rows : (p + 1) * rows, side * LANES : (side + 1) * LANES]
                    out[2, :, at] = out[2, :, at] + part
            return 0

        lax.fori_loop(0, pairs // PAIRS, body, 0)


def shards(state, sigma, vert, bal_temp, chi_coef, scales, classes, owner):
    n_lat = lax.axis_size("lat")
    n_lon = lax.axis_size("lon")
    devices = n_lat * n_lon
    nvars, rows, merged = state.shape
    levels = vert.shape[1]
    lon = merged // levels
    half = lon // 2
    pairs = half // 2
    pieces = (lon + LANES - 1) // LANES
    count = nvars * levels
    capacity = (count + devices - 1) // devices + 1
    i_lat = lax.axis_index("lat")
    i_lon = lax.axis_index("lon")

    up_lat, up_lon = ([(i, i + 1) for i in range(n - 1)] for n in (n_lat, n_lon))
    down_lat, down_lon = ([(j, i) for i, j in up] for up in (up_lat, up_lon))

    def row(i):
        return jnp.concatenate([state[2, i : i + 1, :], sigma[0, i : i + 1, :]], axis=1)

    north = lax.ppermute(row(rows - 1), "lat", up_lat)
    south = lax.ppermute(row(0), "lat", down_lat)
    west = lax.ppermute(state[2, :, merged - levels :], "lon", up_lon)
    east = lax.ppermute(state[2, :, :levels], "lon", down_lon)
    place = jnp.stack([i_lat, i_lon]).astype(jnp.int32)

    anywhere = pl.BlockSpec(memory_space=pl.ANY)
    steps = pairs // BLOCK

    def part(v, side):
        return pl.BlockSpec((1, rows, BLOCK * LANES), lambda g: (v, 0, g + side * steps))

    width = half // n_lat
    shapes = [(nvars, half, rows, LANES), (nvars, rows, half, LANES), (n_lat, nvars, 4 * width, LANES)]

    def lat_call(nv, first, body, arrays, specs, name, aliases, more=()):
        return pl.pallas_call(
            body,
            grid=(steps,),
            in_specs=specs,
            out_specs=[
                pl.BlockSpec((nv, 2 * BLOCK, rows, LANES), lambda g: (first, g, 0, 0)),
                pl.BlockSpec((nv, rows, 2 * BLOCK, LANES), lambda g: (first, 0, g, 0)),
                pl.BlockSpec((2 * BLOCK // width, nv, 4 * width, LANES), lambda g: (g, first, 0, 0)),
            ]
            + [full(s) for s in more],
            out_shape=[pltpu.HBM(s, f32) for s in shapes[:2]]
            + [jax.ShapeDtypeStruct(s, f32) for s in shapes[2:] + list(more)],
            scratch_shapes=[
                pltpu.VMEM((2, PAIRS * rows, 256), f32),
                pltpu.VMEM((2 * 768, 256), bf16),
                pltpu.VMEM((nvars, pieces, rows, LANES), f32),
            ],
            compiler_params=params(),
            cost_estimate=pl.CostEstimate(
                flops=nv * 60000000, bytes_accessed=nv * 3 * rows * merged * 4, transcendentals=0
            ),
            input_output_aliases=aliases,
            name=name,
        )(*arrays)

    ins = [scales.reshape(1, -1), classes.reshape(1, count), chi_coef.reshape(1, levels), sigma, vert] + [state] * 4
    specs = [full(x.shape) for x in ins[:5]] + [part(1, 0), part(1, 1), part(2, 0), part(2, 1)]
    ins = [in_hbm(x) for x in ins]
    body = functools.partial(lat_plain, rows, pairs)
    *wue, prm = lat_call(2, 0, body, ins, specs, "lat_chi_temp", {}, [(nvars, 4, LANES)])
    ins = [prm, sigma, vert, bal_temp] + [in_hbm(state)] * 5 + [north, south, west, east]
    ins += [in_hbm(wue[0]), in_hbm(wue[1]), wue[2]]
    specs = [full(x.shape) for x in ins[:4]] + [part(0, 0), part(0, 1), part(1, 0), part(1, 1)]
    specs += [pl.BlockSpec((1, rows, merged), lambda g: (2, 0, 0))]
    specs += [full(x.shape) for x in (north, south, west, east)] + [anywhere] * 3
    aliases = {13: 0, 14: 1, 15: 2}
    w, u, edges = lat_call(1, 2, functools.partial(lat_balance, rows, pairs), ins, specs, "lat_psi", aliases)
    def trade(x):
        return lax.all_to_all(x, "lat", split_axis=0, concat_axis=0, tiled=True)

    shares = trade(edges)

    rb = BLOCK
    local, el, es = pl.pallas_call(
        functools.partial(lon_kernel, rb),
        grid=(rows // rb,),
        in_specs=[
            full(prm.shape),
            pl.BlockSpec((1, rows, lon), lambda g: (0, 0, 0)),
            pl.BlockSpec((nvars, rb, half, LANES), lambda g: (0, g, 0, 0)),
        ],
        out_specs=[
            pl.BlockSpec((nvars, half, rb, LANES), lambda g: (0, 0, g, 0)),
            full((nvars, 4, rows, LANES)),
            full((7, rows, LANES)),
        ],
        out_shape=[
            pltpu.HBM((nvars, half, rows, LANES), f32),
            jax.ShapeDtypeStruct((nvars, 4, rows, LANES), f32),
            jax.ShapeDtypeStruct((7, rows, LANES), f32),
        ],
        compiler_params=params(),
        cost_estimate=pl.CostEstimate(
            flops=180000000, bytes_accessed=6 * rows * merged * 4, transcendentals=0
        ),
        name="lon_tile",
    )(prm, sigma, in_hbm(u))

    def round_lon(x):
        return [x] + [
            lax.ppermute(x, "lon", [(i, (i + s) % n_lon) for i in range(n_lon)]) for s in range(1, n_lon)
        ]

    shares, _ = lax.optimization_barrier((shares, es))
    sent = round_lon(es)
    carries = pl.pallas_call(
        functools.partial(solve_kernel, n_lat, rows),
        grid=(1,),
        in_specs=[full(prm.shape), full(shares.shape)],
        out_specs=full(shares.shape),
        out_shape=jax.ShapeDtypeStruct(shares.shape, f32),
        compiler_params=params(),
        cost_estimate=pl.CostEstimate(flops=1000000, bytes_accessed=2 * shares.size * 4, transcendentals=0),
        name="solve",
    )(prm, shares)
    carries = trade(carries)

    crossed, elc, esc = pl.pallas_call(
        carry_kernel,
        grid=(1,),
        in_specs=[full(prm.shape), full(carries.shape)],
        out_specs=[full((nvars, half, 8, LANES)), full((nvars, 4, 8, LANES)), full((6, 8, LANES))],
        out_shape=[
            jax.ShapeDtypeStruct((nvars, half, 8, LANES), f32),
            jax.ShapeDtypeStruct((nvars, 4, 8, LANES), f32),
            jax.ShapeDtypeStruct((6, 8, LANES), f32),
        ],
        compiler_params=params(),
        cost_estimate=pl.CostEstimate(
            flops=30000000, bytes_accessed=4 * nvars * 12 * half * LANES, transcendentals=0
        ),
        name="lon_carry",
    )(prm, carries)
    sent_x = round_lon(esc)

    packed = 2 * PAIRS

    def columns(r):
        return pl.BlockSpec((nvars, packed, r, LANES), lambda g: (0, g, 0, 0))

    ins = [place, prm, in_hbm(local), in_hbm(w), crossed, el, elc] + sent + sent_x
    specs = [full(x.shape) for x in ins]
    specs[0] = pl.BlockSpec(memory_space=pltpu.SMEM)
    specs[2:5] = [columns(rows), columns(rows), columns(8)]
    y, yx, col, side, energy = pl.pallas_call(
        functools.partial(join_kernel, n_lon, rows, packed, 24),
        grid=(half // packed,),
        in_specs=specs,
        out_specs=[
            columns(rows),
            pl.BlockSpec((packed, 8, LANES), lambda g: (g, 0, 0)),
            full((2, rows, LANES)),
            full((2, rows, LANES)),
            full((nvars, 8, LANES)),
        ],
        out_shape=[
            pltpu.HBM((nvars, half, rows, LANES), f32),
            jax.ShapeDtypeStruct((half, 8, LANES), f32),
            jax.ShapeDtypeStruct((2, rows, LANES), f32),
            jax.ShapeDtypeStruct((2, rows, LANES), f32),
            jax.ShapeDtypeStruct((nvars, 8, LANES), f32),
        ],
        scratch_shapes=[
            pltpu.VMEM((nvars, 4, rows, LANES), f32),
            pltpu.VMEM((nvars, 4, 8, LANES), f32),
            pltpu.VMEM((nvars, 4, half, LANES), f32),
            pltpu.VMEM((nvars, 4, rows, LANES), f32),
            pltpu.VMEM((n_lon, 7, rows, LANES), f32),
            pltpu.VMEM((n_lon, 6, 8, LANES), f32),
        ],
        compiler_params=params(),
        cost_estimate=pl.CostEstimate(
            flops=60000000, bytes_accessed=9 * rows * merged * 4, transcendentals=0
        ),
        name="join",
    )(*ins)

    index = jnp.arange(count, dtype=jnp.int32)
    same = (owner[:, None] == owner[None, :]) & (index[None, :] < index[:, None])
    slot = jnp.sum(same.astype(jnp.int32), axis=1)
    target = owner * capacity + slot
    hit = target[:, None] == jnp.arange(devices * capacity)[None, :]
    energy = jnp.sum(energy, axis=1) * prm[:, 3]
    energy = (energy[:, :levels] + energy[:, levels:]).reshape(count)
    table = jnp.sum(jnp.where(hit, energy[:, None], 0.0), axis=0).reshape(devices, capacity)
    table = lax.all_to_all(table, ("lat", "lon"), split_axis=0, concat_axis=0, tiled=True)
    slab_energy = (jnp.sum(table, axis=0) / (devices * rows * lon))[None, :]

    ins = [prm, sigma, north, south, vert, bal_temp, col, side, in_hbm(y), yx]
    specs = [full(x.shape) for x in ins]
    specs[8] = columns(rows)
    specs[9] = pl.BlockSpec((packed, 8, LANES), lambda g: (g, 0, 0))
    applied = pl.pallas_call(
        functools.partial(end_kernel, rows, pairs),
        grid=(half // packed,),
        in_specs=specs,
        out_specs=full(state.shape),
        out_shape=jax.ShapeDtypeStruct(state.shape, f32),
        scratch_shapes=[
            pltpu.VMEM((nvars, PAIRS * rows, 256), f32),
            pltpu.VMEM((8, merged), f32),
            pltpu.VMEM((2, rows, LANES), f32),
            pltpu.VMEM((4 * 768, 256), bf16),
            pltpu.VMEM((nvars, pieces, rows, LANES), f32),
            pltpu.VMEM((pieces, 8, LANES), f32),
        ],
        compiler_params=params(),
        cost_estimate=pl.CostEstimate(
            flops=300000000, bytes_accessed=6 * rows * merged * 4, transcendentals=0
        ),
        name="finish",
    )(*ins)
    return (applied, slab_energy)


def solution(mesh):
    return jax.shard_map(
        shards,
        mesh=mesh,
        in_specs=(P(None, "lat", "lon"), P(None, "lat", "lon"), P(), P(), P(), P(), P(), P()),
        out_specs=(P(None, "lat", "lon"), P(("lat", "lon"), None)),
        check_vma=False,
    )
```

```python
import functools

import jax
import jax.numpy as jnp
from jax import lax
from jax.experimental import pallas as pl
from jax.experimental.pallas import tpu as pltpu
from jax.sharding import PartitionSpec as P

highest = lax.Precision.HIGHEST
f32 = jnp.float32
bf16 = jnp.bfloat16
LANES = 128
PAIRS = 8
BLOCK = 24
ORDER = (1, 2, 0)
LIMIT = 30 * 1024 * 1024


def params():
    return pltpu.CompilerParams(vmem_limit_bytes=LIMIT)


def in_hbm(x):
    return pltpu.with_memory_space_constraint(x, pltpu.HBM)


def full(shape):
    return pl.BlockSpec(shape, lambda g: (0,) * len(shape))


def swap(x):
    return pltpu.roll(x, 64, x.ndim - 1)


def low_lanes(shape):
    return lax.broadcasted_iota(jnp.int32, shape, len(shape) - 1) < 64


def halves(x):
    hi = x.astype(bf16)
    return hi, (x - hi.astype(f32)).astype(bf16)


def dot(x, y):
    return jnp.dot(x, y, preferred_element_type=f32)


def split(x):
    hi, lo = halves(x)
    return jnp.concatenate([hi, lo, hi], axis=1)


def product(x, weights):
    return dot(split(x), weights)


def expand(mat, mixed):
    wide = quad(mat)
    wide = jnp.concatenate([wide, wide], axis=1)
    wide = jnp.concatenate([wide, wide], axis=0)
    src = lax.broadcasted_iota(jnp.int32, (256, 256), 0) // 64
    dst = lax.broadcasted_iota(jnp.int32, (256, 256), 1) // 64
    if mixed:
        src = jnp.where(src == 1, 2, jnp.where(src == 2, 1, src))
    return halves(jnp.where(src == dst, wide, 0.0))


def quad(mat):
    if mat.shape[0] == LANES:
        return mat
    wide = jnp.concatenate([mat, mat], axis=1)
    return jnp.concatenate([wide, wide], axis=0)


def constants(length, decay, m):
    span = jnp.exp(-float(m) / length)
    d = 1.0 - decay * decay
    k1 = decay * (1.0 - span * span) / d
    k2 = (m * span - decay * decay * (span - span * span * span) / d) / d
    tail = decay * decay * (1.0 + span * span) * (1.0 - span * span) / d
    k3 = decay / (d * d) * (1.0 - (2.0 * m + 1.0) * span * span + tail)
    return span, k1, k2, k3


def responses(length, decay, m):
    j = lax.broadcasted_iota(jnp.int32, (m, LANES), 0).astype(f32)
    up = jnp.exp(-j / length)
    down = jnp.exp(-(m - j) / length)
    span = jnp.exp(-float(m) / length)
    d = 1.0 - decay * decay
    diff = up - span * down
    g3 = decay * diff / d
    g2 = ((m - j) * down - decay * decay * (span * up - span * span * down) / d) / d
    part = decay * decay * (1.0 + span * span) * diff / d
    g1 = decay / (d * d) * ((j + 1.0) * up - (2.0 * m + 1.0 - j) * span * down + part)
    return g1, g2, g3, down


def pick(all_carries, me):
    out = []
    for cs in all_carries:
        mine = cs[0]
        for t in range(1, len(cs)):
            mine = jnp.where(me == t, cs[t], mine)
        out.append(mine)
    return out


def solve_carries(n, edge, const):
    span, k1, k2, k3 = const
    first = edge(0, 0)
    zero = jnp.zeros_like(first)
    e1 = [first] + [edge(t, 0) for t in range(1, n)]
    c1, c2, c3, c4 = ([None] * n for _ in range(4))
    c = zero
    for t in range(n):
        c1[t] = c
        c = e1[t] + span * c
    c = zero
    for t in reversed(range(n)):
        c2[t] = c
        c = edge(t, 1) + k1 * c1[t] + span * c
    c = zero
    for t in range(n):
        c3[t] = c
        c = edge(t, 2) + k2 * c1[t] + k1 * c2[t] + span * c
    c = zero
    for t in reversed(range(n)):
        c4[t] = c
        c = edge(t, 3) + k3 * c1[t] + k2 * c2[t] + k1 * c3[t] + span * c
    return c1, c2, c3, c4


def cascade(count, load, store, decay, start):
    step = 24
    edges = []
    for stage in range(4):
        back = stage % 2 == 1

        def body(b, states, back=back):
            base = (count // step - 1 - b) * step if back else b * step
            order = range(step - 1, -1, -1) if back else range(step)
            for o in order:
                new = [decay_k * s + x for decay_k, s, x in zip(decay, states, load(base + o))]
                store(base + o, new)
                states = new
            return tuple(states)

        states = lax.fori_loop(0, count // step, body, tuple(start))
        edges.append(list(states))
    return edges


def stage_sigma(sigma, sg, variables):
    lon = sigma.shape[2]
    for v in variables:
        for at in range(0, lon, LANES):
            width = min(LANES, lon - at)
            sg[v, at // LANES, :, 0:width] = sigma[v, :, at : at + width]


def sigma_tile(sg, v, m, high):
    idx = 2 * (m & 63) + high
    return jnp.take_along_axis(sg[v, m >> 6], idx, axis=1, mode="promise_in_bounds")


def set_weights(weights, k, mat, mixed):
    hi, lo = expand(mat, mixed)
    weights[768 * k : 768 * k + 256] = hi
    weights[768 * k + 256 : 768 * k + 512] = hi
    weights[768 * k + 512 : 768 * k + 768] = lo


def weight(weights, k):
    return weights[768 * k : 768 * (k + 1)]


def lat_filter(vs, rows, prm, u_ref, e_ref, p_ref):
    nv = len(vs)
    decay = [prm[v, 1:2, :] for v in vs]

    def load(i):
        return [u_ref[k, i] for k in range(nv)]

    def store(i, values):
        for k in range(nv):
            u_ref[k, i] = values[k]

    zero = jnp.zeros((u_ref.shape[2], LANES), f32)
    edges = cascade(rows, load, store, decay, [zero] * nv)
    for k in range(nv):
        for j in range(0, u_ref.shape[2], 8):
            block = [edges[3 - e][k][j : j + 8] * decay[k] for e in range(4)]
            block = jnp.stack(block + [jnp.zeros((8, LANES), f32)] * 4)
            p_ref[k, j : j + 8] = jnp.swapaxes(block, 0, 1)
    width = e_ref.shape[2] // 4
    for e in range(4):
        for k in range(nv):
            for c in range(e_ref.shape[0]):
                e_ref[c, k, e * width : (e + 1) * width] = edges[e][k][c * width : (c + 1) * width]


def put_mixed(k, b, rows, res, w_ref, u_ref):
    base = b * 2 * PAIRS
    for p in range(PAIRS):
        part = res[p * rows : (p + 1) * rows]
        w_ref[k, base + 2 * p] = part[:, :LANES]
        w_ref[k, base + 2 * p + 1] = part[:, LANES:]
    at = pl.ds(pl.multiple_of(base, 2 * PAIRS), 2 * PAIRS)
    u_ref[k, :, at, :] = jnp.swapaxes(w_ref[k, at], 0, 1)


def set_params(scales, classes, chi_coef, prm):
    coef = jnp.concatenate([chi_coef[...], chi_coef[...]], axis=1)
    for v in range(3):
        kind = classes[:, 64 * v : 64 * (v + 1)]
        kind = jnp.concatenate([kind, kind], axis=1)
        length = jnp.zeros((1, LANES), f32)
        for n in range(scales.shape[1]):
            length = jnp.where(kind == n, scales[:, n : n + 1], length)
        decay = jnp.exp(-1.0 / length)
        norm = 1.0 - decay
        norm = norm * norm
        norm = norm * norm
        prm[v, 0:1, :] = length
        prm[v, 1:2, :] = decay
        prm[v, 2:3, :] = coef
        prm[v, 3:4, :] = length * jnp.sqrt(length) * norm * norm


def lat_plain(
    rows, pairs, scales, classes, chi_coef, sigma, vert, b1lo, b1hi, b2lo, b2hi,
    w_ref, u_ref, e_ref, p_ref, prm, xs, wt, sg,
):
    g = pl.program_id(0)

    @pl.when(g == 0)
    def _():
        set_params(scales, classes, chi_coef, prm)
        set_weights(wt, 0, vert[1], True)
        set_weights(wt, 1, vert[2], True)
        stage_sigma(sigma, sg, (1, 2))

    lane = lax.broadcasted_iota(jnp.int32, (rows, LANES), 1)
    high = (lane >= 64).astype(jnp.int32)

    def body(b, _):
        for p in range(PAIRS):
            at = slice(p * rows, (p + 1) * rows)
            cols = pl.ds(pl.multiple_of((b * PAIRS + p) * LANES, LANES), LANES)
            m = g * BLOCK + b * PAIRS + p
            for k, sides in enumerate(((b1lo, b1hi), (b2lo, b2hi))):
                for side in range(2):
                    s = sigma_tile(sg, k + 1, m + side * pairs, high)
                    xs[k, at, side * LANES : (side + 1) * LANES] = sides[side][0, :, cols] * s
        for k in range(2):
            put_mixed(k, b, rows, product(xs[k], weight(wt, k)), w_ref, u_ref)
        return 0

    lax.fori_loop(0, BLOCK // PAIRS, body, 0)
    lat_filter((1, 2), rows, prm, u_ref, e_ref, p_ref)


def lat_balance(
    rows, pairs, prm, sigma, vert, bal, plo, phi, clo, chi, temp, north, south, west, east, w_in, u_in, e_in, p_in,
    w_ref, u_ref, e_ref, p_ref, xs, wt, sg,
):
    del w_in, u_in, e_in, p_in
    g = pl.program_id(0)

    @pl.when(g == 0)
    def _():
        set_weights(wt, 0, vert[0], True)
        (bh, bl), (vh, vl) = halves(bal[...]), halves(vert[0])
        set_weights(wt, 1, dot(bh, vh) + dot(bl, vh) + dot(bh, vl), True)
        stage_sigma(sigma, sg, (0,))

    lane = lax.broadcasted_iota(jnp.int32, (rows, LANES), 1)
    row_id = lax.broadcasted_iota(jnp.int32, (rows, LANES), 0)
    high = (lane >= 64).astype(jnp.int32)
    chi_row = prm[0, 2:3, :]
    last = 2 * pairs - 1
    beyond = [jnp.concatenate([x[...], x[...]], axis=1) for x in (west, east)]

    def at_tile(m):
        return pl.ds(pl.multiple_of(m * LANES, LANES), LANES)

    def laplace(m):
        x = temp[0, :, at_tile(m)]
        left = jnp.where(m == 0, beyond[0], temp[0, :, at_tile(jnp.maximum(m - 1, 0))])
        right = jnp.where(m == last, beyond[1], temp[0, :, at_tile(jnp.minimum(m + 1, last))])
        beside = swap(x + jnp.where(lane >= 64, left, right))
        above = jnp.where(row_id == 0, north[:, at_tile(m)], pltpu.roll(x, 1, 0))
        below = jnp.where(row_id == rows - 1, south[:, at_tile(m)], pltpu.roll(x, rows - 1, 0))
        return 4.0 * x - beside - above - below

    def body(b, _):
        for p in range(PAIRS):
            at = slice(p * rows, (p + 1) * rows)
            cols = at_tile(b * PAIRS + p)
            m = g * BLOCK + b * PAIRS + p
            for side, (pr, cr) in enumerate(((plo, clo), (phi, chi))):
                s = sigma_tile(sg, 0, m + side * pairs, high)
                to = slice(side * LANES, (side + 1) * LANES)
                xs[0, at, to] = (pr[0, :, cols] + chi_row * cr[0, :, cols]) * s
                xs[1, at, to] = laplace(m + side * pairs) * s
        res = dot(jnp.concatenate([split(xs[0]), split(xs[1])], axis=1), wt[...])
        put_mixed(0, b, rows, res, w_ref, u_ref)
        return 0

    lax.fori_loop(0, BLOCK // PAIRS, body, 0)
    lat_filter((0,), rows, prm, u_ref, e_ref, p_ref)


def lon_filter(prm, rb, o_ref, el_ref, put, at):
    half = o_ref.shape[1]
    nv = len(ORDER)
    decay = [prm[v, 1:2, :] for v in ORDER]

    def load(j):
        return [o_ref[k, j] for k in range(nv)]

    def store(j, values):
        for k in range(nv):
            o_ref[k, j] = values[k]

    edges = cascade(half, load, store, decay, [jnp.zeros((rb, LANES), f32)] * nv)
    low = low_lanes((rb, LANES))
    for k, v in enumerate(ORDER):
        span, k1, k2, k3 = constants(prm[v, 0:1, :], prm[v, 1:2, :], half)
        e1, e2, e3, e4 = (edges[e][k] for e in range(4))
        c1 = jnp.where(low, 0.0, swap(e1))
        t1 = e1 + span * c1
        t2 = e2 + k1 * c1
        c2 = jnp.where(low, swap(t2), 0.0)
        t2 = t2 + span * c2
        t3 = e3 + k2 * c1 + k1 * c2
        c3 = jnp.where(low, 0.0, swap(t3))
        t3 = t3 + span * c3
        t4 = e4 + k3 * c1 + k2 * c2 + k1 * c3
        c4 = jnp.where(low, swap(t4), 0.0)
        t4 = t4 + span * c4
        put(2 * k, jnp.where(low, t2, t1))
        put(2 * k + 1, jnp.where(low, t4, t3))
        for e, x in enumerate((e1, e2, e3, e4)):
            el_ref[k, e, at, :] = x


def lon_kernel(rows, rb, prm, sigma, u_ref, w_ref, o_ref, el_ref, es_ref, px_ref, dot_ref, rx_ref, ry_ref):
    g = pl.program_id(0)
    half = u_ref.shape[2]

    @pl.when(g == 0)
    def _():
        x = sigma[0]
        lon = x.shape[1]
        es_ref[6] = jnp.where(low_lanes((x.shape[0], LANES)), x[:, 0:1], x[:, lon - 1 : lon])
        dot_ref[...] = jnp.zeros_like(dot_ref)
        for k, v in enumerate(ORDER):
            for e, r in enumerate(responses(prm[v, 0:1, :], prm[v, 1:2, :], half)):
                rx_ref[k, e] = r
            for e, r in enumerate(responses(prm[v, 0:1, :], prm[v, 1:2, :], rows)):
                ry_ref[k, e] = r

    def turn(b, _):
        at = pl.ds(pl.multiple_of(b * 8, 8), 8)
        for k in range(len(ORDER)):
            for q in range(0, rb, 8):
                o_ref[k, at, q : q + 8, :] = jnp.swapaxes(u_ref[k, q : q + 8, at, :], 0, 1)
        return 0

    lax.fori_loop(0, half // 8, turn, 0)
    at = pl.ds(pl.multiple_of(g * rb, 8), rb)

    def put(i, x):
        es_ref[i, at, :] = x

    lon_filter(prm, rb, o_ref, el_ref, put, at)
    zero = jnp.zeros((rb, LANES), f32)
    for k in range(len(ORDER)):

        def body(b, sums, k=k):
            base = pl.multiple_of(b * 8, 8)
            rx = [rx_ref[k, e, pl.ds(base, 8), :] for e in range(4)]
            sums = list(sums)
            for o in range(8):
                x = w_ref[k, base + o]
                sums[4] = sums[4] + x * o_ref[k, base + o]
                for e in range(4):
                    sums[e] = sums[e] + x * rx[e][o : o + 1, :]
            return tuple(sums)

        sums = lax.fori_loop(0, half // 8, body, (zero,) * 5)
        for e in range(4):
            px_ref[k, e, at, :] = sums[e]
        dot_ref[k] += jnp.sum(sums[4].reshape(rb // 8, 8, LANES), axis=0)


def solve_kernel(n_lat, rows, prm, edges, carries):
    width = edges.shape[2] // 4
    for k, v in enumerate(ORDER):
        const = constants(prm[v, 0:1, :], prm[v, 1:2, :], rows)
        c = solve_carries(n_lat, lambda t, e: edges[t, k, e * width : (e + 1) * width, :], const)
        for e in range(4):
            for t in range(n_lat):
                carries[t, k, e * width : (e + 1) * width, :] = c[e][t]


def carry_kernel(prm, carries, o_ref, el_ref, es_ref):
    width = carries.shape[2] // 4
    zero = jnp.zeros((8, LANES), f32)

    def body(d, _):
        for k in range(len(ORDER)):
            for j in range(width):
                at = d * width + j
                o_ref[k, at] = zero
                for e in range(4):
                    o_ref[k, at, e : e + 1, :] = carries[d, k, e * width + j : e * width + j + 1, :]
        return 0

    lax.fori_loop(0, carries.shape[0], body, 0)

    def put(i, x):
        for t in range(es_ref.shape[0]):
            es_ref[t, i] = x

    lon_filter(prm, 8, o_ref, el_ref, put, slice(0, 8))


def close_kernel(
    n_lon, rows, place, prm, x_ref, proj, px, dots, rx, ry, el, elc, esx, *rest
):
    sent = rest[:n_lon]
    carry, full_ref, col_ref, side_ref, energy, esm = rest[n_lon:]
    half = rx.shape[2]
    me = place[1]
    for d in range(n_lon):
        esm[me ^ d] = sent[d][...]
    side_ref[0] = esm[jnp.maximum(me - 1, 0), 6]
    side_ref[1] = esm[jnp.minimum(me + 1, n_lon - 1), 6]
    length = jnp.stack([prm[v, 0:1, :] for v in ORDER])
    decay = jnp.stack([prm[v, 1:2, :] for v in ORDER])
    whole = constants(length, decay, 2 * half)
    span, k1, k2, k3 = constants(length, decay, half)
    low = low_lanes((len(ORDER), rows + 8, LANES))
    cache = {}

    def both(main, more):
        parts = [jnp.concatenate([main(k), more(k)], axis=0) for k in range(len(ORDER))]
        return jnp.stack(parts)

    def edge(t, e):
        i = e // 2
        if (t, i) not in cache:
            x = both(lambda k: esm[t, 2 * k + i], lambda k: esx[t, 2 * k + i])
            y = swap(x)
            cache[t, i] = (jnp.where(low, y, x), jnp.where(low, x, y))
        return cache[t, i][e % 2]

    d1, d2, d3, d4 = pick(solve_carries(n_lon, edge, whole), me)
    e1, e2, e3, e4 = (both(lambda k, e=e: el[k, e], lambda k, e=e: elc[k, e]) for e in range(4))
    c1 = jnp.where(low, d1, swap(e1 + span * d1))
    c2 = jnp.where(low, swap(e2 + k1 * c1 + span * d2), d2)
    c3 = jnp.where(low, d3, swap(e3 + k2 * c1 + k1 * c2 + span * d3))
    c4 = jnp.where(low, swap(e4 + k3 * c1 + k2 * c2 + k1 * c3 + span * d4), d4)
    for k, v in enumerate(ORDER):
        more = [c[k, rows:] for c in (c1, c2, c3, c4)]
        sums = jnp.zeros((rows, LANES), f32)
        for e, c in enumerate((c1, c2, c3, c4)):
            carry[k, e] = c[k, :rows]
            sums = sums + c[k, :rows] * px[k, e]

        def body(b, total, k=k, more=more):
            base = pl.multiple_of(b * 8, 8)
            r = [rx[k, e, pl.ds(base, 8), :] for e in range(4)]
            for o in range(8):
                x = x_ref[k, base + o]
                for e in range(4):
                    x = x + r[e][o : o + 1, :] * more[e]
                full_ref[k, base + o] = x
                total = total + x * proj[k, base + o]
            return total

        total = lax.fori_loop(0, half // 8, body, dots[k])
        energy[v] = total + jnp.sum(sums.reshape(rows // 8, 8, LANES), axis=0)
        if v == 0:
            for i, d in enumerate((d3, d4)):
                y = d[k, :rows]
                for e in range(4):
                    y = y + ry[k, e] * d[k, rows + e : rows + e + 1]
                col_ref[i] = y


def end_kernel(
    rows, pairs, rq, place, prm, sigma, north, south, vert, bal, col, side, carry, rx_ref, ry_ref, u_ref, x_ref,
    out, xs, zx, zc, wt, sg, sx,
):
    g = pl.program_id(0)
    half = 2 * pairs
    lon = sigma.shape[2]
    merged = out.shape[2]

    @pl.when(g == 0)
    def _():
        for v in range(3):
            scaled = quad(vert[v]) * prm[v, 3:4, :]
            set_weights(wt, v, scaled.T, True)
        set_weights(wt, 3, quad(bal[...]).T, False)
        stage_sigma(sigma, sg, (0, 1, 2))
        for at in range(0, lon, LANES):
            width = min(LANES, lon - at)
            sx[at // LANES, 0:1, 0:width] = north[:, merged + at : merged + at + width]
            sx[at // LANES, 1:2, 0:width] = south[:, merged + at : merged + at + width]

    lane = lax.broadcasted_iota(jnp.int32, (rows, LANES), 1)
    high = (lane >= 64).astype(jnp.int32)
    high8 = high[0:8]
    chi_row = prm[0, 2:3, :]

    def at_tile(m):
        return pl.ds(pl.multiple_of(m * LANES, LANES), LANES)

    row8 = lax.broadcasted_iota(jnp.int32, (8, LANES), 0)
    beyond = [None] * (2 * PAIRS)
    for k, v in enumerate(ORDER):
        for q in range(0, rows, rq):
            c = [carry[k, e, q : q + rq, :] for e in range(4)]
            ry = [ry_ref[k, e, q : q + rq, :] for e in range(4)]
            rx = [rx_ref[k, e, pl.ds(pl.multiple_of(g * 2 * PAIRS, 8), 2 * PAIRS), :] for e in range(4)]
            for p in range(2 * PAIRS):
                x = x_ref[k, p]
                y = u_ref[k, p, q : q + rq, :]
                for e in range(4):
                    y = y + rx[e][p : p + 1, :] * c[e] + ry[e] * x[e : e + 1, :]
                at = (p // 2) * rows + q
                xs[k, at : at + rq, (p % 2) * LANES : (p % 2 + 1) * LANES] = y
                if v == 0 and q == 0:
                    x = pltpu.roll(x, 6, 0)
                    above = jnp.where(place[0] > 0, x + prm[0, 1:2, :] * y[0:1, :], 0.0)
                    beyond[p] = jnp.where(row8 == 0, above, jnp.where(row8 == 1, x, 0.0))

    @pl.when(g == 0)
    def _():
        first = col[0] + prm[0, 1:2, :] * xs[ORDER.index(0), 0:rows, 0:LANES]
        lhs = jnp.where(lane < 64, jnp.where(place[1] > 0, first, 0.0), col[1])
        lhs = jnp.concatenate([lhs, jnp.zeros_like(lhs)], axis=1)
        res = product(lhs, weight(wt, 0))
        zc[0] = swap(res[:, :LANES] * swap(side[0]))
        zc[1] = res[:, LANES:] * side[1]

    lhs = jnp.concatenate(
        [jnp.concatenate(beyond[2 * p : 2 * p + 2], axis=1) for p in range(PAIRS)], axis=0
    )
    res = product(lhs, weight(wt, 0))
    for p in range(PAIRS):
        m = g * PAIRS + p
        for side in range(2):
            tile = m + side * pairs
            s = jnp.take_along_axis(sx[tile >> 6], 2 * (tile & 63) + high8, axis=1, mode="promise_in_bounds")
            part = res[p * 8 : (p + 1) * 8, side * LANES : (side + 1) * LANES]
            zx[:, at_tile(tile)] = jnp.where(row8 < 2, part * s, 0.0)
    results = {v: product(xs[k], weight(wt, v)) for k, v in enumerate(ORDER)}
    for p in range(PAIRS):
        m = g * PAIRS + p
        for side in range(2):
            at = at_tile(m + side * pairs)
            z = [
                results[v][p * rows : (p + 1) * rows, side * LANES : (side + 1) * LANES]
                * sigma_tile(sg, v, m + side * pairs, high)
                for v in range(3)
            ]
            out[0, :, at] = z[0]
            out[1, :, at] = z[1] + chi_row * z[0]
            out[2, :, at] = z[2]

    @pl.when(g == pl.num_programs(0) - 1)
    def _():
        row_id = lax.broadcasted_iota(jnp.int32, (rows, LANES), 0)
        last = half - 1

        def body(b, _):
            for p in range(PAIRS):
                for side in range(2):
                    m = b * PAIRS + p + side * pairs
                    x = out[0, :, at_tile(m)]
                    left = jnp.where(m == 0, zc[0], out[0, :, at_tile(jnp.maximum(m - 1, 0))])
                    right = jnp.where(m == last, zc[1], out[0, :, at_tile(jnp.minimum(m + 1, last))])
                    beside = swap(x + jnp.where(lane >= 64, left, right))
                    above = jnp.where(row_id == 0, zx[0:1, at_tile(m)], pltpu.roll(x, 1, 0))
                    below = jnp.where(row_id == rows - 1, zx[1:2, at_tile(m)], pltpu.roll(x, rows - 1, 0))
                    lap = 4.0 * x - beside - above - below
                    xs[0, p * rows : (p + 1) * rows, side * LANES : (side + 1) * LANES] = lap
            res = product(xs[0], weight(wt, 3))
            for p in range(PAIRS):
                for side in range(2):
                    at = at_tile(b * PAIRS + p + side * pairs)
                    part = res[p * rows : (p + 1) * rows, side * LANES : (side + 1) * LANES]
                    out[2, :, at] = out[2, :, at] + part
            return 0

        lax.fori_loop(0, pairs // PAIRS, body, 0)


def shards(state, sigma, vert, bal_temp, chi_coef, scales, classes, owner):
    n_lat = lax.axis_size("lat")
    n_lon = lax.axis_size("lon")
    devices = n_lat * n_lon
    nvars, rows, merged = state.shape
    levels = vert.shape[1]
    lon = merged // levels
    half = lon // 2
    pairs = half // 2
    pieces = (lon + LANES - 1) // LANES
    count = nvars * levels
    capacity = (count + devices - 1) // devices + 1
    i_lat = lax.axis_index("lat")
    i_lon = lax.axis_index("lon")

    up_lat, up_lon = ([(i, i + 1) for i in range(n - 1)] for n in (n_lat, n_lon))
    down_lat, down_lon = ([(j, i) for i, j in up] for up in (up_lat, up_lon))

    def row(i):
        return jnp.concatenate([state[2, i : i + 1, :], sigma[0, i : i + 1, :]], axis=1)

    north = lax.ppermute(row(rows - 1), "lat", up_lat)
    south = lax.ppermute(row(0), "lat", down_lat)
    west = lax.ppermute(state[2, :, merged - levels :], "lon", up_lon)
    east = lax.ppermute(state[2, :, :levels], "lon", down_lon)
    place = jnp.stack([i_lat, i_lon]).astype(jnp.int32)

    anywhere = pl.BlockSpec(memory_space=pl.ANY)
    steps = pairs // BLOCK

    def part(v, side):
        return pl.BlockSpec((1, rows, BLOCK * LANES), lambda g: (v, 0, g + side * steps))

    width = half // n_lat
    shapes = [(nvars, half, rows, LANES), (nvars, rows, half, LANES), (n_lat, nvars, 4 * width, LANES)]
    shapes.append((nvars, half, 8, LANES))

    def lat_call(nv, first, body, arrays, specs, name, aliases, more=()):
        return pl.pallas_call(
            body,
            grid=(steps,),
            in_specs=specs,
            out_specs=[
                pl.BlockSpec((nv, 2 * BLOCK, rows, LANES), lambda g: (first, g, 0, 0)),
                pl.BlockSpec((nv, rows, 2 * BLOCK, LANES), lambda g: (first, 0, g, 0)),
                pl.BlockSpec((2 * BLOCK // width, nv, 4 * width, LANES), lambda g: (g, first, 0, 0)),
                pl.BlockSpec((nv, 2 * BLOCK, 8, LANES), lambda g: (first, g, 0, 0)),
            ]
            + [full(s) for s in more],
            out_shape=[pltpu.HBM(s, f32) for s in shapes[:2]]
            + [jax.ShapeDtypeStruct(s, f32) for s in shapes[2:] + list(more)],
            scratch_shapes=[
                pltpu.VMEM((2, PAIRS * rows, 256), f32),
                pltpu.VMEM((2 * 768, 256), bf16),
                pltpu.VMEM((nvars, pieces, rows, LANES), f32),
            ],
            compiler_params=params(),
            cost_estimate=pl.CostEstimate(
                flops=nv * 60000000, bytes_accessed=nv * 3 * rows * merged * 4, transcendentals=0
            ),
            input_output_aliases=aliases,
            name=name,
        )(*arrays)

    ins = [scales.reshape(1, -1), classes.reshape(1, count), chi_coef.reshape(1, levels), sigma, vert] + [state] * 4
    specs = [full(x.shape) for x in ins[:5]] + [part(1, 0), part(1, 1), part(2, 0), part(2, 1)]
    ins = [in_hbm(x) for x in ins]
    body = functools.partial(lat_plain, rows, pairs)
    *wue, prm = lat_call(2, 0, body, ins, specs, "lat_chi_temp", {}, [(nvars, 4, LANES)])
    ins = [prm, sigma, vert, bal_temp] + [in_hbm(state)] * 5 + [north, south, west, east]
    ins += [in_hbm(wue[0]), in_hbm(wue[1]), wue[2], wue[3]]
    specs = [full(x.shape) for x in ins[:4]] + [part(0, 0), part(0, 1), part(1, 0), part(1, 1)]
    specs += [pl.BlockSpec((1, rows, merged), lambda g: (2, 0, 0))]
    specs += [full(x.shape) for x in (north, south, west, east)] + [anywhere] * 4
    aliases = {13: 0, 14: 1, 15: 2, 16: 3}
    w, u, edges, proj = lat_call(1, 2, functools.partial(lat_balance, rows, pairs), ins, specs, "lat_psi", aliases)
    def trade(x, axis):
        return lax.all_to_all(x, axis, split_axis=0, concat_axis=0, tiled=True)

    shares = trade(edges, "lat")

    rb = BLOCK
    local, el, es, px, dots, rx, ry = pl.pallas_call(
        functools.partial(lon_kernel, rows, rb),
        grid=(rows // rb,),
        in_specs=[
            full(prm.shape),
            pl.BlockSpec((1, rows, lon), lambda g: (0, 0, 0)),
            pl.BlockSpec((nvars, rb, half, LANES), lambda g: (0, g, 0, 0)),
            pl.BlockSpec((nvars, half, rb, LANES), lambda g: (0, 0, g, 0)),
        ],
        out_specs=[
            pl.BlockSpec((nvars, half, rb, LANES), lambda g: (0, 0, g, 0)),
            full((nvars, 4, rows, LANES)),
            full((7, rows, LANES)),
            full((nvars, 4, rows, LANES)),
            full((nvars, 8, LANES)),
            full((nvars, 4, half, LANES)),
            full((nvars, 4, rows, LANES)),
        ],
        out_shape=[
            pltpu.HBM((nvars, half, rows, LANES), f32),
            jax.ShapeDtypeStruct((nvars, 4, rows, LANES), f32),
            jax.ShapeDtypeStruct((7, rows, LANES), f32),
            jax.ShapeDtypeStruct((nvars, 4, rows, LANES), f32),
            jax.ShapeDtypeStruct((nvars, 8, LANES), f32),
            jax.ShapeDtypeStruct((nvars, 4, half, LANES), f32),
            jax.ShapeDtypeStruct((nvars, 4, rows, LANES), f32),
        ],
        compiler_params=params(),
        cost_estimate=pl.CostEstimate(
            flops=180000000, bytes_accessed=6 * rows * merged * 4, transcendentals=0
        ),
        name="lon_tile",
    )(prm, sigma, in_hbm(u), in_hbm(w))

    def round_lon(x):
        return [x] + [
            lax.ppermute(x, "lon", [(i, i ^ s) for i in range(n_lon)]) for s in range(1, n_lon)
        ]

    shares, _ = lax.optimization_barrier((shares, es))
    sent = round_lon(es)
    carries = pl.pallas_call(
        functools.partial(solve_kernel, n_lat, rows),
        grid=(1,),
        in_specs=[full(prm.shape), full(shares.shape)],
        out_specs=full(shares.shape),
        out_shape=jax.ShapeDtypeStruct(shares.shape, f32),
        compiler_params=params(),
        cost_estimate=pl.CostEstimate(flops=1000000, bytes_accessed=2 * shares.size * 4, transcendentals=0),
        name="solve",
    )(prm, shares)
    carries = trade(carries, "lat")

    crossed, elc, esc = pl.pallas_call(
        carry_kernel,
        grid=(1,),
        in_specs=[full(prm.shape), full(carries.shape)],
        out_specs=[full((nvars, half, 8, LANES)), full((nvars, 4, 8, LANES)), full((n_lon, 6, 8, LANES))],
        out_shape=[
            jax.ShapeDtypeStruct((nvars, half, 8, LANES), f32),
            jax.ShapeDtypeStruct((nvars, 4, 8, LANES), f32),
            jax.ShapeDtypeStruct((n_lon, 6, 8, LANES), f32),
        ],
        compiler_params=params(),
        cost_estimate=pl.CostEstimate(
            flops=30000000, bytes_accessed=4 * nvars * 12 * half * LANES, transcendentals=0
        ),
        name="lon_carry",
    )(prm, carries)
    sent_x = trade(esc, "lon")

    packed = 2 * PAIRS

    def columns(r):
        return pl.BlockSpec((nvars, packed, r, LANES), lambda g: (0, g, 0, 0))

    ins = [place, prm, crossed, proj, px, dots, rx, ry, el, elc, sent_x] + sent
    specs = [full(x.shape) for x in ins]
    specs[0] = pl.BlockSpec(memory_space=pltpu.SMEM)
    shapes = [
        (nvars, 4, rows, LANES),
        (nvars, half, 8, LANES),
        (2, rows, LANES),
        (2, rows, LANES),
        (nvars, 8, LANES),
    ]
    carry, crossed, col, side, energy = pl.pallas_call(
        functools.partial(close_kernel, n_lon, rows),
        grid=(1,),
        in_specs=specs,
        out_specs=[full(x) for x in shapes],
        out_shape=[jax.ShapeDtypeStruct(x, f32) for x in shapes],
        scratch_shapes=[pltpu.VMEM((n_lon, 7, rows, LANES), f32)],
        compiler_params=params(),
        cost_estimate=pl.CostEstimate(flops=10000000, bytes_accessed=4000000, transcendentals=0),
        name="close",
    )(*ins)

    index = jnp.arange(count, dtype=jnp.int32)
    same = (owner[:, None] == owner[None, :]) & (index[None, :] < index[:, None])
    slot = jnp.sum(same.astype(jnp.int32), axis=1)
    target = owner * capacity + slot
    hit = target[:, None] == jnp.arange(devices * capacity)[None, :]
    energy = jnp.sum(energy, axis=1) * prm[:, 3]
    energy = (energy[:, :levels] + energy[:, levels:]).reshape(count)
    table = jnp.sum(jnp.where(hit, energy[:, None], 0.0), axis=0).reshape(devices, capacity)
    table = lax.all_to_all(table, ("lat", "lon"), split_axis=0, concat_axis=0, tiled=True)
    slab_energy = (jnp.sum(table, axis=0) / (devices * rows * lon))[None, :]

    ins = [place, prm, sigma, north, south, vert, bal_temp, col, side, carry, rx, ry, in_hbm(local), crossed]
    specs = [full(x.shape) for x in ins]
    specs[0] = pl.BlockSpec(memory_space=pltpu.SMEM)
    specs[-2:] = [columns(rows), columns(8)]
    applied = pl.pallas_call(
        functools.partial(end_kernel, rows, pairs, 24),
        grid=(half // packed,),
        in_specs=specs,
        out_specs=full(state.shape),
        out_shape=jax.ShapeDtypeStruct(state.shape, f32),
        scratch_shapes=[
            pltpu.VMEM((nvars, PAIRS * rows, 256), f32),
            pltpu.VMEM((8, merged), f32),
            pltpu.VMEM((2, rows, LANES), f32),
            pltpu.VMEM((4 * 768, 256), bf16),
            pltpu.VMEM((nvars, pieces, rows, LANES), f32),
            pltpu.VMEM((pieces, 8, LANES), f32),
        ],
        compiler_params=params(),
        cost_estimate=pl.CostEstimate(
            flops=300000000, bytes_accessed=6 * rows * merged * 4, transcendentals=0
        ),
        name="finish",
    )(*ins)
    return (applied, slab_energy)


def solution(mesh):
    return jax.shard_map(
        shards,
        mesh=mesh,
        in_specs=(P(None, "lat", "lon"), P(None, "lat", "lon"), P(), P(), P(), P(), P(), P()),
        out_specs=(P(None, "lat", "lon"), P(("lat", "lon"), None)),
        check_vma=False,
    )
```

```python
import functools

import jax
import jax.numpy as jnp
from jax import lax
from jax.experimental import pallas as pl
from jax.experimental.pallas import tpu as pltpu
from jax.sharding import PartitionSpec as P

highest = lax.Precision.HIGHEST
f32 = jnp.float32
bf16 = jnp.bfloat16
LANES = 128
PAIRS = 8
BLOCK = 24
ORDER = (1, 2, 0)
LIMIT = 30 * 1024 * 1024


def params():
    return pltpu.CompilerParams(vmem_limit_bytes=LIMIT)


def in_hbm(x):
    return pltpu.with_memory_space_constraint(x, pltpu.HBM)


def full(shape):
    return pl.BlockSpec(shape, lambda g: (0,) * len(shape))


def swap(x):
    return pltpu.roll(x, 64, x.ndim - 1)


def low_lanes(shape):
    return lax.broadcasted_iota(jnp.int32, shape, len(shape) - 1) < 64


def halves(x):
    hi = x.astype(bf16)
    return hi, (x - hi.astype(f32)).astype(bf16)


def dot(x, y):
    return jnp.dot(x, y, preferred_element_type=f32)


def split(x):
    hi, lo = halves(x)
    return jnp.concatenate([hi, lo, hi], axis=1)


def product(x, weights):
    return dot(split(x), weights)


def expand(mat, mixed):
    wide = quad(mat)
    wide = jnp.concatenate([wide, wide], axis=1)
    wide = jnp.concatenate([wide, wide], axis=0)
    src = lax.broadcasted_iota(jnp.int32, (256, 256), 0) // 64
    dst = lax.broadcasted_iota(jnp.int32, (256, 256), 1) // 64
    if mixed:
        src = jnp.where(src == 1, 2, jnp.where(src == 2, 1, src))
    return halves(jnp.where(src == dst, wide, 0.0))


def quad(mat):
    if mat.shape[0] == LANES:
        return mat
    wide = jnp.concatenate([mat, mat], axis=1)
    return jnp.concatenate([wide, wide], axis=0)


def constants(length, decay, m):
    span = jnp.exp(-float(m) / length)
    d = 1.0 - decay * decay
    k1 = decay * (1.0 - span * span) / d
    k2 = (m * span - decay * decay * (span - span * span * span) / d) / d
    tail = decay * decay * (1.0 + span * span) * (1.0 - span * span) / d
    k3 = decay / (d * d) * (1.0 - (2.0 * m + 1.0) * span * span + tail)
    return span, k1, k2, k3


def responses(length, decay, m):
    j = lax.broadcasted_iota(jnp.int32, (m, LANES), 0).astype(f32)
    up = jnp.exp(-j / length)
    down = jnp.exp(-(m - j) / length)
    span = jnp.exp(-float(m) / length)
    d = 1.0 - decay * decay
    diff = up - span * down
    g3 = decay * diff / d
    g2 = ((m - j) * down - decay * decay * (span * up - span * span * down) / d) / d
    part = decay * decay * (1.0 + span * span) * diff / d
    g1 = decay / (d * d) * ((j + 1.0) * up - (2.0 * m + 1.0 - j) * span * down + part)
    return g1, g2, g3, down


def pick(all_carries, me):
    out = []
    for cs in all_carries:
        mine = cs[0]
        for t in range(1, len(cs)):
            mine = jnp.where(me == t, cs[t], mine)
        out.append(mine)
    return out


def solve_carries(n, edge, const):
    span, k1, k2, k3 = const
    first = edge(0, 0)
    zero = jnp.zeros_like(first)
    e1 = [first] + [edge(t, 0) for t in range(1, n)]
    c1, c2, c3, c4 = ([None] * n for _ in range(4))
    c = zero
    for t in range(n):
        c1[t] = c
        c = e1[t] + span * c
    c = zero
    for t in reversed(range(n)):
        c2[t] = c
        c = edge(t, 1) + k1 * c1[t] + span * c
    c = zero
    for t in range(n):
        c3[t] = c
        c = edge(t, 2) + k2 * c1[t] + k1 * c2[t] + span * c
    c = zero
    for t in reversed(range(n)):
        c4[t] = c
        c = edge(t, 3) + k3 * c1[t] + k2 * c2[t] + k1 * c3[t] + span * c
    return c1, c2, c3, c4


def cascade(count, load, store, decay, start):
    step = 24
    edges = []
    for stage in range(4):
        back = stage % 2 == 1

        def body(b, states, back=back):
            base = (count // step - 1 - b) * step if back else b * step
            order = range(step - 1, -1, -1) if back else range(step)
            for o in order:
                new = [decay_k * s + x for decay_k, s, x in zip(decay, states, load(base + o))]
                store(base + o, new)
                states = new
            return tuple(states)

        states = lax.fori_loop(0, count // step, body, tuple(start))
        edges.append(list(states))
    return edges


def stage_sigma(sigma, sg, variables):
    lon = sigma.shape[2]
    for v in variables:
        for at in range(0, lon, LANES):
            width = min(LANES, lon - at)
            sg[v, at // LANES, :, 0:width] = sigma[v, :, at : at + width]


def sigma_tile(sg, v, m, high):
    idx = 2 * (m & 63) + high
    return jnp.take_along_axis(sg[v, m >> 6], idx, axis=1, mode="promise_in_bounds")


def set_weights(weights, k, mat, mixed):
    hi, lo = expand(mat, mixed)
    weights[768 * k : 768 * k + 256] = hi
    weights[768 * k + 256 : 768 * k + 512] = hi
    weights[768 * k + 512 : 768 * k + 768] = lo


def weight(weights, k):
    return weights[768 * k : 768 * (k + 1)]


def lat_filter(vs, rows, prm, u_ref, e_ref, p_ref):
    nv = len(vs)
    decay = [prm[v, 1:2, :] for v in vs]

    def load(i):
        return [u_ref[k, i] for k in range(nv)]

    def store(i, values):
        for k in range(nv):
            u_ref[k, i] = values[k]

    zero = jnp.zeros((u_ref.shape[2], LANES), f32)
    edges = cascade(rows, load, store, decay, [zero] * nv)
    for k in range(nv):
        for j in range(0, u_ref.shape[2], 8):
            block = [edges[3 - e][k][j : j + 8] * decay[k] for e in range(4)]
            block = jnp.stack(block + [jnp.zeros((8, LANES), f32)] * 4)
            p_ref[k, j : j + 8] = jnp.swapaxes(block, 0, 1)
    width = e_ref.shape[2] // 4
    for e in range(4):
        for k in range(nv):
            for c in range(e_ref.shape[0]):
                e_ref[c, k, e * width : (e + 1) * width] = edges[e][k][c * width : (c + 1) * width]


def put_mixed(k, b, rows, res, w_ref, u_ref):
    base = b * 2 * PAIRS
    for p in range(PAIRS):
        part = res[p * rows : (p + 1) * rows]
        w_ref[k, base + 2 * p] = part[:, :LANES]
        w_ref[k, base + 2 * p + 1] = part[:, LANES:]
    at = pl.ds(pl.multiple_of(base, 2 * PAIRS), 2 * PAIRS)
    u_ref[k, :, at, :] = jnp.swapaxes(w_ref[k, at], 0, 1)


def set_params(scales, classes, chi_coef, prm):
    coef = jnp.concatenate([chi_coef[...], chi_coef[...]], axis=1)
    for v in range(3):
        kind = classes[:, 64 * v : 64 * (v + 1)]
        kind = jnp.concatenate([kind, kind], axis=1)
        length = jnp.zeros((1, LANES), f32)
        for n in range(scales.shape[1]):
            length = jnp.where(kind == n, scales[:, n : n + 1], length)
        decay = jnp.exp(-1.0 / length)
        norm = 1.0 - decay
        norm = norm * norm
        norm = norm * norm
        prm[v, 0:1, :] = length
        prm[v, 1:2, :] = decay
        prm[v, 2:3, :] = coef
        prm[v, 3:4, :] = length * jnp.sqrt(length) * norm * norm


def lat_plain(
    rows, pairs, scales, classes, chi_coef, sigma, vert, b1lo, b1hi, b2lo, b2hi,
    w_ref, u_ref, e_ref, p_ref, prm, xs, wt, sg,
):
    g = pl.program_id(0)

    @pl.when(g == 0)
    def _():
        set_params(scales, classes, chi_coef, prm)
        set_weights(wt, 0, vert[1], True)
        set_weights(wt, 1, vert[2], True)
        stage_sigma(sigma, sg, (1, 2))

    lane = lax.broadcasted_iota(jnp.int32, (rows, LANES), 1)
    high = (lane >= 64).astype(jnp.int32)

    def body(b, _):
        for p in range(PAIRS):
            at = slice(p * rows, (p + 1) * rows)
            cols = pl.ds(pl.multiple_of((b * PAIRS + p) * LANES, LANES), LANES)
            m = g * BLOCK + b * PAIRS + p
            for k, sides in enumerate(((b1lo, b1hi), (b2lo, b2hi))):
                for side in range(2):
                    s = sigma_tile(sg, k + 1, m + side * pairs, high)
                    xs[k, at, side * LANES : (side + 1) * LANES] = sides[side][0, :, cols] * s
        for k in range(2):
            put_mixed(k, b, rows, product(xs[k], weight(wt, k)), w_ref, u_ref)
        return 0

    lax.fori_loop(0, BLOCK // PAIRS, body, 0)
    lat_filter((1, 2), rows, prm, u_ref, e_ref, p_ref)


def lat_balance(
    rows, pairs, prm, sigma, vert, bal, plo, phi, clo, chi, temp, north, south, west, east, w_in, u_in, e_in, p_in,
    w_ref, u_ref, e_ref, p_ref, xs, wt, sg,
):
    del w_in, u_in, e_in, p_in
    g = pl.program_id(0)

    @pl.when(g == 0)
    def _():
        set_weights(wt, 0, vert[0], True)
        (bh, bl), (vh, vl) = halves(bal[...]), halves(vert[0])
        set_weights(wt, 1, dot(bh, vh) + dot(bl, vh) + dot(bh, vl), True)
        stage_sigma(sigma, sg, (0,))

    lane = lax.broadcasted_iota(jnp.int32, (rows, LANES), 1)
    row_id = lax.broadcasted_iota(jnp.int32, (rows, LANES), 0)
    high = (lane >= 64).astype(jnp.int32)
    chi_row = prm[0, 2:3, :]
    last = 2 * pairs - 1
    beyond = [jnp.concatenate([x[...], x[...]], axis=1) for x in (west, east)]

    def at_tile(m):
        return pl.ds(pl.multiple_of(m * LANES, LANES), LANES)

    def laplace(m):
        x = temp[0, :, at_tile(m)]
        left = jnp.where(m == 0, beyond[0], temp[0, :, at_tile(jnp.maximum(m - 1, 0))])
        right = jnp.where(m == last, beyond[1], temp[0, :, at_tile(jnp.minimum(m + 1, last))])
        beside = swap(x + jnp.where(lane >= 64, left, right))
        above = jnp.where(row_id == 0, north[:, at_tile(m)], pltpu.roll(x, 1, 0))
        below = jnp.where(row_id == rows - 1, south[:, at_tile(m)], pltpu.roll(x, rows - 1, 0))
        return 4.0 * x - beside - above - below

    def body(b, _):
        for p in range(PAIRS):
            at = slice(p * rows, (p + 1) * rows)
            cols = at_tile(b * PAIRS + p)
            m = g * BLOCK + b * PAIRS + p
            for side, (pr, cr) in enumerate(((plo, clo), (phi, chi))):
                s = sigma_tile(sg, 0, m + side * pairs, high)
                to = slice(side * LANES, (side + 1) * LANES)
                xs[0, at, to] = (pr[0, :, cols] + chi_row * cr[0, :, cols]) * s
                xs[1, at, to] = laplace(m + side * pairs) * s
        res = dot(jnp.concatenate([split(xs[0]), split(xs[1])], axis=1), wt[...])
        put_mixed(0, b, rows, res, w_ref, u_ref)
        return 0

    lax.fori_loop(0, BLOCK // PAIRS, body, 0)
    lat_filter((0,), rows, prm, u_ref, e_ref, p_ref)


def lon_filter(prm, rb, o_ref, el_ref, put, at):
    half = o_ref.shape[1]
    nv = len(ORDER)
    decay = [prm[v, 1:2, :] for v in ORDER]

    def load(j):
        return [o_ref[k, j] for k in range(nv)]

    def store(j, values):
        for k in range(nv):
            o_ref[k, j] = values[k]

    edges = cascade(half, load, store, decay, [jnp.zeros((rb, LANES), f32)] * nv)
    low = low_lanes((rb, LANES))
    for k, v in enumerate(ORDER):
        span, k1, k2, k3 = constants(prm[v, 0:1, :], prm[v, 1:2, :], half)
        e1, e2, e3, e4 = (edges[e][k] for e in range(4))
        c1 = jnp.where(low, 0.0, swap(e1))
        t1 = e1 + span * c1
        t2 = e2 + k1 * c1
        c2 = jnp.where(low, swap(t2), 0.0)
        t2 = t2 + span * c2
        t3 = e3 + k2 * c1 + k1 * c2
        c3 = jnp.where(low, 0.0, swap(t3))
        t3 = t3 + span * c3
        t4 = e4 + k3 * c1 + k2 * c2 + k1 * c3
        c4 = jnp.where(low, swap(t4), 0.0)
        t4 = t4 + span * c4
        put(2 * k, jnp.where(low, t2, t1))
        put(2 * k + 1, jnp.where(low, t4, t3))
        for e, x in enumerate((e1, e2, e3, e4)):
            el_ref[k, e, at, :] = x


def lon_kernel(rows, rb, prm, sigma, u_ref, w_ref, o_ref, el_ref, es_ref, px_ref, dot_ref, rx_ref, ry_ref):
    g = pl.program_id(0)
    half = u_ref.shape[2]

    @pl.when(g == 0)
    def _():
        x = sigma[0]
        lon = x.shape[1]
        es_ref[6] = jnp.where(low_lanes((x.shape[0], LANES)), x[:, 0:1], x[:, lon - 1 : lon])
        dot_ref[...] = jnp.zeros_like(dot_ref)
        for k, v in enumerate(ORDER):
            for e, r in enumerate(responses(prm[v, 0:1, :], prm[v, 1:2, :], half)):
                rx_ref[k, e] = r
            for e, r in enumerate(responses(prm[v, 0:1, :], prm[v, 1:2, :], rows)):
                ry_ref[k, e] = r

    def turn(b, _):
        at = pl.ds(pl.multiple_of(b * 8, 8), 8)
        for k in range(len(ORDER)):
            for q in range(0, rb, 8):
                o_ref[k, at, q : q + 8, :] = jnp.swapaxes(u_ref[k, q : q + 8, at, :], 0, 1)
        return 0

    lax.fori_loop(0, half // 8, turn, 0)
    at = pl.ds(pl.multiple_of(g * rb, 8), rb)

    def put(i, x):
        es_ref[i, at, :] = x

    lon_filter(prm, rb, o_ref, el_ref, put, at)
    zero = jnp.zeros((rb, LANES), f32)
    for k in range(len(ORDER)):

        def body(b, sums, k=k):
            base = pl.multiple_of(b * 8, 8)
            rx = [rx_ref[k, e, pl.ds(base, 8), :] for e in range(4)]
            sums = list(sums)
            for o in range(8):
                x = w_ref[k, base + o]
                sums[4] = sums[4] + x * o_ref[k, base + o]
                for e in range(4):
                    sums[e] = sums[e] + x * rx[e][o : o + 1, :]
            return tuple(sums)

        sums = lax.fori_loop(0, half // 8, body, (zero,) * 5)
        for e in range(4):
            px_ref[k, e, at, :] = sums[e]
        dot_ref[k] += jnp.sum(sums[4].reshape(rb // 8, 8, LANES), axis=0)


def solve_kernel(n_lat, rows, prm, edges, carries):
    width = edges.shape[2] // 4
    for k, v in enumerate(ORDER):
        const = constants(prm[v, 0:1, :], prm[v, 1:2, :], rows)
        c = solve_carries(n_lat, lambda t, e: edges[t, k, e * width : (e + 1) * width, :], const)
        for e in range(4):
            for t in range(n_lat):
                carries[t, k, e * width : (e + 1) * width, :] = c[e][t]


def carry_kernel(prm, carries, o_ref, el_ref, es_ref):
    width = carries.shape[2] // 4
    zero = jnp.zeros((8, LANES), f32)

    def body(d, _):
        for k in range(len(ORDER)):
            for j in range(width):
                at = d * width + j
                o_ref[k, at] = zero
                for e in range(4):
                    o_ref[k, at, e : e + 1, :] = carries[d, k, e * width + j : e * width + j + 1, :]
        return 0

    lax.fori_loop(0, carries.shape[0], body, 0)

    def put(i, x):
        for t in range(es_ref.shape[0]):
            es_ref[t, i] = x

    lon_filter(prm, 8, o_ref, el_ref, put, slice(0, 8))


def close_kernel(
    n_lon, rows, devices, capacity, cells, place, target, prm, x_ref, proj, px, dots, rx, ry, el, elc, esx, *rest
):
    sent = rest[:n_lon]
    carry, full_ref, col_ref, side_ref, table, esm = rest[n_lon:]
    half = rx.shape[2]
    me = place[1]
    for d in range(n_lon):
        esm[me ^ d] = sent[d][...]
    side_ref[0] = esm[jnp.maximum(me - 1, 0), 6]
    side_ref[1] = esm[jnp.minimum(me + 1, n_lon - 1), 6]
    length = jnp.stack([prm[v, 0:1, :] for v in ORDER])
    decay = jnp.stack([prm[v, 1:2, :] for v in ORDER])
    whole = constants(length, decay, 2 * half)
    span, k1, k2, k3 = constants(length, decay, half)
    low = low_lanes((len(ORDER), rows + 8, LANES))
    cache = {}

    def both(main, more):
        parts = [jnp.concatenate([main(k), more(k)], axis=0) for k in range(len(ORDER))]
        return jnp.stack(parts)

    def edge(t, e):
        i = e // 2
        if (t, i) not in cache:
            x = both(lambda k: esm[t, 2 * k + i], lambda k: esx[t, 2 * k + i])
            y = swap(x)
            cache[t, i] = (jnp.where(low, y, x), jnp.where(low, x, y))
        return cache[t, i][e % 2]

    d1, d2, d3, d4 = pick(solve_carries(n_lon, edge, whole), me)
    e1, e2, e3, e4 = (both(lambda k, e=e: el[k, e], lambda k, e=e: elc[k, e]) for e in range(4))
    c1 = jnp.where(low, d1, swap(e1 + span * d1))
    c2 = jnp.where(low, swap(e2 + k1 * c1 + span * d2), d2)
    c3 = jnp.where(low, d3, swap(e3 + k2 * c1 + k1 * c2 + span * d3))
    c4 = jnp.where(low, swap(e4 + k3 * c1 + k2 * c2 + k1 * c3 + span * d4), d4)
    lane = lax.broadcasted_iota(jnp.int32, (devices, LANES), 1)
    first_slot = lax.broadcasted_iota(jnp.int32, (devices, LANES), 0) * capacity
    owned = jnp.zeros((devices, LANES), f32)
    for k, v in enumerate(ORDER):
        more = [c[k, rows:] for c in (c1, c2, c3, c4)]
        sums = jnp.zeros((rows, LANES), f32)
        for e, c in enumerate((c1, c2, c3, c4)):
            carry[k, e] = c[k, :rows]
            sums = sums + c[k, :rows] * px[k, e]

        def body(b, total, k=k, more=more):
            base = pl.multiple_of(b * 8, 8)
            r = [rx[k, e, pl.ds(base, 8), :] for e in range(4)]
            for o in range(8):
                x = x_ref[k, base + o]
                for e in range(4):
                    x = x + r[e][o : o + 1, :] * more[e]
                full_ref[k, base + o] = x
                total = total + x * proj[k, base + o]
            return total

        total = lax.fori_loop(0, half // 8, body, dots[k])
        total = total + jnp.sum(sums.reshape(rows // 8, 8, LANES), axis=0)
        total = jnp.sum(total, axis=0, keepdims=True)
        total = (total + swap(total)) * prm[v, 3:4, :] * (1.0 / cells)
        where = target[:, 64 * v : 64 * (v + 1)]
        where = jnp.concatenate([where, where], axis=1) - first_slot
        for s in range(capacity):
            mine = jnp.where((lane < 64) & (where == s), total, 0.0)
            owned = owned + jnp.where(lane == s, jnp.sum(mine, axis=1, keepdims=True), 0.0)
        if v == 0:
            for i, d in enumerate((d3, d4)):
                y = d[k, :rows]
                for e in range(4):
                    y = y + ry[k, e] * d[k, rows + e : rows + e + 1]
                col_ref[i] = y
    table[...] = owned


def end_kernel(
    rows, pairs, rq, place, prm, sigma, north, south, vert, bal, col, side, carry, rx_ref, ry_ref, u_ref, x_ref,
    out_ref, out, xs, zx, zc, wt, sg, sx, sems,
):
    g = pl.program_id(0)
    half = 2 * pairs
    lon = sigma.shape[2]
    merged = out.shape[2]
    steps = pairs // PAIRS

    def copy(v, side_at, step):
        first = pl.multiple_of((step * PAIRS + side_at * pairs) * LANES, LANES)
        cols = pl.ds(first, PAIRS * LANES)
        return pltpu.make_async_copy(out.at[v, :, cols], out_ref.at[v, :, cols], sems.at[v, side_at, step])

    @pl.when(g == 0)
    def _():
        for v in range(3):
            scaled = quad(vert[v]) * prm[v, 3:4, :]
            set_weights(wt, v, scaled.T, True)
        set_weights(wt, 3, quad(bal[...]).T, False)
        stage_sigma(sigma, sg, (0, 1, 2))
        for at in range(0, lon, LANES):
            width = min(LANES, lon - at)
            sx[at // LANES, 0:1, 0:width] = north[:, merged + at : merged + at + width]
            sx[at // LANES, 1:2, 0:width] = south[:, merged + at : merged + at + width]

    lane = lax.broadcasted_iota(jnp.int32, (rows, LANES), 1)
    high = (lane >= 64).astype(jnp.int32)
    high8 = high[0:8]
    chi_row = prm[0, 2:3, :]

    def at_tile(m):
        return pl.ds(pl.multiple_of(m * LANES, LANES), LANES)

    row8 = lax.broadcasted_iota(jnp.int32, (8, LANES), 0)
    beyond = [None] * (2 * PAIRS)
    for k, v in enumerate(ORDER):
        for q in range(0, rows, rq):
            c = [carry[k, e, q : q + rq, :] for e in range(4)]
            ry = [ry_ref[k, e, q : q + rq, :] for e in range(4)]
            rx = [rx_ref[k, e, pl.ds(pl.multiple_of(g * 2 * PAIRS, 8), 2 * PAIRS), :] for e in range(4)]
            for p in range(2 * PAIRS):
                x = x_ref[k, p]
                y = u_ref[k, p, q : q + rq, :]
                for e in range(4):
                    y = y + rx[e][p : p + 1, :] * c[e] + ry[e] * x[e : e + 1, :]
                at = (p // 2) * rows + q
                xs[k, at : at + rq, (p % 2) * LANES : (p % 2 + 1) * LANES] = y
                if v == 0 and q == 0:
                    x = pltpu.roll(x, 6, 0)
                    above = jnp.where(place[0] > 0, x + prm[0, 1:2, :] * y[0:1, :], 0.0)
                    beyond[p] = jnp.where(row8 == 0, above, jnp.where(row8 == 1, x, 0.0))

    @pl.when(g == 0)
    def _():
        first = col[0] + prm[0, 1:2, :] * xs[ORDER.index(0), 0:rows, 0:LANES]
        lhs = jnp.where(lane < 64, jnp.where(place[1] > 0, first, 0.0), col[1])
        lhs = jnp.concatenate([lhs, jnp.zeros_like(lhs)], axis=1)
        res = product(lhs, weight(wt, 0))
        zc[0] = swap(res[:, :LANES] * swap(side[0]))
        zc[1] = res[:, LANES:] * side[1]

    lhs = jnp.concatenate(
        [jnp.concatenate(beyond[2 * p : 2 * p + 2], axis=1) for p in range(PAIRS)], axis=0
    )
    res = product(lhs, weight(wt, 0))
    for p in range(PAIRS):
        m = g * PAIRS + p
        for side in range(2):
            tile = m + side * pairs
            s = jnp.take_along_axis(sx[tile >> 6], 2 * (tile & 63) + high8, axis=1, mode="promise_in_bounds")
            part = res[p * 8 : (p + 1) * 8, side * LANES : (side + 1) * LANES]
            zx[:, at_tile(tile)] = jnp.where(row8 < 2, part * s, 0.0)
    results = {v: product(xs[k], weight(wt, v)) for k, v in enumerate(ORDER)}
    for p in range(PAIRS):
        m = g * PAIRS + p
        for side in range(2):
            at = at_tile(m + side * pairs)
            z = [
                results[v][p * rows : (p + 1) * rows, side * LANES : (side + 1) * LANES]
                * sigma_tile(sg, v, m + side * pairs, high)
                for v in range(3)
            ]
            out[0, :, at] = z[0]
            out[1, :, at] = z[1] + chi_row * z[0]
            out[2, :, at] = z[2]
    for v in range(2):
        for side_at in range(2):
            copy(v, side_at, g).start()

    @pl.when(g == pl.num_programs(0) - 1)
    def _():
        row_id = lax.broadcasted_iota(jnp.int32, (rows, LANES), 0)
        last = half - 1

        def body(b, _):
            for p in range(PAIRS):
                for side in range(2):
                    m = b * PAIRS + p + side * pairs
                    x = out[0, :, at_tile(m)]
                    left = jnp.where(m == 0, zc[0], out[0, :, at_tile(jnp.maximum(m - 1, 0))])
                    right = jnp.where(m == last, zc[1], out[0, :, at_tile(jnp.minimum(m + 1, last))])
                    beside = swap(x + jnp.where(lane >= 64, left, right))
                    above = jnp.where(row_id == 0, zx[0:1, at_tile(m)], pltpu.roll(x, 1, 0))
                    below = jnp.where(row_id == rows - 1, zx[1:2, at_tile(m)], pltpu.roll(x, rows - 1, 0))
                    lap = 4.0 * x - beside - above - below
                    xs[0, p * rows : (p + 1) * rows, side * LANES : (side + 1) * LANES] = lap
            res = product(xs[0], weight(wt, 3))
            for p in range(PAIRS):
                for side in range(2):
                    at = at_tile(b * PAIRS + p + side * pairs)
                    part = res[p * rows : (p + 1) * rows, side * LANES : (side + 1) * LANES]
                    out[2, :, at] = out[2, :, at] + part
            for side_at in range(2):
                copy(2, side_at, b).start()
            return 0

        lax.fori_loop(0, steps, body, 0)
        for v in range(3):
            for side_at in range(2):
                for step in range(steps):
                    copy(v, side_at, step).wait()


def shards(state, sigma, vert, bal_temp, chi_coef, scales, classes, owner):
    n_lat = lax.axis_size("lat")
    n_lon = lax.axis_size("lon")
    devices = n_lat * n_lon
    nvars, rows, merged = state.shape
    levels = vert.shape[1]
    lon = merged // levels
    half = lon // 2
    pairs = half // 2
    pieces = (lon + LANES - 1) // LANES
    count = nvars * levels
    capacity = (count + devices - 1) // devices + 1
    i_lat = lax.axis_index("lat")
    i_lon = lax.axis_index("lon")

    up_lat, up_lon = ([(i, i + 1) for i in range(n - 1)] for n in (n_lat, n_lon))
    down_lat, down_lon = ([(j, i) for i, j in up] for up in (up_lat, up_lon))

    def row(i):
        return jnp.concatenate([state[2, i : i + 1, :], sigma[0, i : i + 1, :]], axis=1)

    north = lax.ppermute(row(rows - 1), "lat", up_lat)
    south = lax.ppermute(row(0), "lat", down_lat)
    west = lax.ppermute(state[2, :, merged - levels :], "lon", up_lon)
    east = lax.ppermute(state[2, :, :levels], "lon", down_lon)
    place = jnp.stack([i_lat, i_lon]).astype(jnp.int32)

    anywhere = pl.BlockSpec(memory_space=pl.ANY)
    steps = pairs // BLOCK

    def part(v, side):
        return pl.BlockSpec((1, rows, BLOCK * LANES), lambda g: (v, 0, g + side * steps))

    width = half // n_lat
    shapes = [(nvars, half, rows, LANES), (nvars, rows, half, LANES), (n_lat, nvars, 4 * width, LANES)]
    shapes.append((nvars, half, 8, LANES))

    def lat_call(nv, first, body, arrays, specs, name, aliases, more=()):
        return pl.pallas_call(
            body,
            grid=(steps,),
            in_specs=specs,
            out_specs=[
                pl.BlockSpec((nv, 2 * BLOCK, rows, LANES), lambda g: (first, g, 0, 0)),
                pl.BlockSpec((nv, rows, 2 * BLOCK, LANES), lambda g: (first, 0, g, 0)),
                pl.BlockSpec((2 * BLOCK // width, nv, 4 * width, LANES), lambda g: (g, first, 0, 0)),
                pl.BlockSpec((nv, 2 * BLOCK, 8, LANES), lambda g: (first, g, 0, 0)),
            ]
            + [full(s) for s in more],
            out_shape=[jax.ShapeDtypeStruct(s, f32) if n == 2 else pltpu.HBM(s, f32) for n, s in enumerate(shapes)]
            + [pltpu.HBM(s, f32) for s in more],
            scratch_shapes=[
                pltpu.VMEM((2, PAIRS * rows, 256), f32),
                pltpu.VMEM((2 * 768, 256), bf16),
                pltpu.VMEM((nvars, pieces, rows, LANES), f32),
            ],
            compiler_params=params(),
            cost_estimate=pl.CostEstimate(
                flops=nv * 60000000, bytes_accessed=nv * 3 * rows * merged * 4, transcendentals=0
            ),
            input_output_aliases=aliases,
            name=name,
        )(*arrays)

    ins = [scales.reshape(1, -1), classes.reshape(1, count), chi_coef.reshape(1, levels), sigma, vert] + [state] * 4
    specs = [full(x.shape) for x in ins[:5]] + [part(1, 0), part(1, 1), part(2, 0), part(2, 1)]
    ins = [in_hbm(x) for x in ins]
    body = functools.partial(lat_plain, rows, pairs)
    *wue, prm = lat_call(2, 0, body, ins, specs, "lat_chi_temp", {}, [(nvars, 4, LANES)])
    ins = [in_hbm(x) for x in [prm, sigma, vert, bal_temp] + [state] * 5] + [north, south, west, east]
    ins += [in_hbm(wue[0]), in_hbm(wue[1]), wue[2], in_hbm(wue[3])]
    specs = [full(x.shape) for x in ins[:4]] + [part(0, 0), part(0, 1), part(1, 0), part(1, 1)]
    specs += [pl.BlockSpec((1, rows, merged), lambda g: (2, 0, 0))]
    specs += [full(x.shape) for x in (north, south, west, east)] + [anywhere] * 4
    aliases = {13: 0, 14: 1, 15: 2, 16: 3}
    w, u, edges, proj = lat_call(1, 2, functools.partial(lat_balance, rows, pairs), ins, specs, "lat_psi", aliases)
    def trade(x, axis):
        return lax.all_to_all(x, axis, split_axis=0, concat_axis=0, tiled=True)

    shares = trade(edges, "lat")

    rb = BLOCK
    local, el, es, px, dots, rx, ry = pl.pallas_call(
        functools.partial(lon_kernel, rows, rb),
        grid=(rows // rb,),
        in_specs=[
            full(prm.shape),
            pl.BlockSpec((1, rows, lon), lambda g: (0, 0, 0)),
            pl.BlockSpec((nvars, rb, half, LANES), lambda g: (0, g, 0, 0)),
            pl.BlockSpec((nvars, half, rb, LANES), lambda g: (0, 0, g, 0)),
        ],
        out_specs=[
            pl.BlockSpec((nvars, half, rb, LANES), lambda g: (0, 0, g, 0)),
            full((nvars, 4, rows, LANES)),
            full((7, rows, LANES)),
            full((nvars, 4, rows, LANES)),
            full((nvars, 8, LANES)),
            full((nvars, 4, half, LANES)),
            full((nvars, 4, rows, LANES)),
        ],
        out_shape=[
            pltpu.HBM((nvars, half, rows, LANES), f32),
            pltpu.HBM((nvars, 4, rows, LANES), f32),
            jax.ShapeDtypeStruct((7, rows, LANES), f32),
            pltpu.HBM((nvars, 4, rows, LANES), f32),
            pltpu.HBM((nvars, 8, LANES), f32),
            pltpu.HBM((nvars, 4, half, LANES), f32),
            pltpu.HBM((nvars, 4, rows, LANES), f32),
        ],
        compiler_params=params(),
        cost_estimate=pl.CostEstimate(
            flops=180000000, bytes_accessed=6 * rows * merged * 4, transcendentals=0
        ),
        name="lon_tile",
    )(*[in_hbm(x) for x in (prm, sigma, u, w)])

    def round_lon(x):
        return [x] + [
            lax.ppermute(x, "lon", [(i, i ^ s) for i in range(n_lon)]) for s in range(1, n_lon)
        ]

    shares, _ = lax.optimization_barrier((shares, es))
    sent = round_lon(es)
    carries = pl.pallas_call(
        functools.partial(solve_kernel, n_lat, rows),
        grid=(1,),
        in_specs=[full(prm.shape), full(shares.shape)],
        out_specs=full(shares.shape),
        out_shape=jax.ShapeDtypeStruct(shares.shape, f32),
        compiler_params=params(),
        cost_estimate=pl.CostEstimate(flops=1000000, bytes_accessed=2 * shares.size * 4, transcendentals=0),
        name="solve",
    )(in_hbm(prm), shares)
    carries = trade(carries, "lat")

    crossed, elc, esc = pl.pallas_call(
        carry_kernel,
        grid=(1,),
        in_specs=[full(prm.shape), full(carries.shape)],
        out_specs=[full((nvars, half, 8, LANES)), full((nvars, 4, 8, LANES)), full((n_lon, 6, 8, LANES))],
        out_shape=[
            pltpu.HBM((nvars, half, 8, LANES), f32),
            pltpu.HBM((nvars, 4, 8, LANES), f32),
            jax.ShapeDtypeStruct((n_lon, 6, 8, LANES), f32),
        ],
        compiler_params=params(),
        cost_estimate=pl.CostEstimate(
            flops=30000000, bytes_accessed=4 * nvars * 12 * half * LANES, transcendentals=0
        ),
        name="lon_carry",
    )(in_hbm(prm), carries)
    sent_x = trade(esc, "lon")

    packed = 2 * PAIRS

    def columns(r):
        return pl.BlockSpec((nvars, packed, r, LANES), lambda g: (0, g, 0, 0))

    index = jnp.arange(count, dtype=jnp.int32)
    same = (owner[:, None] == owner[None, :]) & (index[None, :] < index[:, None])
    target = (owner * capacity + jnp.sum(same.astype(jnp.int32), axis=1)).reshape(1, count)

    ins = [in_hbm(x) for x in (prm, crossed, proj, px, dots, rx, ry, el, elc)]
    ins = [place, target] + ins + [sent_x] + sent
    specs = [full(x.shape) for x in ins]
    specs[0] = pl.BlockSpec(memory_space=pltpu.SMEM)
    shapes = [(nvars, 4, rows, LANES), (nvars, half, 8, LANES), (2, rows, LANES), (2, rows, LANES)]
    carry, crossed, col, side, table = pl.pallas_call(
        functools.partial(close_kernel, n_lon, rows, devices, capacity, devices * rows * lon),
        grid=(1,),
        in_specs=specs,
        out_specs=[full(x) for x in shapes] + [full((devices, LANES))],
        out_shape=[pltpu.HBM(x, f32) for x in shapes] + [jax.ShapeDtypeStruct((devices, LANES), f32)],
        scratch_shapes=[pltpu.VMEM((n_lon, 7, rows, LANES), f32)],
        compiler_params=params(),
        cost_estimate=pl.CostEstimate(flops=10000000, bytes_accessed=4000000, transcendentals=0),
        name="close",
    )(*ins)
    table = trade(table, ("lat", "lon"))
    slab_energy = jnp.sum(table, axis=0, keepdims=True)[:, :capacity]

    ins = [prm, sigma, north, south, vert, bal_temp, col, side, carry, rx, ry, local, crossed]
    ins = [place] + [in_hbm(x) for x in ins]
    specs = [full(x.shape) for x in ins]
    specs[0] = pl.BlockSpec(memory_space=pltpu.SMEM)
    specs[-2:] = [columns(rows), columns(8)]
    applied = pl.pallas_call(
        functools.partial(end_kernel, rows, pairs, 24),
        grid=(half // packed,),
        in_specs=specs,
        out_specs=anywhere,
        out_shape=jax.ShapeDtypeStruct(state.shape, f32),
        scratch_shapes=[
            pltpu.VMEM(state.shape, f32),
            pltpu.VMEM((nvars, PAIRS * rows, 256), f32),
            pltpu.VMEM((8, merged), f32),
            pltpu.VMEM((2, rows, LANES), f32),
            pltpu.VMEM((4 * 768, 256), bf16),
            pltpu.VMEM((nvars, pieces, rows, LANES), f32),
            pltpu.VMEM((pieces, 8, LANES), f32),
            pltpu.SemaphoreType.DMA((3, 2, pairs // PAIRS)),
        ],
        compiler_params=params(),
        cost_estimate=pl.CostEstimate(
            flops=300000000, bytes_accessed=6 * rows * merged * 4, transcendentals=0
        ),
        name="finish",
    )(*ins)
    return (applied, slab_energy)


def solution(mesh):
    return jax.shard_map(
        shards,
        mesh=mesh,
        in_specs=(P(None, "lat", "lon"), P(None, "lat", "lon"), P(), P(), P(), P(), P(), P()),
        out_specs=(P(None, "lat", "lon"), P(("lat", "lon"), None)),
        check_vma=False,
    )
```

```python
import functools

import jax
import jax.numpy as jnp
from jax import lax
from jax.experimental import pallas as pl
from jax.experimental.pallas import tpu as pltpu
from jax.sharding import PartitionSpec as P

highest = lax.Precision.HIGHEST
f32 = jnp.float32
bf16 = jnp.bfloat16
LANES = 128
PAIRS = 8
BLOCK = 24
ORDER = (1, 2, 0)
LIMIT = 30 * 1024 * 1024


def params():
    return pltpu.CompilerParams(vmem_limit_bytes=LIMIT)


def in_hbm(x):
    return pltpu.with_memory_space_constraint(x, pltpu.HBM)


def full(shape):
    return pl.BlockSpec(shape, lambda g: (0,) * len(shape))


def swap(x):
    return pltpu.roll(x, 64, x.ndim - 1)


def low_lanes(shape):
    return lax.broadcasted_iota(jnp.int32, shape, len(shape) - 1) < 64


def halves(x):
    hi = x.astype(bf16)
    return hi, (x - hi.astype(f32)).astype(bf16)


def dot(x, y):
    return jnp.dot(x, y, preferred_element_type=f32)


def split(x):
    hi, lo = halves(x)
    return jnp.concatenate([hi, lo, hi], axis=1)


def product(x, weights):
    return dot(split(x), weights)


def expand(mat, mixed):
    wide = quad(mat)
    wide = jnp.concatenate([wide, wide], axis=1)
    wide = jnp.concatenate([wide, wide], axis=0)
    src = lax.broadcasted_iota(jnp.int32, (256, 256), 0) // 64
    dst = lax.broadcasted_iota(jnp.int32, (256, 256), 1) // 64
    if mixed:
        src = jnp.where(src == 1, 2, jnp.where(src == 2, 1, src))
    return halves(jnp.where(src == dst, wide, 0.0))


def quad(mat):
    if mat.shape[0] == LANES:
        return mat
    wide = jnp.concatenate([mat, mat], axis=1)
    return jnp.concatenate([wide, wide], axis=0)


def constants(length, decay, m):
    span = jnp.exp(-float(m) / length)
    d = 1.0 - decay * decay
    k1 = decay * (1.0 - span * span) / d
    k2 = (m * span - decay * decay * (span - span * span * span) / d) / d
    tail = decay * decay * (1.0 + span * span) * (1.0 - span * span) / d
    k3 = decay / (d * d) * (1.0 - (2.0 * m + 1.0) * span * span + tail)
    return span, k1, k2, k3


def responses(length, decay, m):
    j = lax.broadcasted_iota(jnp.int32, (m, LANES), 0).astype(f32)
    up = jnp.exp(-j / length)
    down = jnp.exp(-(m - j) / length)
    span = jnp.exp(-float(m) / length)
    d = 1.0 - decay * decay
    diff = up - span * down
    g3 = decay * diff / d
    g2 = ((m - j) * down - decay * decay * (span * up - span * span * down) / d) / d
    part = decay * decay * (1.0 + span * span) * diff / d
    g1 = decay / (d * d) * ((j + 1.0) * up - (2.0 * m + 1.0 - j) * span * down + part)
    return g1, g2, g3, down


def pick(all_carries, me):
    out = []
    for cs in all_carries:
        mine = cs[0]
        for t in range(1, len(cs)):
            mine = jnp.where(me == t, cs[t], mine)
        out.append(mine)
    return out


def solve_carries(n, edge, const):
    span, k1, k2, k3 = const
    first = edge(0, 0)
    zero = jnp.zeros_like(first)
    e1 = [first] + [edge(t, 0) for t in range(1, n)]
    c1, c2, c3, c4 = ([None] * n for _ in range(4))
    c = zero
    for t in range(n):
        c1[t] = c
        c = e1[t] + span * c
    c = zero
    for t in reversed(range(n)):
        c2[t] = c
        c = edge(t, 1) + k1 * c1[t] + span * c
    c = zero
    for t in range(n):
        c3[t] = c
        c = edge(t, 2) + k2 * c1[t] + k1 * c2[t] + span * c
    c = zero
    for t in reversed(range(n)):
        c4[t] = c
        c = edge(t, 3) + k3 * c1[t] + k2 * c2[t] + k1 * c3[t] + span * c
    return c1, c2, c3, c4


def cascade(count, load, store, decay, start):
    step = 24
    edges = []
    for stage in range(4):
        back = stage % 2 == 1

        def body(b, states, back=back):
            base = (count // step - 1 - b) * step if back else b * step
            order = range(step - 1, -1, -1) if back else range(step)
            for o in order:
                new = [decay_k * s + x for decay_k, s, x in zip(decay, states, load(base + o))]
                store(base + o, new)
                states = new
            return tuple(states)

        states = lax.fori_loop(0, count // step, body, tuple(start))
        edges.append(list(states))
    return edges


def stage_sigma(sigma, sg, variables):
    lon = sigma.shape[2]
    for v in variables:
        for at in range(0, lon, LANES):
            width = min(LANES, lon - at)
            sg[v, at // LANES, :, 0:width] = sigma[v, :, at : at + width]


def sigma_tile(sg, v, m, high):
    idx = 2 * (m & 63) + high
    return jnp.take_along_axis(sg[v, m >> 6], idx, axis=1, mode="promise_in_bounds")


def set_weights(weights, k, mat, mixed):
    hi, lo = expand(mat, mixed)
    weights[768 * k : 768 * k + 256] = hi
    weights[768 * k + 256 : 768 * k + 512] = hi
    weights[768 * k + 512 : 768 * k + 768] = lo


def weight(weights, k):
    return weights[768 * k : 768 * (k + 1)]


def store_start(w_ref, w_hbm, first, sem):
    nv, count = w_ref.shape[:2]
    at = pl.ds(pl.multiple_of(pl.program_id(0) * count, 8), count)
    copy = pltpu.make_async_copy(w_ref, w_hbm.at[first : first + nv, at], sem)
    copy.start()
    return copy


def lat_filter(vs, rows, prm, u_ref, e_ref, p_ref):
    nv = len(vs)
    decay = [prm[v, 1:2, :] for v in vs]

    def load(i):
        return [u_ref[k, i] for k in range(nv)]

    def store(i, values):
        for k in range(nv):
            u_ref[k, i] = values[k]

    zero = jnp.zeros((u_ref.shape[2], LANES), f32)
    edges = cascade(rows, load, store, decay, [zero] * nv)
    for k in range(nv):
        for j in range(0, u_ref.shape[2], 8):
            block = [edges[3 - e][k][j : j + 8] * decay[k] for e in range(4)]
            block = jnp.stack(block + [jnp.zeros((8, LANES), f32)] * 4)
            p_ref[k, j : j + 8] = jnp.swapaxes(block, 0, 1)
    width = e_ref.shape[2] // 4
    for e in range(4):
        for k in range(nv):
            for c in range(e_ref.shape[0]):
                e_ref[c, k, e * width : (e + 1) * width] = edges[e][k][c * width : (c + 1) * width]


def put_mixed(k, b, rows, res, w_ref, u_ref):
    base = b * 2 * PAIRS
    for p in range(PAIRS):
        part = res[p * rows : (p + 1) * rows]
        w_ref[k, base + 2 * p] = part[:, :LANES]
        w_ref[k, base + 2 * p + 1] = part[:, LANES:]
    at = pl.ds(pl.multiple_of(base, 2 * PAIRS), 2 * PAIRS)
    u_ref[k, :, at, :] = jnp.swapaxes(w_ref[k, at], 0, 1)


def set_params(scales, classes, chi_coef, prm):
    coef = jnp.concatenate([chi_coef[...], chi_coef[...]], axis=1)
    for v in range(3):
        kind = classes[:, 64 * v : 64 * (v + 1)]
        kind = jnp.concatenate([kind, kind], axis=1)
        length = jnp.zeros((1, LANES), f32)
        for n in range(scales.shape[1]):
            length = jnp.where(kind == n, scales[:, n : n + 1], length)
        decay = jnp.exp(-1.0 / length)
        norm = 1.0 - decay
        norm = norm * norm
        norm = norm * norm
        prm[v, 0:1, :] = length
        prm[v, 1:2, :] = decay
        prm[v, 2:3, :] = coef
        prm[v, 3:4, :] = length * jnp.sqrt(length) * norm * norm


def lat_plain(
    rows, pairs, scales, classes, chi_coef, sigma, vert, b1lo, b1hi, b2lo, b2hi,
    w_hbm, u_ref, e_ref, p_ref, prm, xs, wt, sg, w_ref, sem,
):
    g = pl.program_id(0)

    @pl.when(g == 0)
    def _():
        set_params(scales, classes, chi_coef, prm)
        set_weights(wt, 0, vert[1], True)
        set_weights(wt, 1, vert[2], True)
        stage_sigma(sigma, sg, (1, 2))

    lane = lax.broadcasted_iota(jnp.int32, (rows, LANES), 1)
    high = (lane >= 64).astype(jnp.int32)

    def body(b, _):
        for p in range(PAIRS):
            at = slice(p * rows, (p + 1) * rows)
            cols = pl.ds(pl.multiple_of((b * PAIRS + p) * LANES, LANES), LANES)
            m = g * BLOCK + b * PAIRS + p
            for k, sides in enumerate(((b1lo, b1hi), (b2lo, b2hi))):
                for side in range(2):
                    s = sigma_tile(sg, k + 1, m + side * pairs, high)
                    xs[k, at, side * LANES : (side + 1) * LANES] = sides[side][0, :, cols] * s
        for k in range(2):
            put_mixed(k, b, rows, product(xs[k], weight(wt, k)), w_ref, u_ref)
        return 0

    lax.fori_loop(0, BLOCK // PAIRS, body, 0)
    copy = store_start(w_ref, w_hbm, 0, sem)
    lat_filter((1, 2), rows, prm, u_ref, e_ref, p_ref)
    copy.wait()


def lat_balance(
    rows, pairs, prm, sigma, vert, bal, plo, phi, clo, chi, temp, north, south, west, east, w_in, u_in, e_in, p_in,
    w_hbm, u_ref, e_ref, p_ref, xs, wt, sg, w_ref, sem,
):
    del w_in, u_in, e_in, p_in
    g = pl.program_id(0)

    @pl.when(g == 0)
    def _():
        set_weights(wt, 0, vert[0], True)
        (bh, bl), (vh, vl) = halves(bal[...]), halves(vert[0])
        set_weights(wt, 1, dot(bh, vh) + dot(bl, vh) + dot(bh, vl), True)
        stage_sigma(sigma, sg, (0,))

    lane = lax.broadcasted_iota(jnp.int32, (rows, LANES), 1)
    row_id = lax.broadcasted_iota(jnp.int32, (rows, LANES), 0)
    high = (lane >= 64).astype(jnp.int32)
    chi_row = prm[0, 2:3, :]
    last = 2 * pairs - 1
    beyond = [jnp.concatenate([x[...], x[...]], axis=1) for x in (west, east)]

    def at_tile(m):
        return pl.ds(pl.multiple_of(m * LANES, LANES), LANES)

    def laplace(m):
        x = temp[0, :, at_tile(m)]
        left = jnp.where(m == 0, beyond[0], temp[0, :, at_tile(jnp.maximum(m - 1, 0))])
        right = jnp.where(m == last, beyond[1], temp[0, :, at_tile(jnp.minimum(m + 1, last))])
        beside = swap(x + jnp.where(lane >= 64, left, right))
        above = jnp.where(row_id == 0, north[:, at_tile(m)], pltpu.roll(x, 1, 0))
        below = jnp.where(row_id == rows - 1, south[:, at_tile(m)], pltpu.roll(x, rows - 1, 0))
        return 4.0 * x - beside - above - below

    def body(b, _):
        for p in range(PAIRS):
            at = slice(p * rows, (p + 1) * rows)
            cols = at_tile(b * PAIRS + p)
            m = g * BLOCK + b * PAIRS + p
            for side, (pr, cr) in enumerate(((plo, clo), (phi, chi))):
                s = sigma_tile(sg, 0, m + side * pairs, high)
                to = slice(side * LANES, (side + 1) * LANES)
                xs[0, at, to] = (pr[0, :, cols] + chi_row * cr[0, :, cols]) * s
                xs[1, at, to] = laplace(m + side * pairs) * s
        res = dot(jnp.concatenate([split(xs[0]), split(xs[1])], axis=1), wt[...])
        put_mixed(0, b, rows, res, w_ref, u_ref)
        return 0

    lax.fori_loop(0, BLOCK // PAIRS, body, 0)
    copy = store_start(w_ref, w_hbm, 2, sem)
    lat_filter((0,), rows, prm, u_ref, e_ref, p_ref)
    copy.wait()


def lon_filter(prm, rb, o_ref, el_ref, put, at):
    half = o_ref.shape[1]
    nv = len(ORDER)
    decay = [prm[v, 1:2, :] for v in ORDER]

    def load(j):
        return [o_ref[k, j] for k in range(nv)]

    def store(j, values):
        for k in range(nv):
            o_ref[k, j] = values[k]

    edges = cascade(half, load, store, decay, [jnp.zeros((rb, LANES), f32)] * nv)
    low = low_lanes((rb, LANES))
    for k, v in enumerate(ORDER):
        span, k1, k2, k3 = constants(prm[v, 0:1, :], prm[v, 1:2, :], half)
        e1, e2, e3, e4 = (edges[e][k] for e in range(4))
        c1 = jnp.where(low, 0.0, swap(e1))
        t1 = e1 + span * c1
        t2 = e2 + k1 * c1
        c2 = jnp.where(low, swap(t2), 0.0)
        t2 = t2 + span * c2
        t3 = e3 + k2 * c1 + k1 * c2
        c3 = jnp.where(low, 0.0, swap(t3))
        t3 = t3 + span * c3
        t4 = e4 + k3 * c1 + k2 * c2 + k1 * c3
        c4 = jnp.where(low, swap(t4), 0.0)
        t4 = t4 + span * c4
        put(2 * k, jnp.where(low, t2, t1))
        put(2 * k + 1, jnp.where(low, t4, t3))
        for e, x in enumerate((e1, e2, e3, e4)):
            el_ref[k, e, at, :] = x


def lon_kernel(
    rows, rb, prm, sigma, u_ref, w_hbm, o_hbm, el_ref, es_ref, px_ref, dot_ref, rx_ref, ry_ref, w_ref, o_ref, sems
):
    g = pl.program_id(0)
    half = u_ref.shape[2]
    at = pl.ds(pl.multiple_of(g * rb, 8), rb)
    load_w = pltpu.make_async_copy(w_hbm.at[:, :, at, :], w_ref, sems.at[0])
    load_w.start()

    @pl.when(g == 0)
    def _():
        x = sigma[0]
        lon = x.shape[1]
        es_ref[6] = jnp.where(low_lanes((x.shape[0], LANES)), x[:, 0:1], x[:, lon - 1 : lon])
        dot_ref[...] = jnp.zeros_like(dot_ref)
        for k, v in enumerate(ORDER):
            for e, r in enumerate(responses(prm[v, 0:1, :], prm[v, 1:2, :], half)):
                rx_ref[k, e] = r
            for e, r in enumerate(responses(prm[v, 0:1, :], prm[v, 1:2, :], rows)):
                ry_ref[k, e] = r

    def turn(b, _):
        at = pl.ds(pl.multiple_of(b * 8, 8), 8)
        for k in range(len(ORDER)):
            for q in range(0, rb, 8):
                o_ref[k, at, q : q + 8, :] = jnp.swapaxes(u_ref[k, q : q + 8, at, :], 0, 1)
        return 0

    lax.fori_loop(0, half // 8, turn, 0)

    def put(i, x):
        es_ref[i, at, :] = x

    lon_filter(prm, rb, o_ref, el_ref, put, at)
    store_o = pltpu.make_async_copy(o_ref, o_hbm.at[:, :, at, :], sems.at[1])
    store_o.start()
    load_w.wait()
    zero = jnp.zeros((rb, LANES), f32)
    for k in range(len(ORDER)):

        def body(b, sums, k=k):
            base = pl.multiple_of(b * 8, 8)
            rx = [rx_ref[k, e, pl.ds(base, 8), :] for e in range(4)]
            sums = list(sums)
            for o in range(8):
                x = w_ref[k, base + o]
                sums[4] = sums[4] + x * o_ref[k, base + o]
                for e in range(4):
                    sums[e] = sums[e] + x * rx[e][o : o + 1, :]
            return tuple(sums)

        sums = lax.fori_loop(0, half // 8, body, (zero,) * 5)
        for e in range(4):
            px_ref[k, e, at, :] = sums[e]
        dot_ref[k] += jnp.sum(sums[4].reshape(rb // 8, 8, LANES), axis=0)
    store_o.wait()


def solve_kernel(n_lat, rows, prm, edges, carries):
    width = edges.shape[2] // 4
    for k, v in enumerate(ORDER):
        const = constants(prm[v, 0:1, :], prm[v, 1:2, :], rows)
        c = solve_carries(n_lat, lambda t, e: edges[t, k, e * width : (e + 1) * width, :], const)
        for e in range(4):
            for t in range(n_lat):
                carries[t, k, e * width : (e + 1) * width, :] = c[e][t]


def carry_kernel(prm, carries, o_ref, el_ref, es_ref):
    width = carries.shape[2] // 4
    zero = jnp.zeros((8, LANES), f32)

    def body(d, _):
        for k in range(len(ORDER)):
            for j in range(width):
                at = d * width + j
                o_ref[k, at] = zero
                for e in range(4):
                    o_ref[k, at, e : e + 1, :] = carries[d, k, e * width + j : e * width + j + 1, :]
        return 0

    lax.fori_loop(0, carries.shape[0], body, 0)

    def put(i, x):
        es_ref[i] = x

    lon_filter(prm, 8, o_ref, el_ref, put, slice(0, 8))


def close_kernel(
    n_lon, rows, devices, capacity, cells, place, target, prm, x_ref, proj, px, dots, rx, ry, el, elc, *rest
):
    sent, sent_x = rest[:n_lon], rest[n_lon : 2 * n_lon]
    carry, full_ref, col_ref, side_ref, table, esm, esx = rest[2 * n_lon :]
    half = rx.shape[2]
    me = place[1]
    for d in range(n_lon):
        esm[me ^ d] = sent[d][...]
        esx[me ^ d] = sent_x[d][...]
    side_ref[0] = esm[jnp.maximum(me - 1, 0), 6]
    side_ref[1] = esm[jnp.minimum(me + 1, n_lon - 1), 6]
    length = jnp.stack([prm[v, 0:1, :] for v in ORDER])
    decay = jnp.stack([prm[v, 1:2, :] for v in ORDER])
    whole = constants(length, decay, 2 * half)
    span, k1, k2, k3 = constants(length, decay, half)
    low = low_lanes((len(ORDER), rows + 8, LANES))
    cache = {}

    def both(main, more):
        parts = [jnp.concatenate([main(k), more(k)], axis=0) for k in range(len(ORDER))]
        return jnp.stack(parts)

    def edge(t, e):
        i = e // 2
        if (t, i) not in cache:
            x = both(lambda k: esm[t, 2 * k + i], lambda k: esx[t, 2 * k + i])
            y = swap(x)
            cache[t, i] = (jnp.where(low, y, x), jnp.where(low, x, y))
        return cache[t, i][e % 2]

    d1, d2, d3, d4 = pick(solve_carries(n_lon, edge, whole), me)
    e1, e2, e3, e4 = (both(lambda k, e=e: el[k, e], lambda k, e=e: elc[k, e]) for e in range(4))
    c1 = jnp.where(low, d1, swap(e1 + span * d1))
    c2 = jnp.where(low, swap(e2 + k1 * c1 + span * d2), d2)
    c3 = jnp.where(low, d3, swap(e3 + k2 * c1 + k1 * c2 + span * d3))
    c4 = jnp.where(low, swap(e4 + k3 * c1 + k2 * c2 + k1 * c3 + span * d4), d4)
    lane = lax.broadcasted_iota(jnp.int32, (devices, LANES), 1)
    first_slot = lax.broadcasted_iota(jnp.int32, (devices, LANES), 0) * capacity
    owned = jnp.zeros((devices, LANES), f32)
    for k, v in enumerate(ORDER):
        more = [c[k, rows:] for c in (c1, c2, c3, c4)]
        sums = jnp.zeros((rows, LANES), f32)
        for e, c in enumerate((c1, c2, c3, c4)):
            carry[k, e] = c[k, :rows]
            sums = sums + c[k, :rows] * px[k, e]

        def body(b, total, k=k, more=more):
            base = pl.multiple_of(b * 8, 8)
            r = [rx[k, e, pl.ds(base, 8), :] for e in range(4)]
            for o in range(8):
                x = x_ref[k, base + o]
                for e in range(4):
                    x = x + r[e][o : o + 1, :] * more[e]
                full_ref[k, base + o] = x
                total = total + x * proj[k, base + o]
            return total

        total = lax.fori_loop(0, half // 8, body, dots[k])
        total = total + jnp.sum(sums.reshape(rows // 8, 8, LANES), axis=0)
        total = jnp.sum(total, axis=0, keepdims=True)
        total = (total + swap(total)) * prm[v, 3:4, :] * (1.0 / cells)
        where = target[:, 64 * v : 64 * (v + 1)]
        where = jnp.concatenate([where, where], axis=1) - first_slot
        for s in range(capacity):
            mine = jnp.where((lane < 64) & (where == s), total, 0.0)
            owned = owned + jnp.where(lane == s, jnp.sum(mine, axis=1, keepdims=True), 0.0)
        if v == 0:
            for i, d in enumerate((d3, d4)):
                y = d[k, :rows]
                for e in range(4):
                    y = y + ry[k, e] * d[k, rows + e : rows + e + 1]
                col_ref[i] = y
    table[...] = owned


def end_kernel(
    rows, pairs, rq, place, prm, sigma, north, south, vert, bal, col, side, carry, rx_ref, ry_ref, u_ref, x_ref,
    out_ref, out, xs, zx, zc, wt, sg, sx, sems,
):
    g = pl.program_id(0)
    half = 2 * pairs
    lon = sigma.shape[2]
    merged = out.shape[2]
    steps = pairs // PAIRS

    def copy(v, side_at, step):
        first = pl.multiple_of((step * PAIRS + side_at * pairs) * LANES, LANES)
        cols = pl.ds(first, PAIRS * LANES)
        return pltpu.make_async_copy(out.at[v, :, cols], out_ref.at[v, :, cols], sems.at[v, side_at, step])

    @pl.when(g == 0)
    def _():
        for v in range(3):
            scaled = quad(vert[v]) * prm[v, 3:4, :]
            set_weights(wt, v, scaled.T, True)
        set_weights(wt, 3, quad(bal[...]).T, False)
        stage_sigma(sigma, sg, (0, 1, 2))
        for at in range(0, lon, LANES):
            width = min(LANES, lon - at)
            sx[at // LANES, 0:1, 0:width] = north[:, merged + at : merged + at + width]
            sx[at // LANES, 1:2, 0:width] = south[:, merged + at : merged + at + width]

    lane = lax.broadcasted_iota(jnp.int32, (rows, LANES), 1)
    high = (lane >= 64).astype(jnp.int32)
    high8 = high[0:8]
    chi_row = prm[0, 2:3, :]

    def at_tile(m):
        return pl.ds(pl.multiple_of(m * LANES, LANES), LANES)

    row8 = lax.broadcasted_iota(jnp.int32, (8, LANES), 0)
    beyond = [None] * (2 * PAIRS)
    for k, v in enumerate(ORDER):
        for q in range(0, rows, rq):
            c = [carry[k, e, q : q + rq, :] for e in range(4)]
            ry = [ry_ref[k, e, q : q + rq, :] for e in range(4)]
            rx = [rx_ref[k, e, pl.ds(pl.multiple_of(g * 2 * PAIRS, 8), 2 * PAIRS), :] for e in range(4)]
            for p in range(2 * PAIRS):
                x = x_ref[k, p]
                y = u_ref[k, p, q : q + rq, :]
                for e in range(4):
                    y = y + rx[e][p : p + 1, :] * c[e] + ry[e] * x[e : e + 1, :]
                at = (p // 2) * rows + q
                xs[k, at : at + rq, (p % 2) * LANES : (p % 2 + 1) * LANES] = y
                if v == 0 and q == 0:
                    x = pltpu.roll(x, 6, 0)
                    above = jnp.where(place[0] > 0, x + prm[0, 1:2, :] * y[0:1, :], 0.0)
                    beyond[p] = jnp.where(row8 == 0, above, jnp.where(row8 == 1, x, 0.0))

    @pl.when(g == 0)
    def _():
        first = col[0] + prm[0, 1:2, :] * xs[ORDER.index(0), 0:rows, 0:LANES]
        lhs = jnp.where(lane < 64, jnp.where(place[1] > 0, first, 0.0), col[1])
        lhs = jnp.concatenate([lhs, jnp.zeros_like(lhs)], axis=1)
        res = product(lhs, weight(wt, 0))
        zc[0] = swap(res[:, :LANES] * swap(side[0]))
        zc[1] = res[:, LANES:] * side[1]

    lhs = jnp.concatenate(
        [jnp.concatenate(beyond[2 * p : 2 * p + 2], axis=1) for p in range(PAIRS)], axis=0
    )
    res = product(lhs, weight(wt, 0))
    for p in range(PAIRS):
        m = g * PAIRS + p
        for side in range(2):
            tile = m + side * pairs
            s = jnp.take_along_axis(sx[tile >> 6], 2 * (tile & 63) + high8, axis=1, mode="promise_in_bounds")
            part = res[p * 8 : (p + 1) * 8, side * LANES : (side + 1) * LANES]
            zx[:, at_tile(tile)] = jnp.where(row8 < 2, part * s, 0.0)
    results = {v: product(xs[k], weight(wt, v)) for k, v in enumerate(ORDER)}
    for p in range(PAIRS):
        m = g * PAIRS + p
        for side in range(2):
            at = at_tile(m + side * pairs)
            z = [
                results[v][p * rows : (p + 1) * rows, side * LANES : (side + 1) * LANES]
                * sigma_tile(sg, v, m + side * pairs, high)
                for v in range(3)
            ]
            out[0, :, at] = z[0]
            out[1, :, at] = z[1] + chi_row * z[0]
            out[2, :, at] = z[2]
    for v in range(2):
        for side_at in range(2):
            copy(v, side_at, g).start()

    @pl.when(g == pl.num_programs(0) - 1)
    def _():
        row_id = lax.broadcasted_iota(jnp.int32, (rows, LANES), 0)
        last = half - 1

        def body(b, _):
            for p in range(PAIRS):
                for side in range(2):
                    m = b * PAIRS + p + side * pairs
                    x = out[0, :, at_tile(m)]
                    left = jnp.where(m == 0, zc[0], out[0, :, at_tile(jnp.maximum(m - 1, 0))])
                    right = jnp.where(m == last, zc[1], out[0, :, at_tile(jnp.minimum(m + 1, last))])
                    beside = swap(x + jnp.where(lane >= 64, left, right))
                    above = jnp.where(row_id == 0, zx[0:1, at_tile(m)], pltpu.roll(x, 1, 0))
                    below = jnp.where(row_id == rows - 1, zx[1:2, at_tile(m)], pltpu.roll(x, rows - 1, 0))
                    lap = 4.0 * x - beside - above - below
                    xs[0, p * rows : (p + 1) * rows, side * LANES : (side + 1) * LANES] = lap
            res = product(xs[0], weight(wt, 3))
            for p in range(PAIRS):
                for side in range(2):
                    at = at_tile(b * PAIRS + p + side * pairs)
                    part = res[p * rows : (p + 1) * rows, side * LANES : (side + 1) * LANES]
                    out[2, :, at] = out[2, :, at] + part
            for side_at in range(2):
                copy(2, side_at, b).start()
            return 0

        lax.fori_loop(0, steps, body, 0)
        for v in range(3):
            for side_at in range(2):
                for step in range(steps):
                    copy(v, side_at, step).wait()


def shards(state, sigma, vert, bal_temp, chi_coef, scales, classes, owner):
    n_lat = lax.axis_size("lat")
    n_lon = lax.axis_size("lon")
    devices = n_lat * n_lon
    nvars, rows, merged = state.shape
    levels = vert.shape[1]
    lon = merged // levels
    half = lon // 2
    pairs = half // 2
    pieces = (lon + LANES - 1) // LANES
    count = nvars * levels
    capacity = (count + devices - 1) // devices + 1
    i_lat = lax.axis_index("lat")
    i_lon = lax.axis_index("lon")

    up_lat, up_lon = ([(i, i + 1) for i in range(n - 1)] for n in (n_lat, n_lon))
    down_lat, down_lon = ([(j, i) for i, j in up] for up in (up_lat, up_lon))

    def row(i):
        return jnp.concatenate([state[2, i : i + 1, :], sigma[0, i : i + 1, :]], axis=1)

    north = lax.ppermute(row(rows - 1), "lat", up_lat)
    south = lax.ppermute(row(0), "lat", down_lat)
    west = lax.ppermute(state[2, :, merged - levels :], "lon", up_lon)
    east = lax.ppermute(state[2, :, :levels], "lon", down_lon)
    place = jnp.stack([i_lat, i_lon]).astype(jnp.int32)

    anywhere = pl.BlockSpec(memory_space=pl.ANY)
    steps = pairs // BLOCK

    def part(v, side):
        return pl.BlockSpec((1, rows, BLOCK * LANES), lambda g: (v, 0, g + side * steps))

    width = half // n_lat
    shapes = [(nvars, half, rows, LANES), (nvars, rows, half, LANES), (n_lat, nvars, 4 * width, LANES)]
    shapes.append((nvars, half, 8, LANES))

    def lat_call(nv, first, body, arrays, specs, name, aliases, more=()):
        return pl.pallas_call(
            body,
            grid=(steps,),
            in_specs=specs,
            out_specs=[
                anywhere,
                pl.BlockSpec((nv, rows, 2 * BLOCK, LANES), lambda g: (first, 0, g, 0)),
                pl.BlockSpec((2 * BLOCK // width, nv, 4 * width, LANES), lambda g: (g, first, 0, 0)),
                pl.BlockSpec((nv, 2 * BLOCK, 8, LANES), lambda g: (first, g, 0, 0)),
            ]
            + [full(s) for s in more],
            out_shape=[jax.ShapeDtypeStruct(s, f32) if n == 2 else pltpu.HBM(s, f32) for n, s in enumerate(shapes)]
            + [jax.ShapeDtypeStruct(s, f32) for s in more],
            scratch_shapes=[
                pltpu.VMEM((2, PAIRS * rows, 256), f32),
                pltpu.VMEM((2 * 768, 256), bf16),
                pltpu.VMEM((nvars, pieces, rows, LANES), f32),
                pltpu.VMEM((nv, 2 * BLOCK, rows, LANES), f32),
                pltpu.SemaphoreType.DMA(()),
            ],
            compiler_params=params(),
            cost_estimate=pl.CostEstimate(
                flops=nv * 60000000, bytes_accessed=nv * 3 * rows * merged * 4, transcendentals=0
            ),
            input_output_aliases=aliases,
            name=name,
        )(*arrays)

    ins = [scales.reshape(1, -1), classes.reshape(1, count), chi_coef.reshape(1, levels), sigma, vert] + [state] * 4
    specs = [full(x.shape) for x in ins[:5]] + [part(1, 0), part(1, 1), part(2, 0), part(2, 1)]
    ins = [in_hbm(x) for x in ins]
    body = functools.partial(lat_plain, rows, pairs)
    *wue, prm = lat_call(2, 0, body, ins, specs, "lat_chi_temp", {}, [(nvars, 4, LANES)])
    ins = [prm] + [in_hbm(x) for x in [sigma, vert, bal_temp] + [state] * 5] + [north, south, west, east]
    ins += [in_hbm(wue[0]), in_hbm(wue[1]), wue[2], in_hbm(wue[3])]
    specs = [full(x.shape) for x in ins[:4]] + [part(0, 0), part(0, 1), part(1, 0), part(1, 1)]
    specs += [pl.BlockSpec((1, rows, merged), lambda g: (2, 0, 0))]
    specs += [full(x.shape) for x in (north, south, west, east)] + [anywhere] * 4
    aliases = {13: 0, 14: 1, 15: 2, 16: 3}
    w, u, edges, proj = lat_call(1, 2, functools.partial(lat_balance, rows, pairs), ins, specs, "lat_psi", aliases)
    def trade(x, axis):
        return lax.all_to_all(x, axis, split_axis=0, concat_axis=0, tiled=True)

    shares = trade(edges, "lat")

    rb = BLOCK
    local, el, es, px, dots, rx, ry = pl.pallas_call(
        functools.partial(lon_kernel, rows, rb),
        grid=(rows // rb,),
        in_specs=[
            full(prm.shape),
            pl.BlockSpec((1, rows, lon), lambda g: (0, 0, 0)),
            pl.BlockSpec((nvars, rb, half, LANES), lambda g: (0, g, 0, 0)),
            anywhere,
        ],
        out_specs=[
            anywhere,
            full((nvars, 4, rows, LANES)),
            full((7, rows, LANES)),
            full((nvars, 4, rows, LANES)),
            full((nvars, 8, LANES)),
            full((nvars, 4, half, LANES)),
            full((nvars, 4, rows, LANES)),
        ],
        out_shape=[
            pltpu.HBM((nvars, half, rows, LANES), f32),
            pltpu.HBM((nvars, 4, rows, LANES), f32),
            jax.ShapeDtypeStruct((7, rows, LANES), f32),
            pltpu.HBM((nvars, 4, rows, LANES), f32),
            pltpu.HBM((nvars, 8, LANES), f32),
            pltpu.HBM((nvars, 4, half, LANES), f32),
            pltpu.HBM((nvars, 4, rows, LANES), f32),
        ],
        scratch_shapes=[pltpu.VMEM((nvars, half, rb, LANES), f32)] * 2 + [pltpu.SemaphoreType.DMA((2,))],
        compiler_params=params(),
        cost_estimate=pl.CostEstimate(
            flops=180000000, bytes_accessed=6 * rows * merged * 4, transcendentals=0
        ),
        name="lon_tile",
    )(prm, *[in_hbm(x) for x in (sigma, u, w)])

    def round_lon(x):
        return [x] + [
            lax.ppermute(x, "lon", [(i, i ^ s) for i in range(n_lon)]) for s in range(1, n_lon)
        ]

    shares, _ = lax.optimization_barrier((shares, es))
    sent = round_lon(es)
    carries = pl.pallas_call(
        functools.partial(solve_kernel, n_lat, rows),
        grid=(1,),
        in_specs=[full(prm.shape), full(shares.shape)],
        out_specs=full(shares.shape),
        out_shape=jax.ShapeDtypeStruct(shares.shape, f32),
        compiler_params=params(),
        cost_estimate=pl.CostEstimate(flops=1000000, bytes_accessed=2 * shares.size * 4, transcendentals=0),
        name="solve",
    )(prm, shares)
    carries = trade(carries, "lat")

    crossed, elc, esc = pl.pallas_call(
        carry_kernel,
        grid=(1,),
        in_specs=[full(prm.shape), full(carries.shape)],
        out_specs=[full((nvars, half, 8, LANES)), full((nvars, 4, 8, LANES)), full((6, 8, LANES))],
        out_shape=[
            jax.ShapeDtypeStruct((nvars, half, 8, LANES), f32),
            jax.ShapeDtypeStruct((nvars, 4, 8, LANES), f32),
            jax.ShapeDtypeStruct((6, 8, LANES), f32),
        ],
        compiler_params=params(),
        cost_estimate=pl.CostEstimate(
            flops=30000000, bytes_accessed=4 * nvars * 12 * half * LANES, transcendentals=0
        ),
        name="lon_carry",
    )(prm, carries)
    sent_x = round_lon(esc)

    packed = 2 * PAIRS

    def columns(r):
        return pl.BlockSpec((nvars, packed, r, LANES), lambda g: (0, g, 0, 0))

    index = jnp.arange(count, dtype=jnp.int32)
    same = (owner[:, None] == owner[None, :]) & (index[None, :] < index[:, None])
    target = (owner * capacity + jnp.sum(same.astype(jnp.int32), axis=1)).reshape(1, count)

    ins = [in_hbm(x) for x in (proj, px, dots, rx, ry, el)]
    ins = [place, target, prm, crossed] + ins + [elc] + sent + sent_x
    specs = [full(x.shape) for x in ins]
    specs[0] = pl.BlockSpec(memory_space=pltpu.SMEM)
    shapes = [(nvars, 4, rows, LANES), (nvars, half, 8, LANES), (2, rows, LANES), (2, rows, LANES)]
    carry, crossed, col, side, table = pl.pallas_call(
        functools.partial(close_kernel, n_lon, rows, devices, capacity, devices * rows * lon),
        grid=(1,),
        in_specs=specs,
        out_specs=[full(x) for x in shapes] + [full((devices, LANES))],
        out_shape=[pltpu.HBM(x, f32) for x in shapes] + [jax.ShapeDtypeStruct((devices, LANES), f32)],
        scratch_shapes=[pltpu.VMEM((n_lon, 7, rows, LANES), f32), pltpu.VMEM((n_lon, 6, 8, LANES), f32)],
        compiler_params=params(),
        cost_estimate=pl.CostEstimate(flops=10000000, bytes_accessed=4000000, transcendentals=0),
        name="close",
    )(*ins)
    table = trade(table, ("lat", "lon"))
    slab_energy = jnp.sum(table, axis=0, keepdims=True)[:, :capacity]

    ins = [prm, sigma, north, south, vert, bal_temp, col, side, carry, rx, ry, local, crossed]
    ins = [place] + [in_hbm(x) for x in ins]
    specs = [full(x.shape) for x in ins]
    specs[0] = pl.BlockSpec(memory_space=pltpu.SMEM)
    specs[-2:] = [columns(rows), columns(8)]
    applied = pl.pallas_call(
        functools.partial(end_kernel, rows, pairs, 24),
        grid=(half // packed,),
        in_specs=specs,
        out_specs=anywhere,
        out_shape=jax.ShapeDtypeStruct(state.shape, f32),
        scratch_shapes=[
            pltpu.VMEM(state.shape, f32),
            pltpu.VMEM((nvars, PAIRS * rows, 256), f32),
            pltpu.VMEM((8, merged), f32),
            pltpu.VMEM((2, rows, LANES), f32),
            pltpu.VMEM((4 * 768, 256), bf16),
            pltpu.VMEM((nvars, pieces, rows, LANES), f32),
            pltpu.VMEM((pieces, 8, LANES), f32),
            pltpu.SemaphoreType.DMA((3, 2, pairs // PAIRS)),
        ],
        compiler_params=params(),
        cost_estimate=pl.CostEstimate(
            flops=300000000, bytes_accessed=6 * rows * merged * 4, transcendentals=0
        ),
        name="finish",
    )(*ins)
    return (applied, slab_energy)


def solution(mesh):
    return jax.shard_map(
        shards,
        mesh=mesh,
        in_specs=(P(None, "lat", "lon"), P(None, "lat", "lon"), P(), P(), P(), P(), P(), P()),
        out_specs=(P(None, "lat", "lon"), P(("lat", "lon"), None)),
        check_vma=False,
    )
```

```python
import functools

import jax
import jax.numpy as jnp
from jax import lax
from jax.experimental import pallas as pl
from jax.experimental.pallas import tpu as pltpu
from jax.sharding import PartitionSpec as P

highest = lax.Precision.HIGHEST
f32 = jnp.float32
bf16 = jnp.bfloat16
LANES = 128
PAIRS = 8
BLOCK = 24
ORDER = (1, 2, 0)
LIMIT = 30 * 1024 * 1024


def params():
    return pltpu.CompilerParams(vmem_limit_bytes=LIMIT)


def in_hbm(x):
    return pltpu.with_memory_space_constraint(x, pltpu.HBM)


def full(shape):
    return pl.BlockSpec(shape, lambda g: (0,) * len(shape))


def swap(x):
    return pltpu.roll(x, 64, x.ndim - 1)


def low_lanes(shape):
    return lax.broadcasted_iota(jnp.int32, shape, len(shape) - 1) < 64


def halves(x):
    hi = x.astype(bf16)
    return hi, (x - hi.astype(f32)).astype(bf16)


def dot(x, y):
    return jnp.dot(x, y, preferred_element_type=f32)


def split(x):
    hi, lo = halves(x)
    return jnp.concatenate([hi, lo, hi], axis=1)


def product(x, weights):
    return dot(split(x), weights)


def expand(mat, mixed):
    wide = quad(mat)
    wide = jnp.concatenate([wide, wide], axis=1)
    wide = jnp.concatenate([wide, wide], axis=0)
    src = lax.broadcasted_iota(jnp.int32, (256, 256), 0) // 64
    dst = lax.broadcasted_iota(jnp.int32, (256, 256), 1) // 64
    if mixed:
        src = jnp.where(src == 1, 2, jnp.where(src == 2, 1, src))
    return halves(jnp.where(src == dst, wide, 0.0))


def quad(mat):
    if mat.shape[0] == LANES:
        return mat
    wide = jnp.concatenate([mat, mat], axis=1)
    return jnp.concatenate([wide, wide], axis=0)


def constants(length, decay, m):
    span = jnp.exp(-float(m) / length)
    d = 1.0 - decay * decay
    k1 = decay * (1.0 - span * span) / d
    k2 = (m * span - decay * decay * (span - span * span * span) / d) / d
    tail = decay * decay * (1.0 + span * span) * (1.0 - span * span) / d
    k3 = decay / (d * d) * (1.0 - (2.0 * m + 1.0) * span * span + tail)
    return span, k1, k2, k3


def responses(length, decay, m):
    j = lax.broadcasted_iota(jnp.int32, (m, LANES), 0).astype(f32)
    up = jnp.exp(-j / length)
    down = jnp.exp(-(m - j) / length)
    span = jnp.exp(-float(m) / length)
    d = 1.0 - decay * decay
    diff = up - span * down
    g3 = decay * diff / d
    g2 = ((m - j) * down - decay * decay * (span * up - span * span * down) / d) / d
    part = decay * decay * (1.0 + span * span) * diff / d
    g1 = decay / (d * d) * ((j + 1.0) * up - (2.0 * m + 1.0 - j) * span * down + part)
    return g1, g2, g3, down


def pick(all_carries, me):
    out = []
    for cs in all_carries:
        mine = cs[0]
        for t in range(1, len(cs)):
            mine = jnp.where(me == t, cs[t], mine)
        out.append(mine)
    return out


def solve_carries(n, edge, const):
    span, k1, k2, k3 = const
    first = edge(0, 0)
    zero = jnp.zeros_like(first)
    e1 = [first] + [edge(t, 0) for t in range(1, n)]
    c1, c2, c3, c4 = ([None] * n for _ in range(4))
    c = zero
    for t in range(n):
        c1[t] = c
        c = e1[t] + span * c
    c = zero
    for t in reversed(range(n)):
        c2[t] = c
        c = edge(t, 1) + k1 * c1[t] + span * c
    c = zero
    for t in range(n):
        c3[t] = c
        c = edge(t, 2) + k2 * c1[t] + k1 * c2[t] + span * c
    c = zero
    for t in reversed(range(n)):
        c4[t] = c
        c = edge(t, 3) + k3 * c1[t] + k2 * c2[t] + k1 * c3[t] + span * c
    return c1, c2, c3, c4


def cascade(count, load, store, decay, start):
    step = 24
    edges = []
    for stage in range(4):
        back = stage % 2 == 1

        def body(b, states, back=back):
            base = (count // step - 1 - b) * step if back else b * step
            order = range(step - 1, -1, -1) if back else range(step)
            for o in order:
                new = [decay_k * s + x for decay_k, s, x in zip(decay, states, load(base + o))]
                store(base + o, new)
                states = new
            return tuple(states)

        states = lax.fori_loop(0, count // step, body, tuple(start))
        edges.append(list(states))
    return edges


def stage_sigma(sigma, sg, variables):
    lon = sigma.shape[2]
    for v in variables:
        for at in range(0, lon, LANES):
            width = min(LANES, lon - at)
            sg[v, at // LANES, :, 0:width] = sigma[v, :, at : at + width]


def sigma_tile(sg, v, m, high):
    idx = 2 * (m & 63) + high
    return jnp.take_along_axis(sg[v, m >> 6], idx, axis=1, mode="promise_in_bounds")


def set_weights(weights, k, mat, mixed):
    hi, lo = expand(mat, mixed)
    weights[768 * k : 768 * k + 256] = hi
    weights[768 * k + 256 : 768 * k + 512] = hi
    weights[768 * k + 512 : 768 * k + 768] = lo


def weight(weights, k):
    return weights[768 * k : 768 * (k + 1)]


def lat_filter(vs, rows, prm, u_ref, e_ref, p_ref):
    nv = len(vs)
    decay = [prm[v, 1:2, :] for v in vs]

    def load(i):
        return [u_ref[k, i] for k in range(nv)]

    def store(i, values):
        for k in range(nv):
            u_ref[k, i] = values[k]

    zero = jnp.zeros((u_ref.shape[2], LANES), f32)
    edges = cascade(rows, load, store, decay, [zero] * nv)
    for k in range(nv):
        for j in range(0, u_ref.shape[2], 8):
            block = [edges[3 - e][k][j : j + 8] * decay[k] for e in range(4)]
            block = jnp.stack(block + [jnp.zeros((8, LANES), f32)] * 4)
            p_ref[k, j : j + 8] = jnp.swapaxes(block, 0, 1)
    width = e_ref.shape[2] // 4
    for e in range(4):
        for k in range(nv):
            for c in range(e_ref.shape[0]):
                e_ref[c, k, e * width : (e + 1) * width] = edges[e][k][c * width : (c + 1) * width]


def put_mixed(k, b, rows, res, w_ref, u_ref):
    base = b * 2 * PAIRS
    for p in range(PAIRS):
        part = res[p * rows : (p + 1) * rows]
        w_ref[k, base + 2 * p] = part[:, :LANES]
        w_ref[k, base + 2 * p + 1] = part[:, LANES:]
    at = pl.ds(pl.multiple_of(base, 2 * PAIRS), 2 * PAIRS)
    u_ref[k, :, at, :] = jnp.swapaxes(w_ref[k, at], 0, 1)


def set_params(scales, classes, chi_coef, prm):
    coef = jnp.concatenate([chi_coef[...], chi_coef[...]], axis=1)
    for v in range(3):
        kind = classes[:, 64 * v : 64 * (v + 1)]
        kind = jnp.concatenate([kind, kind], axis=1)
        length = jnp.zeros((1, LANES), f32)
        for n in range(scales.shape[1]):
            length = jnp.where(kind == n, scales[:, n : n + 1], length)
        decay = jnp.exp(-1.0 / length)
        norm = 1.0 - decay
        norm = norm * norm
        norm = norm * norm
        prm[v, 0:1, :] = length
        prm[v, 1:2, :] = decay
        prm[v, 2:3, :] = coef
        prm[v, 3:4, :] = length * jnp.sqrt(length) * norm * norm


def lat_plain(
    rows, pairs, scales, classes, chi_coef, sigma, vert, b1lo, b1hi, b2lo, b2hi,
    w_ref, u_ref, e_ref, p_ref, prm, xs, wt, sg,
):
    g = pl.program_id(0)

    @pl.when(g == 0)
    def _():
        set_params(scales, classes, chi_coef, prm)
        set_weights(wt, 0, vert[1], True)
        set_weights(wt, 1, vert[2], True)
        stage_sigma(sigma, sg, (1, 2))

    lane = lax.broadcasted_iota(jnp.int32, (rows, LANES), 1)
    high = (lane >= 64).astype(jnp.int32)

    def body(b, _):
        for p in range(PAIRS):
            at = slice(p * rows, (p + 1) * rows)
            cols = pl.ds(pl.multiple_of((b * PAIRS + p) * LANES, LANES), LANES)
            m = g * BLOCK + b * PAIRS + p
            for k, sides in enumerate(((b1lo, b1hi), (b2lo, b2hi))):
                for side in range(2):
                    s = sigma_tile(sg, k + 1, m + side * pairs, high)
                    xs[k, at, side * LANES : (side + 1) * LANES] = sides[side][0, :, cols] * s
        for k in range(2):
            put_mixed(k, b, rows, product(xs[k], weight(wt, k)), w_ref, u_ref)
        return 0

    lax.fori_loop(0, BLOCK // PAIRS, body, 0)
    lat_filter((1, 2), rows, prm, u_ref, e_ref, p_ref)


def lat_balance(
    rows, pairs, prm, sigma, vert, bal, plo, phi, clo, chi, tlo, thi, tll, tlr, thl, thr, north, south, west, east, w_in, u_in, e_in, p_in,
    w_ref, u_ref, e_ref, p_ref, xs, wt, sg,
):
    del w_in, u_in, e_in, p_in
    g = pl.program_id(0)

    @pl.when(g == 0)
    def _():
        set_weights(wt, 0, vert[0], True)
        (bh, bl), (vh, vl) = halves(bal[...]), halves(vert[0])
        set_weights(wt, 1, dot(bh, vh) + dot(bl, vh) + dot(bh, vl), True)
        stage_sigma(sigma, sg, (0,))

    lane = lax.broadcasted_iota(jnp.int32, (rows, LANES), 1)
    row_id = lax.broadcasted_iota(jnp.int32, (rows, LANES), 0)
    high = (lane >= 64).astype(jnp.int32)
    chi_row = prm[0, 2:3, :]
    last = 2 * pairs - 1
    beyond = [jnp.concatenate([x[...], x[...]], axis=1) for x in (west, east)]

    def at_tile(m):
        return pl.ds(pl.multiple_of(m * LANES, LANES), LANES)

    sides = ((tlo, tll, tlr), (thi, thl, thr))

    def laplace(b, o, side):
        temp, before, after = sides[side]
        p = b * PAIRS + o
        m = g * BLOCK + p + side * pairs
        x = temp[0, :, at_tile(p)]
        left = temp[0, :, at_tile(jnp.maximum(p - 1, 0))]
        if o == 0:
            left = jnp.where(p == 0, before[0], left)
            if side == 0:
                left = jnp.where(m == 0, beyond[0], left)
        right = temp[0, :, at_tile(jnp.minimum(p + 1, BLOCK - 1))]
        if o == PAIRS - 1:
            right = jnp.where(p == BLOCK - 1, after[0], right)
            if side == 1:
                right = jnp.where(m == last, beyond[1], right)
        beside = swap(x + jnp.where(lane >= 64, left, right))
        above = jnp.where(row_id == 0, north[:, at_tile(m)], pltpu.roll(x, 1, 0))
        below = jnp.where(row_id == rows - 1, south[:, at_tile(m)], pltpu.roll(x, rows - 1, 0))
        return 4.0 * x - beside - above - below

    def body(b, _):
        for p in range(PAIRS):
            at = slice(p * rows, (p + 1) * rows)
            cols = at_tile(b * PAIRS + p)
            m = g * BLOCK + b * PAIRS + p
            for side, (pr, cr) in enumerate(((plo, clo), (phi, chi))):
                s = sigma_tile(sg, 0, m + side * pairs, high)
                to = slice(side * LANES, (side + 1) * LANES)
                xs[0, at, to] = (pr[0, :, cols] + chi_row * cr[0, :, cols]) * s
                xs[1, at, to] = laplace(b, p, side) * s
        res = dot(jnp.concatenate([split(xs[0]), split(xs[1])], axis=1), wt[...])
        put_mixed(0, b, rows, res, w_ref, u_ref)
        return 0

    lax.fori_loop(0, BLOCK // PAIRS, body, 0)
    lat_filter((0,), rows, prm, u_ref, e_ref, p_ref)


def lon_filter(prm, rb, o_ref, el_ref, put, at):
    half = o_ref.shape[1]
    nv = len(ORDER)
    decay = [prm[v, 1:2, :] for v in ORDER]

    def load(j):
        return [o_ref[k, j] for k in range(nv)]

    def store(j, values):
        for k in range(nv):
            o_ref[k, j] = values[k]

    edges = cascade(half, load, store, decay, [jnp.zeros((rb, LANES), f32)] * nv)
    low = low_lanes((rb, LANES))
    for k, v in enumerate(ORDER):
        span, k1, k2, k3 = constants(prm[v, 0:1, :], prm[v, 1:2, :], half)
        e1, e2, e3, e4 = (edges[e][k] for e in range(4))
        c1 = jnp.where(low, 0.0, swap(e1))
        t1 = e1 + span * c1
        t2 = e2 + k1 * c1
        c2 = jnp.where(low, swap(t2), 0.0)
        t2 = t2 + span * c2
        t3 = e3 + k2 * c1 + k1 * c2
        c3 = jnp.where(low, 0.0, swap(t3))
        t3 = t3 + span * c3
        t4 = e4 + k3 * c1 + k2 * c2 + k1 * c3
        c4 = jnp.where(low, swap(t4), 0.0)
        t4 = t4 + span * c4
        put(2 * k, jnp.where(low, t2, t1))
        put(2 * k + 1, jnp.where(low, t4, t3))
        for e, x in enumerate((e1, e2, e3, e4)):
            el_ref[k, e, at, :] = x


def lon_kernel(
    rows, rb, prm, u_ref, w_hbm, o_hbm, el_ref, es_ref, px_ref, dot_ref, rx_ref, ry_ref, w_ref, o_ref, sems
):
    g = pl.program_id(0)
    half = u_ref.shape[2]
    at = pl.ds(pl.multiple_of(g * rb, 8), rb)
    load_w = pltpu.make_async_copy(w_hbm.at[:, :, at, :], w_ref, sems.at[0])
    load_w.start()

    @pl.when(g == 0)
    def _():
        dot_ref[...] = jnp.zeros_like(dot_ref)
        for k, v in enumerate(ORDER):
            for e, r in enumerate(responses(prm[v, 0:1, :], prm[v, 1:2, :], half)):
                rx_ref[k, e] = r
            for e, r in enumerate(responses(prm[v, 0:1, :], prm[v, 1:2, :], rows)):
                ry_ref[k, e] = r

    def turn(b, _):
        at = pl.ds(pl.multiple_of(b * 8, 8), 8)
        for k in range(len(ORDER)):
            for q in range(0, rb, 8):
                o_ref[k, at, q : q + 8, :] = jnp.swapaxes(u_ref[k, q : q + 8, at, :], 0, 1)
        return 0

    lax.fori_loop(0, half // 8, turn, 0)

    def put(i, x):
        es_ref[i, at, :] = x

    lon_filter(prm, rb, o_ref, el_ref, put, at)
    store_o = pltpu.make_async_copy(o_ref, o_hbm.at[:, :, at, :], sems.at[1])
    store_o.start()
    load_w.wait()
    zero = jnp.zeros((rb, LANES), f32)
    for k in range(len(ORDER)):

        def body(b, sums, k=k):
            base = pl.multiple_of(b * 8, 8)
            rx = [rx_ref[k, e, pl.ds(base, 8), :] for e in range(4)]
            sums = list(sums)
            for o in range(8):
                x = w_ref[k, base + o]
                sums[4] = sums[4] + x * o_ref[k, base + o]
                for e in range(4):
                    sums[e] = sums[e] + x * rx[e][o : o + 1, :]
            return tuple(sums)

        sums = lax.fori_loop(0, half // 8, body, (zero,) * 5)
        for e in range(4):
            px_ref[k, e, at, :] = sums[e]
        dot_ref[k] += jnp.sum(sums[4].reshape(rb // 8, 8, LANES), axis=0)
    store_o.wait()


def solve_kernel(n_lat, rows, prm, edges, carries):
    width = edges.shape[2] // 4
    for k, v in enumerate(ORDER):
        const = constants(prm[v, 0:1, :], prm[v, 1:2, :], rows)
        c = solve_carries(n_lat, lambda t, e: edges[t, k, e * width : (e + 1) * width, :], const)
        for e in range(4):
            for t in range(n_lat):
                carries[t, k, e * width : (e + 1) * width, :] = c[e][t]


def carry_kernel(prm, sigma, carries, o_ref, el_ref, es_ref):
    width = carries.shape[2] // 4
    zero = jnp.zeros((8, LANES), f32)

    def body(d, _):
        for k in range(len(ORDER)):
            for j in range(width):
                at = d * width + j
                o_ref[k, at] = zero
                for e in range(4):
                    o_ref[k, at, e : e + 1, :] = carries[d, k, e * width + j : e * width + j + 1, :]
        return 0

    lax.fori_loop(0, carries.shape[0], body, 0)

    def put(i, x):
        es_ref[i] = x

    lon_filter(prm, 8, o_ref, el_ref, put, slice(0, 8))
    x = sigma[0]
    rows, lon = x.shape
    outer = jnp.where(low_lanes((rows, LANES)), x[:, 0:1], x[:, lon - 1 : lon])
    outer = jnp.concatenate([outer, jnp.zeros((LANES - rows, LANES), f32)], axis=0).T
    es_ref[6] = jnp.concatenate([outer[0:1], outer[64:65], jnp.zeros((6, LANES), f32)], axis=0)


def close_kernel(
    n_lon, rows, devices, capacity, cells, place, target, prm, x_ref, proj, px, dots, rx, ry, el, elc, *rest
):
    sent, sent_x = rest[:n_lon], rest[n_lon : 2 * n_lon]
    carry, full_ref, col_ref, side_ref, table, esm, esx = rest[2 * n_lon :]
    half = rx.shape[2]
    me = place[1]
    for d in range(n_lon):
        esm[me ^ d] = sent[d][...]
        esx[me ^ d] = sent_x[d][...]
    pad = jnp.zeros((LANES - 8, LANES), f32)
    for i, t in enumerate((jnp.maximum(me - 1, 0), jnp.minimum(me + 1, n_lon - 1))):
        outer = jnp.concatenate([esx[t, 6], pad], axis=0).T[:rows, 1 - i : 2 - i]
        side_ref[i] = jnp.broadcast_to(outer, (rows, LANES))
    length = jnp.stack([prm[v, 0:1, :] for v in ORDER])
    decay = jnp.stack([prm[v, 1:2, :] for v in ORDER])
    whole = constants(length, decay, 2 * half)
    span, k1, k2, k3 = constants(length, decay, half)
    low = low_lanes((len(ORDER), rows + 8, LANES))
    cache = {}

    def both(main, more):
        parts = [jnp.concatenate([main(k), more(k)], axis=0) for k in range(len(ORDER))]
        return jnp.stack(parts)

    def edge(t, e):
        i = e // 2
        if (t, i) not in cache:
            x = both(lambda k: esm[t, 2 * k + i], lambda k: esx[t, 2 * k + i])
            y = swap(x)
            cache[t, i] = (jnp.where(low, y, x), jnp.where(low, x, y))
        return cache[t, i][e % 2]

    d1, d2, d3, d4 = pick(solve_carries(n_lon, edge, whole), me)
    e1, e2, e3, e4 = (both(lambda k, e=e: el[k, e], lambda k, e=e: elc[k, e]) for e in range(4))
    c1 = jnp.where(low, d1, swap(e1 + span * d1))
    c2 = jnp.where(low, swap(e2 + k1 * c1 + span * d2), d2)
    c3 = jnp.where(low, d3, swap(e3 + k2 * c1 + k1 * c2 + span * d3))
    c4 = jnp.where(low, swap(e4 + k3 * c1 + k2 * c2 + k1 * c3 + span * d4), d4)
    lane = lax.broadcasted_iota(jnp.int32, (devices, LANES), 1)
    first_slot = lax.broadcasted_iota(jnp.int32, (devices, LANES), 0) * capacity
    owned = jnp.zeros((devices, LANES), f32)
    for k, v in enumerate(ORDER):
        more = [c[k, rows:] for c in (c1, c2, c3, c4)]
        sums = jnp.zeros((rows, LANES), f32)
        for e, c in enumerate((c1, c2, c3, c4)):
            carry[k, e] = c[k, :rows]
            sums = sums + c[k, :rows] * px[k, e]

        def body(b, total, k=k, more=more):
            base = pl.multiple_of(b * 8, 8)
            r = [rx[k, e, pl.ds(base, 8), :] for e in range(4)]
            for o in range(8):
                x = x_ref[k, base + o]
                for e in range(4):
                    x = x + r[e][o : o + 1, :] * more[e]
                full_ref[k, base + o] = x
                total = total + x * proj[k, base + o]
            return total

        total = lax.fori_loop(0, half // 8, body, dots[k])
        total = total + jnp.sum(sums.reshape(rows // 8, 8, LANES), axis=0)
        total = jnp.sum(total, axis=0, keepdims=True)
        total = (total + swap(total)) * prm[v, 3:4, :] * (1.0 / cells)
        where = target[:, 64 * v : 64 * (v + 1)]
        where = jnp.concatenate([where, where], axis=1) - first_slot
        for s in range(capacity):
            mine = jnp.where((lane < 64) & (where == s), total, 0.0)
            owned = owned + jnp.where(lane == s, jnp.sum(mine, axis=1, keepdims=True), 0.0)
        if v == 0:
            for i, d in enumerate((d3, d4)):
                y = d[k, :rows]
                for e in range(4):
                    y = y + ry[k, e] * d[k, rows + e : rows + e + 1]
                col_ref[i] = y
    table[...] = owned


def end_kernel(
    rows, pairs, rq, place, prm, sigma, north, south, vert, bal, col, side, carry, rx_ref, ry_ref, u_ref, x_ref,
    out_ref, out, xs, zx, zc, wt, sg, sx, sems,
):
    g = pl.program_id(0)
    half = 2 * pairs
    lon = sigma.shape[2]
    merged = out.shape[2]
    steps = pairs // PAIRS

    def copy(v, side_at, step):
        first = pl.multiple_of((step * PAIRS + side_at * pairs) * LANES, LANES)
        cols = pl.ds(first, PAIRS * LANES)
        return pltpu.make_async_copy(out.at[v, :, cols], out_ref.at[v, :, cols], sems.at[v, side_at, step])

    @pl.when(g == 0)
    def _():
        for v in range(3):
            scaled = quad(vert[v]) * prm[v, 3:4, :]
            set_weights(wt, v, scaled.T, True)
        set_weights(wt, 3, quad(bal[...]).T, False)
        stage_sigma(sigma, sg, (0, 1, 2))
        for at in range(0, lon, LANES):
            width = min(LANES, lon - at)
            sx[at // LANES, 0:1, 0:width] = north[:, merged + at : merged + at + width]
            sx[at // LANES, 1:2, 0:width] = south[:, merged + at : merged + at + width]

    lane = lax.broadcasted_iota(jnp.int32, (rows, LANES), 1)
    high = (lane >= 64).astype(jnp.int32)
    high8 = high[0:8]
    chi_row = prm[0, 2:3, :]

    def at_tile(m):
        return pl.ds(pl.multiple_of(m * LANES, LANES), LANES)

    row8 = lax.broadcasted_iota(jnp.int32, (8, LANES), 0)
    beyond = [None] * (2 * PAIRS)
    for k, v in enumerate(ORDER):
        for q in range(0, rows, rq):
            c = [carry[k, e, q : q + rq, :] for e in range(4)]
            ry = [ry_ref[k, e, q : q + rq, :] for e in range(4)]
            rx = [rx_ref[k, e, pl.ds(pl.multiple_of(g * 2 * PAIRS, 8), 2 * PAIRS), :] for e in range(4)]
            for p in range(2 * PAIRS):
                x = x_ref[k, p]
                y = u_ref[k, p, q : q + rq, :]
                for e in range(4):
                    y = y + rx[e][p : p + 1, :] * c[e] + ry[e] * x[e : e + 1, :]
                at = (p // 2) * rows + q
                xs[k, at : at + rq, (p % 2) * LANES : (p % 2 + 1) * LANES] = y
                if v == 0 and q == 0:
                    x = pltpu.roll(x, 6, 0)
                    above = jnp.where(place[0] > 0, x + prm[0, 1:2, :] * y[0:1, :], 0.0)
                    beyond[p] = jnp.where(row8 == 0, above, jnp.where(row8 == 1, x, 0.0))

    @pl.when(g == 0)
    def _():
        first = col[0] + prm[0, 1:2, :] * xs[ORDER.index(0), 0:rows, 0:LANES]
        lhs = jnp.where(lane < 64, jnp.where(place[1] > 0, first, 0.0), col[1])
        lhs = jnp.concatenate([lhs, jnp.zeros_like(lhs)], axis=1)
        res = product(lhs, weight(wt, 0))
        zc[0] = swap(res[:, :LANES] * swap(side[0]))
        zc[1] = res[:, LANES:] * side[1]

    lhs = jnp.concatenate(
        [jnp.concatenate(beyond[2 * p : 2 * p + 2], axis=1) for p in range(PAIRS)], axis=0
    )
    res = product(lhs, weight(wt, 0))
    for p in range(PAIRS):
        m = g * PAIRS + p
        for side in range(2):
            tile = m + side * pairs
            s = jnp.take_along_axis(sx[tile >> 6], 2 * (tile & 63) + high8, axis=1, mode="promise_in_bounds")
            part = res[p * 8 : (p + 1) * 8, side * LANES : (side + 1) * LANES]
            zx[:, at_tile(tile)] = jnp.where(row8 < 2, part * s, 0.0)
    results = {v: product(xs[k], weight(wt, v)) for k, v in enumerate(ORDER)}
    for p in range(PAIRS):
        m = g * PAIRS + p
        for side in range(2):
            at = at_tile(m + side * pairs)
            z = [
                results[v][p * rows : (p + 1) * rows, side * LANES : (side + 1) * LANES]
                * sigma_tile(sg, v, m + side * pairs, high)
                for v in range(3)
            ]
            out[0, :, at] = z[0]
            out[1, :, at] = z[1] + chi_row * z[0]
            out[2, :, at] = z[2]
    for v in range(2):
        for side_at in range(2):
            copy(v, side_at, g).start()

    @pl.when(g == pl.num_programs(0) - 1)
    def _():
        row_id = lax.broadcasted_iota(jnp.int32, (rows, LANES), 0)
        last = half - 1

        def body(b, _):
            for p in range(PAIRS):
                for side in range(2):
                    m = b * PAIRS + p + side * pairs
                    x = out[0, :, at_tile(m)]
                    left = jnp.where(m == 0, zc[0], out[0, :, at_tile(jnp.maximum(m - 1, 0))])
                    right = jnp.where(m == last, zc[1], out[0, :, at_tile(jnp.minimum(m + 1, last))])
                    beside = swap(x + jnp.where(lane >= 64, left, right))
                    above = jnp.where(row_id == 0, zx[0:1, at_tile(m)], pltpu.roll(x, 1, 0))
                    below = jnp.where(row_id == rows - 1, zx[1:2, at_tile(m)], pltpu.roll(x, rows - 1, 0))
                    lap = 4.0 * x - beside - above - below
                    xs[0, p * rows : (p + 1) * rows, side * LANES : (side + 1) * LANES] = lap
            res = product(xs[0], weight(wt, 3))
            for p in range(PAIRS):
                for side in range(2):
                    at = at_tile(b * PAIRS + p + side * pairs)
                    part = res[p * rows : (p + 1) * rows, side * LANES : (side + 1) * LANES]
                    out[2, :, at] = out[2, :, at] + part
            for side_at in range(2):
                copy(2, side_at, b).start()
            return 0

        lax.fori_loop(0, steps, body, 0)
        for v in range(3):
            for side_at in range(2):
                for step in range(steps):
                    copy(v, side_at, step).wait()


def shards(state, sigma, vert, bal_temp, chi_coef, scales, classes, owner):
    n_lat = lax.axis_size("lat")
    n_lon = lax.axis_size("lon")
    devices = n_lat * n_lon
    nvars, rows, merged = state.shape
    levels = vert.shape[1]
    lon = merged // levels
    half = lon // 2
    pairs = half // 2
    pieces = (lon + LANES - 1) // LANES
    count = nvars * levels
    capacity = (count + devices - 1) // devices + 1
    i_lat = lax.axis_index("lat")
    i_lon = lax.axis_index("lon")

    up_lat, up_lon = ([(i, i + 1) for i in range(n - 1)] for n in (n_lat, n_lon))
    down_lat, down_lon = ([(j, i) for i, j in up] for up in (up_lat, up_lon))

    def row(i):
        return jnp.concatenate([state[2, i : i + 1, :], sigma[0, i : i + 1, :]], axis=1)

    north = lax.ppermute(row(rows - 1), "lat", up_lat)
    south = lax.ppermute(row(0), "lat", down_lat)
    west = lax.ppermute(state[2, :, merged - levels :], "lon", up_lon)
    east = lax.ppermute(state[2, :, :levels], "lon", down_lon)
    place = jnp.stack([i_lat, i_lon]).astype(jnp.int32)

    anywhere = pl.BlockSpec(memory_space=pl.ANY)
    steps = pairs // BLOCK

    def part(v, side):
        return pl.BlockSpec((1, rows, BLOCK * LANES), lambda g: (v, 0, g + side * steps))

    width = half // n_lat
    shapes = [(nvars, half, rows, LANES), (nvars, rows, half, LANES), (n_lat, nvars, 4 * width, LANES)]
    shapes.append((nvars, half, 8, LANES))

    def lat_call(nv, first, body, arrays, specs, name, aliases, more=()):
        return pl.pallas_call(
            body,
            grid=(steps,),
            in_specs=specs,
            out_specs=[
                pl.BlockSpec((nv, 2 * BLOCK, rows, LANES), lambda g: (first, g, 0, 0)),
                pl.BlockSpec((nv, rows, 2 * BLOCK, LANES), lambda g: (first, 0, g, 0)),
                pl.BlockSpec((2 * BLOCK // width, nv, 4 * width, LANES), lambda g: (g, first, 0, 0)),
                pl.BlockSpec((nv, 2 * BLOCK, 8, LANES), lambda g: (first, g, 0, 0)),
            ]
            + [full(s) for s in more],
            out_shape=[jax.ShapeDtypeStruct(s, f32) if n == 2 else pltpu.HBM(s, f32) for n, s in enumerate(shapes)]
            + [jax.ShapeDtypeStruct(s, f32) for s in more],
            scratch_shapes=[
                pltpu.VMEM((2, PAIRS * rows, 256), f32),
                pltpu.VMEM((2 * 768, 256), bf16),
                pltpu.VMEM((nvars, pieces, rows, LANES), f32),
            ],
            compiler_params=params(),
            cost_estimate=pl.CostEstimate(
                flops=nv * 60000000, bytes_accessed=nv * 3 * rows * merged * 4, transcendentals=0
            ),
            input_output_aliases=aliases,
            name=name,
        )(*arrays)

    ins = [scales.reshape(1, -1), classes.reshape(1, count), chi_coef.reshape(1, levels), sigma, vert] + [state] * 4
    specs = [full(x.shape) for x in ins[:5]] + [part(1, 0), part(1, 1), part(2, 0), part(2, 1)]
    ins = [in_hbm(x) for x in ins]
    body = functools.partial(lat_plain, rows, pairs)
    *wue, prm = lat_call(2, 0, body, ins, specs, "lat_chi_temp", {}, [(nvars, 4, LANES)])
    ins = [prm] + [in_hbm(x) for x in [sigma, vert, bal_temp] + [state] * 10] + [north, south, west, east]
    ins += [in_hbm(wue[0]), in_hbm(wue[1]), wue[2], in_hbm(wue[3])]
    specs = [full(x.shape) for x in ins[:4]] + [part(0, 0), part(0, 1), part(1, 0), part(1, 1)]

    def tile(side, step):
        last = 2 * pairs - 1
        return pl.BlockSpec(
            (1, rows, LANES), lambda g: (2, 0, jnp.clip(g * BLOCK + side * pairs + step, 0, last))
        )

    specs += [part(2, 0), part(2, 1), tile(0, -1), tile(0, BLOCK), tile(1, -1), tile(1, BLOCK)]
    specs += [full(x.shape) for x in (north, south, west, east)] + [anywhere] * 4
    aliases = {18: 0, 19: 1, 20: 2, 21: 3}
    w, u, edges, proj = lat_call(1, 2, functools.partial(lat_balance, rows, pairs), ins, specs, "lat_psi", aliases)
    def trade(x, axis):
        return lax.all_to_all(x, axis, split_axis=0, concat_axis=0, tiled=True)

    shares = trade(edges, "lat")

    rb = BLOCK
    local, el, es, px, dots, rx, ry = pl.pallas_call(
        functools.partial(lon_kernel, rows, rb),
        grid=(rows // rb,),
        in_specs=[
            full(prm.shape),
            pl.BlockSpec((nvars, rb, half, LANES), lambda g: (0, g, 0, 0)),
            anywhere,
        ],
        out_specs=[
            anywhere,
            full((nvars, 4, rows, LANES)),
            full((6, rows, LANES)),
            full((nvars, 4, rows, LANES)),
            full((nvars, 8, LANES)),
            full((nvars, 4, half, LANES)),
            full((nvars, 4, rows, LANES)),
        ],
        out_shape=[
            pltpu.HBM((nvars, half, rows, LANES), f32),
            pltpu.HBM((nvars, 4, rows, LANES), f32),
            jax.ShapeDtypeStruct((6, rows, LANES), f32),
            pltpu.HBM((nvars, 4, rows, LANES), f32),
            pltpu.HBM((nvars, 8, LANES), f32),
            pltpu.HBM((nvars, 4, half, LANES), f32),
            pltpu.HBM((nvars, 4, rows, LANES), f32),
        ],
        scratch_shapes=[pltpu.VMEM((nvars, half, rb, LANES), f32)] * 2 + [pltpu.SemaphoreType.DMA((2,))],
        compiler_params=params(),
        cost_estimate=pl.CostEstimate(
            flops=180000000, bytes_accessed=6 * rows * merged * 4, transcendentals=0
        ),
        name="lon_tile",
    )(prm, *[in_hbm(x) for x in (u, w)])

    def round_lon(x):
        return [x] + [
            lax.ppermute(x, "lon", [(i, i ^ s) for i in range(n_lon)]) for s in range(1, n_lon)
        ]

    shares, _ = lax.optimization_barrier((shares, es))
    sent = round_lon(es)
    carries = pl.pallas_call(
        functools.partial(solve_kernel, n_lat, rows),
        grid=(1,),
        in_specs=[full(prm.shape), full(shares.shape)],
        out_specs=full(shares.shape),
        out_shape=jax.ShapeDtypeStruct(shares.shape, f32),
        compiler_params=params(),
        cost_estimate=pl.CostEstimate(flops=1000000, bytes_accessed=2 * shares.size * 4, transcendentals=0),
        name="solve",
    )(prm, shares)
    carries = trade(carries, "lat")

    crossed, elc, esc = pl.pallas_call(
        carry_kernel,
        grid=(1,),
        in_specs=[full(prm.shape), pl.BlockSpec((1, rows, lon), lambda g: (0, 0, 0)), full(carries.shape)],
        out_specs=[full((nvars, half, 8, LANES)), full((nvars, 4, 8, LANES)), full((7, 8, LANES))],
        out_shape=[
            jax.ShapeDtypeStruct((nvars, half, 8, LANES), f32),
            jax.ShapeDtypeStruct((nvars, 4, 8, LANES), f32),
            jax.ShapeDtypeStruct((7, 8, LANES), f32),
        ],
        compiler_params=params(),
        cost_estimate=pl.CostEstimate(
            flops=30000000, bytes_accessed=4 * nvars * 12 * half * LANES, transcendentals=0
        ),
        name="lon_carry",
    )(prm, in_hbm(sigma), carries)
    sent_x = round_lon(esc)

    packed = 2 * PAIRS

    def columns(r):
        return pl.BlockSpec((nvars, packed, r, LANES), lambda g: (0, g, 0, 0))

    index = jnp.arange(count, dtype=jnp.int32)
    same = (owner[:, None] == owner[None, :]) & (index[None, :] < index[:, None])
    target = (owner * capacity + jnp.sum(same.astype(jnp.int32), axis=1)).reshape(1, count)

    ins = [in_hbm(x) for x in (proj, px, dots, rx, ry, el)]
    ins = [place, target, prm, crossed] + ins + [elc] + sent + sent_x
    specs = [full(x.shape) for x in ins]
    specs[0] = pl.BlockSpec(memory_space=pltpu.SMEM)
    shapes = [(nvars, 4, rows, LANES), (nvars, half, 8, LANES), (2, rows, LANES), (2, rows, LANES)]
    carry, crossed, col, side, table = pl.pallas_call(
        functools.partial(close_kernel, n_lon, rows, devices, capacity, devices * rows * lon),
        grid=(1,),
        in_specs=specs,
        out_specs=[full(x) for x in shapes] + [full((devices, LANES))],
        out_shape=[pltpu.HBM(x, f32) for x in shapes] + [jax.ShapeDtypeStruct((devices, LANES), f32)],
        scratch_shapes=[pltpu.VMEM((n_lon, 6, rows, LANES), f32), pltpu.VMEM((n_lon, 7, 8, LANES), f32)],
        compiler_params=params(),
        cost_estimate=pl.CostEstimate(flops=10000000, bytes_accessed=4000000, transcendentals=0),
        name="close",
    )(*ins)
    table = trade(table, ("lat", "lon"))
    slab_energy = jnp.sum(table, axis=0, keepdims=True)[:, :capacity]

    ins = [prm, sigma, north, south, vert, bal_temp, col, side, carry, rx, ry, local, crossed]
    ins = [place] + [in_hbm(x) for x in ins]
    specs = [full(x.shape) for x in ins]
    specs[0] = pl.BlockSpec(memory_space=pltpu.SMEM)
    specs[-2:] = [columns(rows), columns(8)]
    applied = pl.pallas_call(
        functools.partial(end_kernel, rows, pairs, 24),
        grid=(half // packed,),
        in_specs=specs,
        out_specs=anywhere,
        out_shape=jax.ShapeDtypeStruct(state.shape, f32),
        scratch_shapes=[
            pltpu.VMEM(state.shape, f32),
            pltpu.VMEM((nvars, PAIRS * rows, 256), f32),
            pltpu.VMEM((8, merged), f32),
            pltpu.VMEM((2, rows, LANES), f32),
            pltpu.VMEM((4 * 768, 256), bf16),
            pltpu.VMEM((nvars, pieces, rows, LANES), f32),
            pltpu.VMEM((pieces, 8, LANES), f32),
            pltpu.SemaphoreType.DMA((3, 2, pairs // PAIRS)),
        ],
        compiler_params=params(),
        cost_estimate=pl.CostEstimate(
            flops=300000000, bytes_accessed=6 * rows * merged * 4, transcendentals=0
        ),
        name="finish",
    )(*ins)
    return (applied, slab_energy)


def solution(mesh):
    return jax.shard_map(
        shards,
        mesh=mesh,
        in_specs=(P(None, "lat", "lon"), P(None, "lat", "lon"), P(), P(), P(), P(), P(), P()),
        out_specs=(P(None, "lat", "lon"), P(("lat", "lon"), None)),
        check_vma=False,
    )
```

```python
import functools

import jax
import jax.numpy as jnp
from jax import lax
from jax.experimental import pallas as pl
from jax.experimental.pallas import tpu as pltpu
from jax.sharding import PartitionSpec as P

highest = lax.Precision.HIGHEST
f32 = jnp.float32
bf16 = jnp.bfloat16
LANES = 128
PAIRS = 8
BLOCK = 24
ORDER = (1, 2, 0)
LIMIT = 30 * 1024 * 1024


def params():
    return pltpu.CompilerParams(vmem_limit_bytes=LIMIT)


def in_hbm(x):
    return pltpu.with_memory_space_constraint(x, pltpu.HBM)


def full(shape):
    return pl.BlockSpec(shape, lambda g: (0,) * len(shape))


def swap(x):
    return pltpu.roll(x, 64, x.ndim - 1)


def low_lanes(shape):
    return lax.broadcasted_iota(jnp.int32, shape, len(shape) - 1) < 64


def halves(x):
    hi = x.astype(bf16)
    return hi, (x - hi.astype(f32)).astype(bf16)


def dot(x, y):
    return jnp.dot(x, y, preferred_element_type=f32)


def split(x):
    hi, lo = halves(x)
    return jnp.concatenate([hi, lo, hi], axis=1)


def product(x, weights):
    return dot(split(x), weights)


def expand(mat, mixed):
    wide = quad(mat)
    wide = jnp.concatenate([wide, wide], axis=1)
    wide = jnp.concatenate([wide, wide], axis=0)
    src = lax.broadcasted_iota(jnp.int32, (256, 256), 0) // 64
    dst = lax.broadcasted_iota(jnp.int32, (256, 256), 1) // 64
    if mixed:
        src = jnp.where(src == 1, 2, jnp.where(src == 2, 1, src))
    return halves(jnp.where(src == dst, wide, 0.0))


def quad(mat):
    if mat.shape[0] == LANES:
        return mat
    wide = jnp.concatenate([mat, mat], axis=1)
    return jnp.concatenate([wide, wide], axis=0)


def constants(length, decay, m):
    span = jnp.exp(-float(m) / length)
    d = 1.0 - decay * decay
    k1 = decay * (1.0 - span * span) / d
    k2 = (m * span - decay * decay * (span - span * span * span) / d) / d
    tail = decay * decay * (1.0 + span * span) * (1.0 - span * span) / d
    k3 = decay / (d * d) * (1.0 - (2.0 * m + 1.0) * span * span + tail)
    return span, k1, k2, k3


def responses(length, decay, m):
    j = lax.broadcasted_iota(jnp.int32, (m, LANES), 0).astype(f32)
    up = jnp.exp(-j / length)
    down = jnp.exp(-(m - j) / length)
    span = jnp.exp(-float(m) / length)
    d = 1.0 - decay * decay
    diff = up - span * down
    g3 = decay * diff / d
    g2 = ((m - j) * down - decay * decay * (span * up - span * span * down) / d) / d
    part = decay * decay * (1.0 + span * span) * diff / d
    g1 = decay / (d * d) * ((j + 1.0) * up - (2.0 * m + 1.0 - j) * span * down + part)
    return g1, g2, g3, down


def pick(all_carries, me):
    out = []
    for cs in all_carries:
        mine = cs[0]
        for t in range(1, len(cs)):
            mine = jnp.where(me == t, cs[t], mine)
        out.append(mine)
    return out


def solve_carries(n, edge, const):
    span, k1, k2, k3 = const
    first = edge(0, 0)
    zero = jnp.zeros_like(first)
    e1 = [first] + [edge(t, 0) for t in range(1, n)]
    c1, c2, c3, c4 = ([None] * n for _ in range(4))
    c = zero
    for t in range(n):
        c1[t] = c
        c = e1[t] + span * c
    c = zero
    for t in reversed(range(n)):
        c2[t] = c
        c = edge(t, 1) + k1 * c1[t] + span * c
    c = zero
    for t in range(n):
        c3[t] = c
        c = edge(t, 2) + k2 * c1[t] + k1 * c2[t] + span * c
    c = zero
    for t in reversed(range(n)):
        c4[t] = c
        c = edge(t, 3) + k3 * c1[t] + k2 * c2[t] + k1 * c3[t] + span * c
    return c1, c2, c3, c4


def cascade(count, turn, load, store, decay, start):
    step = 24

    def first(b, states):
        blocks = turn(b)
        for o in range(8):
            states = [a * s + x[o] for a, s, x in zip(decay, states, blocks)]
            store(b * 8 + o, states)
        return tuple(states)

    edges = [list(lax.fori_loop(0, count // 8, first, tuple(start)))]
    for stage in range(1, 4):
        back = stage % 2 == 1

        def body(b, states, back=back):
            base = (count // step - 1 - b) * step if back else b * step
            order = range(step - 1, -1, -1) if back else range(step)
            for o in order:
                new = [decay_k * s + x for decay_k, s, x in zip(decay, states, load(base + o))]
                store(base + o, new)
                states = new
            return tuple(states)

        states = lax.fori_loop(0, count // step, body, tuple(start))
        edges.append(list(states))
    return edges


def stage_sigma(sigma, sg, variables):
    lon = sigma.shape[2]
    for v in variables:
        for at in range(0, lon, LANES):
            width = min(LANES, lon - at)
            sg[v, at // LANES, :, 0:width] = sigma[v, :, at : at + width]


def sigma_tile(sg, v, m, high):
    idx = 2 * (m & 63) + high
    return jnp.take_along_axis(sg[v, m >> 6], idx, axis=1, mode="promise_in_bounds")


def set_weights(weights, k, mat, mixed):
    hi, lo = expand(mat, mixed)
    weights[768 * k : 768 * k + 256] = hi
    weights[768 * k + 256 : 768 * k + 512] = hi
    weights[768 * k + 512 : 768 * k + 768] = lo


def weight(weights, k):
    return weights[768 * k : 768 * (k + 1)]


def lat_filter(vs, rows, prm, w_ref, u_ref, e_ref, p_ref):
    nv = len(vs)
    decay = [prm[v, 1:2, :] for v in vs]

    def load(i):
        return [u_ref[k, i] for k in range(nv)]

    def store(i, values):
        for k in range(nv):
            u_ref[k, i] = values[k]

    def turn(b):
        at = pl.ds(pl.multiple_of(b * 8, 8), 8)
        return [jnp.swapaxes(w_ref[k, :, at, :], 0, 1) for k in range(nv)]

    zero = jnp.zeros((u_ref.shape[2], LANES), f32)
    edges = cascade(rows, turn, load, store, decay, [zero] * nv)
    for k in range(nv):
        for j in range(0, u_ref.shape[2], 8):
            block = [edges[3 - e][k][j : j + 8] * decay[k] for e in range(4)]
            block = jnp.stack(block + [jnp.zeros((8, LANES), f32)] * 4)
            p_ref[k, j : j + 8] = jnp.swapaxes(block, 0, 1)
    width = e_ref.shape[2] // 4
    for e in range(4):
        for k in range(nv):
            for c in range(e_ref.shape[0]):
                e_ref[c, k, e * width : (e + 1) * width] = edges[e][k][c * width : (c + 1) * width]


def put_mixed(k, b, rows, res, w_ref):
    base = b * 2 * PAIRS
    for p in range(PAIRS):
        part = res[p * rows : (p + 1) * rows]
        w_ref[k, base + 2 * p] = part[:, :LANES]
        w_ref[k, base + 2 * p + 1] = part[:, LANES:]


def set_params(scales, classes, chi_coef, prm):
    coef = jnp.concatenate([chi_coef[...], chi_coef[...]], axis=1)
    for v in range(3):
        kind = classes[:, 64 * v : 64 * (v + 1)]
        kind = jnp.concatenate([kind, kind], axis=1)
        length = jnp.zeros((1, LANES), f32)
        for n in range(scales.shape[1]):
            length = jnp.where(kind == n, scales[:, n : n + 1], length)
        decay = jnp.exp(-1.0 / length)
        norm = 1.0 - decay
        norm = norm * norm
        norm = norm * norm
        prm[v, 0:1, :] = length
        prm[v, 1:2, :] = decay
        prm[v, 2:3, :] = coef
        prm[v, 3:4, :] = length * jnp.sqrt(length) * norm * norm


def lat_plain(
    rows, pairs, scales, classes, chi_coef, sigma, vert, b1lo, b1hi, b2lo, b2hi,
    w_ref, u_ref, e_ref, p_ref, prm, xs, wt, sg,
):
    g = pl.program_id(0)

    @pl.when(g == 0)
    def _():
        set_params(scales, classes, chi_coef, prm)
        set_weights(wt, 0, vert[1], True)
        set_weights(wt, 1, vert[2], True)
        stage_sigma(sigma, sg, (1, 2))

    lane = lax.broadcasted_iota(jnp.int32, (rows, LANES), 1)
    high = (lane >= 64).astype(jnp.int32)

    def body(b, _):
        for p in range(PAIRS):
            at = slice(p * rows, (p + 1) * rows)
            cols = pl.ds(pl.multiple_of((b * PAIRS + p) * LANES, LANES), LANES)
            m = g * BLOCK + b * PAIRS + p
            for k, sides in enumerate(((b1lo, b1hi), (b2lo, b2hi))):
                for side in range(2):
                    s = sigma_tile(sg, k + 1, m + side * pairs, high)
                    xs[k, at, side * LANES : (side + 1) * LANES] = sides[side][0, :, cols] * s
        for k in range(2):
            put_mixed(k, b, rows, product(xs[k], weight(wt, k)), w_ref)
        return 0

    lax.fori_loop(0, BLOCK // PAIRS, body, 0)
    lat_filter((1, 2), rows, prm, w_ref, u_ref, e_ref, p_ref)


def lat_balance(
    rows, pairs, prm, sigma, vert, bal, plo, phi, clo, chi, tlo, thi, tll, tlr, thl, thr, north, south, west, east, w_in, u_in, e_in, p_in,
    w_ref, u_ref, e_ref, p_ref, xs, wt, sg,
):
    del w_in, u_in, e_in, p_in
    g = pl.program_id(0)

    @pl.when(g == 0)
    def _():
        set_weights(wt, 0, vert[0], True)
        (bh, bl), (vh, vl) = halves(bal[...]), halves(vert[0])
        set_weights(wt, 1, dot(bh, vh) + dot(bl, vh) + dot(bh, vl), True)
        stage_sigma(sigma, sg, (0,))

    lane = lax.broadcasted_iota(jnp.int32, (rows, LANES), 1)
    row_id = lax.broadcasted_iota(jnp.int32, (rows, LANES), 0)
    high = (lane >= 64).astype(jnp.int32)
    chi_row = prm[0, 2:3, :]
    last = 2 * pairs - 1
    beyond = [jnp.concatenate([x[...], x[...]], axis=1) for x in (west, east)]

    def at_tile(m):
        return pl.ds(pl.multiple_of(m * LANES, LANES), LANES)

    sides = ((tlo, tll, tlr), (thi, thl, thr))

    def laplace(b, o, side):
        temp, before, after = sides[side]
        p = b * PAIRS + o
        m = g * BLOCK + p + side * pairs
        x = temp[0, :, at_tile(p)]
        left = temp[0, :, at_tile(jnp.maximum(p - 1, 0))]
        if o == 0:
            left = jnp.where(p == 0, before[0], left)
            if side == 0:
                left = jnp.where(m == 0, beyond[0], left)
        right = temp[0, :, at_tile(jnp.minimum(p + 1, BLOCK - 1))]
        if o == PAIRS - 1:
            right = jnp.where(p == BLOCK - 1, after[0], right)
            if side == 1:
                right = jnp.where(m == last, beyond[1], right)
        beside = swap(x + jnp.where(lane >= 64, left, right))
        above = jnp.where(row_id == 0, north[:, at_tile(m)], pltpu.roll(x, 1, 0))
        below = jnp.where(row_id == rows - 1, south[:, at_tile(m)], pltpu.roll(x, rows - 1, 0))
        return 4.0 * x - beside - above - below

    def body(b, _):
        for p in range(PAIRS):
            at = slice(p * rows, (p + 1) * rows)
            cols = at_tile(b * PAIRS + p)
            m = g * BLOCK + b * PAIRS + p
            for side, (pr, cr) in enumerate(((plo, clo), (phi, chi))):
                s = sigma_tile(sg, 0, m + side * pairs, high)
                to = slice(side * LANES, (side + 1) * LANES)
                xs[0, at, to] = (pr[0, :, cols] + chi_row * cr[0, :, cols]) * s
                xs[1, at, to] = laplace(b, p, side) * s
        res = dot(jnp.concatenate([split(xs[0]), split(xs[1])], axis=1), wt[...])
        put_mixed(0, b, rows, res, w_ref)
        return 0

    lax.fori_loop(0, BLOCK // PAIRS, body, 0)
    lat_filter((0,), rows, prm, w_ref, u_ref, e_ref, p_ref)


def lon_filter(prm, rb, turn, o_ref, el_ref, put, at):
    half = o_ref.shape[1]
    nv = len(ORDER)
    decay = [prm[v, 1:2, :] for v in ORDER]

    def load(j):
        return [o_ref[k, j] for k in range(nv)]

    def store(j, values):
        for k in range(nv):
            o_ref[k, j] = values[k]

    edges = cascade(half, turn, load, store, decay, [jnp.zeros((rb, LANES), f32)] * nv)
    low = low_lanes((rb, LANES))
    for k, v in enumerate(ORDER):
        span, k1, k2, k3 = constants(prm[v, 0:1, :], prm[v, 1:2, :], half)
        e1, e2, e3, e4 = (edges[e][k] for e in range(4))
        c1 = jnp.where(low, 0.0, swap(e1))
        t1 = e1 + span * c1
        t2 = e2 + k1 * c1
        c2 = jnp.where(low, swap(t2), 0.0)
        t2 = t2 + span * c2
        t3 = e3 + k2 * c1 + k1 * c2
        c3 = jnp.where(low, 0.0, swap(t3))
        t3 = t3 + span * c3
        t4 = e4 + k3 * c1 + k2 * c2 + k1 * c3
        c4 = jnp.where(low, swap(t4), 0.0)
        t4 = t4 + span * c4
        put(2 * k, jnp.where(low, t2, t1))
        put(2 * k + 1, jnp.where(low, t4, t3))
        for e, x in enumerate((e1, e2, e3, e4)):
            el_ref[k, e, at, :] = x


def lon_kernel(
    rows, rb, prm, u_hbm, w_hbm, o_hbm, el_ref, es_ref, px_ref, dot_ref, rx_ref, ry_ref, u_all, w_ref, o_ref, sems
):
    g = pl.program_id(0)
    half = o_ref.shape[1]
    at = pl.ds(pl.multiple_of(g * rb, 8), rb)

    def load_u(step):
        return pltpu.make_async_copy(u_hbm.at[:, pl.ds(step * rb, rb)], u_all.at[step], sems.at[2 + step])

    @pl.when(g == 0)
    def _():
        for step in range(rows // rb):
            load_u(step).start()
        dot_ref[...] = jnp.zeros_like(dot_ref)
        for k, v in enumerate(ORDER):
            for e, r in enumerate(responses(prm[v, 0:1, :], prm[v, 1:2, :], half)):
                rx_ref[k, e] = r
            for e, r in enumerate(responses(prm[v, 0:1, :], prm[v, 1:2, :], rows)):
                ry_ref[k, e] = r

    load_u(g).wait()
    load_w = pltpu.make_async_copy(w_hbm.at[:, :, at, :], w_ref, sems.at[0])
    load_w.start()
    u_ref = u_all.at[g]

    def turn(b):
        cols = pl.ds(pl.multiple_of(b * 8, 8), 8)
        return [jnp.swapaxes(u_ref[k, :, cols, :], 0, 1) for k in range(len(ORDER))]

    def put(i, x):
        es_ref[i, at, :] = x

    lon_filter(prm, rb, turn, o_ref, el_ref, put, at)
    store_o = pltpu.make_async_copy(o_ref, o_hbm.at[:, :, at, :], sems.at[1])
    store_o.start()
    load_w.wait()
    zero = jnp.zeros((rb, LANES), f32)
    for k in range(len(ORDER)):

        def body(b, sums, k=k):
            base = pl.multiple_of(b * 8, 8)
            rx = [rx_ref[k, e, pl.ds(base, 8), :] for e in range(4)]
            sums = list(sums)
            for o in range(8):
                x = w_ref[k, base + o]
                sums[4] = sums[4] + x * o_ref[k, base + o]
                for e in range(4):
                    sums[e] = sums[e] + x * rx[e][o : o + 1, :]
            return tuple(sums)

        sums = lax.fori_loop(0, half // 8, body, (zero,) * 5)
        for e in range(4):
            px_ref[k, e, at, :] = sums[e]
        dot_ref[k] += jnp.sum(sums[4].reshape(rb // 8, 8, LANES), axis=0)
    store_o.wait()


def solve_kernel(n_lat, rows, prm, edges, carries):
    width = edges.shape[2] // 4
    for k, v in enumerate(ORDER):
        const = constants(prm[v, 0:1, :], prm[v, 1:2, :], rows)
        c = solve_carries(n_lat, lambda t, e: edges[t, k, e * width : (e + 1) * width, :], const)
        for e in range(4):
            for t in range(n_lat):
                carries[t, k, e * width : (e + 1) * width, :] = c[e][t]


def carry_kernel(prm, sigma, carries, o_ref, el_ref, es_ref):
    width = carries.shape[2] // 4
    zero = jnp.zeros((8, LANES), f32)

    def body(d, _):
        for k in range(len(ORDER)):
            for j in range(width):
                at = d * width + j
                o_ref[k, at] = zero
                for e in range(4):
                    o_ref[k, at, e : e + 1, :] = carries[d, k, e * width + j : e * width + j + 1, :]
        return 0

    lax.fori_loop(0, carries.shape[0], body, 0)

    def put(i, x):
        es_ref[i] = x

    def turn(b):
        return [o_ref[k, pl.ds(pl.multiple_of(b * 8, 8), 8)] for k in range(len(ORDER))]

    lon_filter(prm, 8, turn, o_ref, el_ref, put, slice(0, 8))
    x = sigma[0]
    rows, lon = x.shape
    outer = jnp.where(low_lanes((rows, LANES)), x[:, 0:1], x[:, lon - 1 : lon])
    outer = jnp.concatenate([outer, jnp.zeros((LANES - rows, LANES), f32)], axis=0).T
    es_ref[6] = jnp.concatenate([outer[0:1], outer[64:65], jnp.zeros((6, LANES), f32)], axis=0)


def close_kernel(
    n_lon, rows, devices, capacity, cells, place, target, prm, x_ref, proj, px, dots, rx, ry, el, elc, *rest
):
    sent, sent_x = rest[:n_lon], rest[n_lon : 2 * n_lon]
    carry, full_ref, col_ref, side_ref, table, esm, esx = rest[2 * n_lon :]
    half = rx.shape[2]
    me = place[1]
    for d in range(n_lon):
        esm[me ^ d] = sent[d][...]
        esx[me ^ d] = sent_x[d][...]
    pad = jnp.zeros((LANES - 8, LANES), f32)
    for i, t in enumerate((jnp.maximum(me - 1, 0), jnp.minimum(me + 1, n_lon - 1))):
        outer = jnp.concatenate([esx[t, 6], pad], axis=0).T[:rows, 1 - i : 2 - i]
        side_ref[i] = jnp.broadcast_to(outer, (rows, LANES))
    length = jnp.stack([prm[v, 0:1, :] for v in ORDER])
    decay = jnp.stack([prm[v, 1:2, :] for v in ORDER])
    whole = constants(length, decay, 2 * half)
    span, k1, k2, k3 = constants(length, decay, half)
    low = low_lanes((len(ORDER), rows + 8, LANES))
    cache = {}

    def both(main, more):
        parts = [jnp.concatenate([main(k), more(k)], axis=0) for k in range(len(ORDER))]
        return jnp.stack(parts)

    def edge(t, e):
        i = e // 2
        if (t, i) not in cache:
            x = both(lambda k: esm[t, 2 * k + i], lambda k: esx[t, 2 * k + i])
            y = swap(x)
            cache[t, i] = (jnp.where(low, y, x), jnp.where(low, x, y))
        return cache[t, i][e % 2]

    d1, d2, d3, d4 = pick(solve_carries(n_lon, edge, whole), me)
    e1, e2, e3, e4 = (both(lambda k, e=e: el[k, e], lambda k, e=e: elc[k, e]) for e in range(4))
    c1 = jnp.where(low, d1, swap(e1 + span * d1))
    c2 = jnp.where(low, swap(e2 + k1 * c1 + span * d2), d2)
    c3 = jnp.where(low, d3, swap(e3 + k2 * c1 + k1 * c2 + span * d3))
    c4 = jnp.where(low, swap(e4 + k3 * c1 + k2 * c2 + k1 * c3 + span * d4), d4)
    lane = lax.broadcasted_iota(jnp.int32, (devices, LANES), 1)
    first_slot = lax.broadcasted_iota(jnp.int32, (devices, LANES), 0) * capacity
    owned = jnp.zeros((devices, LANES), f32)
    for k, v in enumerate(ORDER):
        more = [c[k, rows:] for c in (c1, c2, c3, c4)]
        sums = jnp.zeros((rows, LANES), f32)
        for e, c in enumerate((c1, c2, c3, c4)):
            carry[k, e] = c[k, :rows]
            sums = sums + c[k, :rows] * px[k, e]

        def body(b, total, k=k, more=more):
            base = pl.multiple_of(b * 8, 8)
            r = [rx[k, e, pl.ds(base, 8), :] for e in range(4)]
            for o in range(8):
                x = x_ref[k, base + o]
                for e in range(4):
                    x = x + r[e][o : o + 1, :] * more[e]
                full_ref[k, base + o] = x
                total = total + x * proj[k, base + o]
            return total

        total = lax.fori_loop(0, half // 8, body, dots[k])
        total = total + jnp.sum(sums.reshape(rows // 8, 8, LANES), axis=0)
        total = jnp.sum(total, axis=0, keepdims=True)
        total = (total + swap(total)) * prm[v, 3:4, :] * (1.0 / cells)
        where = target[:, 64 * v : 64 * (v + 1)]
        where = jnp.concatenate([where, where], axis=1) - first_slot
        for s in range(capacity):
            mine = jnp.where((lane < 64) & (where == s), total, 0.0)
            owned = owned + jnp.where(lane == s, jnp.sum(mine, axis=1, keepdims=True), 0.0)
        if v == 0:
            for i, d in enumerate((d3, d4)):
                y = d[k, :rows]
                for e in range(4):
                    y = y + ry[k, e] * d[k, rows + e : rows + e + 1]
                col_ref[i] = y
    table[...] = owned


def end_kernel(
    rows, pairs, rq, place, prm, sigma, north, south, vert, bal, col, side, carry, rx_ref, ry_ref, u_ref, x_ref,
    out_ref, out, xs, zx, zc, wt, sg, sx, sems,
):
    g = pl.program_id(0)
    half = 2 * pairs
    lon = sigma.shape[2]
    merged = out.shape[2]
    steps = pairs // PAIRS

    def copy(v, side_at, step):
        first = pl.multiple_of((step * PAIRS + side_at * pairs) * LANES, LANES)
        cols = pl.ds(first, PAIRS * LANES)
        return pltpu.make_async_copy(out.at[v, :, cols], out_ref.at[v, :, cols], sems.at[v, side_at, step])

    @pl.when(g == 0)
    def _():
        for v in range(3):
            scaled = quad(vert[v]) * prm[v, 3:4, :]
            set_weights(wt, v, scaled.T, True)
        set_weights(wt, 3, quad(bal[...]).T, False)
        stage_sigma(sigma, sg, (0, 1, 2))
        for at in range(0, lon, LANES):
            width = min(LANES, lon - at)
            sx[at // LANES, 0:1, 0:width] = north[:, merged + at : merged + at + width]
            sx[at // LANES, 1:2, 0:width] = south[:, merged + at : merged + at + width]

    lane = lax.broadcasted_iota(jnp.int32, (rows, LANES), 1)
    high = (lane >= 64).astype(jnp.int32)
    high8 = high[0:8]
    chi_row = prm[0, 2:3, :]

    def at_tile(m):
        return pl.ds(pl.multiple_of(m * LANES, LANES), LANES)

    row8 = lax.broadcasted_iota(jnp.int32, (8, LANES), 0)
    beyond = [None] * (2 * PAIRS)
    for k, v in enumerate(ORDER):
        for q in range(0, rows, rq):
            c = [carry[k, e, q : q + rq, :] for e in range(4)]
            ry = [ry_ref[k, e, q : q + rq, :] for e in range(4)]
            rx = [rx_ref[k, e, pl.ds(pl.multiple_of(g * 2 * PAIRS, 8), 2 * PAIRS), :] for e in range(4)]
            for p in range(2 * PAIRS):
                x = x_ref[k, p]
                y = u_ref[k, p, q : q + rq, :]
                for e in range(4):
                    y = y + rx[e][p : p + 1, :] * c[e] + ry[e] * x[e : e + 1, :]
                at = (p // 2) * rows + q
                xs[k, at : at + rq, (p % 2) * LANES : (p % 2 + 1) * LANES] = y
                if v == 0 and q == 0:
                    x = pltpu.roll(x, 6, 0)
                    above = jnp.where(place[0] > 0, x + prm[0, 1:2, :] * y[0:1, :], 0.0)
                    beyond[p] = jnp.where(row8 == 0, above, jnp.where(row8 == 1, x, 0.0))

    @pl.when(g == 0)
    def _():
        first = col[0] + prm[0, 1:2, :] * xs[ORDER.index(0), 0:rows, 0:LANES]
        lhs = jnp.where(lane < 64, jnp.where(place[1] > 0, first, 0.0), col[1])
        lhs = jnp.concatenate([lhs, jnp.zeros_like(lhs)], axis=1)
        res = product(lhs, weight(wt, 0))
        zc[0] = swap(res[:, :LANES] * swap(side[0]))
        zc[1] = res[:, LANES:] * side[1]

    lhs = jnp.concatenate(
        [jnp.concatenate(beyond[2 * p : 2 * p + 2], axis=1) for p in range(PAIRS)], axis=0
    )
    res = product(lhs, weight(wt, 0))
    for p in range(PAIRS):
        m = g * PAIRS + p
        for side in range(2):
            tile = m + side * pairs
            s = jnp.take_along_axis(sx[tile >> 6], 2 * (tile & 63) + high8, axis=1, mode="promise_in_bounds")
            part = res[p * 8 : (p + 1) * 8, side * LANES : (side + 1) * LANES]
            zx[:, at_tile(tile)] = jnp.where(row8 < 2, part * s, 0.0)
    results = {v: product(xs[k], weight(wt, v)) for k, v in enumerate(ORDER)}
    for p in range(PAIRS):
        m = g * PAIRS + p
        for side in range(2):
            at = at_tile(m + side * pairs)
            z = [
                results[v][p * rows : (p + 1) * rows, side * LANES : (side + 1) * LANES]
                * sigma_tile(sg, v, m + side * pairs, high)
                for v in range(3)
            ]
            out[0, :, at] = z[0]
            out[1, :, at] = z[1] + chi_row * z[0]
            out[2, :, at] = z[2]
    for v in range(2):
        for side_at in range(2):
            copy(v, side_at, g).start()

    @pl.when(g == pl.num_programs(0) - 1)
    def _():
        row_id = lax.broadcasted_iota(jnp.int32, (rows, LANES), 0)
        last = half - 1

        def body(b, _):
            for p in range(PAIRS):
                for side in range(2):
                    m = b * PAIRS + p + side * pairs
                    x = out[0, :, at_tile(m)]
                    left = jnp.where(m == 0, zc[0], out[0, :, at_tile(jnp.maximum(m - 1, 0))])
                    right = jnp.where(m == last, zc[1], out[0, :, at_tile(jnp.minimum(m + 1, last))])
                    beside = swap(x + jnp.where(lane >= 64, left, right))
                    above = jnp.where(row_id == 0, zx[0:1, at_tile(m)], pltpu.roll(x, 1, 0))
                    below = jnp.where(row_id == rows - 1, zx[1:2, at_tile(m)], pltpu.roll(x, rows - 1, 0))
                    lap = 4.0 * x - beside - above - below
                    xs[0, p * rows : (p + 1) * rows, side * LANES : (side + 1) * LANES] = lap
            res = product(xs[0], weight(wt, 3))
            for p in range(PAIRS):
                for side in range(2):
                    at = at_tile(b * PAIRS + p + side * pairs)
                    part = res[p * rows : (p + 1) * rows, side * LANES : (side + 1) * LANES]
                    out[2, :, at] = out[2, :, at] + part
            for side_at in range(2):
                copy(2, side_at, b).start()
            return 0

        lax.fori_loop(0, steps, body, 0)
        for v in range(3):
            for side_at in range(2):
                for step in range(steps):
                    copy(v, side_at, step).wait()


def shards(state, sigma, vert, bal_temp, chi_coef, scales, classes, owner):
    n_lat = lax.axis_size("lat")
    n_lon = lax.axis_size("lon")
    devices = n_lat * n_lon
    nvars, rows, merged = state.shape
    levels = vert.shape[1]
    lon = merged // levels
    half = lon // 2
    pairs = half // 2
    pieces = (lon + LANES - 1) // LANES
    count = nvars * levels
    capacity = (count + devices - 1) // devices + 1
    i_lat = lax.axis_index("lat")
    i_lon = lax.axis_index("lon")

    up_lat, up_lon = ([(i, i + 1) for i in range(n - 1)] for n in (n_lat, n_lon))
    down_lat, down_lon = ([(j, i) for i, j in up] for up in (up_lat, up_lon))

    def row(i):
        return jnp.concatenate([state[2, i : i + 1, :], sigma[0, i : i + 1, :]], axis=1)

    north = lax.ppermute(row(rows - 1), "lat", up_lat)
    south = lax.ppermute(row(0), "lat", down_lat)
    west = lax.ppermute(state[2, :, merged - levels :], "lon", up_lon)
    east = lax.ppermute(state[2, :, :levels], "lon", down_lon)
    place = jnp.stack([i_lat, i_lon]).astype(jnp.int32)

    anywhere = pl.BlockSpec(memory_space=pl.ANY)
    steps = pairs // BLOCK

    def part(v, side):
        return pl.BlockSpec((1, rows, BLOCK * LANES), lambda g: (v, 0, g + side * steps))

    width = half // n_lat
    shapes = [(nvars, half, rows, LANES), (nvars, rows, half, LANES), (n_lat, nvars, 4 * width, LANES)]
    shapes.append((nvars, half, 8, LANES))

    def lat_call(nv, first, body, arrays, specs, name, aliases, more=()):
        return pl.pallas_call(
            body,
            grid=(steps,),
            in_specs=specs,
            out_specs=[
                pl.BlockSpec((nv, 2 * BLOCK, rows, LANES), lambda g: (first, g, 0, 0)),
                pl.BlockSpec((nv, rows, 2 * BLOCK, LANES), lambda g: (first, 0, g, 0)),
                pl.BlockSpec((2 * BLOCK // width, nv, 4 * width, LANES), lambda g: (g, first, 0, 0)),
                pl.BlockSpec((nv, 2 * BLOCK, 8, LANES), lambda g: (first, g, 0, 0)),
            ]
            + [full(s) for s in more],
            out_shape=[jax.ShapeDtypeStruct(s, f32) if n == 2 else pltpu.HBM(s, f32) for n, s in enumerate(shapes)]
            + [jax.ShapeDtypeStruct(s, f32) for s in more],
            scratch_shapes=[
                pltpu.VMEM((2, PAIRS * rows, 256), f32),
                pltpu.VMEM((2 * 768, 256), bf16),
                pltpu.VMEM((nvars, pieces, rows, LANES), f32),
            ],
            compiler_params=params(),
            cost_estimate=pl.CostEstimate(
                flops=nv * 60000000, bytes_accessed=nv * 3 * rows * merged * 4, transcendentals=0
            ),
            input_output_aliases=aliases,
            name=name,
        )(*arrays)

    ins = [scales.reshape(1, -1), classes.reshape(1, count), chi_coef.reshape(1, levels), sigma, vert] + [state] * 4
    specs = [full(x.shape) for x in ins[:5]] + [part(1, 0), part(1, 1), part(2, 0), part(2, 1)]
    ins = [in_hbm(x) for x in ins]
    body = functools.partial(lat_plain, rows, pairs)
    *wue, prm = lat_call(2, 0, body, ins, specs, "lat_chi_temp", {}, [(nvars, 4, LANES)])
    ins = [prm] + [in_hbm(x) for x in [sigma, vert, bal_temp] + [state] * 10] + [north, south, west, east]
    ins += [in_hbm(wue[0]), in_hbm(wue[1]), wue[2], in_hbm(wue[3])]
    specs = [full(x.shape) for x in ins[:4]] + [part(0, 0), part(0, 1), part(1, 0), part(1, 1)]

    def tile(side, step):
        last = 2 * pairs - 1
        return pl.BlockSpec(
            (1, rows, LANES), lambda g: (2, 0, jnp.clip(g * BLOCK + side * pairs + step, 0, last))
        )

    specs += [part(2, 0), part(2, 1), tile(0, -1), tile(0, BLOCK), tile(1, -1), tile(1, BLOCK)]
    specs += [full(x.shape) for x in (north, south, west, east)] + [anywhere] * 4
    aliases = {18: 0, 19: 1, 20: 2, 21: 3}
    w, u, edges, proj = lat_call(1, 2, functools.partial(lat_balance, rows, pairs), ins, specs, "lat_psi", aliases)
    def trade(x, axis):
        return lax.all_to_all(x, axis, split_axis=0, concat_axis=0, tiled=True)

    shares = trade(edges, "lat")

    rb = BLOCK
    local, el, es, px, dots, rx, ry = pl.pallas_call(
        functools.partial(lon_kernel, rows, rb),
        grid=(rows // rb,),
        in_specs=[
            full(prm.shape),
            anywhere,
            anywhere,
        ],
        out_specs=[
            anywhere,
            full((nvars, 4, rows, LANES)),
            full((6, rows, LANES)),
            full((nvars, 4, rows, LANES)),
            full((nvars, 8, LANES)),
            full((nvars, 4, half, LANES)),
            full((nvars, 4, rows, LANES)),
        ],
        out_shape=[
            pltpu.HBM((nvars, half, rows, LANES), f32),
            pltpu.HBM((nvars, 4, rows, LANES), f32),
            jax.ShapeDtypeStruct((6, rows, LANES), f32),
            pltpu.HBM((nvars, 4, rows, LANES), f32),
            pltpu.HBM((nvars, 8, LANES), f32),
            pltpu.HBM((nvars, 4, half, LANES), f32),
            pltpu.HBM((nvars, 4, rows, LANES), f32),
        ],
        scratch_shapes=[pltpu.VMEM((rows // rb, nvars, rb, half, LANES), f32)]
        + [pltpu.VMEM((nvars, half, rb, LANES), f32)] * 2
        + [pltpu.SemaphoreType.DMA((2 + rows // rb,))],
        compiler_params=params(),
        cost_estimate=pl.CostEstimate(
            flops=180000000, bytes_accessed=6 * rows * merged * 4, transcendentals=0
        ),
        name="lon_tile",
    )(prm, *[in_hbm(x) for x in (u, w)])

    def round_lon(x):
        return [x] + [
            lax.ppermute(x, "lon", [(i, i ^ s) for i in range(n_lon)]) for s in range(1, n_lon)
        ]

    shares, _ = lax.optimization_barrier((shares, es))
    sent = round_lon(es)
    carries = pl.pallas_call(
        functools.partial(solve_kernel, n_lat, rows),
        grid=(1,),
        in_specs=[full(prm.shape), full(shares.shape)],
        out_specs=full(shares.shape),
        out_shape=jax.ShapeDtypeStruct(shares.shape, f32),
        compiler_params=params(),
        cost_estimate=pl.CostEstimate(flops=1000000, bytes_accessed=2 * shares.size * 4, transcendentals=0),
        name="solve",
    )(prm, shares)
    carries = trade(carries, "lat")

    crossed, elc, esc = pl.pallas_call(
        carry_kernel,
        grid=(1,),
        in_specs=[full(prm.shape), pl.BlockSpec((1, rows, lon), lambda g: (0, 0, 0)), full(carries.shape)],
        out_specs=[full((nvars, half, 8, LANES)), full((nvars, 4, 8, LANES)), full((7, 8, LANES))],
        out_shape=[
            jax.ShapeDtypeStruct((nvars, half, 8, LANES), f32),
            jax.ShapeDtypeStruct((nvars, 4, 8, LANES), f32),
            jax.ShapeDtypeStruct((7, 8, LANES), f32),
        ],
        compiler_params=params(),
        cost_estimate=pl.CostEstimate(
            flops=30000000, bytes_accessed=4 * nvars * 12 * half * LANES, transcendentals=0
        ),
        name="lon_carry",
    )(prm, in_hbm(sigma), carries)
    sent_x = round_lon(esc)

    packed = 2 * PAIRS

    def columns(r):
        return pl.BlockSpec((nvars, packed, r, LANES), lambda g: (0, g, 0, 0))

    index = jnp.arange(count, dtype=jnp.int32)
    same = (owner[:, None] == owner[None, :]) & (index[None, :] < index[:, None])
    target = (owner * capacity + jnp.sum(same.astype(jnp.int32), axis=1)).reshape(1, count)

    ins = [in_hbm(x) for x in (proj, px, dots, rx, ry, el)]
    ins = [place, target, prm, crossed] + ins + [elc] + sent + sent_x
    specs = [full(x.shape) for x in ins]
    specs[0] = pl.BlockSpec(memory_space=pltpu.SMEM)
    shapes = [(nvars, 4, rows, LANES), (nvars, half, 8, LANES), (2, rows, LANES), (2, rows, LANES)]
    carry, crossed, col, side, table = pl.pallas_call(
        functools.partial(close_kernel, n_lon, rows, devices, capacity, devices * rows * lon),
        grid=(1,),
        in_specs=specs,
        out_specs=[full(x) for x in shapes] + [full((devices, LANES))],
        out_shape=[pltpu.HBM(x, f32) for x in shapes] + [jax.ShapeDtypeStruct((devices, LANES), f32)],
        scratch_shapes=[pltpu.VMEM((n_lon, 6, rows, LANES), f32), pltpu.VMEM((n_lon, 7, 8, LANES), f32)],
        compiler_params=params(),
        cost_estimate=pl.CostEstimate(flops=10000000, bytes_accessed=4000000, transcendentals=0),
        name="close",
    )(*ins)
    table = trade(table, ("lat", "lon"))
    slab_energy = jnp.sum(table, axis=0, keepdims=True)[:, :capacity]

    ins = [prm, sigma, north, south, vert, bal_temp, col, side, carry, rx, ry, local, crossed]
    ins = [place] + [in_hbm(x) for x in ins]
    specs = [full(x.shape) for x in ins]
    specs[0] = pl.BlockSpec(memory_space=pltpu.SMEM)
    specs[-2:] = [columns(rows), columns(8)]
    applied = pl.pallas_call(
        functools.partial(end_kernel, rows, pairs, 24),
        grid=(half // packed,),
        in_specs=specs,
        out_specs=anywhere,
        out_shape=jax.ShapeDtypeStruct(state.shape, f32),
        scratch_shapes=[
            pltpu.VMEM(state.shape, f32),
            pltpu.VMEM((nvars, PAIRS * rows, 256), f32),
            pltpu.VMEM((8, merged), f32),
            pltpu.VMEM((2, rows, LANES), f32),
            pltpu.VMEM((4 * 768, 256), bf16),
            pltpu.VMEM((nvars, pieces, rows, LANES), f32),
            pltpu.VMEM((pieces, 8, LANES), f32),
            pltpu.SemaphoreType.DMA((3, 2, pairs // PAIRS)),
        ],
        compiler_params=params(),
        cost_estimate=pl.CostEstimate(
            flops=300000000, bytes_accessed=6 * rows * merged * 4, transcendentals=0
        ),
        name="finish",
    )(*ins)
    return (applied, slab_energy)


def solution(mesh):
    return jax.shard_map(
        shards,
        mesh=mesh,
        in_specs=(P(None, "lat", "lon"), P(None, "lat", "lon"), P(), P(), P(), P(), P(), P()),
        out_specs=(P(None, "lat", "lon"), P(("lat", "lon"), None)),
        check_vma=False,
    )
```

```python
import functools

import jax
import jax.numpy as jnp
from jax import lax
from jax.experimental import pallas as pl
from jax.experimental.pallas import tpu as pltpu
from jax.sharding import PartitionSpec as P

highest = lax.Precision.HIGHEST
f32 = jnp.float32
bf16 = jnp.bfloat16
LANES = 128
PAIRS = 8
BLOCK = 24
ORDER = (1, 2, 0)
LIMIT = 30 * 1024 * 1024


def params():
    return pltpu.CompilerParams(vmem_limit_bytes=LIMIT)


def in_hbm(x):
    return pltpu.with_memory_space_constraint(x, pltpu.HBM)


def full(shape):
    return pl.BlockSpec(shape, lambda g: (0,) * len(shape))


def swap(x):
    return pltpu.roll(x, 64, x.ndim - 1)


def low_lanes(shape):
    return lax.broadcasted_iota(jnp.int32, shape, len(shape) - 1) < 64


def halves(x):
    hi = x.astype(bf16)
    return hi, (x - hi.astype(f32)).astype(bf16)


def dot(x, y):
    return jnp.dot(x, y, preferred_element_type=f32)


def split(x):
    hi, lo = halves(x)
    return jnp.concatenate([hi, lo, hi], axis=1)


def product(x, weights):
    return dot(split(x), weights)


def expand(mat, mixed):
    wide = quad(mat)
    wide = jnp.concatenate([wide, wide], axis=1)
    wide = jnp.concatenate([wide, wide], axis=0)
    src = lax.broadcasted_iota(jnp.int32, (256, 256), 0) // 64
    dst = lax.broadcasted_iota(jnp.int32, (256, 256), 1) // 64
    if mixed:
        src = jnp.where(src == 1, 2, jnp.where(src == 2, 1, src))
    return halves(jnp.where(src == dst, wide, 0.0))


def quad(mat):
    if mat.shape[0] == LANES:
        return mat
    wide = jnp.concatenate([mat, mat], axis=1)
    return jnp.concatenate([wide, wide], axis=0)


def constants(length, decay, m):
    span = jnp.exp(-float(m) / length)
    d = 1.0 - decay * decay
    k1 = decay * (1.0 - span * span) / d
    k2 = (m * span - decay * decay * (span - span * span * span) / d) / d
    tail = decay * decay * (1.0 + span * span) * (1.0 - span * span) / d
    k3 = decay / (d * d) * (1.0 - (2.0 * m + 1.0) * span * span + tail)
    return span, k1, k2, k3


def responses(length, decay, m):
    j = lax.broadcasted_iota(jnp.int32, (m, LANES), 0).astype(f32)
    up = jnp.exp(-j / length)
    down = jnp.exp(-(m - j) / length)
    span = jnp.exp(-float(m) / length)
    d = 1.0 - decay * decay
    diff = up - span * down
    g3 = decay * diff / d
    g2 = ((m - j) * down - decay * decay * (span * up - span * span * down) / d) / d
    part = decay * decay * (1.0 + span * span) * diff / d
    g1 = decay / (d * d) * ((j + 1.0) * up - (2.0 * m + 1.0 - j) * span * down + part)
    return g1, g2, g3, down


def pick(all_carries, me):
    out = []
    for cs in all_carries:
        mine = cs[0]
        for t in range(1, len(cs)):
            mine = jnp.where(me == t, cs[t], mine)
        out.append(mine)
    return out


def solve_carries(n, edge, const):
    span, k1, k2, k3 = const
    first = edge(0, 0)
    zero = jnp.zeros_like(first)
    e1 = [first] + [edge(t, 0) for t in range(1, n)]
    c1, c2, c3, c4 = ([None] * n for _ in range(4))
    c = zero
    for t in range(n):
        c1[t] = c
        c = e1[t] + span * c
    c = zero
    for t in reversed(range(n)):
        c2[t] = c
        c = edge(t, 1) + k1 * c1[t] + span * c
    c = zero
    for t in range(n):
        c3[t] = c
        c = edge(t, 2) + k2 * c1[t] + k1 * c2[t] + span * c
    c = zero
    for t in reversed(range(n)):
        c4[t] = c
        c = edge(t, 3) + k3 * c1[t] + k2 * c2[t] + k1 * c3[t] + span * c
    return c1, c2, c3, c4


def cascade(count, load, store, decay, start):
    step = 24
    edges = []
    for stage in range(4):
        back = stage % 2 == 1

        def body(b, states, back=back):
            base = (count // step - 1 - b) * step if back else b * step
            order = range(step - 1, -1, -1) if back else range(step)
            for o in order:
                new = [decay_k * s + x for decay_k, s, x in zip(decay, states, load(base + o))]
                store(base + o, new)
                states = new
            return tuple(states)

        states = lax.fori_loop(0, count // step, body, tuple(start))
        edges.append(list(states))
    return edges


def stage_sigma(sigma, sg, variables):
    lon = sigma.shape[2]
    for v in variables:
        for at in range(0, lon, LANES):
            width = min(LANES, lon - at)
            sg[v, at // LANES, :, 0:width] = sigma[v, :, at : at + width]


def sigma_tile(sg, v, m, high):
    idx = 2 * (m & 63) + high
    return jnp.take_along_axis(sg[v, m >> 6], idx, axis=1, mode="promise_in_bounds")


def set_weights(weights, k, mat, mixed):
    hi, lo = expand(mat, mixed)
    weights[768 * k : 768 * k + 256] = hi
    weights[768 * k + 256 : 768 * k + 512] = hi
    weights[768 * k + 512 : 768 * k + 768] = lo


def weight(weights, k):
    return weights[768 * k : 768 * (k + 1)]


def lat_filter(vs, rows, prm, u_ref, e_ref, p_ref):
    nv = len(vs)
    decay = [prm[v, 1:2, :] for v in vs]

    def load(i):
        return [u_ref[k, i] for k in range(nv)]

    def store(i, values):
        for k in range(nv):
            u_ref[k, i] = values[k]

    zero = jnp.zeros((u_ref.shape[2], LANES), f32)
    edges = cascade(rows, load, store, decay, [zero] * nv)
    for k in range(nv):
        for j in range(0, u_ref.shape[2], 8):
            block = [edges[3 - e][k][j : j + 8] * decay[k] for e in range(4)]
            block = jnp.stack(block + [jnp.zeros((8, LANES), f32)] * 4)
            p_ref[k, j : j + 8] = jnp.swapaxes(block, 0, 1)
    width = e_ref.shape[2] // 4
    for e in range(4):
        for k in range(nv):
            for c in range(e_ref.shape[0]):
                e_ref[c, k, e * width : (e + 1) * width] = edges[e][k][c * width : (c + 1) * width]


def put_mixed(k, b, rows, res, w_ref, u_ref):
    base = b * 2 * PAIRS
    for p in range(PAIRS):
        part = res[p * rows : (p + 1) * rows]
        w_ref[k, base + 2 * p] = part[:, :LANES]
        w_ref[k, base + 2 * p + 1] = part[:, LANES:]
    at = pl.ds(pl.multiple_of(base, 2 * PAIRS), 2 * PAIRS)
    u_ref[k, :, at, :] = jnp.swapaxes(w_ref[k, at], 0, 1)


def set_params(scales, classes, chi_coef, prm):
    coef = jnp.concatenate([chi_coef[...], chi_coef[...]], axis=1)
    for v in range(3):
        kind = classes[:, 64 * v : 64 * (v + 1)]
        kind = jnp.concatenate([kind, kind], axis=1)
        length = jnp.zeros((1, LANES), f32)
        for n in range(scales.shape[1]):
            length = jnp.where(kind == n, scales[:, n : n + 1], length)
        decay = jnp.exp(-1.0 / length)
        norm = 1.0 - decay
        norm = norm * norm
        norm = norm * norm
        prm[v, 0:1, :] = length
        prm[v, 1:2, :] = decay
        prm[v, 2:3, :] = coef
        prm[v, 3:4, :] = length * jnp.sqrt(length) * norm * norm


def lat_plain(
    rows, pairs, scales, classes, chi_coef, sigma, vert, b1lo, b1hi, b2lo, b2hi,
    w_ref, u_ref, e_ref, p_ref, prm, xs, wt, sg,
):
    g = pl.program_id(0)

    @pl.when(g == 0)
    def _():
        set_params(scales, classes, chi_coef, prm)
        set_weights(wt, 0, vert[1], True)
        set_weights(wt, 1, vert[2], True)
        stage_sigma(sigma, sg, (1, 2))

    lane = lax.broadcasted_iota(jnp.int32, (rows, LANES), 1)
    high = (lane >= 64).astype(jnp.int32)

    def body(b, _):
        for p in range(PAIRS):
            at = slice(p * rows, (p + 1) * rows)
            cols = pl.ds(pl.multiple_of((b * PAIRS + p) * LANES, LANES), LANES)
            m = g * BLOCK + b * PAIRS + p
            for k, sides in enumerate(((b1lo, b1hi), (b2lo, b2hi))):
                for side in range(2):
                    s = sigma_tile(sg, k + 1, m + side * pairs, high)
                    xs[k, at, side * LANES : (side + 1) * LANES] = sides[side][0, :, cols] * s
        for k in range(2):
            put_mixed(k, b, rows, product(xs[k], weight(wt, k)), w_ref, u_ref)
        return 0

    lax.fori_loop(0, BLOCK // PAIRS, body, 0)
    lat_filter((1, 2), rows, prm, u_ref, e_ref, p_ref)


def lat_balance(
    rows, pairs, prm, sigma, vert, bal, plo, phi, clo, chi, tlo, thi, tll, tlr, thl, thr, north, south, west, east, w_in, u_in, e_in, p_in,
    w_ref, u_ref, e_ref, p_ref, xs, wt, sg,
):
    del w_in, u_in, e_in, p_in
    g = pl.program_id(0)

    @pl.when(g == 0)
    def _():
        set_weights(wt, 0, vert[0], True)
        (bh, bl), (vh, vl) = halves(bal[...]), halves(vert[0])
        set_weights(wt, 1, dot(bh, vh) + dot(bl, vh) + dot(bh, vl), True)
        stage_sigma(sigma, sg, (0,))

    lane = lax.broadcasted_iota(jnp.int32, (rows, LANES), 1)
    row_id = lax.broadcasted_iota(jnp.int32, (rows, LANES), 0)
    high = (lane >= 64).astype(jnp.int32)
    chi_row = prm[0, 2:3, :]
    last = 2 * pairs - 1
    beyond = [jnp.concatenate([x[...], x[...]], axis=1) for x in (west, east)]

    def at_tile(m):
        return pl.ds(pl.multiple_of(m * LANES, LANES), LANES)

    sides = ((tlo, tll, tlr), (thi, thl, thr))

    def laplace(b, o, side):
        temp, before, after = sides[side]
        p = b * PAIRS + o
        m = g * BLOCK + p + side * pairs
        x = temp[0, :, at_tile(p)]
        left = temp[0, :, at_tile(jnp.maximum(p - 1, 0))]
        if o == 0:
            left = jnp.where(p == 0, before[0], left)
            if side == 0:
                left = jnp.where(m == 0, beyond[0], left)
        right = temp[0, :, at_tile(jnp.minimum(p + 1, BLOCK - 1))]
        if o == PAIRS - 1:
            right = jnp.where(p == BLOCK - 1, after[0], right)
            if side == 1:
                right = jnp.where(m == last, beyond[1], right)
        beside = swap(x + jnp.where(lane >= 64, left, right))
        above = jnp.where(row_id == 0, north[:, at_tile(m)], pltpu.roll(x, 1, 0))
        below = jnp.where(row_id == rows - 1, south[:, at_tile(m)], pltpu.roll(x, rows - 1, 0))
        return 4.0 * x - beside - above - below

    def body(b, _):
        for p in range(PAIRS):
            at = slice(p * rows, (p + 1) * rows)
            cols = at_tile(b * PAIRS + p)
            m = g * BLOCK + b * PAIRS + p
            for side, (pr, cr) in enumerate(((plo, clo), (phi, chi))):
                s = sigma_tile(sg, 0, m + side * pairs, high)
                to = slice(side * LANES, (side + 1) * LANES)
                xs[0, at, to] = (pr[0, :, cols] + chi_row * cr[0, :, cols]) * s
                xs[1, at, to] = laplace(b, p, side) * s
        res = dot(jnp.concatenate([split(xs[0]), split(xs[1])], axis=1), wt[...])
        put_mixed(0, b, rows, res, w_ref, u_ref)
        return 0

    lax.fori_loop(0, BLOCK // PAIRS, body, 0)
    lat_filter((0,), rows, prm, u_ref, e_ref, p_ref)


def lon_filter(prm, rb, o_ref, el_ref, put, at):
    half = o_ref.shape[1]
    nv = len(ORDER)
    decay = [prm[v, 1:2, :] for v in ORDER]

    def load(j):
        return [o_ref[k, j] for k in range(nv)]

    def store(j, values):
        for k in range(nv):
            o_ref[k, j] = values[k]

    edges = cascade(half, load, store, decay, [jnp.zeros((rb, LANES), f32)] * nv)
    low = low_lanes((rb, LANES))
    for k, v in enumerate(ORDER):
        span, k1, k2, k3 = constants(prm[v, 0:1, :], prm[v, 1:2, :], half)
        e1, e2, e3, e4 = (edges[e][k] for e in range(4))
        c1 = jnp.where(low, 0.0, swap(e1))
        t1 = e1 + span * c1
        t2 = e2 + k1 * c1
        c2 = jnp.where(low, swap(t2), 0.0)
        t2 = t2 + span * c2
        t3 = e3 + k2 * c1 + k1 * c2
        c3 = jnp.where(low, 0.0, swap(t3))
        t3 = t3 + span * c3
        t4 = e4 + k3 * c1 + k2 * c2 + k1 * c3
        c4 = jnp.where(low, swap(t4), 0.0)
        t4 = t4 + span * c4
        put(2 * k, jnp.where(low, t2, t1))
        put(2 * k + 1, jnp.where(low, t4, t3))
        for e, x in enumerate((e1, e2, e3, e4)):
            el_ref[k, e, at, :] = x


def lon_kernel(
    rows, rb, prm, u_ref, o_ref, el_ref, es_ref, rx_ref, ry_ref
):
    g = pl.program_id(0)
    half = u_ref.shape[2]
    at = pl.ds(pl.multiple_of(g * rb, 8), rb)

    @pl.when(g == 0)
    def _():
        for k, v in enumerate(ORDER):
            for e, r in enumerate(responses(prm[v, 0:1, :], prm[v, 1:2, :], half)):
                rx_ref[k, e] = r
            for e, r in enumerate(responses(prm[v, 0:1, :], prm[v, 1:2, :], rows)):
                ry_ref[k, e] = r

    def turn(b, _):
        at = pl.ds(pl.multiple_of(b * 8, 8), 8)
        for k in range(len(ORDER)):
            for q in range(0, rb, 8):
                o_ref[k, at, q : q + 8, :] = jnp.swapaxes(u_ref[k, q : q + 8, at, :], 0, 1)
        return 0

    lax.fori_loop(0, half // 8, turn, 0)

    def put(i, x):
        es_ref[i, at, :] = x

    lon_filter(prm, rb, o_ref, el_ref, put, at)


def energy_kernel(rows, rq, w_ref, u_ref, rx_ref, px_ref, dot_ref):
    g = pl.program_id(0)
    count = w_ref.shape[1]

    @pl.when(g == 0)
    def _():
        px_ref[...] = jnp.zeros_like(px_ref)
        dot_ref[...] = jnp.zeros_like(dot_ref)

    for k in range(len(ORDER)):
        rx = [rx_ref[k, e, pl.ds(pl.multiple_of(g * count, 8), count), :] for e in range(4)]
        for q in range(0, rows, rq):
            sums = [px_ref[k, e, q : q + rq, :] for e in range(4)] + [jnp.zeros((rq, LANES), f32)]
            for p in range(count):
                x = w_ref[k, p, q : q + rq, :]
                sums[4] = sums[4] + x * u_ref[k, p, q : q + rq, :]
                for e in range(4):
                    sums[e] = sums[e] + x * rx[e][p : p + 1, :]
            for e in range(4):
                px_ref[k, e, q : q + rq, :] = sums[e]
            dot_ref[k] += jnp.sum(sums[4].reshape(rq // 8, 8, LANES), axis=0)


def solve_kernel(n_lat, rows, prm, edges, carries):
    width = edges.shape[2] // 4
    for k, v in enumerate(ORDER):
        const = constants(prm[v, 0:1, :], prm[v, 1:2, :], rows)
        c = solve_carries(n_lat, lambda t, e: edges[t, k, e * width : (e + 1) * width, :], const)
        for e in range(4):
            for t in range(n_lat):
                carries[t, k, e * width : (e + 1) * width, :] = c[e][t]


def carry_kernel(prm, sigma, carries, o_ref, el_ref, es_ref):
    width = carries.shape[2] // 4
    zero = jnp.zeros((8, LANES), f32)

    def body(d, _):
        for k in range(len(ORDER)):
            for j in range(width):
                at = d * width + j
                o_ref[k, at] = zero
                for e in range(4):
                    o_ref[k, at, e : e + 1, :] = carries[d, k, e * width + j : e * width + j + 1, :]
        return 0

    lax.fori_loop(0, carries.shape[0], body, 0)

    def put(i, x):
        es_ref[i] = x

    lon_filter(prm, 8, o_ref, el_ref, put, slice(0, 8))
    x = sigma[0]
    rows, lon = x.shape
    outer = jnp.where(low_lanes((rows, LANES)), x[:, 0:1], x[:, lon - 1 : lon])
    outer = jnp.concatenate([outer, jnp.zeros((LANES - rows, LANES), f32)], axis=0).T
    es_ref[6] = jnp.concatenate([outer[0:1], outer[64:65], jnp.zeros((6, LANES), f32)], axis=0)


def close_kernel(
    n_lon, rows, devices, capacity, cells, place, target, prm, x_ref, proj, px, dots, rx, ry, el, elc, *rest
):
    sent, sent_x = rest[:n_lon], rest[n_lon : 2 * n_lon]
    carry, full_ref, col_ref, side_ref, table, esm, esx = rest[2 * n_lon :]
    half = rx.shape[2]
    me = place[1]
    for d in range(n_lon):
        esm[me ^ d] = sent[d][...]
        esx[me ^ d] = sent_x[d][...]
    pad = jnp.zeros((LANES - 8, LANES), f32)
    for i, t in enumerate((jnp.maximum(me - 1, 0), jnp.minimum(me + 1, n_lon - 1))):
        outer = jnp.concatenate([esx[t, 6], pad], axis=0).T[:rows, 1 - i : 2 - i]
        side_ref[i] = jnp.broadcast_to(outer, (rows, LANES))
    length = jnp.stack([prm[v, 0:1, :] for v in ORDER])
    decay = jnp.stack([prm[v, 1:2, :] for v in ORDER])
    whole = constants(length, decay, 2 * half)
    span, k1, k2, k3 = constants(length, decay, half)
    low = low_lanes((len(ORDER), rows + 8, LANES))
    cache = {}

    def both(main, more):
        parts = [jnp.concatenate([main(k), more(k)], axis=0) for k in range(len(ORDER))]
        return jnp.stack(parts)

    def edge(t, e):
        i = e // 2
        if (t, i) not in cache:
            x = both(lambda k: esm[t, 2 * k + i], lambda k: esx[t, 2 * k + i])
            y = swap(x)
            cache[t, i] = (jnp.where(low, y, x), jnp.where(low, x, y))
        return cache[t, i][e % 2]

    d1, d2, d3, d4 = pick(solve_carries(n_lon, edge, whole), me)
    e1, e2, e3, e4 = (both(lambda k, e=e: el[k, e], lambda k, e=e: elc[k, e]) for e in range(4))
    c1 = jnp.where(low, d1, swap(e1 + span * d1))
    c2 = jnp.where(low, swap(e2 + k1 * c1 + span * d2), d2)
    c3 = jnp.where(low, d3, swap(e3 + k2 * c1 + k1 * c2 + span * d3))
    c4 = jnp.where(low, swap(e4 + k3 * c1 + k2 * c2 + k1 * c3 + span * d4), d4)
    lane = lax.broadcasted_iota(jnp.int32, (devices, LANES), 1)
    first_slot = lax.broadcasted_iota(jnp.int32, (devices, LANES), 0) * capacity
    owned = jnp.zeros((devices, LANES), f32)
    for k, v in enumerate(ORDER):
        more = [c[k, rows:] for c in (c1, c2, c3, c4)]
        sums = jnp.zeros((rows, LANES), f32)
        for e, c in enumerate((c1, c2, c3, c4)):
            carry[k, e] = c[k, :rows]
            sums = sums + c[k, :rows] * px[k, e]

        def body(b, total, k=k, more=more):
            base = pl.multiple_of(b * 8, 8)
            r = [rx[k, e, pl.ds(base, 8), :] for e in range(4)]
            for o in range(8):
                x = x_ref[k, base + o]
                for e in range(4):
                    x = x + r[e][o : o + 1, :] * more[e]
                full_ref[k, base + o] = x
                total = total + x * proj[k, base + o]
            return total

        total = lax.fori_loop(0, half // 8, body, dots[k])
        total = total + jnp.sum(sums.reshape(rows // 8, 8, LANES), axis=0)
        total = jnp.sum(total, axis=0, keepdims=True)
        total = (total + swap(total)) * prm[v, 3:4, :] * (1.0 / cells)
        where = target[:, 64 * v : 64 * (v + 1)]
        where = jnp.concatenate([where, where], axis=1) - first_slot
        for s in range(capacity):
            mine = jnp.where((lane < 64) & (where == s), total, 0.0)
            owned = owned + jnp.where(lane == s, jnp.sum(mine, axis=1, keepdims=True), 0.0)
        if v == 0:
            for i, d in enumerate((d3, d4)):
                y = d[k, :rows]
                for e in range(4):
                    y = y + ry[k, e] * d[k, rows + e : rows + e + 1]
                col_ref[i] = y
    table[...] = owned


def end_kernel(
    rows, pairs, rq, place, prm, sigma, north, south, vert, bal, col, side, carry, rx_ref, ry_ref, u_ref, x_ref,
    out_ref, out, xs, zx, zc, wt, sg, sx, sems,
):
    g = pl.program_id(0)
    half = 2 * pairs
    lon = sigma.shape[2]
    merged = out.shape[2]
    steps = pairs // PAIRS

    def copy(v, side_at, step):
        first = pl.multiple_of((step * PAIRS + side_at * pairs) * LANES, LANES)
        cols = pl.ds(first, PAIRS * LANES)
        return pltpu.make_async_copy(out.at[v, :, cols], out_ref.at[v, :, cols], sems.at[v, side_at, step])

    @pl.when(g == 0)
    def _():
        for v in range(3):
            scaled = quad(vert[v]) * prm[v, 3:4, :]
            set_weights(wt, v, scaled.T, True)
        set_weights(wt, 3, quad(bal[...]).T, False)
        stage_sigma(sigma, sg, (0, 1, 2))
        for at in range(0, lon, LANES):
            width = min(LANES, lon - at)
            sx[at // LANES, 0:1, 0:width] = north[:, merged + at : merged + at + width]
            sx[at // LANES, 1:2, 0:width] = south[:, merged + at : merged + at + width]

    lane = lax.broadcasted_iota(jnp.int32, (rows, LANES), 1)
    high = (lane >= 64).astype(jnp.int32)
    high8 = high[0:8]
    chi_row = prm[0, 2:3, :]

    def at_tile(m):
        return pl.ds(pl.multiple_of(m * LANES, LANES), LANES)

    row8 = lax.broadcasted_iota(jnp.int32, (8, LANES), 0)
    beyond = [None] * (2 * PAIRS)
    for k, v in enumerate(ORDER):
        for q in range(0, rows, rq):
            c = [carry[k, e, q : q + rq, :] for e in range(4)]
            ry = [ry_ref[k, e, q : q + rq, :] for e in range(4)]
            rx = [rx_ref[k, e, pl.ds(pl.multiple_of(g * 2 * PAIRS, 8), 2 * PAIRS), :] for e in range(4)]
            for p in range(2 * PAIRS):
                x = x_ref[k, p]
                y = u_ref[k, p, q : q + rq, :]
                for e in range(4):
                    y = y + rx[e][p : p + 1, :] * c[e] + ry[e] * x[e : e + 1, :]
                at = (p // 2) * rows + q
                xs[k, at : at + rq, (p % 2) * LANES : (p % 2 + 1) * LANES] = y
                if v == 0 and q == 0:
                    x = pltpu.roll(x, 6, 0)
                    above = jnp.where(place[0] > 0, x + prm[0, 1:2, :] * y[0:1, :], 0.0)
                    beyond[p] = jnp.where(row8 == 0, above, jnp.where(row8 == 1, x, 0.0))

    @pl.when(g == 0)
    def _():
        first = col[0] + prm[0, 1:2, :] * xs[ORDER.index(0), 0:rows, 0:LANES]
        lhs = jnp.where(lane < 64, jnp.where(place[1] > 0, first, 0.0), col[1])
        lhs = jnp.concatenate([lhs, jnp.zeros_like(lhs)], axis=1)
        res = product(lhs, weight(wt, 0))
        zc[0] = swap(res[:, :LANES] * swap(side[0]))
        zc[1] = res[:, LANES:] * side[1]

    lhs = jnp.concatenate(
        [jnp.concatenate(beyond[2 * p : 2 * p + 2], axis=1) for p in range(PAIRS)], axis=0
    )
    res = product(lhs, weight(wt, 0))
    for p in range(PAIRS):
        m = g * PAIRS + p
        for side in range(2):
            tile = m + side * pairs
            s = jnp.take_along_axis(sx[tile >> 6], 2 * (tile & 63) + high8, axis=1, mode="promise_in_bounds")
            part = res[p * 8 : (p + 1) * 8, side * LANES : (side + 1) * LANES]
            zx[:, at_tile(tile)] = jnp.where(row8 < 2, part * s, 0.0)
    results = {v: product(xs[k], weight(wt, v)) for k, v in enumerate(ORDER)}
    for p in range(PAIRS):
        m = g * PAIRS + p
        for side in range(2):
            at = at_tile(m + side * pairs)
            z = [
                results[v][p * rows : (p + 1) * rows, side * LANES : (side + 1) * LANES]
                * sigma_tile(sg, v, m + side * pairs, high)
                for v in range(3)
            ]
            out[0, :, at] = z[0]
            out[1, :, at] = z[1] + chi_row * z[0]
            out[2, :, at] = z[2]
    for v in range(2):
        for side_at in range(2):
            copy(v, side_at, g).start()

    @pl.when(g == pl.num_programs(0) - 1)
    def _():
        row_id = lax.broadcasted_iota(jnp.int32, (rows, LANES), 0)
        last = half - 1

        def body(b, _):
            for p in range(PAIRS):
                for side in range(2):
                    m = b * PAIRS + p + side * pairs
                    x = out[0, :, at_tile(m)]
                    left = jnp.where(m == 0, zc[0], out[0, :, at_tile(jnp.maximum(m - 1, 0))])
                    right = jnp.where(m == last, zc[1], out[0, :, at_tile(jnp.minimum(m + 1, last))])
                    beside = swap(x + jnp.where(lane >= 64, left, right))
                    above = jnp.where(row_id == 0, zx[0:1, at_tile(m)], pltpu.roll(x, 1, 0))
                    below = jnp.where(row_id == rows - 1, zx[1:2, at_tile(m)], pltpu.roll(x, rows - 1, 0))
                    lap = 4.0 * x - beside - above - below
                    xs[0, p * rows : (p + 1) * rows, side * LANES : (side + 1) * LANES] = lap
            res = product(xs[0], weight(wt, 3))
            for p in range(PAIRS):
                for side in range(2):
                    at = at_tile(b * PAIRS + p + side * pairs)
                    part = res[p * rows : (p + 1) * rows, side * LANES : (side + 1) * LANES]
                    out[2, :, at] = out[2, :, at] + part
            for side_at in range(2):
                copy(2, side_at, b).start()
            return 0

        lax.fori_loop(0, steps, body, 0)
        for v in range(3):
            for side_at in range(2):
                for step in range(steps):
                    copy(v, side_at, step).wait()


def shards(state, sigma, vert, bal_temp, chi_coef, scales, classes, owner):
    n_lat = lax.axis_size("lat")
    n_lon = lax.axis_size("lon")
    devices = n_lat * n_lon
    nvars, rows, merged = state.shape
    levels = vert.shape[1]
    lon = merged // levels
    half = lon // 2
    pairs = half // 2
    pieces = (lon + LANES - 1) // LANES
    count = nvars * levels
    capacity = (count + devices - 1) // devices + 1
    i_lat = lax.axis_index("lat")
    i_lon = lax.axis_index("lon")

    up_lat, up_lon = ([(i, i + 1) for i in range(n - 1)] for n in (n_lat, n_lon))
    down_lat, down_lon = ([(j, i) for i, j in up] for up in (up_lat, up_lon))

    def row(i):
        return jnp.concatenate([state[2, i : i + 1, :], sigma[0, i : i + 1, :]], axis=1)

    north = lax.ppermute(row(rows - 1), "lat", up_lat)
    south = lax.ppermute(row(0), "lat", down_lat)
    west = lax.ppermute(state[2, :, merged - levels :], "lon", up_lon)
    east = lax.ppermute(state[2, :, :levels], "lon", down_lon)
    place = jnp.stack([i_lat, i_lon]).astype(jnp.int32)

    anywhere = pl.BlockSpec(memory_space=pl.ANY)
    steps = pairs // BLOCK

    def part(v, side):
        return pl.BlockSpec((1, rows, BLOCK * LANES), lambda g: (v, 0, g + side * steps))

    width = half // n_lat
    shapes = [(nvars, half, rows, LANES), (nvars, rows, half, LANES), (n_lat, nvars, 4 * width, LANES)]
    shapes.append((nvars, half, 8, LANES))

    def lat_call(nv, first, body, arrays, specs, name, aliases, more=()):
        return pl.pallas_call(
            body,
            grid=(steps,),
            in_specs=specs,
            out_specs=[
                pl.BlockSpec((nv, 2 * BLOCK, rows, LANES), lambda g: (first, g, 0, 0)),
                pl.BlockSpec((nv, rows, 2 * BLOCK, LANES), lambda g: (first, 0, g, 0)),
                pl.BlockSpec((2 * BLOCK // width, nv, 4 * width, LANES), lambda g: (g, first, 0, 0)),
                pl.BlockSpec((nv, 2 * BLOCK, 8, LANES), lambda g: (first, g, 0, 0)),
            ]
            + [full(s) for s in more],
            out_shape=[jax.ShapeDtypeStruct(s, f32) if n == 2 else pltpu.HBM(s, f32) for n, s in enumerate(shapes)]
            + [jax.ShapeDtypeStruct(s, f32) for s in more],
            scratch_shapes=[
                pltpu.VMEM((2, PAIRS * rows, 256), f32),
                pltpu.VMEM((2 * 768, 256), bf16),
                pltpu.VMEM((nvars, pieces, rows, LANES), f32),
            ],
            compiler_params=params(),
            cost_estimate=pl.CostEstimate(
                flops=nv * 60000000, bytes_accessed=nv * 3 * rows * merged * 4, transcendentals=0
            ),
            input_output_aliases=aliases,
            name=name,
        )(*arrays)

    ins = [scales.reshape(1, -1), classes.reshape(1, count), chi_coef.reshape(1, levels), sigma, vert] + [state] * 4
    specs = [full(x.shape) for x in ins[:5]] + [part(1, 0), part(1, 1), part(2, 0), part(2, 1)]
    ins = [in_hbm(x) for x in ins]
    body = functools.partial(lat_plain, rows, pairs)
    *wue, prm = lat_call(2, 0, body, ins, specs, "lat_chi_temp", {}, [(nvars, 4, LANES)])
    ins = [prm] + [in_hbm(x) for x in [sigma, vert, bal_temp] + [state] * 10] + [north, south, west, east]
    ins += [in_hbm(wue[0]), in_hbm(wue[1]), wue[2], in_hbm(wue[3])]
    specs = [full(x.shape) for x in ins[:4]] + [part(0, 0), part(0, 1), part(1, 0), part(1, 1)]

    def tile(side, step):
        last = 2 * pairs - 1
        return pl.BlockSpec(
            (1, rows, LANES), lambda g: (2, 0, jnp.clip(g * BLOCK + side * pairs + step, 0, last))
        )

    specs += [part(2, 0), part(2, 1), tile(0, -1), tile(0, BLOCK), tile(1, -1), tile(1, BLOCK)]
    specs += [full(x.shape) for x in (north, south, west, east)] + [anywhere] * 4
    aliases = {18: 0, 19: 1, 20: 2, 21: 3}
    w, u, edges, proj = lat_call(1, 2, functools.partial(lat_balance, rows, pairs), ins, specs, "lat_psi", aliases)
    def trade(x, axis):
        return lax.all_to_all(x, axis, split_axis=0, concat_axis=0, tiled=True)

    shares = trade(edges, "lat")

    rb = BLOCK
    local, el, es, rx, ry = pl.pallas_call(
        functools.partial(lon_kernel, rows, rb),
        grid=(rows // rb,),
        in_specs=[
            full(prm.shape),
            pl.BlockSpec((nvars, rb, half, LANES), lambda g: (0, g, 0, 0)),
        ],
        out_specs=[
            pl.BlockSpec((nvars, half, rb, LANES), lambda g: (0, 0, g, 0)),
            full((nvars, 4, rows, LANES)),
            full((6, rows, LANES)),
            full((nvars, 4, half, LANES)),
            full((nvars, 4, rows, LANES)),
        ],
        out_shape=[
            pltpu.HBM((nvars, half, rows, LANES), f32),
            pltpu.HBM((nvars, 4, rows, LANES), f32),
            jax.ShapeDtypeStruct((6, rows, LANES), f32),
            pltpu.HBM((nvars, 4, half, LANES), f32),
            pltpu.HBM((nvars, 4, rows, LANES), f32),
        ],
        compiler_params=params(),
        cost_estimate=pl.CostEstimate(
            flops=180000000, bytes_accessed=6 * rows * merged * 4, transcendentals=0
        ),
        name="lon_tile",
    )(prm, in_hbm(u))

    def round_lon(x):
        return [x] + [
            lax.ppermute(x, "lon", [(i, i ^ s) for i in range(n_lon)]) for s in range(1, n_lon)
        ]

    shares, _ = lax.optimization_barrier((shares, es))
    sent = round_lon(es)
    carries = pl.pallas_call(
        functools.partial(solve_kernel, n_lat, rows),
        grid=(1,),
        in_specs=[full(prm.shape), full(shares.shape)],
        out_specs=full(shares.shape),
        out_shape=jax.ShapeDtypeStruct(shares.shape, f32),
        compiler_params=params(),
        cost_estimate=pl.CostEstimate(flops=1000000, bytes_accessed=2 * shares.size * 4, transcendentals=0),
        name="solve",
    )(prm, shares)
    carries = trade(carries, "lat")

    packed = 2 * PAIRS

    def columns(r):
        return pl.BlockSpec((nvars, packed, r, LANES), lambda g: (0, g, 0, 0))

    px, dots = pl.pallas_call(
        functools.partial(energy_kernel, rows, 24),
        grid=(half // packed,),
        in_specs=[columns(rows), columns(rows), full(rx.shape)],
        out_specs=[full((nvars, 4, rows, LANES)), full((nvars, 8, LANES))],
        out_shape=[pltpu.HBM((nvars, 4, rows, LANES), f32), pltpu.HBM((nvars, 8, LANES), f32)],
        compiler_params=params(),
        cost_estimate=pl.CostEstimate(flops=20000000, bytes_accessed=6 * rows * merged * 4, transcendentals=0),
        name="energy",
    )(in_hbm(w), in_hbm(local), in_hbm(rx))
    carries, _ = lax.optimization_barrier((carries, px))

    crossed, elc, esc = pl.pallas_call(
        carry_kernel,
        grid=(1,),
        in_specs=[full(prm.shape), pl.BlockSpec((1, rows, lon), lambda g: (0, 0, 0)), full(carries.shape)],
        out_specs=[full((nvars, half, 8, LANES)), full((nvars, 4, 8, LANES)), full((7, 8, LANES))],
        out_shape=[
            jax.ShapeDtypeStruct((nvars, half, 8, LANES), f32),
            jax.ShapeDtypeStruct((nvars, 4, 8, LANES), f32),
            jax.ShapeDtypeStruct((7, 8, LANES), f32),
        ],
        compiler_params=params(),
        cost_estimate=pl.CostEstimate(
            flops=30000000, bytes_accessed=4 * nvars * 12 * half * LANES, transcendentals=0
        ),
        name="lon_carry",
    )(prm, in_hbm(sigma), carries)
    sent_x = round_lon(esc)

    index = jnp.arange(count, dtype=jnp.int32)
    same = (owner[:, None] == owner[None, :]) & (index[None, :] < index[:, None])
    target = (owner * capacity + jnp.sum(same.astype(jnp.int32), axis=1)).reshape(1, count)

    ins = [in_hbm(x) for x in (proj, px, dots, rx, ry, el)]
    ins = [place, target, prm, crossed] + ins + [elc] + sent + sent_x
    specs = [full(x.shape) for x in ins]
    specs[0] = pl.BlockSpec(memory_space=pltpu.SMEM)
    shapes = [(nvars, 4, rows, LANES), (nvars, half, 8, LANES), (2, rows, LANES), (2, rows, LANES)]
    carry, crossed, col, side, table = pl.pallas_call(
        functools.partial(close_kernel, n_lon, rows, devices, capacity, devices * rows * lon),
        grid=(1,),
        in_specs=specs,
        out_specs=[full(x) for x in shapes] + [full((devices, LANES))],
        out_shape=[pltpu.HBM(x, f32) for x in shapes] + [jax.ShapeDtypeStruct((devices, LANES), f32)],
        scratch_shapes=[pltpu.VMEM((n_lon, 6, rows, LANES), f32), pltpu.VMEM((n_lon, 7, 8, LANES), f32)],
        compiler_params=params(),
        cost_estimate=pl.CostEstimate(flops=10000000, bytes_accessed=4000000, transcendentals=0),
        name="close",
    )(*ins)
    table = trade(table, ("lat", "lon"))
    slab_energy = jnp.sum(table, axis=0, keepdims=True)[:, :capacity]

    ins = [prm, sigma, north, south, vert, bal_temp, col, side, carry, rx, ry, local, crossed]
    ins = [place] + [in_hbm(x) for x in ins]
    specs = [full(x.shape) for x in ins]
    specs[0] = pl.BlockSpec(memory_space=pltpu.SMEM)
    specs[-2:] = [columns(rows), columns(8)]
    applied = pl.pallas_call(
        functools.partial(end_kernel, rows, pairs, 24),
        grid=(half // packed,),
        in_specs=specs,
        out_specs=anywhere,
        out_shape=jax.ShapeDtypeStruct(state.shape, f32),
        scratch_shapes=[
            pltpu.VMEM(state.shape, f32),
            pltpu.VMEM((nvars, PAIRS * rows, 256), f32),
            pltpu.VMEM((8, merged), f32),
            pltpu.VMEM((2, rows, LANES), f32),
            pltpu.VMEM((4 * 768, 256), bf16),
            pltpu.VMEM((nvars, pieces, rows, LANES), f32),
            pltpu.VMEM((pieces, 8, LANES), f32),
            pltpu.SemaphoreType.DMA((3, 2, pairs // PAIRS)),
        ],
        compiler_params=params(),
        cost_estimate=pl.CostEstimate(
            flops=300000000, bytes_accessed=6 * rows * merged * 4, transcendentals=0
        ),
        name="finish",
    )(*ins)
    return (applied, slab_energy)


def solution(mesh):
    return jax.shard_map(
        shards,
        mesh=mesh,
        in_specs=(P(None, "lat", "lon"), P(None, "lat", "lon"), P(), P(), P(), P(), P(), P()),
        out_specs=(P(None, "lat", "lon"), P(("lat", "lon"), None)),
        check_vma=False,
    )
```

```python
import functools

import jax
import jax.numpy as jnp
from jax import lax
from jax.experimental import pallas as pl
from jax.experimental.pallas import tpu as pltpu
from jax.sharding import PartitionSpec as P

highest = lax.Precision.HIGHEST
f32 = jnp.float32
bf16 = jnp.bfloat16
LANES = 128
PAIRS = 8
BLOCK = 24
ORDER = (1, 2, 0)
LIMIT = 30 * 1024 * 1024


def params():
    return pltpu.CompilerParams(vmem_limit_bytes=LIMIT)


def in_hbm(x):
    return pltpu.with_memory_space_constraint(x, pltpu.HBM)


def full(shape):
    return pl.BlockSpec(shape, lambda g: (0,) * len(shape))


def swap(x):
    return pltpu.roll(x, 64, x.ndim - 1)


def low_lanes(shape):
    return lax.broadcasted_iota(jnp.int32, shape, len(shape) - 1) < 64


def halves(x):
    hi = x.astype(bf16)
    return hi, (x - hi.astype(f32)).astype(bf16)


def dot(x, y):
    return jnp.dot(x, y, preferred_element_type=f32)


def split(x):
    hi, lo = halves(x)
    return jnp.concatenate([hi, lo, hi], axis=1)


def product(x, weights):
    return dot(split(x), weights)


def expand(mat, mixed):
    wide = quad(mat)
    wide = jnp.concatenate([wide, wide], axis=1)
    wide = jnp.concatenate([wide, wide], axis=0)
    src = lax.broadcasted_iota(jnp.int32, (256, 256), 0) // 64
    dst = lax.broadcasted_iota(jnp.int32, (256, 256), 1) // 64
    if mixed:
        src = jnp.where(src == 1, 2, jnp.where(src == 2, 1, src))
    return halves(jnp.where(src == dst, wide, 0.0))


def quad(mat):
    if mat.shape[0] == LANES:
        return mat
    wide = jnp.concatenate([mat, mat], axis=1)
    return jnp.concatenate([wide, wide], axis=0)


def constants(length, decay, m):
    span = jnp.exp(-float(m) / length)
    d = 1.0 - decay * decay
    k1 = decay * (1.0 - span * span) / d
    k2 = (m * span - decay * decay * (span - span * span * span) / d) / d
    tail = decay * decay * (1.0 + span * span) * (1.0 - span * span) / d
    k3 = decay / (d * d) * (1.0 - (2.0 * m + 1.0) * span * span + tail)
    return span, k1, k2, k3


def responses(length, decay, m):
    j = lax.broadcasted_iota(jnp.int32, (m, LANES), 0).astype(f32)
    up = jnp.exp(-j / length)
    down = jnp.exp(-(m - j) / length)
    span = jnp.exp(-float(m) / length)
    d = 1.0 - decay * decay
    diff = up - span * down
    g3 = decay * diff / d
    g2 = ((m - j) * down - decay * decay * (span * up - span * span * down) / d) / d
    part = decay * decay * (1.0 + span * span) * diff / d
    g1 = decay / (d * d) * ((j + 1.0) * up - (2.0 * m + 1.0 - j) * span * down + part)
    return g1, g2, g3, down


def pick(all_carries, me):
    out = []
    for cs in all_carries:
        mine = cs[0]
        for t in range(1, len(cs)):
            mine = jnp.where(me == t, cs[t], mine)
        out.append(mine)
    return out


def solve_carries(n, edge, const):
    span, k1, k2, k3 = const
    first = edge(0, 0)
    zero = jnp.zeros_like(first)
    e1 = [first] + [edge(t, 0) for t in range(1, n)]
    c1, c2, c3, c4 = ([None] * n for _ in range(4))
    c = zero
    for t in range(n):
        c1[t] = c
        c = e1[t] + span * c
    c = zero
    for t in reversed(range(n)):
        c2[t] = c
        c = edge(t, 1) + k1 * c1[t] + span * c
    c = zero
    for t in range(n):
        c3[t] = c
        c = edge(t, 2) + k2 * c1[t] + k1 * c2[t] + span * c
    c = zero
    for t in reversed(range(n)):
        c4[t] = c
        c = edge(t, 3) + k3 * c1[t] + k2 * c2[t] + k1 * c3[t] + span * c
    return c1, c2, c3, c4


def cascade(count, load, store, decay, start):
    step = 24
    edges = []
    for stage in range(4):
        back = stage % 2 == 1

        def body(b, states, back=back):
            base = (count // step - 1 - b) * step if back else b * step
            order = range(step - 1, -1, -1) if back else range(step)
            for o in order:
                new = [decay_k * s + x for decay_k, s, x in zip(decay, states, load(base + o))]
                store(base + o, new)
                states = new
            return tuple(states)

        states = lax.fori_loop(0, count // step, body, tuple(start))
        edges.append(list(states))
    return edges


def stage_sigma(sigma, sg, variables):
    lon = sigma.shape[2]
    for v in variables:
        for at in range(0, lon, LANES):
            width = min(LANES, lon - at)
            sg[v, at // LANES, :, 0:width] = sigma[v, :, at : at + width]


def sigma_tile(sg, v, m, high):
    idx = 2 * (m & 63) + high
    return jnp.take_along_axis(sg[v, m >> 6], idx, axis=1, mode="promise_in_bounds")


def set_weights(weights, k, mat, mixed):
    hi, lo = expand(mat, mixed)
    weights[768 * k : 768 * k + 256] = hi
    weights[768 * k + 256 : 768 * k + 512] = hi
    weights[768 * k + 512 : 768 * k + 768] = lo


def weight(weights, k):
    return weights[768 * k : 768 * (k + 1)]


def lat_filter(vs, rows, prm, u_ref, e_ref, p_ref):
    nv = len(vs)
    decay = [prm[v, 1:2, :] for v in vs]

    def load(i):
        return [u_ref[k, i] for k in range(nv)]

    def store(i, values):
        for k in range(nv):
            u_ref[k, i] = values[k]

    zero = jnp.zeros((u_ref.shape[2], LANES), f32)
    edges = cascade(rows, load, store, decay, [zero] * nv)
    for k in range(nv):
        for j in range(0, u_ref.shape[2], 8):
            block = [edges[3 - e][k][j : j + 8] * decay[k] for e in range(4)]
            block = jnp.stack(block + [jnp.zeros((8, LANES), f32)] * 4)
            p_ref[k, j : j + 8] = jnp.swapaxes(block, 0, 1)
    width = e_ref.shape[2] // 4
    for e in range(4):
        for k in range(nv):
            for c in range(e_ref.shape[0]):
                e_ref[c, k, e * width : (e + 1) * width] = edges[e][k][c * width : (c + 1) * width]


def put_mixed(k, b, rows, res, w_ref, u_ref):
    base = b * 2 * PAIRS
    for p in range(PAIRS):
        part = res[p * rows : (p + 1) * rows]
        w_ref[k, base + 2 * p] = part[:, :LANES]
        w_ref[k, base + 2 * p + 1] = part[:, LANES:]
    at = pl.ds(pl.multiple_of(base, 2 * PAIRS), 2 * PAIRS)
    u_ref[k, :, at, :] = jnp.swapaxes(w_ref[k, at], 0, 1)


def set_params(scales, classes, chi_coef, prm):
    coef = jnp.concatenate([chi_coef[...], chi_coef[...]], axis=1)
    for v in range(3):
        kind = classes[:, 64 * v : 64 * (v + 1)]
        kind = jnp.concatenate([kind, kind], axis=1)
        length = jnp.zeros((1, LANES), f32)
        for n in range(scales.shape[1]):
            length = jnp.where(kind == n, scales[:, n : n + 1], length)
        decay = jnp.exp(-1.0 / length)
        norm = 1.0 - decay
        norm = norm * norm
        norm = norm * norm
        prm[v, 0:1, :] = length
        prm[v, 1:2, :] = decay
        prm[v, 2:3, :] = coef
        prm[v, 3:4, :] = length * jnp.sqrt(length) * norm * norm


def lat_plain(
    rows, pairs, scales, classes, chi_coef, sigma, vert, b1lo, b1hi, b2lo, b2hi,
    w_ref, u_ref, e_ref, p_ref, prm, xs, wt, sg,
):
    g = pl.program_id(0)

    @pl.when(g == 0)
    def _():
        set_params(scales, classes, chi_coef, prm)
        set_weights(wt, 0, vert[1], True)
        set_weights(wt, 1, vert[2], True)
        stage_sigma(sigma, sg, (1, 2))

    lane = lax.broadcasted_iota(jnp.int32, (rows, LANES), 1)
    high = (lane >= 64).astype(jnp.int32)

    def body(b, _):
        for p in range(PAIRS):
            at = slice(p * rows, (p + 1) * rows)
            cols = pl.ds(pl.multiple_of((b * PAIRS + p) * LANES, LANES), LANES)
            m = g * BLOCK + b * PAIRS + p
            for k, sides in enumerate(((b1lo, b1hi), (b2lo, b2hi))):
                for side in range(2):
                    s = sigma_tile(sg, k + 1, m + side * pairs, high)
                    xs[k, at, side * LANES : (side + 1) * LANES] = sides[side][0, :, cols] * s
        for k in range(2):
            put_mixed(k, b, rows, product(xs[k], weight(wt, k)), w_ref, u_ref)
        return 0

    lax.fori_loop(0, BLOCK // PAIRS, body, 0)
    lat_filter((1, 2), rows, prm, u_ref, e_ref, p_ref)


def lat_balance(
    rows, pairs, prm, sigma, vert, bal, plo, phi, clo, chi, tlo, thi, tll, tlr, thl, thr, north, south, west, east, w_in, u_in, e_in, p_in,
    w_ref, u_ref, e_ref, p_ref, xs, wt, sg,
):
    del w_in, u_in, e_in, p_in
    g = pl.program_id(0)

    @pl.when(g == 0)
    def _():
        set_weights(wt, 0, vert[0], True)
        (bh, bl), (vh, vl) = halves(bal[...]), halves(vert[0])
        set_weights(wt, 1, dot(bh, vh) + dot(bl, vh) + dot(bh, vl), True)
        stage_sigma(sigma, sg, (0,))

    lane = lax.broadcasted_iota(jnp.int32, (rows, LANES), 1)
    row_id = lax.broadcasted_iota(jnp.int32, (rows, LANES), 0)
    high = (lane >= 64).astype(jnp.int32)
    chi_row = prm[0, 2:3, :]
    last = 2 * pairs - 1
    beyond = [jnp.concatenate([x[...], x[...]], axis=1) for x in (west, east)]

    def at_tile(m):
        return pl.ds(pl.multiple_of(m * LANES, LANES), LANES)

    sides = ((tlo, tll, tlr), (thi, thl, thr))

    def laplace(b, o, side):
        temp, before, after = sides[side]
        p = b * PAIRS + o
        m = g * BLOCK + p + side * pairs
        x = temp[0, :, at_tile(p)]
        left = temp[0, :, at_tile(jnp.maximum(p - 1, 0))]
        if o == 0:
            left = jnp.where(p == 0, before[0], left)
            if side == 0:
                left = jnp.where(m == 0, beyond[0], left)
        right = temp[0, :, at_tile(jnp.minimum(p + 1, BLOCK - 1))]
        if o == PAIRS - 1:
            right = jnp.where(p == BLOCK - 1, after[0], right)
            if side == 1:
                right = jnp.where(m == last, beyond[1], right)
        beside = swap(x + jnp.where(lane >= 64, left, right))
        above = jnp.where(row_id == 0, north[:, at_tile(m)], pltpu.roll(x, 1, 0))
        below = jnp.where(row_id == rows - 1, south[:, at_tile(m)], pltpu.roll(x, rows - 1, 0))
        return 4.0 * x - beside - above - below

    def body(b, _):
        for p in range(PAIRS):
            at = slice(p * rows, (p + 1) * rows)
            cols = at_tile(b * PAIRS + p)
            m = g * BLOCK + b * PAIRS + p
            for side, (pr, cr) in enumerate(((plo, clo), (phi, chi))):
                s = sigma_tile(sg, 0, m + side * pairs, high)
                to = slice(side * LANES, (side + 1) * LANES)
                xs[0, at, to] = (pr[0, :, cols] + chi_row * cr[0, :, cols]) * s
                xs[1, at, to] = laplace(b, p, side) * s
        res = dot(jnp.concatenate([split(xs[0]), split(xs[1])], axis=1), wt[...])
        put_mixed(0, b, rows, res, w_ref, u_ref)
        return 0

    lax.fori_loop(0, BLOCK // PAIRS, body, 0)
    lat_filter((0,), rows, prm, u_ref, e_ref, p_ref)


def lon_filter(prm, rb, o_ref, el_ref, put, at):
    half = o_ref.shape[1]
    nv = len(ORDER)
    decay = [prm[v, 1:2, :] for v in ORDER]

    def load(j):
        return [o_ref[k, j] for k in range(nv)]

    def store(j, values):
        for k in range(nv):
            o_ref[k, j] = values[k]

    edges = cascade(half, load, store, decay, [jnp.zeros((rb, LANES), f32)] * nv)
    low = low_lanes((rb, LANES))
    for k, v in enumerate(ORDER):
        span, k1, k2, k3 = constants(prm[v, 0:1, :], prm[v, 1:2, :], half)
        e1, e2, e3, e4 = (edges[e][k] for e in range(4))
        c1 = jnp.where(low, 0.0, swap(e1))
        t1 = e1 + span * c1
        t2 = e2 + k1 * c1
        c2 = jnp.where(low, swap(t2), 0.0)
        t2 = t2 + span * c2
        t3 = e3 + k2 * c1 + k1 * c2
        c3 = jnp.where(low, 0.0, swap(t3))
        t3 = t3 + span * c3
        t4 = e4 + k3 * c1 + k2 * c2 + k1 * c3
        c4 = jnp.where(low, swap(t4), 0.0)
        t4 = t4 + span * c4
        put(2 * k, jnp.where(low, t2, t1))
        put(2 * k + 1, jnp.where(low, t4, t3))
        for e, x in enumerate((e1, e2, e3, e4)):
            el_ref[k, e, at, :] = x


def lon_kernel(
    rows, rb, prm, u_ref, o_ref, el_ref, es_ref, rx_ref, ry_ref
):
    g = pl.program_id(0)
    half = u_ref.shape[2]
    at = pl.ds(pl.multiple_of(g * rb, 8), rb)

    @pl.when(g == 0)
    def _():
        for k, v in enumerate(ORDER):
            for e, r in enumerate(responses(prm[v, 0:1, :], prm[v, 1:2, :], half)):
                rx_ref[k, e] = r
            for e, r in enumerate(responses(prm[v, 0:1, :], prm[v, 1:2, :], rows)):
                ry_ref[k, e] = r

    def turn(b, _):
        at = pl.ds(pl.multiple_of(b * 8, 8), 8)
        for k in range(len(ORDER)):
            for q in range(0, rb, 8):
                o_ref[k, at, q : q + 8, :] = jnp.swapaxes(u_ref[k, q : q + 8, at, :], 0, 1)
        return 0

    lax.fori_loop(0, half // 8, turn, 0)

    def put(i, x):
        es_ref[i, at, :] = x

    lon_filter(prm, rb, o_ref, el_ref, put, at)


def energy_kernel(rows, rq, w_ref, u_ref, rx_ref, px_ref, dot_ref):
    g = pl.program_id(0)
    count = w_ref.shape[1]

    @pl.when(g == 0)
    def _():
        px_ref[...] = jnp.zeros_like(px_ref)
        dot_ref[...] = jnp.zeros_like(dot_ref)

    for k in range(w_ref.shape[0]):
        rx = [rx_ref[k, e, pl.ds(pl.multiple_of(g * count, 8), count), :] for e in range(4)]
        for q in range(0, rows, rq):
            sums = [px_ref[k, e, q : q + rq, :] for e in range(4)] + [jnp.zeros((rq, LANES), f32)]
            for p in range(count):
                x = w_ref[k, p, q : q + rq, :]
                sums[4] = sums[4] + x * u_ref[k, p, q : q + rq, :]
                for e in range(4):
                    sums[e] = sums[e] + x * rx[e][p : p + 1, :]
            for e in range(4):
                px_ref[k, e, q : q + rq, :] = sums[e]
            dot_ref[k] += jnp.sum(sums[4].reshape(rq // 8, 8, LANES), axis=0)


def solve_kernel(n_lat, rows, prm, edges, carries):
    width = edges.shape[2] // 4
    for k, v in enumerate(ORDER):
        const = constants(prm[v, 0:1, :], prm[v, 1:2, :], rows)
        c = solve_carries(n_lat, lambda t, e: edges[t, k, e * width : (e + 1) * width, :], const)
        for e in range(4):
            for t in range(n_lat):
                carries[t, k, e * width : (e + 1) * width, :] = c[e][t]


def carry_kernel(prm, sigma, carries, o_ref, el_ref, es_ref):
    width = carries.shape[2] // 4
    zero = jnp.zeros((8, LANES), f32)

    def body(d, _):
        for k in range(len(ORDER)):
            for j in range(width):
                at = d * width + j
                o_ref[k, at] = zero
                for e in range(4):
                    o_ref[k, at, e : e + 1, :] = carries[d, k, e * width + j : e * width + j + 1, :]
        return 0

    lax.fori_loop(0, carries.shape[0], body, 0)

    def put(i, x):
        es_ref[i] = x

    lon_filter(prm, 8, o_ref, el_ref, put, slice(0, 8))
    x = sigma[0]
    rows, lon = x.shape
    outer = jnp.where(low_lanes((rows, LANES)), x[:, 0:1], x[:, lon - 1 : lon])
    outer = jnp.concatenate([outer, jnp.zeros((LANES - rows, LANES), f32)], axis=0).T
    es_ref[6] = jnp.concatenate([outer[0:1], outer[64:65], jnp.zeros((6, LANES), f32)], axis=0)


def close_kernel(
    n_lon, rows, devices, capacity, cells, place, target, prm, x_ref, proj, px, dots, px0, dots0, rx, ry, el, elc, *rest
):
    sent, sent_x = rest[:n_lon], rest[n_lon : 2 * n_lon]
    carry, full_ref, col_ref, side_ref, table, esm, esx = rest[2 * n_lon :]
    half = rx.shape[2]
    me = place[1]
    for d in range(n_lon):
        esm[me ^ d] = sent[d][...]
        esx[me ^ d] = sent_x[d][...]
    pad = jnp.zeros((LANES - 8, LANES), f32)
    for i, t in enumerate((jnp.maximum(me - 1, 0), jnp.minimum(me + 1, n_lon - 1))):
        outer = jnp.concatenate([esx[t, 6], pad], axis=0).T[:rows, 1 - i : 2 - i]
        side_ref[i] = jnp.broadcast_to(outer, (rows, LANES))
    length = jnp.stack([prm[v, 0:1, :] for v in ORDER])
    decay = jnp.stack([prm[v, 1:2, :] for v in ORDER])
    whole = constants(length, decay, 2 * half)
    span, k1, k2, k3 = constants(length, decay, half)
    low = low_lanes((len(ORDER), rows + 8, LANES))
    cache = {}

    def both(main, more):
        parts = [jnp.concatenate([main(k), more(k)], axis=0) for k in range(len(ORDER))]
        return jnp.stack(parts)

    def edge(t, e):
        i = e // 2
        if (t, i) not in cache:
            x = both(lambda k: esm[t, 2 * k + i], lambda k: esx[t, 2 * k + i])
            y = swap(x)
            cache[t, i] = (jnp.where(low, y, x), jnp.where(low, x, y))
        return cache[t, i][e % 2]

    d1, d2, d3, d4 = pick(solve_carries(n_lon, edge, whole), me)
    e1, e2, e3, e4 = (both(lambda k, e=e: el[k, e], lambda k, e=e: elc[k, e]) for e in range(4))
    c1 = jnp.where(low, d1, swap(e1 + span * d1))
    c2 = jnp.where(low, swap(e2 + k1 * c1 + span * d2), d2)
    c3 = jnp.where(low, d3, swap(e3 + k2 * c1 + k1 * c2 + span * d3))
    c4 = jnp.where(low, swap(e4 + k3 * c1 + k2 * c2 + k1 * c3 + span * d4), d4)
    lane = lax.broadcasted_iota(jnp.int32, (devices, LANES), 1)
    first_slot = lax.broadcasted_iota(jnp.int32, (devices, LANES), 0) * capacity
    owned = jnp.zeros((devices, LANES), f32)
    for k, v in enumerate(ORDER):
        more = [c[k, rows:] for c in (c1, c2, c3, c4)]
        sums = jnp.zeros((rows, LANES), f32)
        for e, c in enumerate((c1, c2, c3, c4)):
            carry[k, e] = c[k, :rows]
            sums = sums + c[k, :rows] * (px[k, e] if k < 2 else px0[0, e])

        def body(b, total, k=k, more=more):
            base = pl.multiple_of(b * 8, 8)
            r = [rx[k, e, pl.ds(base, 8), :] for e in range(4)]
            for o in range(8):
                x = x_ref[k, base + o]
                for e in range(4):
                    x = x + r[e][o : o + 1, :] * more[e]
                full_ref[k, base + o] = x
                total = total + x * proj[k, base + o]
            return total

        total = lax.fori_loop(0, half // 8, body, dots[k] if k < 2 else dots0[0])
        total = total + jnp.sum(sums.reshape(rows // 8, 8, LANES), axis=0)
        total = jnp.sum(total, axis=0, keepdims=True)
        total = (total + swap(total)) * prm[v, 3:4, :] * (1.0 / cells)
        where = target[:, 64 * v : 64 * (v + 1)]
        where = jnp.concatenate([where, where], axis=1) - first_slot
        for s in range(capacity):
            mine = jnp.where((lane < 64) & (where == s), total, 0.0)
            owned = owned + jnp.where(lane == s, jnp.sum(mine, axis=1, keepdims=True), 0.0)
        if v == 0:
            for i, d in enumerate((d3, d4)):
                y = d[k, :rows]
                for e in range(4):
                    y = y + ry[k, e] * d[k, rows + e : rows + e + 1]
                col_ref[i] = y
    table[...] = owned


def end_kernel(
    rows, pairs, rq, place, prm, sigma, north, south, vert, bal, col, side, carry, rx_ref, ry_ref, u_ref, x_ref,
    out_ref, out, xs, zx, zc, wt, sg, sx, sems,
):
    g = pl.program_id(0)
    half = 2 * pairs
    lon = sigma.shape[2]
    merged = out.shape[2]
    steps = pairs // PAIRS

    def copy(v, side_at, step):
        first = pl.multiple_of((step * PAIRS + side_at * pairs) * LANES, LANES)
        cols = pl.ds(first, PAIRS * LANES)
        return pltpu.make_async_copy(out.at[v, :, cols], out_ref.at[v, :, cols], sems.at[v, side_at, step])

    @pl.when(g == 0)
    def _():
        for v in range(3):
            scaled = quad(vert[v]) * prm[v, 3:4, :]
            set_weights(wt, v, scaled.T, True)
        set_weights(wt, 3, quad(bal[...]).T, False)
        stage_sigma(sigma, sg, (0, 1, 2))
        for at in range(0, lon, LANES):
            width = min(LANES, lon - at)
            sx[at // LANES, 0:1, 0:width] = north[:, merged + at : merged + at + width]
            sx[at // LANES, 1:2, 0:width] = south[:, merged + at : merged + at + width]

    lane = lax.broadcasted_iota(jnp.int32, (rows, LANES), 1)
    high = (lane >= 64).astype(jnp.int32)
    high8 = high[0:8]
    chi_row = prm[0, 2:3, :]

    def at_tile(m):
        return pl.ds(pl.multiple_of(m * LANES, LANES), LANES)

    row8 = lax.broadcasted_iota(jnp.int32, (8, LANES), 0)
    beyond = [None] * (2 * PAIRS)
    for k, v in enumerate(ORDER):
        for q in range(0, rows, rq):
            c = [carry[k, e, q : q + rq, :] for e in range(4)]
            ry = [ry_ref[k, e, q : q + rq, :] for e in range(4)]
            rx = [rx_ref[k, e, pl.ds(pl.multiple_of(g * 2 * PAIRS, 8), 2 * PAIRS), :] for e in range(4)]
            for p in range(2 * PAIRS):
                x = x_ref[k, p]
                y = u_ref[k, p, q : q + rq, :]
                for e in range(4):
                    y = y + rx[e][p : p + 1, :] * c[e] + ry[e] * x[e : e + 1, :]
                at = (p // 2) * rows + q
                xs[k, at : at + rq, (p % 2) * LANES : (p % 2 + 1) * LANES] = y
                if v == 0 and q == 0:
                    x = pltpu.roll(x, 6, 0)
                    above = jnp.where(place[0] > 0, x + prm[0, 1:2, :] * y[0:1, :], 0.0)
                    beyond[p] = jnp.where(row8 == 0, above, jnp.where(row8 == 1, x, 0.0))

    @pl.when(g == 0)
    def _():
        first = col[0] + prm[0, 1:2, :] * xs[ORDER.index(0), 0:rows, 0:LANES]
        lhs = jnp.where(lane < 64, jnp.where(place[1] > 0, first, 0.0), col[1])
        lhs = jnp.concatenate([lhs, jnp.zeros_like(lhs)], axis=1)
        res = product(lhs, weight(wt, 0))
        zc[0] = swap(res[:, :LANES] * swap(side[0]))
        zc[1] = res[:, LANES:] * side[1]

    lhs = jnp.concatenate(
        [jnp.concatenate(beyond[2 * p : 2 * p + 2], axis=1) for p in range(PAIRS)], axis=0
    )
    res = product(lhs, weight(wt, 0))
    for p in range(PAIRS):
        m = g * PAIRS + p
        for side in range(2):
            tile = m + side * pairs
            s = jnp.take_along_axis(sx[tile >> 6], 2 * (tile & 63) + high8, axis=1, mode="promise_in_bounds")
            part = res[p * 8 : (p + 1) * 8, side * LANES : (side + 1) * LANES]
            zx[:, at_tile(tile)] = jnp.where(row8 < 2, part * s, 0.0)
    results = {v: product(xs[k], weight(wt, v)) for k, v in enumerate(ORDER)}
    for p in range(PAIRS):
        m = g * PAIRS + p
        for side in range(2):
            at = at_tile(m + side * pairs)
            z = [
                results[v][p * rows : (p + 1) * rows, side * LANES : (side + 1) * LANES]
                * sigma_tile(sg, v, m + side * pairs, high)
                for v in range(3)
            ]
            out[0, :, at] = z[0]
            out[1, :, at] = z[1] + chi_row * z[0]
            out[2, :, at] = z[2]
    for v in range(2):
        for side_at in range(2):
            copy(v, side_at, g).start()

    @pl.when(g == pl.num_programs(0) - 1)
    def _():
        row_id = lax.broadcasted_iota(jnp.int32, (rows, LANES), 0)
        last = half - 1

        def body(b, _):
            for p in range(PAIRS):
                for side in range(2):
                    m = b * PAIRS + p + side * pairs
                    x = out[0, :, at_tile(m)]
                    left = jnp.where(m == 0, zc[0], out[0, :, at_tile(jnp.maximum(m - 1, 0))])
                    right = jnp.where(m == last, zc[1], out[0, :, at_tile(jnp.minimum(m + 1, last))])
                    beside = swap(x + jnp.where(lane >= 64, left, right))
                    above = jnp.where(row_id == 0, zx[0:1, at_tile(m)], pltpu.roll(x, 1, 0))
                    below = jnp.where(row_id == rows - 1, zx[1:2, at_tile(m)], pltpu.roll(x, rows - 1, 0))
                    lap = 4.0 * x - beside - above - below
                    xs[0, p * rows : (p + 1) * rows, side * LANES : (side + 1) * LANES] = lap
            res = product(xs[0], weight(wt, 3))
            for p in range(PAIRS):
                for side in range(2):
                    at = at_tile(b * PAIRS + p + side * pairs)
                    part = res[p * rows : (p + 1) * rows, side * LANES : (side + 1) * LANES]
                    out[2, :, at] = out[2, :, at] + part
            for side_at in range(2):
                copy(2, side_at, b).start()
            return 0

        lax.fori_loop(0, steps, body, 0)
        for v in range(3):
            for side_at in range(2):
                for step in range(steps):
                    copy(v, side_at, step).wait()


def shards(state, sigma, vert, bal_temp, chi_coef, scales, classes, owner):
    n_lat = lax.axis_size("lat")
    n_lon = lax.axis_size("lon")
    devices = n_lat * n_lon
    nvars, rows, merged = state.shape
    levels = vert.shape[1]
    lon = merged // levels
    half = lon // 2
    pairs = half // 2
    pieces = (lon + LANES - 1) // LANES
    count = nvars * levels
    capacity = (count + devices - 1) // devices + 1
    i_lat = lax.axis_index("lat")
    i_lon = lax.axis_index("lon")

    up_lat, up_lon = ([(i, i + 1) for i in range(n - 1)] for n in (n_lat, n_lon))
    down_lat, down_lon = ([(j, i) for i, j in up] for up in (up_lat, up_lon))

    def row(i):
        return jnp.concatenate([state[2, i : i + 1, :], sigma[0, i : i + 1, :]], axis=1)

    north = lax.ppermute(row(rows - 1), "lat", up_lat)
    south = lax.ppermute(row(0), "lat", down_lat)
    west = lax.ppermute(state[2, :, merged - levels :], "lon", up_lon)
    east = lax.ppermute(state[2, :, :levels], "lon", down_lon)
    place = jnp.stack([i_lat, i_lon]).astype(jnp.int32)

    anywhere = pl.BlockSpec(memory_space=pl.ANY)
    steps = pairs // BLOCK

    def part(v, side):
        return pl.BlockSpec((1, rows, BLOCK * LANES), lambda g: (v, 0, g + side * steps))

    width = half // n_lat
    shapes = [(nvars, half, rows, LANES), (nvars, rows, half, LANES), (n_lat, nvars, 4 * width, LANES)]
    shapes.append((nvars, half, 8, LANES))

    def lat_call(nv, first, body, arrays, specs, name, aliases, more=()):
        return pl.pallas_call(
            body,
            grid=(steps,),
            in_specs=specs,
            out_specs=[
                pl.BlockSpec((nv, 2 * BLOCK, rows, LANES), lambda g: (first, g, 0, 0)),
                pl.BlockSpec((nv, rows, 2 * BLOCK, LANES), lambda g: (first, 0, g, 0)),
                pl.BlockSpec((2 * BLOCK // width, nv, 4 * width, LANES), lambda g: (g, first, 0, 0)),
                pl.BlockSpec((nv, 2 * BLOCK, 8, LANES), lambda g: (first, g, 0, 0)),
            ]
            + [full(s) for s in more],
            out_shape=[jax.ShapeDtypeStruct(s, f32) if n == 2 else pltpu.HBM(s, f32) for n, s in enumerate(shapes)]
            + [jax.ShapeDtypeStruct(s, f32) for s in more],
            scratch_shapes=[
                pltpu.VMEM((2, PAIRS * rows, 256), f32),
                pltpu.VMEM((2 * 768, 256), bf16),
                pltpu.VMEM((nvars, pieces, rows, LANES), f32),
            ],
            compiler_params=params(),
            cost_estimate=pl.CostEstimate(
                flops=nv * 60000000, bytes_accessed=nv * 3 * rows * merged * 4, transcendentals=0
            ),
            input_output_aliases=aliases,
            name=name,
        )(*arrays)

    ins = [scales.reshape(1, -1), classes.reshape(1, count), chi_coef.reshape(1, levels), sigma, vert] + [state] * 4
    specs = [full(x.shape) for x in ins[:5]] + [part(1, 0), part(1, 1), part(2, 0), part(2, 1)]
    ins = [in_hbm(x) for x in ins]
    body = functools.partial(lat_plain, rows, pairs)
    *wue, prm = lat_call(2, 0, body, ins, specs, "lat_chi_temp", {}, [(nvars, 4, LANES)])
    ins = [prm] + [in_hbm(x) for x in [sigma, vert, bal_temp] + [state] * 10] + [north, south, west, east]
    ins += [in_hbm(wue[0]), in_hbm(wue[1]), wue[2], in_hbm(wue[3])]
    specs = [full(x.shape) for x in ins[:4]] + [part(0, 0), part(0, 1), part(1, 0), part(1, 1)]

    def tile(side, step):
        last = 2 * pairs - 1
        return pl.BlockSpec(
            (1, rows, LANES), lambda g: (2, 0, jnp.clip(g * BLOCK + side * pairs + step, 0, last))
        )

    specs += [part(2, 0), part(2, 1), tile(0, -1), tile(0, BLOCK), tile(1, -1), tile(1, BLOCK)]
    specs += [full(x.shape) for x in (north, south, west, east)] + [anywhere] * 4
    aliases = {18: 0, 19: 1, 20: 2, 21: 3}
    w, u, edges, proj = lat_call(1, 2, functools.partial(lat_balance, rows, pairs), ins, specs, "lat_psi", aliases)
    def trade(x, axis):
        return lax.all_to_all(x, axis, split_axis=0, concat_axis=0, tiled=True)

    shares = trade(edges, "lat")

    rb = BLOCK
    local, el, es, rx, ry = pl.pallas_call(
        functools.partial(lon_kernel, rows, rb),
        grid=(rows // rb,),
        in_specs=[
            full(prm.shape),
            pl.BlockSpec((nvars, rb, half, LANES), lambda g: (0, g, 0, 0)),
        ],
        out_specs=[
            pl.BlockSpec((nvars, half, rb, LANES), lambda g: (0, 0, g, 0)),
            full((nvars, 4, rows, LANES)),
            full((6, rows, LANES)),
            full((nvars, 4, half, LANES)),
            full((nvars, 4, rows, LANES)),
        ],
        out_shape=[
            pltpu.HBM((nvars, half, rows, LANES), f32),
            pltpu.HBM((nvars, 4, rows, LANES), f32),
            jax.ShapeDtypeStruct((6, rows, LANES), f32),
            pltpu.HBM((nvars, 4, half, LANES), f32),
            pltpu.HBM((nvars, 4, rows, LANES), f32),
        ],
        compiler_params=params(),
        cost_estimate=pl.CostEstimate(
            flops=180000000, bytes_accessed=6 * rows * merged * 4, transcendentals=0
        ),
        name="lon_tile",
    )(prm, in_hbm(u))

    def round_lon(x):
        return [x] + [
            lax.ppermute(x, "lon", [(i, i ^ s) for i in range(n_lon)]) for s in range(1, n_lon)
        ]

    shares, _ = lax.optimization_barrier((shares, es))
    sent = round_lon(es)
    carries = pl.pallas_call(
        functools.partial(solve_kernel, n_lat, rows),
        grid=(1,),
        in_specs=[full(prm.shape), full(shares.shape)],
        out_specs=full(shares.shape),
        out_shape=jax.ShapeDtypeStruct(shares.shape, f32),
        compiler_params=params(),
        cost_estimate=pl.CostEstimate(flops=1000000, bytes_accessed=2 * shares.size * 4, transcendentals=0),
        name="solve",
    )(prm, shares)
    carries = trade(carries, "lat")

    packed = 2 * PAIRS

    def columns(r):
        return pl.BlockSpec((nvars, packed, r, LANES), lambda g: (0, g, 0, 0))

    def energy_call(nv, first, table, name):
        def block(r):
            return pl.BlockSpec((nv, packed, r, LANES), lambda g: (first, g, 0, 0))

        return pl.pallas_call(
            functools.partial(energy_kernel, rows, 24),
            grid=(half // packed,),
            in_specs=[
                block(rows),
                block(rows),
                pl.BlockSpec((nv, 4, half, LANES), lambda g: (first, 0, 0, 0)),
            ],
            out_specs=[full((nv, 4, rows, LANES)), full((nv, 8, LANES))],
            out_shape=[pltpu.HBM((nv, 4, rows, LANES), f32), pltpu.HBM((nv, 8, LANES), f32)],
            compiler_params=params(),
            cost_estimate=pl.CostEstimate(
                flops=nv * 7000000, bytes_accessed=2 * nv * rows * merged * 4, transcendentals=0
            ),
            name=name,
        )(in_hbm(w), in_hbm(local), in_hbm(table))

    px, dots = energy_call(2, 0, rx, "energy_chi_temp")
    carries, _ = lax.optimization_barrier((carries, px))

    crossed, elc, esc = pl.pallas_call(
        carry_kernel,
        grid=(1,),
        in_specs=[full(prm.shape), pl.BlockSpec((1, rows, lon), lambda g: (0, 0, 0)), full(carries.shape)],
        out_specs=[full((nvars, half, 8, LANES)), full((nvars, 4, 8, LANES)), full((7, 8, LANES))],
        out_shape=[
            jax.ShapeDtypeStruct((nvars, half, 8, LANES), f32),
            jax.ShapeDtypeStruct((nvars, 4, 8, LANES), f32),
            jax.ShapeDtypeStruct((7, 8, LANES), f32),
        ],
        compiler_params=params(),
        cost_estimate=pl.CostEstimate(
            flops=30000000, bytes_accessed=4 * nvars * 12 * half * LANES, transcendentals=0
        ),
        name="lon_carry",
    )(prm, in_hbm(sigma), carries)
    sent_x = round_lon(esc)
    table, _ = lax.optimization_barrier((rx, esc))
    px0, dots0 = energy_call(1, 2, table, "energy_psi")

    index = jnp.arange(count, dtype=jnp.int32)
    same = (owner[:, None] == owner[None, :]) & (index[None, :] < index[:, None])
    target = (owner * capacity + jnp.sum(same.astype(jnp.int32), axis=1)).reshape(1, count)

    ins = [in_hbm(x) for x in (proj, px, dots, px0, dots0, rx, ry, el)]
    ins = [place, target, prm, crossed] + ins + [elc] + sent + sent_x
    specs = [full(x.shape) for x in ins]
    specs[0] = pl.BlockSpec(memory_space=pltpu.SMEM)
    shapes = [(nvars, 4, rows, LANES), (nvars, half, 8, LANES), (2, rows, LANES), (2, rows, LANES)]
    carry, crossed, col, side, table = pl.pallas_call(
        functools.partial(close_kernel, n_lon, rows, devices, capacity, devices * rows * lon),
        grid=(1,),
        in_specs=specs,
        out_specs=[full(x) for x in shapes] + [full((devices, LANES))],
        out_shape=[pltpu.HBM(x, f32) for x in shapes] + [jax.ShapeDtypeStruct((devices, LANES), f32)],
        scratch_shapes=[pltpu.VMEM((n_lon, 6, rows, LANES), f32), pltpu.VMEM((n_lon, 7, 8, LANES), f32)],
        compiler_params=params(),
        cost_estimate=pl.CostEstimate(flops=10000000, bytes_accessed=4000000, transcendentals=0),
        name="close",
    )(*ins)
    table = trade(table, ("lat", "lon"))
    slab_energy = jnp.sum(table, axis=0, keepdims=True)[:, :capacity]

    ins = [prm, sigma, north, south, vert, bal_temp, col, side, carry, rx, ry, local, crossed]
    ins = [place] + [in_hbm(x) for x in ins]
    specs = [full(x.shape) for x in ins]
    specs[0] = pl.BlockSpec(memory_space=pltpu.SMEM)
    specs[-2:] = [columns(rows), columns(8)]
    applied = pl.pallas_call(
        functools.partial(end_kernel, rows, pairs, 24),
        grid=(half // packed,),
        in_specs=specs,
        out_specs=anywhere,
        out_shape=jax.ShapeDtypeStruct(state.shape, f32),
        scratch_shapes=[
            pltpu.VMEM(state.shape, f32),
            pltpu.VMEM((nvars, PAIRS * rows, 256), f32),
            pltpu.VMEM((8, merged), f32),
            pltpu.VMEM((2, rows, LANES), f32),
            pltpu.VMEM((4 * 768, 256), bf16),
            pltpu.VMEM((nvars, pieces, rows, LANES), f32),
            pltpu.VMEM((pieces, 8, LANES), f32),
            pltpu.SemaphoreType.DMA((3, 2, pairs // PAIRS)),
        ],
        compiler_params=params(),
        cost_estimate=pl.CostEstimate(
            flops=300000000, bytes_accessed=6 * rows * merged * 4, transcendentals=0
        ),
        name="finish",
    )(*ins)
    return (applied, slab_energy)


def solution(mesh):
    return jax.shard_map(
        shards,
        mesh=mesh,
        in_specs=(P(None, "lat", "lon"), P(None, "lat", "lon"), P(), P(), P(), P(), P(), P()),
        out_specs=(P(None, "lat", "lon"), P(("lat", "lon"), None)),
        check_vma=False,
    )
```
